128 devices in a mesh: band: 32 (over x, z, core), level: 4 (over y).
Axes of the slice: x: 4, y: 4, z: 4, core: 2. Of those that a mesh axis runs over, the one named last changes fastest.
Arguments:
- lower_nodes: bfloat16 [393216, 64], P(('band', 'level')), may hold values from -6 to 6
- latent: bfloat16 [98304, 64], P(('band', 'level')), may hold values from -6 to 6
- up_feat: bfloat16 [786432, 64], P(('band', 'level')), may hold values from -6 to 6
- down_feat: bfloat16 [786432, 64], P(('band', 'level')), may hold values from -6 to 6
- up_send: int32 [1536, 128], P(('band', 'level')), may hold values from 0 to 3071
- up_counts: int32 [128, 12], P(('band', 'level')), may hold values from 0 to 128, as said below
- up_senders: int32 [786432], P(('band', 'level')), may hold values from 0 to 1535, as said below
- up_targets: int32 [786432], P(('band', 'level')), may hold values from 0 to 767
- down_send: int32 [1536, 128], P(('band', 'level')), may hold values from 0 to 767
- down_counts: int32 [128, 12], P(('band', 'level')), may hold values from 0 to 128, as said below
- down_senders: int32 [786432], P(('band', 'level')), may hold values from 0 to 1535, as said below
- down_targets: int32 [786432], P(('band', 'level')), may hold values from 0 to 3071
- edge_w1: bfloat16 [2, 192, 64], replicated, may hold values from -0.4375 to 0.4375
- edge_w2: bfloat16 [2, 64, 64], replicated, may hold values from -0.75 to 0.75
- node_w1: bfloat16 [2, 128, 64], replicated, may hold values from -0.5 to 0.5
- node_w2: bfloat16 [2, 64, 64], replicated, may hold values from -0.75 to 0.75
- biases: float32 [2, 6, 64], replicated, may hold values from -1.5 to 1.5
- norm_gains: float32 [2, 2, 64], replicated, may hold values from 0.5 to 1.5
- lower_cot: float32 [393216, 64], P(('band', 'level')), may hold values from -6 to 6
- upper_cot: float32 [98304, 64], P(('band', 'level')), may hold values from -6 to 6
Outputs:
- lower_out: float32 [393216, 64], P(('band', 'level'))
- upper_out: float32 [98304, 64], P(('band', 'level'))
- grad_lower: float32 [393216, 64], P(('band', 'level'))
- grad_latent: float32 [98304, 64], P(('band', 'level'))
- grad_up_feat: float32 [786432, 64], P(('band', 'level'))
- grad_down_feat: float32 [786432, 64], P(('band', 'level'))
- grad_edge_w1: float32 [2, 192, 64], replicated
- grad_edge_w2: float32 [2, 64, 64], replicated
- grad_node_w1: float32 [2, 128, 64], replicated
- grad_node_w2: float32 [2, 64, 64], replicated
- grad_biases: float32 [2, 6, 64], replicated
- grad_gains: float32 [2, 2, 64], replicated
The draws below stay inside these ranges and needn't reach their ends.
Inputs may be any that keep to these rules, and one draw needn't show every extreme that they name: `up_counts`: 0 exactly where band (band of d) + k - 1 lies outside the grid, else 1 to 128; 128 in some entry of every row. `up_senders`: every edge reads a live slot: q mod 128 < up_counts[d, q // 128]; the most and 0 are reached. `down_counts`: 0 exactly where band (band of d) + k - 1 lies outside the grid, else 1 to 128; 128 in some entry of every row. `down_senders`: every edge reads a live slot: q mod 128 < down_counts[d, q // 128]; the most and 0 are reached.
All inputs are finite; a program needn't handle non-finite values.
Results may differ from the reference program's by a relative error of at most 0.02.
Values may be sent and summed in bfloat16 or wider, within the bound.
No kernel may reach another device: no remote copies, remote signals or barrier semaphores. Data moves between devices by JAX's collectives and lax.ppermute only.
A program may use at most 128 MiB of HBM per device.

```python
import jax
import jax.numpy as jnp
from jax import lax

D = 64
NL = 3072
CAP = 128
NU = 768
EDGES = 6144
BANDS = 32
LEVELS = 4
PEERS = 12
NL_ALL = 393216
NU_ALL = 98304
EDGES_ALL = 786432
DEVICES = 128


def count_table(key, salt):
    key = jax.random.fold_in(key, salt)
    first_key, second_key, third_key = jax.random.split(key, 3)
    values = jax.random.randint(first_key, (DEVICES, PEERS), 1, CAP + 1, dtype=jnp.int32)
    device_ids = jnp.arange(DEVICES, dtype=jnp.int32)
    band_ids = device_ids // LEVELS
    offsets = jnp.arange(PEERS, dtype=jnp.int32) // LEVELS
    source_band = band_ids[:, None] + offsets[None, :] - 1
    valid = (source_band >= 0) & (source_band < BANDS)
    picked_offset = jax.random.randint(second_key, (DEVICES,), 0, 3, dtype=jnp.int32)
    picked_band = band_ids + picked_offset - 1
    picked_offset = jnp.where((picked_band >= 0) & (picked_band < BANDS), picked_offset, 1)
    picked_level = jax.random.randint(third_key, (DEVICES,), 0, LEVELS, dtype=jnp.int32)
    chosen = picked_offset * LEVELS + picked_level
    chosen = jnp.where(device_ids == 0, PEERS - 1, chosen)
    columns = jnp.arange(PEERS, dtype=jnp.int32)
    values = jnp.where(columns[None, :] == chosen[:, None], CAP, values)
    return jnp.where(valid, values, 0).astype(jnp.int32)


def live_senders(counts, key):
    totals = jnp.sum(counts, axis=1)
    picks = jax.random.randint(key, (DEVICES, EDGES), 0, totals[:, None], dtype=jnp.int32)
    running = jnp.cumsum(counts, axis=1).astype(jnp.int32)
    starts = running - counts
    peer_pick = jnp.sum((running[:, None, :] <= picks[:, :, None]).astype(jnp.int32), axis=2)
    within = picks - jnp.take_along_axis(starts, peer_pick, axis=1)
    flat = (peer_pick * CAP + within).astype(jnp.int32).reshape(-1)
    flat = flat.at[0].set(PEERS * CAP - 1)
    flat = flat.at[DEVICES * EDGES - 1].set(0)
    return flat.astype(jnp.int32)


def draw_up_counts(key, part):
    return count_table(key, 21)


def draw_down_counts(key, part):
    return count_table(key, 22)


def draw_up_senders(key, part):
    counts = count_table(key, 21)
    key = jax.random.fold_in(key, 31)
    return live_senders(counts, key)


def draw_down_senders(key, part):
    counts = count_table(key, 22)
    key = jax.random.fold_in(key, 32)
    return live_senders(counts, key)


def plant(entries, own_key, least, high):
    spot = [jax.random.randint(jax.random.fold_in(own_key, axis), (), 0, length) for axis, length in enumerate(entries.shape)]
    longest = entries.shape.index(max(entries.shape))
    beside = spot[:longest] + [(spot[longest] + 1) % entries.shape[longest]] + spot[longest + 1:]
    return entries.at[tuple(spot)].set(least).at[tuple(beside)].set(high)


def level_of(own_key, shape, shards, least, top_value):
    def one(position, blocks):
        heights = jax.random.uniform(jax.random.fold_in(jax.random.fold_in(own_key, 6), position), (blocks,), jnp.float32, least / len(shards), top_value / len(shards))
        return jnp.repeat(jnp.exp(heights), shape[position] // blocks).reshape((-1,) + (1,) * (len(shape) - position - 1))

    level = one(*shards[0])
    for cut in shards[1:]:
        level = level * one(*cut)
    return level


def noise(rng, shape, scale, bound, cuts=(), kind=jnp.bfloat16):
    drawn = jax.random.normal(rng, shape, jnp.float32) * scale
    if len(cuts) > 0:
        drawn = level_of(rng, shape, cuts, -0.22, 0.18) * drawn
    return jnp.clip(drawn, min=-bound, max=bound).astype(kind)


def setup_inputs(seed: int = 0) -> dict:
    arg_keys = jax.random.split(jax.random.key(seed), 21)
    lower_nodes = noise(arg_keys[0], (NL_ALL, D), 1.0, 6.0, ((0, 128),))
    latent = noise(arg_keys[1], (NU_ALL, D), 1.0, 6.0, ((0, 128),))
    up_feat = noise(arg_keys[2], (EDGES_ALL, D), 1.0, 6.0, ((0, 128),))
    down_feat = noise(arg_keys[3], (EDGES_ALL, D), 1.0, 6.0, ((0, 128),))
    up_send = plant(jax.random.randint(arg_keys[4], (DEVICES * PEERS, CAP), 0, NL), jax.random.fold_in(arg_keys[4], 1), 0, NL - 1).astype(jnp.int32)
    up_counts = draw_up_counts(jax.random.fold_in(arg_keys[20], 71), 0)
    up_senders = draw_up_senders(jax.random.fold_in(arg_keys[20], 71), 0)
    up_targets = plant(jax.random.randint(arg_keys[7], (EDGES_ALL,), 0, NU), jax.random.fold_in(arg_keys[7], 1), 0, NU - 1).astype(jnp.int32)
    down_send = plant(jax.random.randint(arg_keys[8], (DEVICES * PEERS, CAP), 0, NU), jax.random.fold_in(arg_keys[8], 1), 0, NU - 1).astype(jnp.int32)
    down_counts = draw_down_counts(jax.random.fold_in(arg_keys[20], 71), 0)
    down_senders = draw_down_senders(jax.random.fold_in(arg_keys[20], 71), 0)
    down_targets = plant(jax.random.randint(arg_keys[11], (EDGES_ALL,), 0, NL), jax.random.fold_in(arg_keys[11], 1), 0, NL - 1).astype(jnp.int32)
    edge_w1 = noise(arg_keys[12], (2, 3 * D, D), (3 * D) ** -0.5, 0.4375)
    edge_w2 = noise(arg_keys[13], (2, D, D), D ** -0.5, 0.75)
    node_w1 = noise(arg_keys[14], (2, 2 * D, D), (2 * D) ** -0.5, 0.5)
    node_w2 = noise(arg_keys[15], (2, D, D), D ** -0.5, 0.75)
    biases = noise(arg_keys[16], (2, 6, D), 0.3, 1.5, (), jnp.float32)
    norm_gains = jnp.clip(1.0 + 0.1 * jax.random.normal(arg_keys[17], (2, 2, D), jnp.float32), 0.5, 1.5)
    lower_cot = noise(arg_keys[18], (NL_ALL, D), 1.0, 6.0, ((0, 128),), jnp.float32)
    upper_cot = noise(arg_keys[19], (NU_ALL, D), 1.0, 6.0, ((0, 128),), jnp.float32)
    return dict(lower_nodes=lower_nodes, latent=latent, up_feat=up_feat, down_feat=down_feat, up_send=up_send, up_counts=up_counts, up_senders=up_senders, up_targets=up_targets, down_send=down_send, down_counts=down_counts, down_senders=down_senders, down_targets=down_targets, edge_w1=edge_w1, edge_w2=edge_w2, node_w1=node_w1, node_w2=node_w2, biases=biases, norm_gains=norm_gains, lower_cot=lower_cot, upper_cot=upper_cot)


@jax.custom_vjp
def low(v):
    return lax.optimization_barrier(v.astype(jnp.bfloat16)).astype(jnp.float32)

@jax.custom_vjp
def low_back(v):
    return v

def low_keep(v):
    return (low(v), None)

def low_pass(kept, grad):
    return (grad,)

def back_keep(v):
    return (v, None)

def back_low(kept, grad):
    return (low(grad),)
low.defvjp(low_keep, low_pass)
low_back.defvjp(back_keep, back_low)
EPSILON = 1e-05

def layer_norm(values, gain_row, shift_row):
    centre = values - lax.optimization_barrier(jnp.mean(values, axis=-1, keepdims=True))
    spread = lax.optimization_barrier(jnp.mean(centre * centre, axis=-1, keepdims=True))
    return centre * lax.rsqrt(spread + EPSILON) * gain_row + shift_row

def matmul(left_side, right_side):
    return jnp.dot(left_side, right_side, precision=lax.Precision.HIGHEST, preferred_element_type=jnp.float32)

def slot_sources(send_table, source_rows):
    devices = BANDS * LEVELS
    capacity = send_table.shape[1]
    device_ids = jnp.arange(devices, dtype=jnp.int32)
    band_ids = device_ids // LEVELS
    level_ids = device_ids % LEVELS
    offsets = jnp.arange(3, dtype=jnp.int32)
    levels = jnp.arange(LEVELS, dtype=jnp.int32)
    source_band = band_ids[:, None, None] + offsets[None, :, None] - 1
    valid = (source_band >= 0) & (source_band < BANDS)
    source_device = (jnp.clip(source_band, 0, BANDS - 1) * LEVELS + levels[None, None, :]).astype(jnp.int32)
    table_rows = (source_device * PEERS + (2 - offsets)[None, :, None] * LEVELS + level_ids[:, None, None]).astype(jnp.int32)
    local_ids = send_table[table_rows.reshape(-1)].reshape(devices, 3, LEVELS, capacity)
    global_ids = (source_device[..., None] * source_rows + local_ids).astype(jnp.int32)
    valid_rows = jnp.broadcast_to(valid[..., None], (devices, 3, LEVELS, capacity)).astype(jnp.float32)
    return (global_ids.reshape(devices, -1), valid_rows.reshape(devices, -1))

def sweep_layer(params, sources, receivers, features, send_table, counts, senders, targets, source_rows, target_rows):
    edge_one, edge_two, node_one, node_two, biases, gain_rows = params
    devices = counts.shape[0]
    capacity = send_table.shape[1]
    slot_ids, slot_valid = slot_sources(send_table, source_rows)

    def device_step(device_items):
        row_ids, valid_rows, limits, feature_rows, sender_ids, target_ids, local_rows = device_items
        slot_rows = low_back(sources[row_ids] * valid_rows[:, None])
        alive_mask = (sender_ids % capacity < limits[sender_ids // capacity]).astype(jnp.float32)[:, None]
        joined = jnp.concatenate([feature_rows, slot_rows[sender_ids], local_rows[target_ids]], axis=1)
        pre_first = low_back(matmul(joined, edge_one) + biases[0])
        pre_second = low_back(matmul(low(jax.nn.silu(pre_first)), edge_two) + biases[1])
        messages = layer_norm(pre_second, gain_rows[0], biases[2]) * alive_mask
        summed = jax.ops.segment_sum(messages, target_ids, num_segments=target_rows)
        node_input = jnp.concatenate([local_rows, low(summed)], axis=1)
        node_first = low_back(matmul(node_input, node_one) + biases[3])
        node_second = low_back(matmul(low(jax.nn.silu(node_first)), node_two) + biases[4])
        return local_rows + layer_norm(node_second, gain_rows[1], biases[5])
    width_cols = receivers.shape[1]
    results = lax.map(jax.checkpoint(device_step), (slot_ids, slot_valid, counts, features.reshape(devices, -1, width_cols), senders.reshape(devices, -1), targets.reshape(devices, -1), receivers.reshape(devices, target_rows, width_cols)))
    return results.reshape(devices * target_rows, width_cols)

def reference(lower_nodes, latent, up_feat, down_feat, up_send, up_counts, up_senders, up_targets, down_send, down_counts, down_senders, down_targets, edge_w1, edge_w2, node_w1, node_w2, biases, norm_gains, lower_cot, upper_cot):

    def forward(lower_value, latent_value, up_value, down_value, first_edge, second_edge, first_node, second_node, bias_value, gain_value):
        upper_new = sweep_layer((first_edge[0], second_edge[0], first_node[0], second_node[0], bias_value[0], gain_value[0]), lower_value, latent_value, up_value, up_send, up_counts, up_senders, up_targets, NL, NU)
        lower_new = sweep_layer((first_edge[1], second_edge[1], first_node[1], second_node[1], bias_value[1], gain_value[1]), low(upper_new), lower_value, down_value, down_send, down_counts, down_senders, down_targets, NU, NL)
        return (lower_new, upper_new)
    floats = (lower_nodes.astype(jnp.float32), latent.astype(jnp.float32), up_feat.astype(jnp.float32), down_feat.astype(jnp.float32), edge_w1.astype(jnp.float32), edge_w2.astype(jnp.float32), node_w1.astype(jnp.float32), node_w2.astype(jnp.float32), biases.astype(jnp.float32), norm_gains.astype(jnp.float32))
    outputs, pullback = jax.vjp(forward, *floats)
    gradients = pullback((lower_cot.astype(jnp.float32), upper_cot.astype(jnp.float32)))
    return (outputs[0], outputs[1], gradients[0], gradients[1], gradients[2], gradients[3], gradients[4], gradients[5], gradients[6], gradients[7], gradients[8], gradients[9])
```

```python
import functools

import jax
import jax.numpy as jnp
from jax import lax
from jax.experimental import pallas as pl
from jax.experimental.pallas import tpu as pltpu
from jax.sharding import PartitionSpec as P

EPSILON = 1e-05
F32 = jnp.float32
B16 = jnp.bfloat16
D = 64
SLOT_GROUPS, SLOT_COLS = 6, 256
EDGE_BLOCK = 1024
VMEM_BYTES = 56 * 1024 * 1024


def groups_of(rows):
    return (4, rows // 4) if rows > 1024 else (rows // 256, 256)


def dot(a, b):
    return jnp.dot(a, b, preferred_element_type=F32)


def dot_rows(a, b):
    return lax.dot_general(a, b, (((1,), (1,)), ((), ())), preferred_element_type=F32)


def halves(x):
    high = x.astype(B16)
    return high, (x - high.astype(F32)).astype(B16)


def one_hot(column, n):
    rows = lax.broadcasted_iota(jnp.int16, (n, column.shape[1]), 0)
    return jnp.where(rows == column.astype(jnp.int16), jnp.ones((), B16), jnp.zeros((), B16))


def place(index, groups, n):
    group = jnp.zeros_like(index)
    for j in range(1, groups):
        group = group + (index >= j * n).astype(jnp.int32)
    return group, index - group * n


def slot_place(senders, level):
    distance = (level - ((senders >> 7) & 3)) & 3
    block = distance * 3 + (senders >> 9)
    return block >> 1, ((block & 1) << 7) | (senders & 127)


def live(senders, counts_ref):
    peer = senders >> 7
    limit = jnp.zeros_like(senders)
    for j in range(counts_ref.shape[1]):
        limit = jnp.where(peer == j, counts_ref[0, j], limit)
    return ((senders & 127) < limit).astype(F32)


def choose(stacked, group, groups):
    picked = stacked[0:D]
    for j in range(1, groups):
        picked = jnp.where(group == j, stacked[j * D : (j + 1) * D], picked)
    return picked


def pick(table, group, column, groups, n):
    return choose(dot(table[...], one_hot(column, n)), group, groups).astype(B16)


def spread(values, group, groups):
    wide = jnp.broadcast_to(group.astype(jnp.int16), values.shape)
    nothing = jnp.zeros_like(values)
    return jnp.concatenate([jnp.where(wide == j, values, nothing) for j in range(groups)], axis=0)


def add_at(total, values, group, column, groups, n):
    total[...] += dot_rows(spread(values, group, groups), one_hot(column, n))


def pack_table(table, source, groups, n):
    for j in range(groups):
        table[j * D : (j + 1) * D, :] = source[:, j * n : (j + 1) * n]


def columns_of(biases_ref, gains_ref, k):
    return jnp.concatenate([biases_ref[k], gains_ref[k]], axis=0).T


def fold(values):
    total = values[:, 0:128]
    for i in range(128, values.shape[1], 128):
        total = total + values[:, i : i + 128]
    return total


def norm_parts(values):
    centre = values - jnp.sum(values, axis=0, keepdims=True) * (1.0 / D)
    spread_sum = jnp.sum(centre * centre, axis=0, keepdims=True) * (1.0 / D)
    factor = lax.rsqrt(spread_sum + EPSILON)
    return centre * factor, factor


def norm_back(grad, normed, factor, gain):
    scaled = grad * gain
    first = jnp.sum(scaled, axis=0, keepdims=True) * (1.0 / D)
    second = jnp.sum(scaled * normed, axis=0, keepdims=True) * (1.0 / D)
    return factor * (scaled - first - normed * second)


def sigmoid(values):
    return 0.5 * jnp.tanh(0.5 * values) + 0.5


def send_rows(send_ref, k, level):
    return jnp.concatenate(
        [send_ref[pl.ds(k * 4 + ((level + d) & 3), 1), :] for d in range(4)], axis=1
    )


def send_blocks(outs, table, send_ref, level, groups, n):
    for k in range(3):
        group, column = place(send_rows(send_ref, k, level), groups, n)
        rows = pick(table, group, column, groups, n)
        for d in range(4):
            outs[k][d] = rows[:, d * 128 : (d + 1) * 128]


def add_back(total, blocks, send_ref, level, groups, n):
    for k in range(3):
        group, column = place(send_rows(send_ref, k, level), groups, n)
        values = jnp.concatenate([blocks[k][d] for d in range(4)], axis=1)
        add_at(total, values, group, column, groups, n)


def slot_table(table, received):
    for t in range(12):
        table[(t >> 1) * D : ((t >> 1) + 1) * D, (t & 1) * 128 : ((t & 1) + 1) * 128] = received[t // 3][t % 3]


def slot_gradients(outs, sums, weight):
    for j in range(SLOT_GROUPS):
        high, low = halves(sums[j * D : (j + 1) * D, :])
        grads = (dot(weight, high) + dot(weight, low)).astype(B16)
        for t in (2 * j, 2 * j + 1):
            outs[t // 3][t % 3] = grads[:, (t & 1) * 128 : ((t & 1) + 1) * 128]


def over_blocks(total, block, body):
    def step(i, carry):
        body(pl.ds(pl.multiple_of(i * block, block), block))
        return carry

    lax.fori_loop(0, total // block, step, 0)


def send_kernel(level_ref, send_ref, source_ref, down_ref, own_ref, up_ref, table):
    groups, n = groups_of(source_ref.shape[1])
    pack_table(table, source_ref, groups, n)
    send_blocks((down_ref, own_ref, up_ref), table, send_ref, level_ref[0], groups, n)


def part_kernel(k, targets_ref, feat_ref, local_ref, w1_ref, biases_ref, gains_ref, part_ref, table):
    groups, n = groups_of(local_ref.shape[1])
    pack_table(table, local_ref, groups, n)
    columns = columns_of(biases_ref, gains_ref, k)
    weight = jnp.concatenate([w1_ref[k, :, 0:D], w1_ref[k, :, 2 * D : 3 * D]], axis=1)

    def body(s):
        group, column = place(targets_ref[:, s], groups, n)
        picked = pick(table, group, column, groups, n)
        part_ref[:, s] = dot(weight, jnp.concatenate([feat_ref[:, s], picked], axis=0)) + columns[:, 0:1]

    over_blocks(feat_ref.shape[1], EDGE_BLOCK, body)


def edges_forward(k, level, counts_ref, senders_ref, targets_ref, part_ref, table, w1_ref, w2_ref, columns, total, groups, n,
                  slope_ref, normed_ref, hidden_ref, factor_ref, alive_ref):
    weight_slot = w1_ref[k, :, D : 2 * D]
    weight_two = w2_ref[k].astype(F32).T.astype(B16)
    total[...] = jnp.zeros_like(total)

    def body(s):
        senders = senders_ref[:, s]
        group, column = slot_place(senders, level)
        picked = pick(table, group, column, SLOT_GROUPS, SLOT_COLS)
        first = part_ref[:, s] + dot(weight_slot, picked)
        gate = sigmoid(first)
        hidden = (first * gate).astype(B16)
        slope_ref[:, s] = gate * (1.0 + first * (1.0 - gate))
        hidden_ref[:, s] = hidden
        normed, factor = norm_parts(dot(weight_two, hidden) + columns[:, 1:2])
        alive = live(senders, counts_ref)
        normed_ref[:, s] = normed
        factor_ref[:, s] = factor
        alive_ref[:, s] = alive
        messages = ((normed * columns[:, 6:7] + columns[:, 2:3]) * alive).astype(B16)
        group, column = place(targets_ref[:, s], groups, n)
        add_at(total, messages, group, column, groups, n)

    over_blocks(senders_ref.shape[1], EDGE_BLOCK, body)


def node_forward(k, inputs, wn1_ref, weight_two, columns):
    first = dot(wn1_ref[k], inputs) + columns[:, 3:4]
    gate = sigmoid(first)
    hidden = (first * gate).astype(B16)
    slope = gate * (1.0 + first * (1.0 - gate))
    normed, factor = norm_parts(dot(weight_two, hidden) + columns[:, 4:5])
    return hidden, slope, normed, factor


def node_backward(grad, inputs, hidden, slope, normed, factor, wn2, weight_local, columns, node_grads):
    one_ref, two_ref, sums_ref = node_grads
    second = norm_back(grad, normed, factor, columns[:, 7:8]).astype(B16)
    first = (dot(wn2, second) * slope).astype(B16)
    sums_ref[0] += fold(first.astype(F32))
    sums_ref[1] += fold(second.astype(F32))
    sums_ref[2] += fold(grad)
    sums_ref[3] += fold(grad * normed)
    two_ref[...] += dot_rows(hidden, second)
    one_ref[...] += dot_rows(first, inputs)
    return first, grad + dot(weight_local, first)


def clear(refs):
    for ref in refs:
        ref[...] = jnp.zeros_like(ref)


def transposed(weight):
    return weight.astype(F32).T.astype(B16)


def edge_backward(grad_rows, s, k, columns, weight_sum, weight_two, alive_ref, slope_ref, normed_ref, factor_ref, sums_ref):
    grad = dot(weight_sum, grad_rows) * alive_ref[:, s]
    normed = normed_ref[:, s]
    second = norm_back(grad, normed, factor_ref[:, s], columns[:, 6:7]).astype(B16)
    first = (dot(weight_two, second) * slope_ref[:, s]).astype(B16)
    sums_ref[0] += fold(first.astype(F32))
    sums_ref[1] += fold(second.astype(F32))
    sums_ref[2] += fold(grad)
    sums_ref[3] += fold(grad * normed)
    return first, second


def pack_columns(edge_sums, node_sums):
    order = (edge_sums[0], edge_sums[1], edge_sums[2], node_sums[0], node_sums[1], node_sums[2], edge_sums[3], node_sums[3])
    columns = [jnp.sum(v, axis=1, keepdims=True) for v in order]
    lanes = lax.broadcasted_iota(jnp.int32, (D, D), 1)
    packed = jnp.zeros((D, D), F32)
    for i, column in enumerate(columns):
        packed = jnp.where(lanes == i, column, packed)
    return packed


def slot_weight_grads(sums, table):
    total = jnp.zeros((D, D), F32)
    for j in range(SLOT_GROUPS):
        high, low = halves(sums[j * D : (j + 1) * D, :])
        rows = table[j * D : (j + 1) * D, :]
        total = total + dot_rows(high, rows) + dot_rows(low, rows)
    return total


def target_grads(total, local_ref, weight, start_ref, out_ref, groups, n):
    grads = jnp.zeros((D, D), F32)
    for j in range(groups):
        high, low = halves(total[j * D : (j + 1) * D, :])
        s = slice(j * n, (j + 1) * n)
        rows = local_ref[:, s]
        grads = grads + dot_rows(high, rows) + dot_rows(low, rows)
        out_ref[:, s] = start_ref[:, s] + dot(weight, high) + dot(weight, low)
    return grads


def up_forward_kernel(level_ref, counts_ref, senders_ref, targets_ref, part_ref, r0, r1, r2, r3, local_ref, send_ref,
                      w1_ref, w2_ref, wn1_ref, wn2_ref, biases_ref, gains_ref,
                      out_ref, summed_ref, down_ref, own_ref, up_ref, slope_ref, normed_ref, hidden_ref, factor_ref, alive_ref,
                      slots, total, table):
    level = level_ref[0]
    groups, n = groups_of(local_ref.shape[1])
    columns = columns_of(biases_ref, gains_ref, 0)
    slot_table(slots, (r0, r1, r2, r3))
    edges_forward(0, level, counts_ref, senders_ref, targets_ref, part_ref, slots, w1_ref, w2_ref, columns, total, groups, n,
                  slope_ref, normed_ref, hidden_ref, factor_ref, alive_ref)
    weight_two = transposed(wn2_ref[0])
    for j in range(groups):
        s = slice(j * n, (j + 1) * n)
        local = local_ref[:, s]
        summed = total[j * D : (j + 1) * D, :].astype(B16)
        summed_ref[:, s] = summed
        unused, unused, normed, factor = node_forward(0, jnp.concatenate([local, summed], axis=0), wn1_ref, weight_two, columns)
        result = local.astype(F32) + normed * columns[:, 7:8] + columns[:, 5:6]
        out_ref[:, s] = result
        table[j * D : (j + 1) * D, :] = result.astype(B16)
    send_blocks((down_ref, own_ref, up_ref), table, send_ref, level, groups, n)


def down_kernel(level_ref, counts_ref, senders_ref, targets_ref, part_ref, r0, r1, r2, r3, local_ref, cot_ref,
                w1_ref, w2_ref, wn1_ref, wn2_ref, biases_ref, gains_ref,
                out_ref, g0, g1, g2, g3, first_ref, second_ref, hidden_ref, grad_ref, sums_ref, edge_sums, node_sums, wn1_grad, wn2_grad,
                slots, total, table, slope_ref, normed_ref, factor_ref, alive_ref):
    level = level_ref[0]
    groups, n = groups_of(local_ref.shape[1])
    columns = columns_of(biases_ref, gains_ref, 1)
    slot_table(slots, (r0, r1, r2, r3))
    edges_forward(1, level, counts_ref, senders_ref, targets_ref, part_ref, slots, w1_ref, w2_ref, columns, total, groups, n,
                  slope_ref, normed_ref, hidden_ref, factor_ref, alive_ref)
    clear((wn1_grad, wn2_grad, node_sums, edge_sums, sums_ref))
    wn2 = wn2_ref[1]
    wn2_t = transposed(wn2)
    wn1 = transposed(wn1_ref[1])

    def node_step(j, carry):
        s = pl.ds(pl.multiple_of(j * n, n), n)
        rows = pl.ds(pl.multiple_of(j * D, D), D)
        local = local_ref[:, s]
        inputs = jnp.concatenate([local, total[rows, :].astype(B16)], axis=0)
        hidden, slope, normed, factor = node_forward(1, inputs, wn1_ref, wn2_t, columns)
        out_ref[:, s] = local.astype(F32) + normed * columns[:, 7:8] + columns[:, 5:6]
        first, grad_local = node_backward(cot_ref[:, s], inputs, hidden, slope, normed, factor, wn2, wn1[0:D], columns,
                                          (wn1_grad, wn2_grad, node_sums))
        table[rows, :] = first
        grad_ref[:, s] = grad_local
        return carry

    lax.fori_loop(0, groups, node_step, 0)
    weight_two = w2_ref[1]
    weight_slot = transposed(w1_ref[1, :, D : 2 * D])

    def body(s):
        group, column = place(targets_ref[:, s], groups, n)
        grad_rows = pick(table, group, column, groups, n)
        first, second = edge_backward(grad_rows, s, 1, columns, wn1[D : 2 * D], weight_two, alive_ref, slope_ref, normed_ref,
                                      factor_ref, edge_sums)
        first_ref[:, s] = first
        second_ref[:, s] = second
        group, column = slot_place(senders_ref[:, s], level)
        add_at(sums_ref, first, group, column, SLOT_GROUPS, SLOT_COLS)

    over_blocks(senders_ref.shape[1], EDGE_BLOCK, body)
    slot_gradients((g0, g1, g2, g3), sums_ref, weight_slot)


def down_rest_kernel(targets_ref, feat_ref, first_ref, second_ref, hidden_ref, local_ref, r0, r1, r2, r3, sums_ref, start_ref,
                     edge_sums, node_sums, wn1_grad, wn2_grad, w1_ref,
                     feat_grad_ref, grad_ref, packed_ref, slots, total, one_ref, two_ref):
    groups, n = groups_of(local_ref.shape[1])
    clear((total, one_ref, two_ref))
    w1 = transposed(w1_ref[1])
    slot_table(slots, (r0, r1, r2, r3))

    def body(s):
        first = first_ref[:, s]
        group, column = place(targets_ref[:, s], groups, n)
        add_at(total, first, group, column, groups, n)
        feat_grad_ref[:, s] = dot(w1[0:D], first)
        one_ref[...] += dot_rows(first, feat_ref[:, s])
        two_ref[...] += dot_rows(hidden_ref[:, s], second_ref[:, s])

    over_blocks(feat_ref.shape[1], EDGE_BLOCK, body)
    local_grads = target_grads(total, local_ref, w1[2 * D : 3 * D], start_ref, grad_ref, groups, n)
    slot_grads = slot_weight_grads(sums_ref, slots)
    write_packed(packed_ref, one_ref[...], slot_grads, local_grads, two_ref[...], wn1_grad[...], wn2_grad[...],
                 pack_columns(edge_sums, node_sums))


def write_packed(packed_ref, one, slot_grads, local_grads, two, wn1_grad, wn2_grad, columns):
    packed_ref[0] = jnp.concatenate([one, slot_grads, local_grads, two], axis=1)
    packed_ref[1] = jnp.concatenate([wn1_grad, wn2_grad, columns], axis=1)


def up_backward_kernel(level_ref, senders_ref, targets_ref, feat_ref, b0, b1, b2, send_ref, cot_ref, local_ref, summed_ref,
                       r0, r1, r2, r3, slope_ref, normed_ref, hidden_ref, factor_ref, alive_ref, packed_down_ref,
                       w1_ref, w2_ref, wn1_ref, wn2_ref, biases_ref, gains_ref,
                       g0, g1, g2, g3, first_ref, grad_ref, packed_ref,
                       slots, table, back, total, sums, start, one_ref, two_ref, edge_sums, node_sums, wn1_grad, wn2_grad, pieces):
    level = level_ref[0]
    groups, n = groups_of(local_ref.shape[1])
    columns = columns_of(biases_ref, gains_ref, 0)
    clear((back, total, sums, one_ref, two_ref, edge_sums, node_sums, wn1_grad, wn2_grad))
    slot_table(slots, (r0, r1, r2, r3))
    add_back(back, (b0, b1, b2), send_ref, level, groups, n)
    wn2 = wn2_ref[0]
    wn2_t = transposed(wn2)
    wn1 = transposed(wn1_ref[0])
    w1 = transposed(w1_ref[0])
    for j in range(groups):
        s = slice(j * n, (j + 1) * n)
        rows = slice(j * D, (j + 1) * D)
        inputs = jnp.concatenate([local_ref[:, s], summed_ref[:, s]], axis=0)
        hidden, slope, normed, factor = node_forward(0, inputs, wn1_ref, wn2_t, columns)
        first, grad_local = node_backward(cot_ref[:, s] + back[rows, :], inputs, hidden, slope, normed, factor, wn2, wn1[0:D],
                                          columns, (wn1_grad, wn2_grad, node_sums))
        table[rows, :] = first
        start[:, s] = grad_local
    weight_two = w2_ref[0]

    def body(s):
        group, column = place(targets_ref[:, s], groups, n)
        grad_rows = pick(table, group, column, groups, n)
        first, second = edge_backward(grad_rows, s, 0, columns, wn1[D : 2 * D], weight_two, alive_ref, slope_ref, normed_ref,
                                      factor_ref, edge_sums)
        first_ref[:, s] = first
        add_at(total, first, group, column, groups, n)
        group, column = slot_place(senders_ref[:, s], level)
        add_at(sums, first, group, column, SLOT_GROUPS, SLOT_COLS)
        one_ref[...] += dot_rows(first, feat_ref[:, s])
        two_ref[...] += dot_rows(hidden_ref[:, s], second)

    over_blocks(senders_ref.shape[1], EDGE_BLOCK, body)
    slot_gradients((g0, g1, g2, g3), sums, w1[D : 2 * D])
    local_grads = target_grads(total, local_ref, w1[2 * D : 3 * D], start, grad_ref, groups, n)
    slot_grads = slot_weight_grads(sums, slots)
    write_packed(pieces, one_ref[...], slot_grads, local_grads, two_ref[...], wn1_grad[...], wn2_grad[...],
                 pack_columns(edge_sums, node_sums))
    pieces[2] = packed_down_ref[0]
    pieces[3] = packed_down_ref[1]
    for d in range(4):
        packed_ref[d] = pieces[(level + d) & 3]


def feat_grad_kernel(first_ref, w1_ref, out_ref):
    weight = transposed(w1_ref[0, :, 0:D])

    def body(s):
        out_ref[:, s] = dot(weight, first_ref[:, s])

    over_blocks(first_ref.shape[1], EDGE_BLOCK, body)


def lower_grad_kernel(level_ref, b0, b1, b2, send_ref, start_ref, out_ref, total):
    groups, n = groups_of(start_ref.shape[1])
    clear((total,))
    add_back(total, (b0, b1, b2), send_ref, level_ref[0], groups, n)
    for j in range(groups):
        s = slice(j * n, (j + 1) * n)
        out_ref[:, s] = start_ref[:, s] + total[j * D : (j + 1) * D, :]


def unpack_kernel(level_ref, p0, p1, p2, p3, w1_ref, w2_ref, wn1_ref, wn2_ref, biases_ref, gains_ref, pieces):
    level = level_ref[0]
    for d, piece in enumerate((p0, p1, p2, p3)):
        pieces[(level - d) & 3] = piece[...]
    for k in range(2):
        w1_ref[k] = pieces[2 * k, :, 0 : 3 * D]
        w2_ref[k] = pieces[2 * k, :, 3 * D : 4 * D]
        wn1_ref[k] = pieces[2 * k + 1, :, 0 : 2 * D]
        wn2_ref[k] = pieces[2 * k + 1, :, 2 * D : 3 * D]
        rows = pieces[2 * k + 1, :, 3 * D : 4 * D].T
        biases_ref[k] = rows[0:6]
        gains_ref[k] = rows[6:8]


def shape(dims, dtype=F32):
    return jax.ShapeDtypeStruct(dims, dtype)


def call(kernel, name, outs, scratch, scalars=0):
    def run(*operands):
        specs = [
            pl.BlockSpec(memory_space=pltpu.SMEM) if i < scalars else pl.BlockSpec(memory_space=pltpu.VMEM)
            for i in range(len(operands))
        ]
        return pl.pallas_call(
            kernel,
            name=name,
            in_specs=specs,
            out_specs=jax.tree.map(lambda unused: pl.BlockSpec(memory_space=pltpu.VMEM), outs),
            out_shape=outs,
            scratch_shapes=scratch,
            compiler_params=pltpu.CompilerParams(vmem_limit_bytes=VMEM_BYTES),
        )(*operands)

    return run


def along_band(block, step):
    count = lax.axis_size("band")
    pairs = [(i, i + step) for i in range(count) if 0 <= i + step < count]
    return lax.ppermute(block, "band", pairs)


def along_level(block, step):
    count = lax.axis_size("level")
    return lax.ppermute(block, "level", [(i, (i + step) % count) for i in range(count)])


def deliver(down, own, up):
    low, high = along_band(up, 1), along_band(down, -1)
    stacked = [jnp.stack([low[d], own[d], high[d]]) for d in range(4)]
    return [stacked[0]] + [along_level(stacked[d], d) for d in (1, 2, 3)]


def give_back(blocks):
    blocks = [blocks[0]] + [along_level(blocks[d], -d) for d in (1, 2, 3)]
    low = jnp.stack([b[0] for b in blocks])
    own = jnp.stack([b[1] for b in blocks])
    high = jnp.stack([b[2] for b in blocks])
    return along_band(high, 1), own, along_band(low, -1)


def chip_axis(block, stride, length, step):
    count = lax.axis_size("band")
    pairs = []
    for i in range(count):
        at = (i // stride) % length
        pairs.append((i, i + (((at + step) % length) - at) * stride))
    return lax.ppermute(block, "band", pairs)


def reduce_all(pieces):
    total = pieces[0]
    for d in (1, 2, 3):
        total = total + along_level(pieces[d], d)
    count = lax.axis_size("band")
    stride = 1
    while stride < count:
        length = 2 if stride == 1 else 4
        length = min(length, count // stride)
        parts = [chip_axis(total, stride, length, d) for d in range(1, length)]
        for part in parts:
            total = total + part
        stride *= length
    return [total] + [along_level(total, d) for d in (1, 2, 3)]


def shards(
    lower_nodes, latent, up_feat, down_feat, up_send, up_counts, up_senders, up_targets,
    down_send, down_counts, down_senders, down_targets,
    edge_w1, edge_w2, node_w1, node_w2, biases, norm_gains, lower_cot, upper_cot,
):
    lower, upper = lower_nodes.T, latent.T
    feat_up, feat_down = up_feat.T, down_feat.T
    cot_lower, cot_upper = lower_cot.T, upper_cot.T
    w1, wn1 = edge_w1.transpose(0, 2, 1), node_w1.transpose(0, 2, 1)
    w2, wn2 = edge_w2, node_w2
    edges, lower_rows, upper_rows = up_feat.shape[0], lower_nodes.shape[0], latent.shape[0]
    senders_up, targets_up = up_senders.reshape(1, edges), up_targets.reshape(1, edges)
    senders_down, targets_down = down_senders.reshape(1, edges), down_targets.reshape(1, edges)
    level = lax.axis_index("level").astype(jnp.int32).reshape(1)

    lower_groups, lower_n = groups_of(lower_rows)
    upper_groups, upper_n = groups_of(upper_rows)
    lower_table, upper_table = (lower_groups * D, lower_n), (upper_groups * D, upper_n)
    slots = pltpu.VMEM((SLOT_GROUPS * D, SLOT_COLS), B16)
    block = shape((4, D, 128), B16)
    received = shape((3, D, 128), B16)
    wide32, wide16, row = shape((D, edges)), shape((D, edges), B16), shape((1, edges))

    sent = call(send_kernel, "send_lower", [block] * 3, [pltpu.VMEM(lower_table, B16)], 1)(level, up_send, lower)
    up_slots = deliver(*sent)
    part_up = call(functools.partial(part_kernel, 0), "part_up", wide32, [pltpu.VMEM(upper_table, B16)])(
        targets_up, feat_up, upper, w1, biases, norm_gains)
    part_down = call(functools.partial(part_kernel, 1), "part_down", wide32, [pltpu.VMEM(lower_table, B16)])(
        targets_down, feat_down, lower, w1, biases, norm_gains)
    (upper_new, summed_up, *sent, slope, normed, hidden, factor, alive) = call(
        up_forward_kernel, "up_forward",
        [shape((D, upper_rows)), shape((D, upper_rows), B16), block, block, block, wide32, wide32, wide16, row, row],
        [slots, pltpu.VMEM(upper_table, F32), pltpu.VMEM(upper_table, B16)], 2,
    )(level, up_counts, senders_up, targets_up, part_up, *up_slots, upper, down_send, w1, w2, wn1, wn2, biases, norm_gains)
    down_slots = deliver(*sent)
    sums_shape = shape((SLOT_GROUPS * D, SLOT_COLS))
    four = shape((4, D, 128))
    (lower_new, *slot_grads, first_down, second_down, hidden_down, start_lower, sums_down, edge_sums, node_sums, wn1_grad, wn2_grad) = call(
        down_kernel, "down_sweep",
        [shape((D, lower_rows))] + [received] * 4 + [wide16] * 3 + [shape((D, lower_rows)), sums_shape, four, four,
         shape((D, 2 * D)), shape((D, D))],
        [slots, pltpu.VMEM(lower_table, F32), pltpu.VMEM(lower_table, B16), pltpu.VMEM((D, edges), F32),
         pltpu.VMEM((D, edges), F32), pltpu.VMEM((1, edges), F32), pltpu.VMEM((1, edges), F32)], 2,
    )(level, down_counts, senders_down, targets_down, part_down, *down_slots, lower, cot_lower, w1, w2, wn1, wn2, biases, norm_gains)
    down_back = give_back(slot_grads)
    feat_grad_down, start_lower, packed_down = call(
        down_rest_kernel, "down_rest",
        [wide32, shape((D, lower_rows)), shape((2, D, 256))],
        [slots, pltpu.VMEM(lower_table, F32), pltpu.VMEM((D, D), F32), pltpu.VMEM((D, D), F32)],
    )(targets_down, feat_down, first_down, second_down, hidden_down, lower, *down_slots, sums_down, start_lower,
      edge_sums, node_sums, wn1_grad, wn2_grad, w1)
    (*slot_grads, first_up, grad_latent, packed) = call(
        up_backward_kernel, "up_backward",
        [received] * 4 + [wide16, shape((D, upper_rows)), shape((4, D, 256))],
        [slots, pltpu.VMEM(upper_table, B16), pltpu.VMEM(upper_table, F32), pltpu.VMEM(upper_table, F32),
         pltpu.VMEM((SLOT_GROUPS * D, SLOT_COLS), F32), pltpu.VMEM((D, upper_rows), F32),
         pltpu.VMEM((D, D), F32), pltpu.VMEM((D, D), F32), pltpu.VMEM((4, D, 128), F32), pltpu.VMEM((4, D, 128), F32),
         pltpu.VMEM((D, 2 * D), F32), pltpu.VMEM((D, D), F32), pltpu.VMEM((4, D, 256), F32)], 1,
    )(level, senders_up, targets_up, feat_up, *down_back, down_send, cot_upper, upper, summed_up, *up_slots,
      slope, normed, hidden, factor, alive, packed_down, w1, w2, wn1, wn2, biases, norm_gains)
    up_back = give_back(slot_grads)
    reduced = reduce_all([packed[d] for d in range(4)])
    feat_grad_up = call(feat_grad_kernel, "feat_grad_up", wide32, [])(first_up, w1)
    grad_lower = call(lower_grad_kernel, "lower_grad", shape((D, lower_rows)), [pltpu.VMEM(lower_table, F32)], 1)(
        level, *up_back, up_send, start_lower)
    w1_grad, w2_grad, wn1_grad, wn2_grad, bias_grad, gain_grad = call(
        unpack_kernel, "unpack",
        [shape((2, D, 3 * D)), shape((2, D, D)), shape((2, D, 2 * D)), shape((2, D, D)), shape((2, 6, D)), shape((2, 2, D))],
        [pltpu.VMEM((4, D, 256), F32)], 1)(level, *reduced)
    return (
        lower_new.T, upper_new.T, grad_lower.T, grad_latent.T, feat_grad_up.T, feat_grad_down.T,
        w1_grad.transpose(0, 2, 1), w2_grad, wn1_grad.transpose(0, 2, 1), wn2_grad, bias_grad, gain_grad,
    )


def solution(mesh):
    rows, index, whole = P(("band", "level"), None), P(("band", "level")), P()
    placed = (rows,) * 6 + (index, index) + (rows,) * 2 + (index, index) + (whole,) * 6 + (rows,) * 2
    return jax.shard_map(
        shards,
        mesh=mesh,
        in_specs=placed,
        out_specs=(rows,) * 6 + (whole,) * 6,
        check_vma=False,
    )
```

```python
import functools

import jax
import jax.numpy as jnp
from jax import lax
from jax.experimental import pallas as pl
from jax.experimental.pallas import tpu as pltpu
from jax.sharding import PartitionSpec as P

EPSILON = 1e-05
F32 = jnp.float32
B16 = jnp.bfloat16
D = 64
SLOT_GROUPS, SLOT_COLS = 6, 256
EDGE_BLOCK = 1024
VMEM_BYTES = 24 * 1024 * 1024


def groups_of(rows):
    return (4, rows // 4) if rows > 1024 else (rows // 256, 256)


def dot(a, b):
    return jnp.dot(a, b, preferred_element_type=F32)


def dot_rows(a, b):
    return lax.dot_general(a, b, (((1,), (1,)), ((), ())), preferred_element_type=F32)


def halves(x):
    high = x.astype(B16)
    return high, (x - high.astype(F32)).astype(B16)


def one_hot(column, n):
    rows = lax.broadcasted_iota(jnp.int16, (n, column.shape[1]), 0)
    return jnp.where(rows == column.astype(jnp.int16), jnp.ones((), B16), jnp.zeros((), B16))


def place(index, groups, n):
    group = jnp.zeros_like(index)
    for j in range(1, groups):
        group = group + (index >= j * n).astype(jnp.int32)
    return group, index - group * n


def slot_place(senders, level):
    distance = (level - ((senders >> 7) & 3)) & 3
    block = distance * 3 + (senders >> 9)
    return block >> 1, ((block & 1) << 7) | (senders & 127)


def live(senders, counts_ref):
    peer = senders >> 7
    limit = jnp.zeros_like(senders)
    for j in range(counts_ref.shape[1]):
        limit = jnp.where(peer == j, counts_ref[0, j], limit)
    return ((senders & 127) < limit).astype(F32)


def choose(stacked, group, groups):
    picked = stacked[0:D]
    for j in range(1, groups):
        picked = jnp.where(group == j, stacked[j * D : (j + 1) * D], picked)
    return picked


def pick(table, group, column, groups, n):
    return choose(dot(table[...], one_hot(column, n)), group, groups).astype(B16)


def spread(values, group, groups):
    wide = jnp.broadcast_to(group.astype(jnp.int16), values.shape)
    nothing = jnp.zeros_like(values)
    return jnp.concatenate([jnp.where(wide == j, values, nothing) for j in range(groups)], axis=0)


def add_at(total, values, group, column, groups, n):
    total[...] += dot_rows(spread(values, group, groups), one_hot(column, n))


def pack_table(table, source, groups, n):
    for j in range(groups):
        table[j * D : (j + 1) * D, :] = source[:, j * n : (j + 1) * n]


def columns_of(biases_ref, gains_ref, k):
    rows = [biases_ref[i, k : k + 1] for i in range(6)] + [gains_ref[k]]
    return jnp.concatenate(rows, axis=0).T


def fold(values):
    total = values[:, 0:128]
    for i in range(128, values.shape[1], 128):
        total = total + values[:, i : i + 128]
    return total


def norm_parts(values):
    centre = values - jnp.sum(values, axis=0, keepdims=True) * (1.0 / D)
    spread_sum = jnp.sum(centre * centre, axis=0, keepdims=True) * (1.0 / D)
    factor = lax.rsqrt(spread_sum + EPSILON)
    return centre * factor, factor


def norm_back(grad, normed, factor, gain):
    scaled = grad * gain
    first = jnp.sum(scaled, axis=0, keepdims=True) * (1.0 / D)
    second = jnp.sum(scaled * normed, axis=0, keepdims=True) * (1.0 / D)
    return factor * (scaled - first - normed * second)


def sigmoid(values):
    return 0.5 * jnp.tanh(0.5 * values) + 0.5


def send_rows(send_ref, k, level):
    return jnp.concatenate(
        [send_ref[pl.ds(k * 4 + ((level + d) & 3), 1), :] for d in range(4)], axis=1
    )


def send_blocks(outs, table, send_ref, level, groups, n):
    for k in range(3):
        group, column = place(send_rows(send_ref, k, level), groups, n)
        rows = pick(table, group, column, groups, n)
        for d in range(4):
            outs[d][k] = rows[:, d * 128 : (d + 1) * 128]


def add_back(total, blocks, send_ref, level, groups, n):
    for k in range(3):
        group, column = place(send_rows(send_ref, k, level), groups, n)
        values = jnp.concatenate([block_at(blocks, d, k) for d in range(4)], axis=1)
        add_at(total, values, group, column, groups, n)


def block_at(received, d, k):
    return received[k // 2][d] if k != 1 else received[2 + d][1]


def slot_table(table, received):
    for t in range(12):
        table[(t >> 1) * D : ((t >> 1) + 1) * D, (t & 1) * 128 : ((t & 1) + 1) * 128] = block_at(received, t // 3, t % 3)


def slot_gradients(outs, sums, weight):
    for j in range(SLOT_GROUPS):
        high, low = halves(sums[j * D : (j + 1) * D, :])
        grads = (dot(weight, high) + dot(weight, low)).astype(B16)
        for t in (2 * j, 2 * j + 1):
            outs[t // 3][t % 3] = grads[:, (t & 1) * 128 : ((t & 1) + 1) * 128]


def over_blocks(total, block, body):
    def step(i, carry):
        body(pl.ds(pl.multiple_of(i * block, block), block))
        return carry

    lax.fori_loop(0, total // block, step, 0)


def send_kernel(level_ref, send_ref, source_ref, s0, s1, s2, s3, table):
    groups, n = groups_of(source_ref.shape[1])
    pack_table(table, source_ref, groups, n)
    send_blocks((s0, s1, s2, s3), table, send_ref, level_ref[0], groups, n)


def part_kernel(k, start, targets_ref, feat_ref, local_ref, w1_ref, biases_ref, gains_ref, *rest):
    part_ref, table = rest[-2:]
    groups, n = groups_of(local_ref.shape[1])
    pack_table(table, local_ref, groups, n)
    columns = columns_of(biases_ref, gains_ref, k)
    weight = jnp.concatenate([w1_ref[k, :, 0:D], w1_ref[k, :, 2 * D : 3 * D]], axis=1)

    def body(t):
        s = pl.ds(pl.multiple_of(start + t.start, 128), t.size)
        group, column = place(targets_ref[:, s], groups, n)
        picked = pick(table, group, column, groups, n)
        part_ref[:, t] = dot(weight, jnp.concatenate([feat_ref[:, s], picked], axis=0)) + columns[:, 0:1]

    over_blocks(part_ref.shape[1], EDGE_BLOCK, body)


def edges_forward(k, level, counts_ref, senders_ref, targets_ref, parts, table, w1_ref, w2_ref, columns, total, groups, n,
                  slope_ref, normed_ref, hidden_ref, factor_ref, alive_ref):
    weight_slot = w1_ref[k, :, D : 2 * D]
    weight_two = w2_ref[k].astype(F32).T.astype(B16)
    total[...] = jnp.zeros_like(total)

    def body(part_ref, start, t):
        s = pl.ds(pl.multiple_of(start + t.start, 128), t.size)
        senders = senders_ref[:, s]
        group, column = slot_place(senders, level)
        picked = pick(table, group, column, SLOT_GROUPS, SLOT_COLS)
        first = part_ref[:, t] + dot(weight_slot, picked)
        gate = sigmoid(first)
        hidden = (first * gate).astype(B16)
        slope_ref[:, s] = gate * (1.0 + first * (1.0 - gate))
        hidden_ref[:, s] = hidden
        normed, factor = norm_parts(dot(weight_two, hidden) + columns[:, 1:2])
        alive = live(senders, counts_ref)
        normed_ref[:, s] = normed
        factor_ref[:, s] = factor
        alive_ref[:, s] = alive
        messages = ((normed * columns[:, 6:7] + columns[:, 2:3]) * alive).astype(B16)
        group, column = place(targets_ref[:, s], groups, n)
        add_at(total, messages, group, column, groups, n)

    start = 0
    for part_ref in parts:
        over_blocks(part_ref.shape[1], EDGE_BLOCK, functools.partial(body, part_ref, start))
        start += part_ref.shape[1]


def node_forward(k, inputs, wn1_ref, weight_two, columns):
    first = dot(wn1_ref[k], inputs) + columns[:, 3:4]
    gate = sigmoid(first)
    hidden = (first * gate).astype(B16)
    slope = gate * (1.0 + first * (1.0 - gate))
    normed, factor = norm_parts(dot(weight_two, hidden) + columns[:, 4:5])
    return hidden, slope, normed, factor


def node_backward(grad, inputs, hidden, slope, normed, factor, wn2, weight_local, columns, node_grads):
    one_ref, two_ref, sums_ref = node_grads
    second = norm_back(grad, normed, factor, columns[:, 7:8]).astype(B16)
    first = (dot(wn2, second) * slope).astype(B16)
    sums_ref[0] += fold(first.astype(F32))
    sums_ref[1] += fold(second.astype(F32))
    sums_ref[2] += fold(grad)
    sums_ref[3] += fold(grad * normed)
    two_ref[...] += dot_rows(hidden, second)
    one_ref[...] += dot_rows(first, inputs)
    return first, grad + dot(weight_local, first)


def clear(refs):
    for ref in refs:
        ref[...] = jnp.zeros_like(ref)


def transposed(weight):
    return weight.astype(F32).T.astype(B16)


def edge_backward(grad_rows, s, k, columns, weight_sum, weight_two, alive_ref, slope_ref, normed_ref, factor_ref, sums_ref):
    grad = dot(weight_sum, grad_rows) * alive_ref[:, s]
    normed = normed_ref[:, s]
    second = norm_back(grad, normed, factor_ref[:, s], columns[:, 6:7]).astype(B16)
    first = (dot(weight_two, second) * slope_ref[:, s]).astype(B16)
    sums_ref[0] += fold(first.astype(F32))
    sums_ref[1] += fold(second.astype(F32))
    sums_ref[2] += fold(grad)
    sums_ref[3] += fold(grad * normed)
    return first, second


def pack_columns(edge_sums, node_sums):
    order = (edge_sums[0], edge_sums[1], edge_sums[2], node_sums[0], node_sums[1], node_sums[2], edge_sums[3], node_sums[3])
    columns = [jnp.sum(v, axis=1, keepdims=True) for v in order]
    lanes = lax.broadcasted_iota(jnp.int32, (D, D), 1)
    packed = jnp.zeros((D, D), F32)
    for i, column in enumerate(columns):
        packed = jnp.where(lanes == i, column, packed)
    return packed


def slot_weight_grads(sums, table):
    total = jnp.zeros((D, D), F32)
    for j in range(SLOT_GROUPS):
        high, low = halves(sums[j * D : (j + 1) * D, :])
        rows = table[j * D : (j + 1) * D, :]
        total = total + dot_rows(high, rows) + dot_rows(low, rows)
    return total


def target_grads(total, local_ref, weight, start_ref, out_ref, groups, n):
    grads = jnp.zeros((D, D), F32)
    for j in range(groups):
        high, low = halves(total[j * D : (j + 1) * D, :])
        s = slice(j * n, (j + 1) * n)
        rows = local_ref[:, s]
        grads = grads + dot_rows(high, rows) + dot_rows(low, rows)
        out_ref[:, s] = start_ref[:, s] + dot(weight, high) + dot(weight, low)
    return grads


def up_forward_kernel(level_ref, counts_ref, senders_ref, targets_ref, part_ref, low, high, r0, r1, r2, r3, local_ref, send_ref,
                      w1_ref, w2_ref, wn1_ref, wn2_ref, biases_ref, gains_ref,
                      out_ref, summed_ref, s0, s1, s2, s3, slope_ref, normed_ref, hidden_ref, factor_ref, alive_ref,
                      slots, total, table, out, sem):
    level = level_ref[0]
    groups, n = groups_of(local_ref.shape[1])
    columns = columns_of(biases_ref, gains_ref, 0)
    slot_table(slots, (low, high, r0, r1, r2, r3))
    edges_forward(0, level, counts_ref, senders_ref, targets_ref, (part_ref,), slots, w1_ref, w2_ref, columns, total, groups, n,
                  slope_ref, normed_ref, hidden_ref, factor_ref, alive_ref)
    weight_two = transposed(wn2_ref[0])
    for j in range(groups):
        s = slice(j * n, (j + 1) * n)
        local = local_ref[:, s]
        summed = total[j * D : (j + 1) * D, :].astype(B16)
        summed_ref[:, s] = summed
        unused, unused, normed, factor = node_forward(0, jnp.concatenate([local, summed], axis=0), wn1_ref, weight_two, columns)
        result = local.astype(F32) + normed * columns[:, 7:8] + columns[:, 5:6]
        out[:, s] = result
        table[j * D : (j + 1) * D, :] = result.astype(B16)
    copy = pltpu.make_async_copy(out, out_ref, sem)
    copy.start()
    send_blocks((s0, s1, s2, s3), table, send_ref, level, groups, n)
    copy.wait()


def down_kernel(level_ref, counts_ref, senders_ref, targets_ref, part_a, part_b, low, high, r0, r1, r2, r3, local_ref, cot_ref,
                w1_ref, w2_ref, wn1_ref, wn2_ref, biases_ref, gains_ref,
                out_ref, g0, g1, g2, g3, first_ref, second_ref, hidden_ref, grad_ref, sums_ref, edge_sums, node_sums, wn1_grad, wn2_grad,
                slots, total, table, slope_ref, normed_ref, factor_ref, alive_ref, out, sem):
    level = level_ref[0]
    groups, n = groups_of(local_ref.shape[1])
    columns = columns_of(biases_ref, gains_ref, 1)
    slot_table(slots, (low, high, r0, r1, r2, r3))
    edges_forward(1, level, counts_ref, senders_ref, targets_ref, (part_a, part_b), slots, w1_ref, w2_ref, columns, total, groups, n,
                  slope_ref, normed_ref, hidden_ref, factor_ref, alive_ref)
    clear((wn1_grad, wn2_grad, node_sums, edge_sums, sums_ref))
    wn2 = wn2_ref[1]
    wn2_t = transposed(wn2)
    wn1 = transposed(wn1_ref[1])

    def node_step(j, carry):
        s = pl.ds(pl.multiple_of(j * n, n), n)
        rows = pl.ds(pl.multiple_of(j * D, D), D)
        local = local_ref[:, s]
        inputs = jnp.concatenate([local, total[rows, :].astype(B16)], axis=0)
        hidden, slope, normed, factor = node_forward(1, inputs, wn1_ref, wn2_t, columns)
        out[:, s] = local.astype(F32) + normed * columns[:, 7:8] + columns[:, 5:6]
        first, grad_local = node_backward(cot_ref[:, s], inputs, hidden, slope, normed, factor, wn2, wn1[0:D], columns,
                                          (wn1_grad, wn2_grad, node_sums))
        table[rows, :] = first
        grad_ref[:, s] = grad_local
        return carry

    lax.fori_loop(0, groups, node_step, 0)
    copy = pltpu.make_async_copy(out, out_ref, sem)
    copy.start()
    weight_two = w2_ref[1]
    weight_slot = transposed(w1_ref[1, :, D : 2 * D])

    def body(s):
        group, column = place(targets_ref[:, s], groups, n)
        grad_rows = pick(table, group, column, groups, n)
        first, second = edge_backward(grad_rows, s, 1, columns, wn1[D : 2 * D], weight_two, alive_ref, slope_ref, normed_ref,
                                      factor_ref, edge_sums)
        first_ref[:, s] = first
        second_ref[:, s] = second
        group, column = slot_place(senders_ref[:, s], level)
        add_at(sums_ref, first, group, column, SLOT_GROUPS, SLOT_COLS)

    over_blocks(senders_ref.shape[1], EDGE_BLOCK, body)
    slot_gradients((g0, g1, g2, g3), sums_ref, weight_slot)
    copy.wait()


def down_targets_kernel(targets_ref, first_ref, local_ref, start_ref, w1_ref, grad_ref, weight_grad_ref, total):
    groups, n = groups_of(local_ref.shape[1])
    clear((total,))
    weight = transposed(w1_ref[1, :, 2 * D : 3 * D])

    def body(s):
        group, column = place(targets_ref[:, s], groups, n)
        add_at(total, first_ref[:, s], group, column, groups, n)

    over_blocks(first_ref.shape[1], EDGE_BLOCK, body)
    weight_grad_ref[...] = target_grads(total, local_ref, weight, start_ref, grad_ref, groups, n)


def down_rest_kernel(feat_ref, first_ref, second_ref, hidden_ref, low, high, r0, r1, r2, r3, sums_ref, local_grads_ref,
                     edge_sums, node_sums, wn1_grad, wn2_grad, w1_ref, *rest):
    feat_grad_ref, packed_ref, slots, one_ref, two_ref = rest[-5:]
    step = pl.program_id(0)
    weight = transposed(w1_ref[1, :, 0:D])

    @pl.when(step == 0)
    def _():
        clear((one_ref, two_ref))

    s = pl.ds(pl.multiple_of(step * EDGE_BLOCK, EDGE_BLOCK), EDGE_BLOCK)
    first = first_ref[:, s]
    feat_grad_ref[...] = dot(weight, first)
    one_ref[...] += dot_rows(first, feat_ref[...])
    two_ref[...] += dot_rows(hidden_ref[:, s], second_ref[:, s])

    @pl.when(step == pl.num_programs(0) - 1)
    def _():
        slot_table(slots, (low, high, r0, r1, r2, r3))
        slot_grads = slot_weight_grads(sums_ref, slots)
        write_packed(packed_ref, one_ref[...], slot_grads, local_grads_ref[...], two_ref[...], wn1_grad[...], wn2_grad[...],
                     pack_columns(edge_sums, node_sums))


def write_packed(packed_ref, one, slot_grads, local_grads, two, wn1_grad, wn2_grad, columns):
    packed_ref[0] = jnp.concatenate([one, slot_grads, local_grads, two], axis=1)
    packed_ref[1] = jnp.concatenate([wn1_grad, wn2_grad, columns], axis=1)


def up_backward_kernel(level_ref, senders_ref, targets_ref, feat_ref, from_low, from_high, h0, h1, h2, h3,
                       send_ref, cot_ref, local_ref, summed_ref, low, high, r0, r1, r2, r3, slope_ref, normed_ref, hidden_ref, factor_ref, alive_ref, packed_down_ref,
                       w1_ref, w2_ref, wn1_ref, wn2_ref, biases_ref, gains_ref,
                       g0, g1, g2, g3, first_ref, grad_ref, keep_ref, give_ref,
                       slots, table, back, total, sums, start, one_ref, two_ref, edge_sums, node_sums, wn1_grad, wn2_grad, pieces):
    level = level_ref[0]
    groups, n = groups_of(local_ref.shape[1])
    columns = columns_of(biases_ref, gains_ref, 0)
    clear((back, total, sums, one_ref, two_ref, edge_sums, node_sums, wn1_grad, wn2_grad))
    slot_table(slots, (low, high, r0, r1, r2, r3))
    add_back(back, (from_low, from_high, h0, h1, h2, h3), send_ref, level, groups, n)
    wn2 = wn2_ref[0]
    wn2_t = transposed(wn2)
    wn1 = transposed(wn1_ref[0])
    w1 = transposed(w1_ref[0])
    for j in range(groups):
        s = slice(j * n, (j + 1) * n)
        rows = slice(j * D, (j + 1) * D)
        inputs = jnp.concatenate([local_ref[:, s], summed_ref[:, s]], axis=0)
        hidden, slope, normed, factor = node_forward(0, inputs, wn1_ref, wn2_t, columns)
        first, grad_local = node_backward(cot_ref[:, s] + back[rows, :], inputs, hidden, slope, normed, factor, wn2, wn1[0:D],
                                          columns, (wn1_grad, wn2_grad, node_sums))
        table[rows, :] = first
        start[:, s] = grad_local
    weight_two = w2_ref[0]

    def body(s):
        group, column = place(targets_ref[:, s], groups, n)
        grad_rows = pick(table, group, column, groups, n)
        first, second = edge_backward(grad_rows, s, 0, columns, wn1[D : 2 * D], weight_two, alive_ref, slope_ref, normed_ref,
                                      factor_ref, edge_sums)
        first_ref[:, s] = first
        add_at(total, first, group, column, groups, n)
        group, column = slot_place(senders_ref[:, s], level)
        add_at(sums, first, group, column, SLOT_GROUPS, SLOT_COLS)
        one_ref[...] += dot_rows(first, feat_ref[:, s])
        two_ref[...] += dot_rows(hidden_ref[:, s], second)

    over_blocks(senders_ref.shape[1], EDGE_BLOCK, body)
    slot_gradients((g0, g1, g2, g3), sums, w1[D : 2 * D])
    local_grads = target_grads(total, local_ref, w1[2 * D : 3 * D], start, grad_ref, groups, n)
    slot_grads = slot_weight_grads(sums, slots)
    write_packed(pieces, one_ref[...], slot_grads, local_grads, two_ref[...], wn1_grad[...], wn2_grad[...],
                 pack_columns(edge_sums, node_sums))
    core = level_ref[1]
    up_half = jnp.concatenate([pieces[0], pieces[1]], axis=1)
    down_half = jnp.concatenate([packed_down_ref[0], packed_down_ref[1]], axis=1)
    keep_ref[...] = jnp.where(core == 0, up_half, down_half)
    give_ref[...] = jnp.where(core == 0, down_half, up_half).astype(B16)


def feat_grad_kernel(first_ref, w1_ref, out_ref):
    out_ref[...] = dot(transposed(w1_ref[0, :, 0:D]), first_ref[...])


def lower_grad_kernel(ids_ref, from_low, from_high, h0, h1, h2, h3, send_ref, start_ref, out_ref, total):
    groups, n = groups_of(start_ref.shape[1])
    clear((total,))
    add_back(total, (from_low, from_high, h0, h1, h2, h3), send_ref, ids_ref[0], groups, n)
    for j in range(groups):
        s = slice(j * n, (j + 1) * n)
        out_ref[:, s] = start_ref[:, s] + total[j * D : (j + 1) * D, :]


def unpack_kernel(ids_ref, own_ref, other_ref, w1_ref, w2_ref, wn1_ref, wn2_ref, biases_ref, gains_ref):
    core = ids_ref[1]
    own, other = own_ref[...], other_ref[...]
    for k in range(2):
        half = jnp.where(core == k, own, other)
        w1_ref[k] = half[:, 0 : 3 * D]
        w2_ref[k] = half[:, 3 * D : 4 * D]
        wn1_ref[k] = half[:, 4 * D : 6 * D]
        wn2_ref[k] = half[:, 6 * D : 7 * D]
        rows = half[:, 6 * D : 8 * D].T
        for i in range(6):
            biases_ref[i, k : k + 1] = rows[D + i : D + i + 1]
        gains_ref[k] = rows[D + 6 : D + 8]


def shape(dims, dtype=F32):
    return jax.ShapeDtypeStruct(dims, dtype)


def call(kernel, name, outs, scratch, scalars=0, stored=(), streamed=None, final=()):
    steps, stream_in, stream_out = streamed if streamed else (1, (), ())

    def run(*operands, after=()):
        def whole(space):
            return pl.BlockSpec(memory_space=space)

        def cut(x):
            return pl.BlockSpec((x.shape[0], x.shape[1] // steps), lambda i: (0, i))

        in_specs, placed = [], []
        for i, x in enumerate(operands):
            if i < scalars:
                in_specs.append(whole(pltpu.SMEM))
            elif i in stream_in:
                in_specs.append(cut(x))
            else:
                in_specs.append(whole(pltpu.VMEM))
                x = pltpu.with_memory_space_constraint(x, pltpu.VMEM)
            placed.append(x)
        in_specs += [whole(pl.ANY) for _ in after]
        out_specs, out_shape = [], []
        for i, x in enumerate(outs):
            if i in stream_out:
                out_specs.append(cut(x))
                out_shape.append(x)
            elif i in stored:
                out_specs.append(whole(pl.ANY))
                out_shape.append(x)
            elif i in final:
                out_specs.append(whole(pltpu.VMEM))
                out_shape.append(x)
            else:
                out_specs.append(whole(pltpu.VMEM))
                out_shape.append(pltpu.VMEM(x.shape, x.dtype))
        return pl.pallas_call(
            kernel,
            name=name,
            grid=(steps,) if streamed else (),
            in_specs=in_specs,
            out_specs=out_specs,
            out_shape=out_shape,
            scratch_shapes=scratch,
            compiler_params=pltpu.CompilerParams(vmem_limit_bytes=VMEM_BYTES),
        )(*placed, *after)

    return run


def along_band(block, step):
    count = lax.axis_size("band")
    return lax.ppermute(block, "band", [(i, (i + step) % count) for i in range(count)])


def along_level(block, step):
    count = lax.axis_size("level")
    return lax.ppermute(block, "level", [(i, (i + step) % count) for i in range(count)])


def across_bands(blocks):
    up = along_band(jnp.stack([b[2] for b in blocks]), 1)
    down = along_band(jnp.stack([b[0] for b in blocks]), -1)
    return [up, down] + blocks


def along_levels(blocks, sign):
    return [blocks[0]] + [along_level(blocks[d], sign * d) for d in (1, 2, 3)]


def chip_axis(block, stride, length, step):
    count = lax.axis_size("band")
    pairs = []
    for i in range(count):
        at = (i // stride) % length
        pairs.append((i, i + (((at + step) % length) - at) * stride))
    return lax.ppermute(block, "band", pairs)


def rounded(values):
    return lax.reduce_precision(values, 8, 7)


def sum_of_four(values, send):
    own = rounded(values)
    sent = own.astype(B16)
    first, second, third = (send(sent, d).astype(F32) for d in (1, 2, 3))
    return (own + second) + (first + third)


def reduce_all(keep, give):
    total = rounded(keep) + chip_axis(give, 1, 2, 1).astype(F32)
    total = sum_of_four(total, along_level)
    total = sum_of_four(total, lambda v, d: chip_axis(v, 2, 4, d))
    total = sum_of_four(total, lambda v, d: chip_axis(v, 8, 4, d))
    return total, chip_axis(total, 1, 2, 1)


def shards(
    lower_nodes, latent, up_feat, down_feat, up_send, up_counts, up_senders, up_targets,
    down_send, down_counts, down_senders, down_targets,
    edge_w1, edge_w2, node_w1, node_w2, biases, norm_gains, lower_cot, upper_cot,
):
    lower, upper = lower_nodes.T, latent.T
    feat_up, feat_down = up_feat.T, down_feat.T
    cot_lower, cot_upper = lower_cot.T, upper_cot.T
    w1, wn1 = edge_w1.transpose(0, 2, 1), node_w1.transpose(0, 2, 1)
    w2, wn2 = edge_w2, node_w2
    edges, lower_rows, upper_rows = up_feat.shape[0], lower_nodes.shape[0], latent.shape[0]
    senders_up, targets_up = up_senders.reshape(1, edges), up_targets.reshape(1, edges)
    senders_down, targets_down = down_senders.reshape(1, edges), down_targets.reshape(1, edges)
    bias_rows = biases.transpose(1, 0, 2)
    ids = jnp.stack([lax.axis_index("level"), lax.axis_index("band") & 1]).astype(jnp.int32)

    lower_groups, lower_n = groups_of(lower_rows)
    upper_groups, upper_n = groups_of(upper_rows)
    lower_table, upper_table = (lower_groups * D, lower_n), (upper_groups * D, upper_n)
    slots = pltpu.VMEM((SLOT_GROUPS * D, SLOT_COLS), B16)
    received = shape((3, D, 128), B16)
    wide32, wide16, row = shape((D, edges)), shape((D, edges), B16), shape((1, edges))
    steps = edges // EDGE_BLOCK

    sent = call(send_kernel, "send_lower", [received] * 4, [pltpu.VMEM(lower_table, B16)], 1)(ids, up_send, lower)
    up_slots = across_bands(along_levels(sent, 1))
    (part_up,) = call(functools.partial(part_kernel, 0, 0), "part_up", [wide32], [pltpu.VMEM(upper_table, B16)])(
        targets_up, feat_up, upper, w1, bias_rows, norm_gains)
    half = edges // 2
    (part_a,) = call(functools.partial(part_kernel, 1, 0), "part_down_a", [shape((D, half))], [pltpu.VMEM(lower_table, B16)])(
        targets_down, feat_down, lower, w1, bias_rows, norm_gains)
    (upper_new, summed_up, s0, s1, s2, s3, slope, normed, hidden, factor, alive) = call(
        up_forward_kernel, "up_forward",
        [shape((D, upper_rows)), shape((D, upper_rows), B16)] + [received] * 4 + [wide32, wide32, wide16, row, row],
        [slots, pltpu.VMEM(upper_table, F32), pltpu.VMEM(upper_table, B16), pltpu.VMEM((D, upper_rows), F32),
         pltpu.SemaphoreType.DMA], 2, (0,),
    )(ids, up_counts, senders_up, targets_up, part_up, *up_slots, upper, down_send, w1, w2, wn1, wn2, bias_rows, norm_gains)
    sent = along_levels([s0, s1, s2, s3], 1)
    (part_b,) = call(functools.partial(part_kernel, 1, half), "part_down_b", [shape((D, half))], [pltpu.VMEM(lower_table, B16)])(
        targets_down, feat_down, lower, w1, bias_rows, norm_gains, after=(s0,))
    down_slots = across_bands(sent)
    sums_shape = shape((SLOT_GROUPS * D, SLOT_COLS))
    four = shape((4, D, 128))
    (lower_new, g0, g1, g2, g3, first_down, second_down, hidden_down, start_lower, sums_down, edge_sums, node_sums, wn1_grad, wn2_grad) = call(
        down_kernel, "down_sweep",
        [shape((D, lower_rows))] + [received] * 4 + [wide16] * 3 + [shape((D, lower_rows)), sums_shape, four, four,
         shape((D, 2 * D)), shape((D, D))],
        [slots, pltpu.VMEM(lower_table, F32), pltpu.VMEM(lower_table, B16), pltpu.VMEM((D, edges), F32),
         pltpu.VMEM((D, edges), F32), pltpu.VMEM((1, edges), F32), pltpu.VMEM((1, edges), F32),
         pltpu.VMEM((D, lower_rows), F32), pltpu.SemaphoreType.DMA], 2, (0,),
    )(ids, down_counts, senders_down, targets_down, part_a, part_b, *down_slots, lower, cot_lower, w1, w2, wn1, wn2, bias_rows, norm_gains)
    back = along_levels([g0, g1, g2, g3], -1)
    start_lower, local_grads = call(
        down_targets_kernel, "down_targets", [shape((D, lower_rows)), shape((D, D))], [pltpu.VMEM(lower_table, F32)],
    )(targets_down, first_down, lower, start_lower, w1)
    down_back = across_bands(back)
    feat_grad_down, packed_down = call(
        down_rest_kernel, "down_rest", [wide32, shape((2, D, 256))],
        [slots, pltpu.VMEM((D, D), F32), pltpu.VMEM((D, D), F32)], 0, (), (steps, (0,), (0,)),
    )(feat_down, first_down, second_down, hidden_down, *down_slots, sums_down, local_grads,
      edge_sums, node_sums, wn1_grad, wn2_grad, w1, after=(back[1],))
    (g0, g1, g2, g3, first_up, grad_latent, keep, give) = call(
        up_backward_kernel, "up_backward",
        [received] * 4 + [wide16, shape((D, upper_rows)), shape((D, 512)), shape((D, 512), B16)],
        [slots, pltpu.VMEM(upper_table, B16), pltpu.VMEM(upper_table, F32), pltpu.VMEM(upper_table, F32),
         pltpu.VMEM((SLOT_GROUPS * D, SLOT_COLS), F32), pltpu.VMEM((D, upper_rows), F32),
         pltpu.VMEM((D, D), F32), pltpu.VMEM((D, D), F32), pltpu.VMEM((4, D, 128), F32), pltpu.VMEM((4, D, 128), F32),
         pltpu.VMEM((D, 2 * D), F32), pltpu.VMEM((D, D), F32), pltpu.VMEM((2, D, 256), F32)], 1, (), None, (5,),
    )(ids, senders_up, targets_up, feat_up, *down_back, down_send, cot_upper, upper, summed_up, *up_slots,
      slope, normed, hidden, factor, alive, packed_down, w1, w2, wn1, wn2, bias_rows, norm_gains)
    up_back = across_bands(along_levels([g0, g1, g2, g3], -1))
    reduced = reduce_all(keep, give)
    (feat_grad_up,) = call(feat_grad_kernel, "feat_grad_up", [wide32], [], 0, (), (steps, (0,), (0,)))(first_up, w1)
    (grad_lower,) = call(lower_grad_kernel, "lower_grad", [shape((D, lower_rows))], [pltpu.VMEM(lower_table, F32)], 1, (), None, (0,))(
        ids, *up_back, up_send, start_lower)
    w1_grad, w2_grad, wn1_grad, wn2_grad, bias_grad, gain_grad = call(
        unpack_kernel, "unpack",
        [shape((2, D, 3 * D)), shape((2, D, D)), shape((2, D, 2 * D)), shape((2, D, D)), shape((6, 2, D)), shape((2, 2, D))],
        [], 1, (), None, range(6))(ids, *reduced)
    return (
        lower_new.T, upper_new.T, grad_lower.T, grad_latent.T, feat_grad_up.T, feat_grad_down.T,
        w1_grad.transpose(0, 2, 1), w2_grad, wn1_grad.transpose(0, 2, 1), wn2_grad, bias_grad.transpose(1, 0, 2), gain_grad,
    )


def solution(mesh):
    rows, index, whole = P(("band", "level"), None), P(("band", "level")), P()
    placed = (rows,) * 6 + (index, index) + (rows,) * 2 + (index, index) + (whole,) * 6 + (rows,) * 2
    return jax.shard_map(
        shards,
        mesh=mesh,
        in_specs=placed,
        out_specs=(rows,) * 6 + (whole,) * 6,
        check_vma=False,
    )
```

```python
import functools

import jax
import jax.numpy as jnp
from jax import lax
from jax.experimental import pallas as pl
from jax.experimental.pallas import tpu as pltpu
from jax.sharding import PartitionSpec as P

EPSILON = 1e-05
F32 = jnp.float32
B16 = jnp.bfloat16
D = 64
SLOT_GROUPS, SLOT_COLS = 6, 256
EDGE_BLOCK = 3072
CHUNK = 1024
VMEM_BYTES = 24 * 1024 * 1024


def groups_of(rows):
    return (4, rows // 4) if rows > 1024 else (rows // 256, 256)


def dot(a, b):
    return jnp.dot(a, b, preferred_element_type=F32)


def dot_rows(a, b):
    return lax.dot_general(a, b, (((1,), (1,)), ((), ())), preferred_element_type=F32)


def halves(x):
    high = x.astype(B16)
    return high, (x - high.astype(F32)).astype(B16)


def one_hot(column, n):
    rows = lax.broadcasted_iota(jnp.int16, (n, column.shape[1]), 0)
    return jnp.where(rows == column.astype(jnp.int16), jnp.ones((), B16), jnp.zeros((), B16))


def place(index, groups, n):
    group = jnp.zeros_like(index)
    for j in range(1, groups):
        group = group + (index >= j * n).astype(jnp.int32)
    return group, index - group * n


def slot_place(senders, level):
    distance = (level - ((senders >> 7) & 3)) & 3
    block = distance * 3 + (senders >> 9)
    return block >> 1, ((block & 1) << 7) | (senders & 127)


def live(senders, counts_ref):
    peer = senders >> 7
    limit = jnp.zeros_like(senders)
    for j in range(counts_ref.shape[1]):
        limit = jnp.where(peer == j, counts_ref[0, j], limit)
    return ((senders & 127) < limit).astype(F32)


def choose(stacked, group, groups):
    picked = stacked[0:D]
    for j in range(1, groups):
        picked = jnp.where(group == j, stacked[j * D : (j + 1) * D], picked)
    return picked


def pick(table, group, column, groups, n):
    return choose(dot(table[...], one_hot(column, n)), group, groups).astype(B16)


def spread(values, group, groups):
    wide = jnp.broadcast_to(group.astype(jnp.int16), values.shape)
    nothing = jnp.zeros_like(values)
    return jnp.concatenate([jnp.where(wide == j, values, nothing) for j in range(groups)], axis=0)


def add_at(total, values, group, column, groups, n):
    total[...] += dot_rows(spread(values, group, groups), one_hot(column, n))


def pack_table(table, source, groups, n):
    for j in range(groups):
        table[j * D : (j + 1) * D, :] = source[:, j * n : (j + 1) * n]


def columns_of(biases_ref, gains_ref, k):
    rows = [biases_ref[i, k : k + 1] for i in range(6)] + [gains_ref[k]]
    return jnp.concatenate(rows, axis=0).T


def fold(values):
    total = values[:, 0:128]
    for i in range(128, values.shape[1], 128):
        total = total + values[:, i : i + 128]
    return total


def norm_parts(values):
    centre = values - jnp.sum(values, axis=0, keepdims=True) * (1.0 / D)
    spread_sum = jnp.sum(centre * centre, axis=0, keepdims=True) * (1.0 / D)
    factor = lax.rsqrt(spread_sum + EPSILON)
    return centre * factor, factor


def norm_back(grad, normed, factor, gain):
    scaled = grad * gain
    first = jnp.sum(scaled, axis=0, keepdims=True) * (1.0 / D)
    second = jnp.sum(scaled * normed, axis=0, keepdims=True) * (1.0 / D)
    return factor * (scaled - first - normed * second)


def sigmoid(values):
    return 0.5 * jnp.tanh(0.5 * values) + 0.5


def send_rows(send_ref, k, level):
    return jnp.concatenate(
        [send_ref[pl.ds(k * 4 + ((level + d) & 3), 1), :] for d in range(4)], axis=1
    )


def send_blocks(outs, table, send_ref, level, groups, n):
    for k in range(3):
        group, column = place(send_rows(send_ref, k, level), groups, n)
        rows = pick(table, group, column, groups, n)
        for d in range(4):
            outs[d][k] = rows[:, d * 128 : (d + 1) * 128]


def add_back(total, blocks, send_ref, level, groups, n):
    for k in range(3):
        group, column = place(send_rows(send_ref, k, level), groups, n)
        values = jnp.concatenate([block_at(blocks, d, k) for d in range(4)], axis=1)
        add_at(total, values, group, column, groups, n)


def block_at(received, d, k):
    return received[k // 2][d] if k != 1 else received[2 + d][1]


def slot_table(table, received):
    for t in range(12):
        table[(t >> 1) * D : ((t >> 1) + 1) * D, (t & 1) * 128 : ((t & 1) + 1) * 128] = block_at(received, t // 3, t % 3)


def slot_gradients(outs, sums, weight):
    for j in range(SLOT_GROUPS):
        high, low = halves(sums[j * D : (j + 1) * D, :])
        grads = (dot(weight, high) + dot(weight, low)).astype(B16)
        for t in (2 * j, 2 * j + 1):
            outs[t // 3][t % 3] = grads[:, (t & 1) * 128 : ((t & 1) + 1) * 128]


def over_blocks(total, block, body):
    block = min(block, total)
    if block == total:
        body(pl.ds(0, block))
        return

    def step(i, carry):
        body(pl.ds(pl.multiple_of(i * block, block), block))
        return carry

    lax.fori_loop(0, total // block, step, 0)


def pipelined(stages, spans):
    held = [None] * len(spans)
    for t in range(len(spans) + len(stages) - 1):
        for k in reversed(range(len(stages))):
            i = t - k
            if 0 <= i < len(spans):
                held[i] = stages[k](spans[i], held[i])


def spans_of(parts, chunk):
    spans, start = [], 0
    for ref in parts:
        size = min(chunk, ref.shape[1])
        for at in range(0, ref.shape[1], size):
            spans.append((ref, pl.ds(at, size), pl.ds(start + at, size)))
        start += ref.shape[1]
    return spans


def send_kernel(count, level_ref, *refs):
    sources, refs = refs[:count], refs[count:]
    (s0, s1, s2, s3), held, table, sems = refs[:4], refs[4:-2], refs[-2], refs[-1]
    copies = [pltpu.make_async_copy(a, b, sems.at[i]) for i, (a, b) in enumerate(zip(sources, held))]
    for copy in copies:
        copy.start()
    for copy in copies[:2]:
        copy.wait()
    send_ref, source_ref = held[:2]
    groups, n = groups_of(source_ref.shape[1])
    pack_table(table, source_ref, groups, n)
    send_blocks((s0, s1, s2, s3), table, send_ref, level_ref[0], groups, n)
    for copy in copies[2:]:
        copy.wait()


def part_kernel(k, start, targets_ref, feat_ref, local_ref, w1_ref, biases_ref, gains_ref, *rest):
    part_ref, table = rest[-2:]
    groups, n = groups_of(local_ref.shape[1])
    pack_table(table, local_ref, groups, n)
    columns = columns_of(biases_ref, gains_ref, k)
    weight = jnp.concatenate([w1_ref[k, :, 0:D], w1_ref[k, :, 2 * D : 3 * D]], axis=1)

    def body(t):
        s = pl.ds(pl.multiple_of(start + t.start, 128), t.size)
        group, column = place(targets_ref[:, s], groups, n)
        picked = pick(table, group, column, groups, n)
        part_ref[:, t] = dot(weight, jnp.concatenate([feat_ref[:, s], picked], axis=0)) + columns[:, 0:1]

    over_blocks(part_ref.shape[1], EDGE_BLOCK, body)


def edges_forward(k, level, counts_ref, senders_ref, targets_ref, parts, table, w1_ref, w2_ref, columns, total, groups, n,
                  slope_ref, normed_ref, hidden_ref, factor_ref, alive_ref):
    weight_slot = w1_ref[k, :, D : 2 * D]
    weight_two = w2_ref[k].astype(F32).T.astype(B16)
    total[...] = jnp.zeros_like(total)

    def slot_rows(span, unused):
        senders = senders_ref[:, span[2]]
        group, column = slot_place(senders, level)
        return pick(table, group, column, SLOT_GROUPS, SLOT_COLS)

    def first_layer(span, picked):
        part_ref, t, s = span
        first = part_ref[:, t] + dot(weight_slot, picked)
        gate = sigmoid(first)
        hidden = (first * gate).astype(B16)
        slope_ref[:, s] = gate * (1.0 + first * (1.0 - gate))
        hidden_ref[:, s] = hidden
        return hidden

    def second_layer(span, hidden):
        s = span[2]
        normed, factor = norm_parts(dot(weight_two, hidden) + columns[:, 1:2])
        alive = live(senders_ref[:, s], counts_ref)
        normed_ref[:, s] = normed
        factor_ref[:, s] = factor
        alive_ref[:, s] = alive
        return ((normed * columns[:, 6:7] + columns[:, 2:3]) * alive).astype(B16)

    def sum_messages(span, messages):
        group, column = place(targets_ref[:, span[2]], groups, n)
        add_at(total, messages, group, column, groups, n)

    pipelined((slot_rows, first_layer, second_layer, sum_messages), spans_of(parts, CHUNK))


def node_first(k, inputs, wn1_ref, columns):
    first = dot(wn1_ref[k], inputs) + columns[:, 3:4]
    gate = sigmoid(first)
    return (first * gate).astype(B16), gate * (1.0 + first * (1.0 - gate))


def node_second(hidden, weight_two, columns):
    return norm_parts(dot(weight_two, hidden) + columns[:, 4:5])


def node_second_grad(grad, normed, factor, hidden, columns, two_ref, sums_ref):
    second = norm_back(grad, normed, factor, columns[:, 7:8]).astype(B16)
    sums_ref[1] += fold(second.astype(F32))
    sums_ref[2] += fold(grad)
    sums_ref[3] += fold(grad * normed)
    two_ref[...] += dot_rows(hidden, second)
    return second


def node_first_grad(second, slope, inputs, wn2, one_ref, sums_ref):
    first = (dot(wn2, second) * slope).astype(B16)
    sums_ref[0] += fold(first.astype(F32))
    one_ref[...] += dot_rows(first, inputs)
    return first


def clear(refs):
    for ref in refs:
        ref[...] = jnp.zeros_like(ref)


def transposed(weight):
    return weight.astype(F32).T.astype(B16)


def edge_second(grad_rows, s, columns, weight_sum, alive_ref, normed_ref, factor_ref, sums_ref):
    grad = dot(weight_sum, grad_rows) * alive_ref[:, s]
    normed = normed_ref[:, s]
    second = norm_back(grad, normed, factor_ref[:, s], columns[:, 6:7]).astype(B16)
    sums_ref[1] += fold(second.astype(F32))
    sums_ref[2] += fold(grad)
    sums_ref[3] += fold(grad * normed)
    return second


def edge_first(second, s, weight_two, slope_ref, sums_ref):
    first = (dot(weight_two, second) * slope_ref[:, s]).astype(B16)
    sums_ref[0] += fold(first.astype(F32))
    return first


def pack_columns(edge_sums, node_sums):
    order = (edge_sums[0], edge_sums[1], edge_sums[2], node_sums[0], node_sums[1], node_sums[2], edge_sums[3], node_sums[3])
    columns = [jnp.sum(v, axis=1, keepdims=True) for v in order]
    lanes = lax.broadcasted_iota(jnp.int32, (D, D), 1)
    packed = jnp.zeros((D, D), F32)
    for i, column in enumerate(columns):
        packed = jnp.where(lanes == i, column, packed)
    return packed


def slot_weight_grads(sums, table):
    total = jnp.zeros((D, D), F32)
    for j in range(SLOT_GROUPS):
        high, low = halves(sums[j * D : (j + 1) * D, :])
        rows = table[j * D : (j + 1) * D, :]
        total = total + dot_rows(high, rows) + dot_rows(low, rows)
    return total


def target_grads(total, local_ref, weight, start_ref, out_ref, groups, n):
    grads = jnp.zeros((D, D), F32)
    for j in range(groups):
        high, low = halves(total[j * D : (j + 1) * D, :])
        s = slice(j * n, (j + 1) * n)
        rows = local_ref[:, s]
        grads = grads + dot_rows(high, rows) + dot_rows(low, rows)
        out_ref[:, s] = start_ref[:, s] + dot(weight, high) + dot(weight, low)
    return grads


def up_forward_kernel(level_ref, counts_ref, senders_ref, targets_ref, part_ref, low, high, r0, r1, r2, r3, local_ref, send_ref,
                      w1_ref, w2_ref, wn1_ref, wn2_ref, biases_ref, gains_ref,
                      out_ref, summed_ref, s0, s1, s2, s3, slope_ref, normed_ref, hidden_ref, factor_ref, alive_ref,
                      slots, total, table, out, sem):
    level = level_ref[0]
    groups, n = groups_of(local_ref.shape[1])
    columns = columns_of(biases_ref, gains_ref, 0)
    slot_table(slots, (low, high, r0, r1, r2, r3))
    edges_forward(0, level, counts_ref, senders_ref, targets_ref, (part_ref,), slots, w1_ref, w2_ref, columns, total, groups, n,
                  slope_ref, normed_ref, hidden_ref, factor_ref, alive_ref)
    weight_two = transposed(wn2_ref[0])

    def first_layer(j, unused):
        s = slice(j * n, (j + 1) * n)
        summed = total[j * D : (j + 1) * D, :].astype(B16)
        summed_ref[:, s] = summed
        return node_first(0, jnp.concatenate([local_ref[:, s], summed], axis=0), wn1_ref, columns)

    def second_layer(j, held):
        s = slice(j * n, (j + 1) * n)
        normed, unused = node_second(held[0], weight_two, columns)
        result = local_ref[:, s].astype(F32) + normed * columns[:, 7:8] + columns[:, 5:6]
        out[:, s] = result
        table[j * D : (j + 1) * D, :] = result.astype(B16)

    pipelined((first_layer, second_layer), range(groups))
    copy = pltpu.make_async_copy(out, out_ref, sem)
    copy.start()
    send_blocks((s0, s1, s2, s3), table, send_ref, level, groups, n)
    copy.wait()


def down_kernel(level_ref, counts_ref, senders_ref, targets_ref, part_a, part_b, low, high, r0, r1, r2, r3, local_ref, cot_ref,
                w1_ref, w2_ref, wn1_ref, wn2_ref, biases_ref, gains_ref,
                out_ref, g0, g1, g2, g3, first_ref, second_ref, hidden_ref, grad_ref, sums_ref, edge_sums, node_sums, wn1_grad, wn2_grad,
                slots, total, table, slope_ref, normed_ref, factor_ref, alive_ref, out, sem):
    level = level_ref[0]
    groups, n = groups_of(local_ref.shape[1])
    columns = columns_of(biases_ref, gains_ref, 1)
    slot_table(slots, (low, high, r0, r1, r2, r3))
    edges_forward(1, level, counts_ref, senders_ref, targets_ref, (part_a, part_b), slots, w1_ref, w2_ref, columns, total, groups, n,
                  slope_ref, normed_ref, hidden_ref, factor_ref, alive_ref)
    clear((wn1_grad, wn2_grad, node_sums, edge_sums, sums_ref))
    wn2 = wn2_ref[1]
    wn2_t = transposed(wn2)
    wn1 = transposed(wn1_ref[1])

    def first_layer(j, unused):
        local = local_ref[:, j * n : (j + 1) * n]
        inputs = jnp.concatenate([local, total[j * D : (j + 1) * D, :].astype(B16)], axis=0)
        return inputs, *node_first(1, inputs, wn1_ref, columns)

    def second_layer(j, held):
        inputs, hidden, slope = held
        s = slice(j * n, (j + 1) * n)
        normed, factor = node_second(hidden, wn2_t, columns)
        out[:, s] = local_ref[:, s].astype(F32) + normed * columns[:, 7:8] + columns[:, 5:6]
        return inputs, slope, node_second_grad(cot_ref[:, s], normed, factor, hidden, columns, wn2_grad, node_sums)

    def node_grads(j, held):
        inputs, slope, second = held
        s = slice(j * n, (j + 1) * n)
        first = node_first_grad(second, slope, inputs, wn2, wn1_grad, node_sums)
        table[j * D : (j + 1) * D, :] = first
        grad_ref[:, s] = cot_ref[:, s] + dot(wn1[0:D], first)

    pipelined((first_layer, second_layer, node_grads), range(groups))
    copy = pltpu.make_async_copy(out, out_ref, sem)
    copy.start()
    weight_two = w2_ref[1]
    weight_slot = transposed(w1_ref[1, :, D : 2 * D])

    def grad_rows(span, unused):
        group, column = place(targets_ref[:, span[2]], groups, n)
        return pick(table, group, column, groups, n)

    def second_grad(span, rows):
        return edge_second(rows, span[2], columns, wn1[D : 2 * D], alive_ref, normed_ref, factor_ref, edge_sums)

    def first_grad(span, second):
        s = span[2]
        first = edge_first(second, s, weight_two, slope_ref, edge_sums)
        first_ref[:, s] = first
        second_ref[:, s] = second
        return first

    def sum_slots(span, first):
        group, column = slot_place(senders_ref[:, span[2]], level)
        add_at(sums_ref, first, group, column, SLOT_GROUPS, SLOT_COLS)

    pipelined((grad_rows, second_grad, first_grad, sum_slots), spans_of((first_ref,), CHUNK))
    slot_gradients((g0, g1, g2, g3), sums_ref, weight_slot)
    copy.wait()


def down_targets_kernel(targets_ref, first_ref, local_ref, start_ref, w1_ref, grad_ref, weight_grad_ref, total):
    groups, n = groups_of(local_ref.shape[1])
    clear((total,))
    weight = transposed(w1_ref[1, :, 2 * D : 3 * D])

    def body(s):
        group, column = place(targets_ref[:, s], groups, n)
        add_at(total, first_ref[:, s], group, column, groups, n)

    over_blocks(first_ref.shape[1], EDGE_BLOCK, body)
    weight_grad_ref[...] = target_grads(total, local_ref, weight, start_ref, grad_ref, groups, n)


def down_rest_kernel(feat_ref, first_ref, second_ref, hidden_ref, low, high, r0, r1, r2, r3, sums_ref, local_grads_ref,
                     edge_sums, node_sums, wn1_grad, wn2_grad, w1_ref, *rest):
    feat_grad_ref, packed_ref, slots, one_ref, two_ref = rest[-5:]
    step = pl.program_id(0)
    weight = transposed(w1_ref[1, :, 0:D])

    @pl.when(step == 0)
    def _():
        clear((one_ref, two_ref))

    s = pl.ds(pl.multiple_of(step * EDGE_BLOCK, EDGE_BLOCK), EDGE_BLOCK)
    first = first_ref[:, s]
    feat_grad_ref[...] = dot(weight, first)
    one_ref[...] += dot_rows(first, feat_ref[...])
    two_ref[...] += dot_rows(hidden_ref[:, s], second_ref[:, s])

    @pl.when(step == pl.num_programs(0) - 1)
    def _():
        slot_table(slots, (low, high, r0, r1, r2, r3))
        slot_grads = slot_weight_grads(sums_ref, slots)
        write_packed(packed_ref, one_ref[...], slot_grads, local_grads_ref[...], two_ref[...], wn1_grad[...], wn2_grad[...],
                     pack_columns(edge_sums, node_sums))


def write_packed(packed_ref, one, slot_grads, local_grads, two, wn1_grad, wn2_grad, columns):
    packed_ref[0] = jnp.concatenate([one, slot_grads, local_grads, two], axis=1)
    packed_ref[1] = jnp.concatenate([wn1_grad, wn2_grad, columns], axis=1)


def up_backward_kernel(level_ref, senders_ref, targets_ref, feat_ref, from_low, from_high, h0, h1, h2, h3,
                       send_ref, cot_ref, local_ref, summed_ref, low, high, r0, r1, r2, r3, slope_ref, normed_ref, hidden_ref, factor_ref, alive_ref, packed_down_ref,
                       w1_ref, w2_ref, wn1_ref, wn2_ref, biases_ref, gains_ref,
                       g0, g1, g2, g3, first_ref, grad_ref, keep_ref, give_ref,
                       slots, table, back, total, sums, start, one_ref, two_ref, edge_sums, node_sums, wn1_grad, wn2_grad, pieces):
    level = level_ref[0]
    groups, n = groups_of(local_ref.shape[1])
    columns = columns_of(biases_ref, gains_ref, 0)
    clear((back, total, sums, one_ref, two_ref, edge_sums, node_sums, wn1_grad, wn2_grad))
    slot_table(slots, (low, high, r0, r1, r2, r3))
    add_back(back, (from_low, from_high, h0, h1, h2, h3), send_ref, level, groups, n)
    wn2 = wn2_ref[0]
    wn2_t = transposed(wn2)
    wn1 = transposed(wn1_ref[0])
    w1 = transposed(w1_ref[0])

    def first_layer(j, unused):
        s = slice(j * n, (j + 1) * n)
        inputs = jnp.concatenate([local_ref[:, s], summed_ref[:, s]], axis=0)
        return inputs, *node_first(0, inputs, wn1_ref, columns)

    def second_layer(j, held):
        inputs, hidden, slope = held
        grad = cot_ref[:, j * n : (j + 1) * n] + back[j * D : (j + 1) * D, :]
        normed, factor = node_second(hidden, wn2_t, columns)
        return inputs, slope, grad, node_second_grad(grad, normed, factor, hidden, columns, wn2_grad, node_sums)

    def node_grads(j, held):
        inputs, slope, grad, second = held
        first = node_first_grad(second, slope, inputs, wn2, wn1_grad, node_sums)
        table[j * D : (j + 1) * D, :] = first
        start[:, j * n : (j + 1) * n] = grad + dot(wn1[0:D], first)

    pipelined((first_layer, second_layer, node_grads), range(groups))
    weight_two = w2_ref[0]

    def grad_rows(span, unused):
        group, column = place(targets_ref[:, span[2]], groups, n)
        return pick(table, group, column, groups, n)

    def second_grad(span, rows):
        return edge_second(rows, span[2], columns, wn1[D : 2 * D], alive_ref, normed_ref, factor_ref, edge_sums)

    def first_grad(span, second):
        s = span[2]
        first = edge_first(second, s, weight_two, slope_ref, edge_sums)
        first_ref[:, s] = first
        two_ref[...] += dot_rows(hidden_ref[:, s], second)
        return first

    def sum_rows(span, first):
        s = span[2]
        group, column = place(targets_ref[:, s], groups, n)
        add_at(total, first, group, column, groups, n)
        group, column = slot_place(senders_ref[:, s], level)
        add_at(sums, first, group, column, SLOT_GROUPS, SLOT_COLS)
        one_ref[...] += dot_rows(first, feat_ref[:, s])

    pipelined((grad_rows, second_grad, first_grad, sum_rows), spans_of((first_ref,), CHUNK))
    slot_gradients((g0, g1, g2, g3), sums, w1[D : 2 * D])
    local_grads = target_grads(total, local_ref, w1[2 * D : 3 * D], start, grad_ref, groups, n)
    slot_grads = slot_weight_grads(sums, slots)
    write_packed(pieces, one_ref[...], slot_grads, local_grads, two_ref[...], wn1_grad[...], wn2_grad[...],
                 pack_columns(edge_sums, node_sums))
    core = level_ref[1]
    up_half = jnp.concatenate([pieces[0], pieces[1]], axis=1)
    down_half = jnp.concatenate([packed_down_ref[0], packed_down_ref[1]], axis=1)
    keep_ref[...] = jnp.where(core == 0, up_half, down_half)
    give_ref[...] = jnp.where(core == 0, down_half, up_half).astype(B16)


def feat_grad_kernel(first_ref, w1_ref, out_ref):
    out_ref[...] = dot(transposed(w1_ref[0, :, 0:D]), first_ref[...])


def lower_grad_kernel(ids_ref, from_low, from_high, h0, h1, h2, h3, send_ref, start_ref, out_ref, total):
    groups, n = groups_of(start_ref.shape[1])
    clear((total,))
    add_back(total, (from_low, from_high, h0, h1, h2, h3), send_ref, ids_ref[0], groups, n)
    for j in range(groups):
        s = slice(j * n, (j + 1) * n)
        out_ref[:, s] = start_ref[:, s] + total[j * D : (j + 1) * D, :]


def unpack_kernel(ids_ref, own_ref, other_ref, w1_ref, w2_ref, wn1_ref, wn2_ref, biases_ref, gains_ref):
    core = ids_ref[1]
    own, other = own_ref[...].astype(F32), other_ref[...].astype(F32)
    for k in range(2):
        half = jnp.where(core == k, own, other)
        w1_ref[k] = half[:, 0 : 3 * D]
        w2_ref[k] = half[:, 3 * D : 4 * D]
        wn1_ref[k] = half[:, 4 * D : 6 * D]
        wn2_ref[k] = half[:, 6 * D : 7 * D]
        rows = half[:, 6 * D : 8 * D].T
        for i in range(6):
            biases_ref[i, k : k + 1] = rows[D + i : D + i + 1]
        gains_ref[k] = rows[D + 6 : D + 8]


def shape(dims, dtype=F32):
    return jax.ShapeDtypeStruct(dims, dtype)


def call(kernel, name, outs, scratch, scalars=0, stored=(), streamed=None, final=(), raw=()):
    steps, stream_in, stream_out = streamed if streamed else (1, (), ())

    def run(*operands, after=()):
        def whole(space):
            return pl.BlockSpec(memory_space=space)

        def cut(x):
            return pl.BlockSpec((x.shape[0], x.shape[1] // steps), lambda i: (0, i))

        in_specs, placed = [], []
        for i, x in enumerate(operands):
            if i < scalars:
                in_specs.append(whole(pltpu.SMEM))
            elif i in stream_in:
                in_specs.append(cut(x))
            elif i in raw:
                in_specs.append(whole(pltpu.HBM))
                x = pltpu.with_memory_space_constraint(x, pltpu.HBM)
            else:
                in_specs.append(whole(pltpu.VMEM))
                x = pltpu.with_memory_space_constraint(x, pltpu.VMEM)
            placed.append(x)
        in_specs += [whole(pl.ANY) for _ in after]
        out_specs, out_shape = [], []
        for i, x in enumerate(outs):
            if i in stream_out:
                out_specs.append(cut(x))
                out_shape.append(x)
            elif i in stored:
                out_specs.append(whole(pl.ANY))
                out_shape.append(x)
            elif i in final:
                out_specs.append(whole(pltpu.VMEM))
                out_shape.append(x)
            else:
                out_specs.append(whole(pltpu.VMEM))
                out_shape.append(pltpu.VMEM(x.shape, x.dtype))
        return pl.pallas_call(
            kernel,
            name=name,
            grid=(steps,) if streamed else (),
            in_specs=in_specs,
            out_specs=out_specs,
            out_shape=out_shape,
            scratch_shapes=scratch,
            compiler_params=pltpu.CompilerParams(vmem_limit_bytes=VMEM_BYTES),
        )(*placed, *after)

    return run


def along_band(block, step):
    count = lax.axis_size("band")
    return lax.ppermute(block, "band", [(i, (i + step) % count) for i in range(count)])


def along_level(block, step):
    count = lax.axis_size("level")
    return lax.ppermute(block, "level", [(i, (i + step) % count) for i in range(count)])


def across_bands(blocks):
    up = along_band(jnp.stack([b[2] for b in blocks]), 1)
    down = along_band(jnp.stack([b[0] for b in blocks]), -1)
    return [up, down] + blocks


def along_levels(blocks, sign):
    return [blocks[0]] + [along_level(blocks[d], sign * d) for d in (1, 2, 3)]


def chip_axis(block, stride, length, step):
    count = lax.axis_size("band")
    pairs = []
    for i in range(count):
        at = (i // stride) % length
        pairs.append((i, i + (((at + step) % length) - at) * stride))
    return lax.ppermute(block, "band", pairs)


def rounded(values):
    return lax.reduce_precision(values, 8, 7)


def sum_of_four(values, send):
    own = rounded(values)
    sent = own.astype(B16)
    first, second, third = (send(sent, d).astype(F32) for d in (1, 2, 3))
    return (own + second) + (first + third)


def shards(
    lower_nodes, latent, up_feat, down_feat, up_send, up_counts, up_senders, up_targets,
    down_send, down_counts, down_senders, down_targets,
    edge_w1, edge_w2, node_w1, node_w2, biases, norm_gains, lower_cot, upper_cot,
):
    lower, upper = lower_nodes.T, latent.T
    feat_up, feat_down = up_feat.T, down_feat.T
    cot_lower, cot_upper = lower_cot.T, upper_cot.T
    w1, wn1 = edge_w1.transpose(0, 2, 1), node_w1.transpose(0, 2, 1)
    w2, wn2 = edge_w2, node_w2
    edges, lower_rows, upper_rows = up_feat.shape[0], lower_nodes.shape[0], latent.shape[0]
    senders_up, targets_up = up_senders.reshape(1, edges), up_targets.reshape(1, edges)
    senders_down, targets_down = down_senders.reshape(1, edges), down_targets.reshape(1, edges)
    bias_rows = biases.transpose(1, 0, 2)
    ids = jnp.stack([lax.axis_index("level"), lax.axis_index("band") & 1]).astype(jnp.int32)

    lower_groups, lower_n = groups_of(lower_rows)
    upper_groups, upper_n = groups_of(upper_rows)
    lower_table, upper_table = (lower_groups * D, lower_n), (upper_groups * D, upper_n)
    slots = pltpu.VMEM((SLOT_GROUPS * D, SLOT_COLS), B16)
    received = shape((3, D, 128), B16)
    wide32, wide16, row = shape((D, edges)), shape((D, edges), B16), shape((1, edges))
    steps = edges // EDGE_BLOCK

    early = (up_send, lower, targets_up, feat_up, upper, w1, bias_rows, norm_gains, targets_down, feat_down,
             senders_up, down_send, w2, wn1, wn2, senders_down)
    count = len(early)
    (*sent, up_send, lower, targets_up, feat_up, upper, w1, bias_rows, norm_gains, targets_down, feat_down,
     senders_up, down_send, w2, wn1, wn2, senders_down) = call(
        functools.partial(send_kernel, count), "send_lower", [received] * 4 + [shape(x.shape, x.dtype) for x in early],
        [pltpu.VMEM(lower_table, B16), pltpu.SemaphoreType.DMA((count,))], 1, raw=range(1, count + 1))(ids, *early)
    half = edges // 2
    sent = along_levels(sent, 1)
    (part_up,) = call(functools.partial(part_kernel, 0, 0), "part_up", [wide32], [pltpu.VMEM(upper_table, B16)])(
        targets_up, feat_up, upper, w1, bias_rows, norm_gains)
    sent, part_up = lax.optimization_barrier((sent, part_up))
    up_slots = across_bands(sent)
    (part_a,) = call(functools.partial(part_kernel, 1, 0), "part_down_a", [shape((D, half))], [pltpu.VMEM(lower_table, B16)])(
        targets_down, feat_down, lower, w1, bias_rows, norm_gains, after=(sent[1],))
    up_slots, part_a = lax.optimization_barrier((up_slots, part_a))
    (upper_new, summed_up, s0, s1, s2, s3, slope, normed, hidden, factor, alive) = call(
        up_forward_kernel, "up_forward",
        [shape((D, upper_rows)), shape((D, upper_rows), B16)] + [received] * 4 + [wide32, wide32, wide16, row, row],
        [slots, pltpu.VMEM(upper_table, F32), pltpu.VMEM(upper_table, B16), pltpu.VMEM((D, upper_rows), F32),
         pltpu.SemaphoreType.DMA], 2, (0,),
    )(ids, up_counts, senders_up, targets_up, part_up, *up_slots, upper, down_send, w1, w2, wn1, wn2, bias_rows, norm_gains)
    sent = along_levels([s0, s1, s2, s3], 1)
    (part_b,) = call(functools.partial(part_kernel, 1, half), "part_down_b", [shape((D, half))], [pltpu.VMEM(lower_table, B16)])(
        targets_down, feat_down, lower, w1, bias_rows, norm_gains, after=(s0,))
    sent, part_b = lax.optimization_barrier((sent, part_b))
    down_slots = across_bands(sent)
    sums_shape = shape((SLOT_GROUPS * D, SLOT_COLS))
    four = shape((4, D, 128))
    (lower_new, g0, g1, g2, g3, first_down, second_down, hidden_down, start_lower, sums_down, edge_sums, node_sums, wn1_grad, wn2_grad) = call(
        down_kernel, "down_sweep",
        [shape((D, lower_rows))] + [received] * 4 + [wide16] * 3 + [shape((D, lower_rows)), sums_shape, four, four,
         shape((D, 2 * D)), shape((D, D))],
        [slots, pltpu.VMEM(lower_table, F32), pltpu.VMEM(lower_table, B16), pltpu.VMEM((D, edges), F32),
         pltpu.VMEM((D, edges), F32), pltpu.VMEM((1, edges), F32), pltpu.VMEM((1, edges), F32),
         pltpu.VMEM((D, lower_rows), F32), pltpu.SemaphoreType.DMA], 2, (0,),
    )(ids, down_counts, senders_down, targets_down, part_a, part_b, *down_slots, lower, cot_lower, w1, w2, wn1, wn2, bias_rows, norm_gains)
    back = along_levels([g0, g1, g2, g3], -1)
    start_lower, local_grads = call(
        down_targets_kernel, "down_targets", [shape((D, lower_rows)), shape((D, D))], [pltpu.VMEM(lower_table, F32)],
    )(targets_down, first_down, lower, start_lower, w1)
    back, local_grads = lax.optimization_barrier((back, local_grads))
    down_back = across_bands(back)
    feat_grad_down, packed_down = call(
        down_rest_kernel, "down_rest", [wide32, shape((2, D, 256))],
        [slots, pltpu.VMEM((D, D), F32), pltpu.VMEM((D, D), F32)], 0, (), (steps, (0,), (0,)),
    )(feat_down, first_down, second_down, hidden_down, *down_slots, sums_down, local_grads,
      edge_sums, node_sums, wn1_grad, wn2_grad, w1, after=(back[1],))
    (g0, g1, g2, g3, first_up, grad_latent, keep, give) = call(
        up_backward_kernel, "up_backward",
        [received] * 4 + [wide16, shape((D, upper_rows)), shape((D, 512)), shape((D, 512), B16)],
        [slots, pltpu.VMEM(upper_table, B16), pltpu.VMEM(upper_table, F32), pltpu.VMEM(upper_table, F32),
         pltpu.VMEM((SLOT_GROUPS * D, SLOT_COLS), F32), pltpu.VMEM((D, upper_rows), F32),
         pltpu.VMEM((D, D), F32), pltpu.VMEM((D, D), F32), pltpu.VMEM((4, D, 128), F32), pltpu.VMEM((4, D, 128), F32),
         pltpu.VMEM((D, 2 * D), F32), pltpu.VMEM((D, D), F32), pltpu.VMEM((2, D, 256), F32)], 1, (), None, (5,),
    )(ids, senders_up, targets_up, feat_up, *down_back, down_send, cot_upper, upper, summed_up, *up_slots,
      slope, normed, hidden, factor, alive, packed_down, w1, w2, wn1, wn2, bias_rows, norm_gains)
    (feat_grad_up,) = call(feat_grad_kernel, "feat_grad_up", [wide32], [], 0, (), (steps, (0,), (0,)))(first_up, w1)
    total = rounded(keep) + chip_axis(give, 1, 2, 1).astype(F32)
    back = along_levels([g0, g1, g2, g3], -1)
    total, feat_grad_up = lax.optimization_barrier((total, feat_grad_up))
    total = sum_of_four(total, along_level)
    up_back = across_bands(back)
    total, up_back = lax.optimization_barrier((total, up_back))
    total = sum_of_four(total, lambda v, d: chip_axis(v, 2, 4, d))
    (grad_lower,) = call(lower_grad_kernel, "lower_grad", [shape((D, lower_rows))], [pltpu.VMEM(lower_table, F32)], 1, (), None, (0,))(
        ids, *up_back, up_send, start_lower)
    total, grad_lower = lax.optimization_barrier((total, grad_lower))
    total = sum_of_four(total, lambda v, d: chip_axis(v, 8, 4, d))
    total = rounded(total).astype(B16)
    w1_grad, w2_grad, wn1_grad, wn2_grad, bias_grad, gain_grad = call(
        unpack_kernel, "unpack",
        [shape((2, D, 3 * D)), shape((2, D, D)), shape((2, D, 2 * D)), shape((2, D, D)), shape((6, 2, D)), shape((2, 2, D))],
        [], 1, (), None, range(6))(ids, total, chip_axis(total, 1, 2, 1))
    return (
        lower_new.T, upper_new.T, grad_lower.T, grad_latent.T, feat_grad_up.T, feat_grad_down.T,
        w1_grad.transpose(0, 2, 1), w2_grad, wn1_grad.transpose(0, 2, 1), wn2_grad, bias_grad.transpose(1, 0, 2), gain_grad,
    )


def solution(mesh):
    rows, index, whole = P(("band", "level"), None), P(("band", "level")), P()
    placed = (rows,) * 6 + (index, index) + (rows,) * 2 + (index, index) + (whole,) * 6 + (rows,) * 2
    return jax.shard_map(
        shards,
        mesh=mesh,
        in_specs=placed,
        out_specs=(rows,) * 6 + (whole,) * 6,
        check_vma=False,
    )
```

```python
import functools

import jax
import jax.numpy as jnp
from jax import lax
from jax.experimental import pallas as pl
from jax.experimental.pallas import tpu as pltpu
from jax.sharding import PartitionSpec as P

EPSILON = 1e-05
F32 = jnp.float32
B16 = jnp.bfloat16
D = 64
SLOT_GROUPS, SLOT_COLS = 6, 256
EDGE_BLOCK = 3072
CHUNK = 1024
VMEM_BYTES = 24 * 1024 * 1024


def groups_of(rows):
    return (4, rows // 4) if rows > 1024 else (rows // 256, 256)


def dot(a, b):
    return jnp.dot(a, b, preferred_element_type=F32)


def dot_rows(a, b):
    return lax.dot_general(a, b, (((1,), (1,)), ((), ())), preferred_element_type=F32)


def halves(x):
    high = x.astype(B16)
    return high, (x - high.astype(F32)).astype(B16)


def one_hot(column, n):
    rows = lax.broadcasted_iota(jnp.int16, (n, column.shape[1]), 0)
    return jnp.where(rows == column.astype(jnp.int16), jnp.ones((), B16), jnp.zeros((), B16))


def place(index, groups, n):
    group = jnp.zeros_like(index)
    for j in range(1, groups):
        group = group + (index >= j * n).astype(jnp.int32)
    return group, index - group * n


def slot_place(senders, level):
    distance = (level - ((senders >> 7) & 3)) & 3
    block = distance * 3 + (senders >> 9)
    return block >> 1, ((block & 1) << 7) | (senders & 127)


def live(senders, counts_ref):
    peer = senders >> 7
    limit = jnp.zeros_like(senders)
    for j in range(counts_ref.shape[1]):
        limit = jnp.where(peer == j, counts_ref[0, j], limit)
    return ((senders & 127) < limit).astype(F32)


def choose(stacked, group, groups):
    picked = stacked[0:D]
    for j in range(1, groups):
        picked = jnp.where(group == j, stacked[j * D : (j + 1) * D], picked)
    return picked


def row_of(ref, k, start, size):
    first = start // 128
    return jnp.concatenate([ref[k, r : r + 1, :] for r in range(first, first + size // 128)], axis=1)


def pick(table, group, column, groups, n):
    return choose(dot(table[...], one_hot(column, n)), group, groups).astype(B16)


def spread(values, group, groups):
    wide = jnp.broadcast_to(group.astype(jnp.int16), values.shape)
    nothing = jnp.zeros_like(values)
    return jnp.concatenate([jnp.where(wide == j, values, nothing) for j in range(groups)], axis=0)


def add_at(total, values, group, column, groups, n):
    total[...] += dot_rows(spread(values, group, groups), one_hot(column, n))


def pack_table(table, source, groups, n):
    for j in range(groups):
        table[j * D : (j + 1) * D, :] = source[:, j * n : (j + 1) * n]


def columns_of(biases_ref, gains_ref, k):
    rows = [biases_ref[i, k : k + 1] for i in range(6)] + [gains_ref[k]]
    return jnp.concatenate(rows, axis=0).T


def fold(values):
    total = values[:, 0:128]
    for i in range(128, values.shape[1], 128):
        total = total + values[:, i : i + 128]
    return total


def norm_parts(values):
    centre = values - jnp.sum(values, axis=0, keepdims=True) * (1.0 / D)
    spread_sum = jnp.sum(centre * centre, axis=0, keepdims=True) * (1.0 / D)
    factor = lax.rsqrt(spread_sum + EPSILON)
    return centre * factor, factor


def norm_back(grad, normed, factor, gain):
    scaled = grad * gain
    first = jnp.sum(scaled, axis=0, keepdims=True) * (1.0 / D)
    second = jnp.sum(scaled * normed, axis=0, keepdims=True) * (1.0 / D)
    return factor * (scaled - first - normed * second)


def sigmoid(values):
    return 0.5 * jnp.tanh(0.5 * values) + 0.5


def send_rows(send_ref, k, level):
    return jnp.concatenate(
        [send_ref[pl.ds(k * 4 + ((level + d) & 3), 1), :] for d in range(4)], axis=1
    )


def send_blocks(outs, table, send_ref, level, groups, n):
    for k in range(3):
        group, column = place(send_rows(send_ref, k, level), groups, n)
        rows = pick(table, group, column, groups, n)
        for d in range(4):
            outs[d][k] = rows[:, d * 128 : (d + 1) * 128]


def add_back(total, blocks, send_ref, level, groups, n):
    for k in range(3):
        group, column = place(send_rows(send_ref, k, level), groups, n)
        values = jnp.concatenate([block_at(blocks, d, k) for d in range(4)], axis=1)
        add_at(total, values, group, column, groups, n)


def block_at(received, d, k):
    return received[k // 2][d] if k != 1 else received[2 + d][1]


def slot_table(table, received):
    for t in range(12):
        table[(t >> 1) * D : ((t >> 1) + 1) * D, (t & 1) * 128 : ((t & 1) + 1) * 128] = block_at(received, t // 3, t % 3)


def slot_gradients(outs, sums, weight):
    for j in range(SLOT_GROUPS):
        high, low = halves(sums[j * D : (j + 1) * D, :])
        grads = (dot(weight, high) + dot(weight, low)).astype(B16)
        for t in (2 * j, 2 * j + 1):
            outs[t // 3][t % 3] = grads[:, (t & 1) * 128 : ((t & 1) + 1) * 128]


def over_blocks(total, block, body):
    block = min(block, total)
    if block == total:
        body(pl.ds(0, block))
        return

    def step(i, carry):
        body(pl.ds(pl.multiple_of(i * block, block), block))
        return carry

    lax.fori_loop(0, total // block, step, 0)


def pipelined(stages, spans):
    held = [None] * len(spans)
    for t in range(len(spans) + len(stages) - 1):
        for k in reversed(range(len(stages))):
            i = t - k
            if 0 <= i < len(spans):
                held[i] = stages[k](spans[i], held[i])


def spans_of(parts, chunk):
    spans, start = [], 0
    for which, ref in enumerate(parts):
        size = min(chunk, ref.shape[1])
        for at in range(0, ref.shape[1], size):
            spans.append((which, pl.ds(at, size), pl.ds(start + at, size)))
        start += ref.shape[1]
    return spans


def edge_tables(index_ref, alive_ref, senders, targets, counts_ref, level, rows):
    groups, n = groups_of(rows)
    index_ref[0], index_ref[1] = place(targets, groups, n)
    index_ref[2], index_ref[3] = slot_place(senders, level)
    alive_ref[0] = live(senders, counts_ref)


def tables_kernel(upper_rows, lower_rows, ids_ref, up_counts, down_counts, senders_up, targets_up, senders_down, targets_down,
                  index_up, alive_up, index_down, alive_down):
    level = ids_ref[0]
    edge_tables(index_up, alive_up, senders_up[...], targets_up[...], up_counts, level, upper_rows)
    edge_tables(index_down, alive_down, senders_down[...], targets_down[...], down_counts, level, lower_rows)


def send_kernel(count, ids_ref, *refs):
    sources, refs = refs[:count], refs[count:]
    sent, held, table, sems = refs[:4], refs[4:-2], refs[-2], refs[-1]
    copies = [pltpu.make_async_copy(a, b, sems.at[i]) for i, (a, b) in enumerate(zip(sources, held))]
    for copy in copies:
        copy.start()
    for copy in copies[:2]:
        copy.wait()
    send_ref, source_ref = held[:2]
    groups, n = groups_of(source_ref.shape[1])
    pack_table(table, source_ref, groups, n)
    send_blocks(sent, table, send_ref, ids_ref[0], groups, n)
    for copy in copies[2:]:
        copy.wait()


def part_kernel(k, start, index_ref, feat_ref, local_ref, w1_ref, biases_ref, gains_ref, *rest):
    part_ref, held_ref, table, sem = rest[-4:]
    size = part_ref.shape[1]
    copy = pltpu.make_async_copy(feat_ref.at[:, pl.ds(start, size)], held_ref, sem)
    copy.start()
    groups, n = groups_of(local_ref.shape[1])
    pack_table(table, local_ref, groups, n)
    columns = columns_of(biases_ref, gains_ref, k)
    weight = jnp.concatenate([w1_ref[k, :, 0:D], w1_ref[k, :, 2 * D : 3 * D]], axis=1)
    picked = pick(table, row_of(index_ref, 0, start, size), row_of(index_ref, 1, start, size), groups, n)
    copy.wait()
    part_ref[...] = dot(weight, jnp.concatenate([held_ref[...], picked], axis=0)) + columns[:, 0:1]


def edges_forward(k, parts, alive_ref, index_ref, table, w1_ref, w2_ref, columns, total, groups, n,
                  slope_ref, normed_ref, hidden_ref, factor_ref):
    weight_slot = w1_ref[k, :, D : 2 * D]
    weight_two = w2_ref[k].astype(F32).T.astype(B16)
    total[...] = jnp.zeros_like(total)

    def slot_rows(span, unused):
        a, size = span[2].start, span[2].size
        return pick(table, row_of(index_ref, 2, a, size), row_of(index_ref, 3, a, size), SLOT_GROUPS, SLOT_COLS)

    def first_layer(span, picked):
        which, t, s = span
        first = parts[which][:, t] + dot(weight_slot, picked)
        gate = sigmoid(first)
        hidden = (first * gate).astype(B16)
        slope_ref[:, s] = gate * (1.0 + first * (1.0 - gate))
        hidden_ref[:, s] = hidden
        return hidden

    def second_layer(span, hidden):
        s = span[2]
        normed, factor = norm_parts(dot(weight_two, hidden) + columns[:, 1:2])
        alive = row_of(alive_ref, 0, s.start, s.size)
        normed_ref[:, s] = normed
        factor_ref[:, s] = factor
        return ((normed * columns[:, 6:7] + columns[:, 2:3]) * alive).astype(B16)

    def sum_messages(span, messages):
        a, size = span[2].start, span[2].size
        add_at(total, messages, row_of(index_ref, 0, a, size), row_of(index_ref, 1, a, size), groups, n)

    pipelined((slot_rows, first_layer, second_layer, sum_messages), spans_of(parts, CHUNK))


def node_first(k, inputs, wn1_ref, columns):
    first = dot(wn1_ref[k], inputs) + columns[:, 3:4]
    gate = sigmoid(first)
    return (first * gate).astype(B16), gate * (1.0 + first * (1.0 - gate))


def node_second(hidden, weight_two, columns):
    return norm_parts(dot(weight_two, hidden) + columns[:, 4:5])


def node_second_grad(grad, normed, factor, hidden, columns, two_ref, sums_ref):
    second = norm_back(grad, normed, factor, columns[:, 7:8]).astype(B16)
    sums_ref[1] += fold(second.astype(F32))
    sums_ref[2] += fold(grad)
    sums_ref[3] += fold(grad * normed)
    two_ref[...] += dot_rows(hidden, second)
    return second


def node_first_grad(second, slope, inputs, wn2, one_ref, sums_ref):
    first = (dot(wn2, second) * slope).astype(B16)
    sums_ref[0] += fold(first.astype(F32))
    one_ref[...] += dot_rows(first, inputs)
    return first


def clear(refs):
    for ref in refs:
        ref[...] = jnp.zeros_like(ref)


def transposed(weight):
    return weight.astype(F32).T.astype(B16)


def edge_second(grad_rows, s, columns, weight_sum, alive_ref, normed_ref, factor_ref, sums_ref):
    grad = dot(weight_sum, grad_rows) * row_of(alive_ref, 0, s.start, s.size)
    normed = normed_ref[:, s]
    second = norm_back(grad, normed, factor_ref[:, s], columns[:, 6:7]).astype(B16)
    sums_ref[1] += fold(second.astype(F32))
    sums_ref[2] += fold(grad)
    sums_ref[3] += fold(grad * normed)
    return second


def edge_first(second, s, weight_two, slope_ref, sums_ref):
    first = (dot(weight_two, second) * slope_ref[:, s]).astype(B16)
    sums_ref[0] += fold(first.astype(F32))
    return first


def pack_columns(edge_sums, node_sums):
    order = (edge_sums[0], edge_sums[1], edge_sums[2], node_sums[0], node_sums[1], node_sums[2], edge_sums[3], node_sums[3])
    columns = [jnp.sum(v, axis=1, keepdims=True) for v in order]
    lanes = lax.broadcasted_iota(jnp.int32, (D, D), 1)
    packed = jnp.zeros((D, D), F32)
    for i, column in enumerate(columns):
        packed = jnp.where(lanes == i, column, packed)
    return packed


def slot_weight_grads(sums, table):
    total = jnp.zeros((D, D), F32)
    for j in range(SLOT_GROUPS):
        high, low = halves(sums[j * D : (j + 1) * D, :])
        rows = table[j * D : (j + 1) * D, :]
        total = total + dot_rows(high, rows) + dot_rows(low, rows)
    return total


def target_grads(total, local_ref, weight, start_ref, out_ref, groups, n):
    grads = jnp.zeros((D, D), F32)
    for j in range(groups):
        high, low = halves(total[j * D : (j + 1) * D, :])
        s = slice(j * n, (j + 1) * n)
        rows = local_ref[:, s]
        grads = grads + dot_rows(high, rows) + dot_rows(low, rows)
        out_ref[:, s] = start_ref[:, s] + dot(weight, high) + dot(weight, low)
    return grads


def up_forward_kernel(level_ref, part_ref, alive_ref, index_ref, low, high, r0, r1, r2, r3, local_ref, send_ref,
                      w1_ref, w2_ref, wn1_ref, wn2_ref, biases_ref, gains_ref,
                      out_ref, summed_ref, s0, s1, s2, s3, slope_ref, normed_ref, hidden_ref, factor_ref,
                      slots, total, table, out, sem):
    level = level_ref[0]
    groups, n = groups_of(local_ref.shape[1])
    columns = columns_of(biases_ref, gains_ref, 0)
    slot_table(slots, (low, high, r0, r1, r2, r3))
    edges_forward(0, (part_ref,), alive_ref, index_ref, slots, w1_ref, w2_ref, columns, total, groups, n,
                  slope_ref, normed_ref, hidden_ref, factor_ref)
    weight_two = transposed(wn2_ref[0])

    def first_layer(j, unused):
        s = slice(j * n, (j + 1) * n)
        summed = total[j * D : (j + 1) * D, :].astype(B16)
        summed_ref[:, s] = summed
        return node_first(0, jnp.concatenate([local_ref[:, s], summed], axis=0), wn1_ref, columns)

    def second_layer(j, held):
        s = slice(j * n, (j + 1) * n)
        normed, unused = node_second(held[0], weight_two, columns)
        result = local_ref[:, s].astype(F32) + normed * columns[:, 7:8] + columns[:, 5:6]
        out[:, s] = result
        table[j * D : (j + 1) * D, :] = result.astype(B16)

    pipelined((first_layer, second_layer), range(groups))
    copy = pltpu.make_async_copy(out, out_ref, sem)
    copy.start()
    send_blocks((s0, s1, s2, s3), table, send_ref, level, groups, n)
    copy.wait()


def down_kernel(part_a, part_b, alive_ref, index_ref, low, high, r0, r1, r2, r3, local_ref, cot_ref,
                w1_ref, w2_ref, wn1_ref, wn2_ref, biases_ref, gains_ref,
                out_ref, g0, g1, g2, g3, first_ref, second_ref, hidden_ref, grad_ref, sums_ref, edge_sums, node_sums, wn1_grad, wn2_grad,
                slots, total, table, slope_ref, normed_ref, factor_ref, out, sem):
    groups, n = groups_of(local_ref.shape[1])
    columns = columns_of(biases_ref, gains_ref, 1)
    slot_table(slots, (low, high, r0, r1, r2, r3))
    parts = (part_a, part_b)
    edges_forward(1, parts, alive_ref, index_ref, slots, w1_ref, w2_ref, columns, total, groups, n,
                  slope_ref, normed_ref, hidden_ref, factor_ref)
    clear((wn1_grad, wn2_grad, node_sums, edge_sums, sums_ref))
    wn2 = wn2_ref[1]
    wn2_t = transposed(wn2)
    wn1 = transposed(wn1_ref[1])

    def first_layer(j, unused):
        local = local_ref[:, j * n : (j + 1) * n]
        inputs = jnp.concatenate([local, total[j * D : (j + 1) * D, :].astype(B16)], axis=0)
        return inputs, *node_first(1, inputs, wn1_ref, columns)

    def second_layer(j, held):
        inputs, hidden, slope = held
        s = slice(j * n, (j + 1) * n)
        normed, factor = node_second(hidden, wn2_t, columns)
        out[:, s] = local_ref[:, s].astype(F32) + normed * columns[:, 7:8] + columns[:, 5:6]
        return inputs, slope, node_second_grad(cot_ref[:, s], normed, factor, hidden, columns, wn2_grad, node_sums)

    def node_grads(j, held):
        inputs, slope, second = held
        s = slice(j * n, (j + 1) * n)
        first = node_first_grad(second, slope, inputs, wn2, wn1_grad, node_sums)
        table[j * D : (j + 1) * D, :] = first
        grad_ref[:, s] = cot_ref[:, s] + dot(wn1[0:D], first)

    pipelined((first_layer, second_layer, node_grads), range(groups))
    copy = pltpu.make_async_copy(out, out_ref, sem)
    copy.start()
    weight_two = w2_ref[1]
    weight_slot = transposed(w1_ref[1, :, D : 2 * D])

    def grad_rows(span, unused):
        a, size = span[2].start, span[2].size
        return pick(table, row_of(index_ref, 0, a, size), row_of(index_ref, 1, a, size), groups, n)

    def second_grad(span, rows):
        return edge_second(rows, span[2], columns, wn1[D : 2 * D], alive_ref, normed_ref, factor_ref, edge_sums)

    def first_grad(span, second):
        s = span[2]
        first = edge_first(second, s, weight_two, slope_ref, edge_sums)
        first_ref[:, s] = first
        second_ref[:, s] = second
        return first

    def sum_slots(span, first):
        a, size = span[2].start, span[2].size
        add_at(sums_ref, first, row_of(index_ref, 2, a, size), row_of(index_ref, 3, a, size), SLOT_GROUPS, SLOT_COLS)

    pipelined((grad_rows, second_grad, first_grad, sum_slots), spans_of(parts, CHUNK))
    slot_gradients((g0, g1, g2, g3), sums_ref, weight_slot)
    copy.wait()


def down_targets_kernel(index_ref, first_ref, local_ref, start_ref, w1_ref, grad_ref, weight_grad_ref, total):
    groups, n = groups_of(local_ref.shape[1])
    weight = transposed(w1_ref[1, :, 2 * D : 3 * D])
    total[...] = jnp.zeros_like(total)
    for a in range(0, first_ref.shape[1], EDGE_BLOCK):
        group, column = row_of(index_ref, 0, a, EDGE_BLOCK), row_of(index_ref, 1, a, EDGE_BLOCK)
        add_at(total, first_ref[:, a : a + EDGE_BLOCK], group, column, groups, n)
    weight_grad_ref[...] = target_grads(total, local_ref, weight, start_ref, grad_ref, groups, n)


def down_rest_kernel(feat_a, feat_b, first_ref, second_ref, hidden_ref, low, high, r0, r1, r2, r3, sums_ref, local_grads_ref,
                     edge_sums, node_sums, wn1_grad, wn2_grad, w1_ref, *rest):
    feat_grad_ref, packed_ref, slots, one_ref, two_ref = rest[-5:]
    step = pl.program_id(0)
    weight = transposed(w1_ref[1, :, 0:D])

    @pl.when(step == 0)
    def _():
        clear((one_ref, two_ref))

    s = pl.ds(pl.multiple_of(step * EDGE_BLOCK, EDGE_BLOCK), EDGE_BLOCK)
    first = first_ref[:, s]
    feat_grad_ref[...] = dot(weight, first)
    one_ref[...] += dot_rows(first, jnp.where(step == 0, feat_a[...], feat_b[...]))
    two_ref[...] += dot_rows(hidden_ref[:, s], second_ref[:, s])

    @pl.when(step == pl.num_programs(0) - 1)
    def _():
        slot_table(slots, (low, high, r0, r1, r2, r3))
        slot_grads = slot_weight_grads(sums_ref, slots)
        write_packed(packed_ref, one_ref[...], slot_grads, local_grads_ref[...], two_ref[...], wn1_grad[...], wn2_grad[...],
                     pack_columns(edge_sums, node_sums))


def write_packed(packed_ref, one, slot_grads, local_grads, two, wn1_grad, wn2_grad, columns):
    packed_ref[0] = jnp.concatenate([one, slot_grads], axis=1)
    packed_ref[1] = jnp.concatenate([local_grads, two], axis=1)
    packed_ref[2] = wn1_grad
    packed_ref[3] = jnp.concatenate([wn2_grad, columns], axis=1)


def up_backward_kernel(level_ref, index_ref, feat_ref, from_low, from_high, h0, h1, h2, h3,
                       send_ref, cot_ref, local_ref, summed_ref, low, high, r0, r1, r2, r3, slope_ref, normed_ref, hidden_ref, factor_ref, alive_ref, packed_down_ref,
                       w1_ref, w2_ref, wn1_ref, wn2_ref, biases_ref, gains_ref,
                       g0, g1, g2, g3, first_ref, grad_ref, keep_ref, give_ref,
                       slots, table, back, total, sums, start, one_ref, two_ref, edge_sums, node_sums, wn1_grad, wn2_grad, pieces):
    level = level_ref[0]
    groups, n = groups_of(local_ref.shape[1])
    columns = columns_of(biases_ref, gains_ref, 0)
    clear((back, total, sums, one_ref, two_ref, edge_sums, node_sums, wn1_grad, wn2_grad))
    slot_table(slots, (low, high, r0, r1, r2, r3))
    add_back(back, (from_low, from_high, h0, h1, h2, h3), send_ref, level, groups, n)
    wn2 = wn2_ref[0]
    wn2_t = transposed(wn2)
    wn1 = transposed(wn1_ref[0])
    w1 = transposed(w1_ref[0])

    def first_layer(j, unused):
        s = slice(j * n, (j + 1) * n)
        inputs = jnp.concatenate([local_ref[:, s], summed_ref[:, s]], axis=0)
        return inputs, *node_first(0, inputs, wn1_ref, columns)

    def second_layer(j, held):
        inputs, hidden, slope = held
        grad = cot_ref[:, j * n : (j + 1) * n] + back[j * D : (j + 1) * D, :]
        normed, factor = node_second(hidden, wn2_t, columns)
        return inputs, slope, grad, node_second_grad(grad, normed, factor, hidden, columns, wn2_grad, node_sums)

    def node_grads(j, held):
        inputs, slope, grad, second = held
        first = node_first_grad(second, slope, inputs, wn2, wn1_grad, node_sums)
        table[j * D : (j + 1) * D, :] = first
        start[:, j * n : (j + 1) * n] = grad + dot(wn1[0:D], first)

    pipelined((first_layer, second_layer, node_grads), range(groups))
    weight_two = w2_ref[0]

    def grad_rows(span, unused):
        a, size = span[2].start, span[2].size
        return pick(table, row_of(index_ref, 0, a, size), row_of(index_ref, 1, a, size), groups, n)

    def second_grad(span, rows):
        return edge_second(rows, span[2], columns, wn1[D : 2 * D], alive_ref, normed_ref, factor_ref, edge_sums)

    def first_grad(span, second):
        s = span[2]
        first = edge_first(second, s, weight_two, slope_ref, edge_sums)
        first_ref[:, s] = first
        two_ref[...] += dot_rows(hidden_ref[:, s], second)
        return first

    def sum_rows(span, first):
        s = span[2]
        rows = [row_of(index_ref, i, s.start, s.size) for i in range(4)]
        add_at(total, first, rows[0], rows[1], groups, n)
        add_at(sums, first, rows[2], rows[3], SLOT_GROUPS, SLOT_COLS)
        one_ref[...] += dot_rows(first, feat_ref[:, s])

    pipelined((grad_rows, second_grad, first_grad, sum_rows), spans_of((first_ref,), CHUNK))
    slot_gradients((g0, g1, g2, g3), sums, w1[D : 2 * D])
    local_grads = target_grads(total, local_ref, w1[2 * D : 3 * D], start, grad_ref, groups, n)
    slot_grads = slot_weight_grads(sums, slots)
    write_packed(pieces, one_ref[...], slot_grads, local_grads, two_ref[...], wn1_grad[...], wn2_grad[...],
                 pack_columns(edge_sums, node_sums))
    core = level_ref[1]
    for p in range(4):
        pieces[4 + p] = packed_down_ref[p]
    for d in range(4):
        piece = (level + d) & 3
        keep_ref[d] = pieces[core * 4 + piece]
        give_ref[d] = pieces[(1 - core) * 4 + piece].astype(B16)


def feat_grad_kernel(first_ref, w1_ref, out_ref):
    out_ref[...] = dot(transposed(w1_ref[0, :, 0:D]), first_ref[...])


def lower_grad_kernel(ids_ref, from_low, from_high, h0, h1, h2, h3, send_ref, start_ref, *rest):
    out_ref, total = rest[-2:]
    groups, n = groups_of(start_ref.shape[1])
    clear((total,))
    add_back(total, (from_low, from_high, h0, h1, h2, h3), send_ref, ids_ref[0], groups, n)
    for j in range(groups):
        s = slice(j * n, (j + 1) * n)
        out_ref[:, s] = start_ref[:, s] + total[j * D : (j + 1) * D, :]


def unpack_kernel(ids_ref, own_ref, other_ref, w1_ref, w2_ref, wn1_ref, wn2_ref, biases_ref, gains_ref, pieces):
    level, core = ids_ref[0], ids_ref[1]
    for d in range(4):
        piece = (level - d) & 3
        pieces[core * 4 + piece] = own_ref[d].astype(F32)
        pieces[(1 - core) * 4 + piece] = other_ref[d].astype(F32)
    for k in range(2):
        w1_ref[k] = jnp.concatenate([pieces[4 * k], pieces[4 * k + 1, :, 0:D]], axis=1)
        w2_ref[k] = pieces[4 * k + 1, :, D : 2 * D]
        wn1_ref[k] = pieces[4 * k + 2]
        wn2_ref[k] = pieces[4 * k + 3, :, 0:D]
        rows = pieces[4 * k + 3].T
        for i in range(6):
            biases_ref[i, k : k + 1] = rows[D + i : D + i + 1]
        gains_ref[k] = rows[D + 6 : D + 8]


def shape(dims, dtype=F32):
    return jax.ShapeDtypeStruct(dims, dtype)


def call(kernel, name, outs, scratch, scalars=0, stored=(), streamed=None, final=(), raw=()):
    steps, stream_in, stream_out = streamed if streamed else (1, (), ())

    def run(*operands, after=()):
        def whole(space):
            return pl.BlockSpec(memory_space=space)

        def cut(x):
            return pl.BlockSpec((x.shape[0], x.shape[1] // steps), lambda i: (0, i))

        in_specs, placed = [], []
        for i, x in enumerate(operands):
            if i < scalars:
                in_specs.append(whole(pltpu.SMEM))
            elif i in stream_in:
                in_specs.append(cut(x))
            elif i in raw:
                in_specs.append(whole(pltpu.HBM))
                x = pltpu.with_memory_space_constraint(x, pltpu.HBM)
            else:
                in_specs.append(whole(pltpu.VMEM))
                x = pltpu.with_memory_space_constraint(x, pltpu.VMEM)
            placed.append(x)
        in_specs += [whole(pl.ANY) for _ in after]
        out_specs, out_shape = [], []
        for i, x in enumerate(outs):
            if i in stream_out:
                out_specs.append(cut(x))
                out_shape.append(x)
            elif i in stored:
                out_specs.append(whole(pl.ANY))
                out_shape.append(x)
            elif i in final:
                out_specs.append(whole(pltpu.VMEM))
                out_shape.append(x)
            else:
                out_specs.append(whole(pltpu.VMEM))
                out_shape.append(pltpu.VMEM(x.shape, x.dtype))
        return pl.pallas_call(
            kernel,
            name=name,
            grid=(steps,) if streamed else (),
            in_specs=in_specs,
            out_specs=out_specs,
            out_shape=out_shape,
            scratch_shapes=scratch,
            compiler_params=pltpu.CompilerParams(vmem_limit_bytes=VMEM_BYTES),
        )(*placed, *after)

    return run


def along_band(block, step):
    count = lax.axis_size("band")
    return lax.ppermute(block, "band", [(i, (i + step) % count) for i in range(count)])


def along_level(block, step):
    count = lax.axis_size("level")
    return lax.ppermute(block, "level", [(i, (i + step) % count) for i in range(count)])


def across_bands(blocks):
    up = along_band(jnp.stack([b[2] for b in blocks]), 1)
    down = along_band(jnp.stack([b[0] for b in blocks]), -1)
    return [up, down] + blocks


def along_levels(blocks, sign):
    return [blocks[0]] + [along_level(blocks[d], sign * d) for d in (1, 2, 3)]


def chip_axis(block, stride, length, step):
    count = lax.axis_size("band")
    pairs = []
    for i in range(count):
        at = (i // stride) % length
        pairs.append((i, i + (((at + step) % length) - at) * stride))
    return lax.ppermute(block, "band", pairs)


def rounded(values):
    return lax.reduce_precision(values, 8, 7)


def sum_of_four(values, send):
    own = rounded(values)
    sent = own.astype(B16)
    first, second, third = (send(sent, d).astype(F32) for d in (1, 2, 3))
    return (own + second) + (first + third)


def shards(
    lower_nodes, latent, up_feat, down_feat, up_send, up_counts, up_senders, up_targets,
    down_send, down_counts, down_senders, down_targets,
    edge_w1, edge_w2, node_w1, node_w2, biases, norm_gains, lower_cot, upper_cot,
):
    lower, upper = lower_nodes.T, latent.T
    feat_up, feat_down = up_feat.T, down_feat.T
    cot_lower, cot_upper = lower_cot.T, upper_cot.T
    w1, wn1 = edge_w1.transpose(0, 2, 1), node_w1.transpose(0, 2, 1)
    w2, wn2 = edge_w2, node_w2
    edges, lower_rows, upper_rows = up_feat.shape[0], lower_nodes.shape[0], latent.shape[0]
    dense = (edges // 128, 128)
    senders_up, targets_up, senders_down, targets_down = (
        x.reshape(dense) for x in (up_senders, up_targets, down_senders, down_targets))
    bias_rows = biases.transpose(1, 0, 2)
    ids = jnp.stack([lax.axis_index("level"), lax.axis_index("band") & 1]).astype(jnp.int32)

    lower_groups, lower_n = groups_of(lower_rows)
    upper_groups, upper_n = groups_of(upper_rows)
    lower_table, upper_table = (lower_groups * D, lower_n), (upper_groups * D, upper_n)
    slots = pltpu.VMEM((SLOT_GROUPS * D, SLOT_COLS), B16)
    received, four, packed = shape((3, D, 128), B16), shape((4, D, 128)), shape((4, D, 128), B16)
    wide32, wide16, row = shape((D, edges)), shape((D, edges), B16), shape((1, edges))
    steps = edges // EDGE_BLOCK
    half = edges // 2

    early = (up_send, lower, senders_up, targets_up, senders_down, targets_down, upper, w1, bias_rows, norm_gains,
             down_send, w2, wn1, wn2)
    count = len(early)
    (*sent, up_send, lower, senders_up, targets_up, senders_down, targets_down, upper, w1, bias_rows,
     norm_gains, down_send, w2, wn1, wn2) = call(
        functools.partial(send_kernel, count), "send_lower", [received] * 4 + [shape(x.shape, x.dtype) for x in early],
        [pltpu.VMEM(lower_table, B16), pltpu.SemaphoreType.DMA((count,))], 1, raw=range(1, count + 1),
    )(ids, *early)
    index, lives = shape((4, *dense), jnp.int32), shape((1, *dense))
    index_up, alive_up, index_down, alive_down = call(
        functools.partial(tables_kernel, upper_rows, lower_rows), "edge_tables", [index, lives, index, lives], [], 3,
    )(ids, up_counts, down_counts, senders_up, targets_up, senders_down, targets_down)

    def part(k, start, size, name, table, index, feat, local, after):
        return call(
            functools.partial(part_kernel, k, start), name, [shape((D, size)), shape((D, size), B16)],
            [pltpu.VMEM(table, B16), pltpu.SemaphoreType.DMA], 0, raw=(1,),
        )(index, feat, local, w1, bias_rows, norm_gains, after=after)

    sent = along_levels(sent, 1)
    part_up, feat_up = part(0, 0, edges, "part_up", upper_table, index_up, feat_up, upper, ())
    sent, part_up = lax.optimization_barrier((sent, part_up))
    up_slots = across_bands(sent)
    part_a, feat_a = part(1, 0, half, "part_down_a", lower_table, index_down, feat_down, lower, (sent[1],))
    up_slots, part_a = lax.optimization_barrier((up_slots, part_a))
    (upper_new, summed_up, s0, s1, s2, s3, slope, normed, hidden, factor) = call(
        up_forward_kernel, "up_forward",
        [shape((D, upper_rows)), shape((D, upper_rows), B16)] + [received] * 4 + [wide32, wide32, wide16, row],
        [slots, pltpu.VMEM(upper_table, F32), pltpu.VMEM(upper_table, B16), pltpu.VMEM((D, upper_rows), F32),
         pltpu.SemaphoreType.DMA], 1, (0,),
    )(ids, part_up, alive_up, index_up, *up_slots, upper, down_send, w1, w2, wn1, wn2, bias_rows, norm_gains)
    sent = along_levels([s0, s1, s2, s3], 1)
    part_b, feat_b = part(1, half, half, "part_down_b", lower_table, index_down, feat_down, lower, (s0,))
    sent, part_b = lax.optimization_barrier((sent, part_b))
    down_slots = across_bands(sent)
    sums_shape = shape((SLOT_GROUPS * D, SLOT_COLS))
    (lower_new, g0, g1, g2, g3, first_down, second_down, hidden_down, start_lower, sums_down, edge_sums, node_sums, wn1_grad, wn2_grad) = call(
        down_kernel, "down_sweep",
        [shape((D, lower_rows))] + [received] * 4 + [wide16] * 3 + [shape((D, lower_rows)), sums_shape, four, four,
         shape((D, 2 * D)), shape((D, D))],
        [slots, pltpu.VMEM(lower_table, F32), pltpu.VMEM(lower_table, B16), pltpu.VMEM((D, edges), F32),
         pltpu.VMEM((D, edges), F32), pltpu.VMEM((1, edges), F32),
         pltpu.VMEM((D, lower_rows), F32), pltpu.SemaphoreType.DMA], 0, (0,),
    )(part_a, part_b, alive_down, index_down, *down_slots, lower, cot_lower, w1, w2, wn1, wn2, bias_rows, norm_gains)
    back = along_levels([g0, g1, g2, g3], -1)
    start_lower, local_grads = call(
        down_targets_kernel, "down_targets", [shape((D, lower_rows)), shape((D, D))], [pltpu.VMEM(lower_table, F32)],
    )(index_down, first_down, lower, start_lower, w1)
    back, local_grads = lax.optimization_barrier((back, local_grads))
    down_back = across_bands(back)
    feat_grad_down, packed_down = call(
        down_rest_kernel, "down_rest", [wide32, four],
        [slots, pltpu.VMEM((D, D), F32), pltpu.VMEM((D, D), F32)], 0, (), (steps, (), (0,)),
    )(feat_a, feat_b, first_down, second_down, hidden_down, *down_slots, sums_down, local_grads,
      edge_sums, node_sums, wn1_grad, wn2_grad, w1, after=(back[1],))
    (g0, g1, g2, g3, first_up, grad_latent, keep, give) = call(
        up_backward_kernel, "up_backward",
        [received] * 4 + [wide16, shape((D, upper_rows)), four, packed],
        [slots, pltpu.VMEM(upper_table, B16), pltpu.VMEM(upper_table, F32), pltpu.VMEM(upper_table, F32),
         pltpu.VMEM((SLOT_GROUPS * D, SLOT_COLS), F32), pltpu.VMEM((D, upper_rows), F32),
         pltpu.VMEM((D, D), F32), pltpu.VMEM((D, D), F32), pltpu.VMEM((4, D, 128), F32), pltpu.VMEM((4, D, 128), F32),
         pltpu.VMEM((D, 2 * D), F32), pltpu.VMEM((D, D), F32), pltpu.VMEM((8, D, 128), F32)], 1, (), None, (5,),
    )(ids, index_up, feat_up, *down_back, down_send, cot_upper, upper, summed_up, *up_slots,
      slope, normed, hidden, factor, alive_up, packed_down, w1, w2, wn1, wn2, bias_rows, norm_gains)

    given = chip_axis(give, 1, 2, 1)
    (feat_grad_up,) = call(feat_grad_kernel, "feat_grad_up", [wide32], [], 0, (), (steps, (0,), (0,)))(first_up, w1)
    given, feat_grad_up, g1, g2, g3 = lax.optimization_barrier((given, feat_grad_up, g1, g2, g3))
    total = rounded(rounded(keep) + given.astype(F32))
    one, two, three = (along_level(total[d].astype(B16), d).astype(F32) for d in (1, 2, 3))
    total = (total[0] + two) + (one + three)
    back = along_levels([g0, g1, g2, g3], -1)
    total, back = lax.optimization_barrier((total, back))
    total = sum_of_four(total, lambda v, d: chip_axis(v, 2, 4, d))
    up_back = across_bands(back)
    (grad_lower,) = call(lower_grad_kernel, "lower_grad", [shape((D, lower_rows))], [pltpu.VMEM(lower_table, F32)], 1, (), None, (0,))(
        ids, *up_back, up_send, start_lower, after=(total,))
    total = sum_of_four(total, lambda v, d: chip_axis(v, 8, 4, d))
    total, grad_lower = lax.optimization_barrier((total, grad_lower))
    total = rounded(total).astype(B16)
    total = jnp.stack([total] + [along_level(total, d) for d in (1, 2, 3)])
    w1_grad, w2_grad, wn1_grad, wn2_grad, bias_grad, gain_grad = call(
        unpack_kernel, "unpack",
        [shape((2, D, 3 * D)), shape((2, D, D)), shape((2, D, 2 * D)), shape((2, D, D)), shape((6, 2, D)), shape((2, 2, D))],
        [pltpu.VMEM((8, D, 128), F32)], 1, (), None, range(6))(ids, total, chip_axis(total, 1, 2, 1))
    return (
        lower_new.T, upper_new.T, grad_lower.T, grad_latent.T, feat_grad_up.T, feat_grad_down.T,
        w1_grad.transpose(0, 2, 1), w2_grad, wn1_grad.transpose(0, 2, 1), wn2_grad, bias_grad.transpose(1, 0, 2), gain_grad,
    )


def solution(mesh):
    rows, index, whole = P(("band", "level"), None), P(("band", "level")), P()
    placed = (rows,) * 6 + (index, index) + (rows,) * 2 + (index, index) + (whole,) * 6 + (rows,) * 2
    return jax.shard_map(
        shards,
        mesh=mesh,
        in_specs=placed,
        out_specs=(rows,) * 6 + (whole,) * 6,
        check_vma=False,
    )
```

```python
import functools

import jax
import jax.numpy as jnp
from jax import lax
from jax.experimental import pallas as pl
from jax.experimental.pallas import tpu as pltpu
from jax.sharding import PartitionSpec as P

EPSILON = 1e-05
F32 = jnp.float32
B16 = jnp.bfloat16
D = 64
SLOT_GROUPS, SLOT_COLS = 6, 256
EDGE_BLOCK = 3072
CHUNK = 1024
VMEM_BYTES = 24 * 1024 * 1024


def groups_of(rows):
    return (4, rows // 4) if rows > 1024 else (rows // 256, 256)


def dot(a, b):
    return jnp.dot(a, b, preferred_element_type=F32)


def dot_rows(a, b):
    return lax.dot_general(a, b, (((1,), (1,)), ((), ())), preferred_element_type=F32)


def halves(x):
    high = x.astype(B16)
    return high, (x - high.astype(F32)).astype(B16)


def one_hot(column, n):
    rows = lax.broadcasted_iota(jnp.int16, (n, column.shape[1]), 0)
    return jnp.where(rows == column.astype(jnp.int16), jnp.ones((), B16), jnp.zeros((), B16))


def place(index, groups, n):
    group = jnp.zeros_like(index)
    for j in range(1, groups):
        group = group + (index >= j * n).astype(jnp.int32)
    return group, index - group * n


def slot_place(senders, level, core):
    distance = (level - ((senders >> 7) & 3)) & 3
    offset = senders >> 9
    source = jnp.where(offset == 1, 2, jnp.where(offset == 2 - 2 * core, 0, 1))
    block = distance * 3 + source
    return block >> 1, ((block & 1) << 7) | (senders & 127)


def live(senders, ids_ref, first):
    peer = senders >> 7
    limit = jnp.zeros_like(senders)
    for j in range(12):
        limit = jnp.where(peer == j, ids_ref[first + j], limit)
    return ((senders & 127) < limit).astype(F32)


def choose(stacked, group, groups):
    picked = stacked[0:D]
    for j in range(1, groups):
        picked = jnp.where(group == j, stacked[j * D : (j + 1) * D], picked)
    return picked


def row_of(ref, k, start, size):
    first = start // 128
    return jnp.concatenate([ref[k, r : r + 1, :] for r in range(first, first + size // 128)], axis=1)


def pick(table, group, column, groups, n):
    return choose(dot(table[...], one_hot(column, n)), group, groups).astype(B16)


def spread(values, group, groups):
    wide = jnp.broadcast_to(group.astype(jnp.int16), values.shape)
    nothing = jnp.zeros_like(values)
    return jnp.concatenate([jnp.where(wide == j, values, nothing) for j in range(groups)], axis=0)


def add_at(total, values, group, column, groups, n):
    total[...] += dot_rows(spread(values, group, groups), one_hot(column, n))


def pack_table(table, source, groups, n):
    for j in range(groups):
        table[j * D : (j + 1) * D, :] = source[:, j * n : (j + 1) * n]


def columns_of(biases_ref, gains_ref, k):
    rows = [biases_ref[i, k : k + 1] for i in range(6)] + [gains_ref[k]]
    return jnp.concatenate(rows, axis=0).T


def fold(values):
    total = values[:, 0:128]
    for i in range(128, values.shape[1], 128):
        total = total + values[:, i : i + 128]
    return total


def norm_parts(values):
    centre = values - jnp.sum(values, axis=0, keepdims=True) * (1.0 / D)
    spread_sum = jnp.sum(centre * centre, axis=0, keepdims=True) * (1.0 / D)
    factor = lax.rsqrt(spread_sum + EPSILON)
    return centre * factor, factor


def norm_back(grad, normed, factor, gain):
    scaled = grad * gain
    first = jnp.sum(scaled, axis=0, keepdims=True) * (1.0 / D)
    second = jnp.sum(scaled * normed, axis=0, keepdims=True) * (1.0 / D)
    return factor * (scaled - first - normed * second)


def sigmoid(values):
    return 0.5 * jnp.tanh(0.5 * values) + 0.5


def send_rows(send_ref, source, ids_ref):
    level, core = ids_ref[0], ids_ref[1]
    offset = (2 - 2 * core, 2 * core, 1)[source]
    return jnp.concatenate(
        [send_ref[pl.ds(offset * 4 + ((level + d) & 3), 1), :] for d in range(4)], axis=1
    )


def send_blocks(outs, table, send_ref, ids_ref, groups, n):
    for j in range(3):
        group, column = place(send_rows(send_ref, j, ids_ref), groups, n)
        rows = pick(table, group, column, groups, n)
        for d in range(4):
            outs[j][d] = rows[:, d * 128 : (d + 1) * 128]


def add_back(total, blocks, send_ref, ids_ref, groups, n):
    for j in range(3):
        group, column = place(send_rows(send_ref, j, ids_ref), groups, n)
        values = jnp.concatenate([block_at(blocks, d, j) for d in range(4)], axis=1)
        add_at(total, values, group, column, groups, n)


def block_at(received, d, j):
    return received[j][0] if d == 0 else received[2 + d][j]


def slot_table(table, received):
    for t in range(12):
        table[(t >> 1) * D : ((t >> 1) + 1) * D, (t & 1) * 128 : ((t & 1) + 1) * 128] = block_at(received, t // 3, t % 3)


def slot_gradients(outs, sums, weight):
    for j in range(SLOT_GROUPS):
        high, low = halves(sums[j * D : (j + 1) * D, :])
        grads = (dot(weight, high) + dot(weight, low)).astype(B16)
        for t in (2 * j, 2 * j + 1):
            outs[t % 3][t // 3] = grads[:, (t & 1) * 128 : ((t & 1) + 1) * 128]


def over_blocks(total, block, body):
    block = min(block, total)
    if block == total:
        body(pl.ds(0, block))
        return

    def step(i, carry):
        body(pl.ds(pl.multiple_of(i * block, block), block))
        return carry

    lax.fori_loop(0, total // block, step, 0)


def pipelined(stages, spans):
    held = [None] * len(spans)
    for t in range(len(spans) + len(stages) - 1):
        for k in reversed(range(len(stages))):
            i = t - k
            if 0 <= i < len(spans):
                held[i] = stages[k](spans[i], held[i])


def spans_of(parts, chunk):
    spans, start = [], 0
    for which, ref in enumerate(parts):
        size = min(chunk, ref.shape[1])
        for at in range(0, ref.shape[1], size):
            spans.append((which, pl.ds(at, size), pl.ds(start + at, size)))
        start += ref.shape[1]
    return spans


def edge_tables(index_ref, alive_ref, senders, targets, ids_ref, first, rows):
    groups, n = groups_of(rows)
    index_ref[0], index_ref[1] = place(targets, groups, n)
    index_ref[2], index_ref[3] = slot_place(senders, ids_ref[0], ids_ref[1])
    alive_ref[0] = live(senders, ids_ref, first)


def tables_kernel(upper_rows, lower_rows, ids_ref, senders_up, targets_up, senders_down, targets_down,
                  index_up, alive_up, index_down, alive_down):
    edge_tables(index_up, alive_up, senders_up[...], targets_up[...], ids_ref, 2, upper_rows)
    edge_tables(index_down, alive_down, senders_down[...], targets_down[...], ids_ref, 14, lower_rows)


def send_kernel(count, ids_ref, *refs):
    sources, refs = refs[:count], refs[count:]
    sent, held, table, sems = refs[:3], refs[3:-2], refs[-2], refs[-1]
    copies = [pltpu.make_async_copy(a, b, sems.at[i]) for i, (a, b) in enumerate(zip(sources, held))]
    for copy in copies:
        copy.start()
    for copy in copies[:2]:
        copy.wait()
    send_ref, source_ref = held[:2]
    groups, n = groups_of(source_ref.shape[1])
    pack_table(table, source_ref, groups, n)
    send_blocks(sent, table, send_ref, ids_ref, groups, n)
    for copy in copies[2:]:
        copy.wait()


def part_kernel(k, start, index_ref, feat_ref, local_ref, w1_ref, biases_ref, gains_ref, *rest):
    part_ref, held_ref, table, sem = rest[-4:]
    size = part_ref.shape[1]
    copy = pltpu.make_async_copy(feat_ref.at[:, pl.ds(start, size)], held_ref, sem)
    copy.start()
    groups, n = groups_of(local_ref.shape[1])
    pack_table(table, local_ref, groups, n)
    columns = columns_of(biases_ref, gains_ref, k)
    weight = jnp.concatenate([w1_ref[k, :, 0:D], w1_ref[k, :, 2 * D : 3 * D]], axis=1)
    picked = pick(table, row_of(index_ref, 0, start, size), row_of(index_ref, 1, start, size), groups, n)
    copy.wait()
    part_ref[...] = dot(weight, jnp.concatenate([held_ref[...], picked], axis=0)) + columns[:, 0:1]


def edges_forward(k, parts, alive_ref, index_ref, table, w1_ref, w2_ref, columns, total, groups, n,
                  slope_ref, normed_ref, hidden_ref, factor_ref):
    weight_slot = w1_ref[k, :, D : 2 * D]
    weight_two = w2_ref[k].astype(F32).T.astype(B16)
    total[...] = jnp.zeros_like(total)

    def slot_rows(span, unused):
        a, size = span[2].start, span[2].size
        return pick(table, row_of(index_ref, 2, a, size), row_of(index_ref, 3, a, size), SLOT_GROUPS, SLOT_COLS)

    def first_layer(span, picked):
        which, t, s = span
        first = parts[which][:, t] + dot(weight_slot, picked)
        gate = sigmoid(first)
        hidden = (first * gate).astype(B16)
        slope_ref[:, s] = gate * (1.0 + first * (1.0 - gate))
        hidden_ref[:, s] = hidden
        return hidden

    def second_layer(span, hidden):
        s = span[2]
        normed, factor = norm_parts(dot(weight_two, hidden) + columns[:, 1:2])
        alive = row_of(alive_ref, 0, s.start, s.size)
        normed_ref[:, s] = normed
        factor_ref[:, s] = factor
        return ((normed * columns[:, 6:7] + columns[:, 2:3]) * alive).astype(B16)

    def sum_messages(span, messages):
        a, size = span[2].start, span[2].size
        add_at(total, messages, row_of(index_ref, 0, a, size), row_of(index_ref, 1, a, size), groups, n)

    pipelined((slot_rows, first_layer, second_layer, sum_messages), spans_of(parts, CHUNK))


def node_first(k, inputs, wn1_ref, columns):
    first = dot(wn1_ref[k], inputs) + columns[:, 3:4]
    gate = sigmoid(first)
    return (first * gate).astype(B16), gate * (1.0 + first * (1.0 - gate))


def node_second(hidden, weight_two, columns):
    return norm_parts(dot(weight_two, hidden) + columns[:, 4:5])


def node_second_grad(grad, normed, factor, hidden, columns, two_ref, sums_ref):
    second = norm_back(grad, normed, factor, columns[:, 7:8]).astype(B16)
    sums_ref[1] += fold(second.astype(F32))
    sums_ref[2] += fold(grad)
    sums_ref[3] += fold(grad * normed)
    two_ref[...] += dot_rows(hidden, second)
    return second


def node_first_grad(second, slope, inputs, wn2, one_ref, sums_ref):
    first = (dot(wn2, second) * slope).astype(B16)
    sums_ref[0] += fold(first.astype(F32))
    one_ref[...] += dot_rows(first, inputs)
    return first


def clear(refs):
    for ref in refs:
        ref[...] = jnp.zeros_like(ref)


def transposed(weight):
    return weight.astype(F32).T.astype(B16)


def edge_second(grad_rows, s, columns, weight_sum, alive_ref, normed_ref, factor_ref, sums_ref):
    grad = dot(weight_sum, grad_rows) * row_of(alive_ref, 0, s.start, s.size)
    normed = normed_ref[:, s]
    second = norm_back(grad, normed, factor_ref[:, s], columns[:, 6:7]).astype(B16)
    sums_ref[1] += fold(second.astype(F32))
    sums_ref[2] += fold(grad)
    sums_ref[3] += fold(grad * normed)
    return second


def edge_first(second, s, weight_two, slope_ref, sums_ref):
    first = (dot(weight_two, second) * slope_ref[:, s]).astype(B16)
    sums_ref[0] += fold(first.astype(F32))
    return first


def pack_columns(edge_sums, node_sums):
    order = (edge_sums[0], edge_sums[1], edge_sums[2], node_sums[0], node_sums[1], node_sums[2], edge_sums[3], node_sums[3])
    columns = [jnp.sum(v, axis=1, keepdims=True) for v in order]
    lanes = lax.broadcasted_iota(jnp.int32, (D, D), 1)
    packed = jnp.zeros((D, D), F32)
    for i, column in enumerate(columns):
        packed = jnp.where(lanes == i, column, packed)
    return packed


def slot_weight_grads(sums, table):
    total = jnp.zeros((D, D), F32)
    for j in range(SLOT_GROUPS):
        high, low = halves(sums[j * D : (j + 1) * D, :])
        rows = table[j * D : (j + 1) * D, :]
        total = total + dot_rows(high, rows) + dot_rows(low, rows)
    return total


def target_grads(total, local_ref, weight, start_ref, out_ref, groups, n):
    grads = jnp.zeros((D, D), F32)
    for j in range(groups):
        high, low = halves(total[j * D : (j + 1) * D, :])
        s = slice(j * n, (j + 1) * n)
        rows = local_ref[:, s]
        grads = grads + dot_rows(high, rows) + dot_rows(low, rows)
        out_ref[:, s] = start_ref[:, s] + dot(weight, high) + dot(weight, low)
    return grads


def up_forward_kernel(ids_ref, part_ref, alive_ref, index_ref, r0, r1, r2, r3, r4, r5, local_ref, send_ref,
                      w1_ref, w2_ref, wn1_ref, wn2_ref, biases_ref, gains_ref,
                      out_ref, summed_ref, s0, s1, s2, slope_ref, normed_ref, hidden_ref, factor_ref,
                      slots, total, table, out, sem):
    groups, n = groups_of(local_ref.shape[1])
    columns = columns_of(biases_ref, gains_ref, 0)
    slot_table(slots, (r0, r1, r2, r3, r4, r5))
    edges_forward(0, (part_ref,), alive_ref, index_ref, slots, w1_ref, w2_ref, columns, total, groups, n,
                  slope_ref, normed_ref, hidden_ref, factor_ref)
    weight_two = transposed(wn2_ref[0])

    def first_layer(j, unused):
        s = slice(j * n, (j + 1) * n)
        summed = total[j * D : (j + 1) * D, :].astype(B16)
        summed_ref[:, s] = summed
        return node_first(0, jnp.concatenate([local_ref[:, s], summed], axis=0), wn1_ref, columns)

    def second_layer(j, held):
        s = slice(j * n, (j + 1) * n)
        normed, unused = node_second(held[0], weight_two, columns)
        result = local_ref[:, s].astype(F32) + normed * columns[:, 7:8] + columns[:, 5:6]
        out[:, s] = result
        table[j * D : (j + 1) * D, :] = result.astype(B16)

    pipelined((first_layer, second_layer), range(groups))
    copy = pltpu.make_async_copy(out, out_ref, sem)
    copy.start()
    send_blocks((s0, s1, s2), table, send_ref, ids_ref, groups, n)
    copy.wait()


def down_kernel(part_a, part_b, alive_ref, index_ref, r0, r1, r2, r3, r4, r5, local_ref, cot_ref,
                w1_ref, w2_ref, wn1_ref, wn2_ref, biases_ref, gains_ref,
                out_ref, g0, g1, g2, first_ref, second_ref, hidden_ref, grad_ref, sums_ref, edge_sums, node_sums, wn1_grad, wn2_grad,
                slots, total, table, slope_ref, normed_ref, factor_ref, out, sem):
    groups, n = groups_of(local_ref.shape[1])
    columns = columns_of(biases_ref, gains_ref, 1)
    slot_table(slots, (r0, r1, r2, r3, r4, r5))
    parts = (part_a, part_b)
    edges_forward(1, parts, alive_ref, index_ref, slots, w1_ref, w2_ref, columns, total, groups, n,
                  slope_ref, normed_ref, hidden_ref, factor_ref)
    clear((wn1_grad, wn2_grad, node_sums, edge_sums, sums_ref))
    wn2 = wn2_ref[1]
    wn2_t = transposed(wn2)
    wn1 = transposed(wn1_ref[1])

    def first_layer(j, unused):
        local = local_ref[:, j * n : (j + 1) * n]
        inputs = jnp.concatenate([local, total[j * D : (j + 1) * D, :].astype(B16)], axis=0)
        return inputs, *node_first(1, inputs, wn1_ref, columns)

    def second_layer(j, held):
        inputs, hidden, slope = held
        s = slice(j * n, (j + 1) * n)
        normed, factor = node_second(hidden, wn2_t, columns)
        out[:, s] = local_ref[:, s].astype(F32) + normed * columns[:, 7:8] + columns[:, 5:6]
        return inputs, slope, node_second_grad(cot_ref[:, s], normed, factor, hidden, columns, wn2_grad, node_sums)

    def node_grads(j, held):
        inputs, slope, second = held
        s = slice(j * n, (j + 1) * n)
        first = node_first_grad(second, slope, inputs, wn2, wn1_grad, node_sums)
        table[j * D : (j + 1) * D, :] = first
        grad_ref[:, s] = cot_ref[:, s] + dot(wn1[0:D], first)

    pipelined((first_layer, second_layer, node_grads), range(groups))
    copy = pltpu.make_async_copy(out, out_ref, sem)
    copy.start()
    weight_two = w2_ref[1]
    weight_slot = transposed(w1_ref[1, :, D : 2 * D])

    def grad_rows(span, unused):
        a, size = span[2].start, span[2].size
        return pick(table, row_of(index_ref, 0, a, size), row_of(index_ref, 1, a, size), groups, n)

    def second_grad(span, rows):
        return edge_second(rows, span[2], columns, wn1[D : 2 * D], alive_ref, normed_ref, factor_ref, edge_sums)

    def first_grad(span, second):
        s = span[2]
        first = edge_first(second, s, weight_two, slope_ref, edge_sums)
        first_ref[:, s] = first
        second_ref[:, s] = second
        return first

    def sum_slots(span, first):
        a, size = span[2].start, span[2].size
        add_at(sums_ref, first, row_of(index_ref, 2, a, size), row_of(index_ref, 3, a, size), SLOT_GROUPS, SLOT_COLS)

    pipelined((grad_rows, second_grad, first_grad, sum_slots), spans_of(parts, CHUNK))
    slot_gradients((g0, g1, g2), sums_ref, weight_slot)
    copy.wait()


def down_targets_kernel(index_ref, first_ref, local_ref, start_ref, w1_ref, grad_ref, weight_grad_ref, total):
    groups, n = groups_of(local_ref.shape[1])
    weight = transposed(w1_ref[1, :, 2 * D : 3 * D])
    total[...] = jnp.zeros_like(total)
    for a in range(0, first_ref.shape[1], EDGE_BLOCK):
        group, column = row_of(index_ref, 0, a, EDGE_BLOCK), row_of(index_ref, 1, a, EDGE_BLOCK)
        add_at(total, first_ref[:, a : a + EDGE_BLOCK], group, column, groups, n)
    weight_grad_ref[...] = target_grads(total, local_ref, weight, start_ref, grad_ref, groups, n)


def down_rest_kernel(feat_a, feat_b, first_ref, second_ref, hidden_ref, r0, r1, r2, r3, r4, r5, sums_ref, local_grads_ref,
                     edge_sums, node_sums, wn1_grad, wn2_grad, w1_ref, *rest):
    feat_grad_ref, packed_ref, slots, one_ref, two_ref = rest[-5:]
    step = pl.program_id(0)
    weight = transposed(w1_ref[1, :, 0:D])

    @pl.when(step == 0)
    def _():
        clear((one_ref, two_ref))

    s = pl.ds(pl.multiple_of(step * EDGE_BLOCK, EDGE_BLOCK), EDGE_BLOCK)
    first = first_ref[:, s]
    feat_grad_ref[...] = dot(weight, first)
    one_ref[...] += dot_rows(first, jnp.where(step == 0, feat_a[...], feat_b[...]))
    two_ref[...] += dot_rows(hidden_ref[:, s], second_ref[:, s])

    @pl.when(step == pl.num_programs(0) - 1)
    def _():
        slot_table(slots, (r0, r1, r2, r3, r4, r5))
        slot_grads = slot_weight_grads(sums_ref, slots)
        write_packed(packed_ref, one_ref[...], slot_grads, local_grads_ref[...], two_ref[...], wn1_grad[...], wn2_grad[...],
                     pack_columns(edge_sums, node_sums))


def write_packed(packed_ref, one, slot_grads, local_grads, two, wn1_grad, wn2_grad, columns):
    packed_ref[0] = jnp.concatenate([one, slot_grads], axis=1)
    packed_ref[1] = jnp.concatenate([local_grads, two], axis=1)
    packed_ref[2] = wn1_grad
    packed_ref[3] = jnp.concatenate([wn2_grad, columns], axis=1)


def up_backward_kernel(ids_ref, index_ref, feat_ref, h0, h1, h2, h3, h4, h5,
                       send_ref, cot_ref, local_ref, summed_ref, r0, r1, r2, r3, r4, r5, slope_ref, normed_ref, hidden_ref, factor_ref, alive_ref, packed_down_ref,
                       w1_ref, w2_ref, wn1_ref, wn2_ref, biases_ref, gains_ref,
                       g0, g1, g2, first_ref, grad_ref, keep_ref,
                       slots, table, back, total, sums, start, one_ref, two_ref, edge_sums, node_sums, wn1_grad, wn2_grad, pieces):
    groups, n = groups_of(local_ref.shape[1])
    columns = columns_of(biases_ref, gains_ref, 0)
    clear((back, total, sums, one_ref, two_ref, edge_sums, node_sums, wn1_grad, wn2_grad))
    slot_table(slots, (r0, r1, r2, r3, r4, r5))
    add_back(back, (h0, h1, h2, h3, h4, h5), send_ref, ids_ref, groups, n)
    wn2 = wn2_ref[0]
    wn2_t = transposed(wn2)
    wn1 = transposed(wn1_ref[0])
    w1 = transposed(w1_ref[0])

    def first_layer(j, unused):
        s = slice(j * n, (j + 1) * n)
        inputs = jnp.concatenate([local_ref[:, s], summed_ref[:, s]], axis=0)
        return inputs, *node_first(0, inputs, wn1_ref, columns)

    def second_layer(j, held):
        inputs, hidden, slope = held
        grad = cot_ref[:, j * n : (j + 1) * n] + back[j * D : (j + 1) * D, :]
        normed, factor = node_second(hidden, wn2_t, columns)
        return inputs, slope, grad, node_second_grad(grad, normed, factor, hidden, columns, wn2_grad, node_sums)

    def node_grads(j, held):
        inputs, slope, grad, second = held
        first = node_first_grad(second, slope, inputs, wn2, wn1_grad, node_sums)
        table[j * D : (j + 1) * D, :] = first
        start[:, j * n : (j + 1) * n] = grad + dot(wn1[0:D], first)

    pipelined((first_layer, second_layer, node_grads), range(groups))
    weight_two = w2_ref[0]

    def grad_rows(span, unused):
        a, size = span[2].start, span[2].size
        return pick(table, row_of(index_ref, 0, a, size), row_of(index_ref, 1, a, size), groups, n)

    def second_grad(span, rows):
        return edge_second(rows, span[2], columns, wn1[D : 2 * D], alive_ref, normed_ref, factor_ref, edge_sums)

    def first_grad(span, second):
        s = span[2]
        first = edge_first(second, s, weight_two, slope_ref, edge_sums)
        first_ref[:, s] = first
        two_ref[...] += dot_rows(hidden_ref[:, s], second)
        return first

    def sum_rows(span, first):
        s = span[2]
        rows = [row_of(index_ref, i, s.start, s.size) for i in range(4)]
        add_at(total, first, rows[0], rows[1], groups, n)
        add_at(sums, first, rows[2], rows[3], SLOT_GROUPS, SLOT_COLS)
        one_ref[...] += dot_rows(first, feat_ref[:, s])

    pipelined((grad_rows, second_grad, first_grad, sum_rows), spans_of((first_ref,), CHUNK))
    slot_gradients((g0, g1, g2), sums, w1[D : 2 * D])
    local_grads = target_grads(total, local_ref, w1[2 * D : 3 * D], start, grad_ref, groups, n)
    slot_grads = slot_weight_grads(sums, slots)
    write_packed(pieces, one_ref[...], slot_grads, local_grads, two_ref[...], wn1_grad[...], wn2_grad[...],
                 pack_columns(edge_sums, node_sums))
    core = ids_ref[1]
    for p in range(4):
        pieces[4 + p] = packed_down_ref[p]
    for p in range(4):
        keep_ref[p] = pieces[core * 4 + p]
        g0[4 + p] = pieces[(1 - core) * 4 + p].astype(B16)


def feat_grad_kernel(first_ref, w1_ref, out_ref):
    out_ref[...] = dot(transposed(w1_ref[0, :, 0:D]), first_ref[...])


def lower_grad_kernel(ids_ref, h0, h1, h2, h3, h4, h5, send_ref, start_ref, out_ref, total):
    groups, n = groups_of(start_ref.shape[1])
    clear((total,))
    add_back(total, (h0, h1, h2, h3, h4, h5), send_ref, ids_ref, groups, n)
    for j in range(groups):
        s = slice(j * n, (j + 1) * n)
        out_ref[:, s] = start_ref[:, s] + total[j * D : (j + 1) * D, :]


def unpack_kernel(ids_ref, own_ref, other_ref, w1_ref, w2_ref, wn1_ref, wn2_ref, biases_ref, gains_ref, pieces):
    core = ids_ref[1]
    for p in range(4):
        pieces[core * 4 + p] = own_ref[p].astype(F32)
        pieces[(1 - core) * 4 + p] = other_ref[p].astype(F32)
    for k in range(2):
        w1_ref[k] = jnp.concatenate([pieces[4 * k], pieces[4 * k + 1, :, 0:D]], axis=1)
        w2_ref[k] = pieces[4 * k + 1, :, D : 2 * D]
        wn1_ref[k] = pieces[4 * k + 2]
        wn2_ref[k] = pieces[4 * k + 3, :, 0:D]
        rows = pieces[4 * k + 3].T
        for i in range(6):
            biases_ref[i, k : k + 1] = rows[D + i : D + i + 1]
        gains_ref[k] = rows[D + 6 : D + 8]


def shape(dims, dtype=F32):
    return jax.ShapeDtypeStruct(dims, dtype)


def call(kernel, name, outs, scratch, scalars=0, stored=(), streamed=None, final=(), raw=()):
    steps, stream_in, stream_out = streamed if streamed else (1, (), ())

    def run(*operands, after=()):
        def whole(space):
            return pl.BlockSpec(memory_space=space)

        def cut(x):
            return pl.BlockSpec((x.shape[0], x.shape[1] // steps), lambda i: (0, i))

        in_specs, placed = [], []
        for i, x in enumerate(operands):
            if i < scalars:
                in_specs.append(whole(pltpu.SMEM))
            elif i in stream_in:
                in_specs.append(cut(x))
            elif i in raw:
                in_specs.append(whole(pltpu.HBM))
                x = pltpu.with_memory_space_constraint(x, pltpu.HBM)
            else:
                in_specs.append(whole(pltpu.VMEM))
                x = pltpu.with_memory_space_constraint(x, pltpu.VMEM)
            placed.append(x)
        in_specs += [whole(pl.ANY) for _ in after]
        out_specs, out_shape = [], []
        for i, x in enumerate(outs):
            if i in stream_out:
                out_specs.append(cut(x))
                out_shape.append(x)
            elif i in stored:
                out_specs.append(whole(pl.ANY))
                out_shape.append(x)
            elif i in final:
                out_specs.append(whole(pltpu.VMEM))
                out_shape.append(x)
            else:
                out_specs.append(whole(pltpu.VMEM))
                out_shape.append(pltpu.VMEM(x.shape, x.dtype))
        return pl.pallas_call(
            kernel,
            name=name,
            grid=(steps,) if streamed else (),
            in_specs=in_specs,
            out_specs=out_specs,
            out_shape=out_shape,
            scratch_shapes=scratch,
            compiler_params=pltpu.CompilerParams(vmem_limit_bytes=VMEM_BYTES),
        )(*placed, *after)

    return run


def core_swap(block):
    return lax.ppermute(block, "band", [(i, i ^ 1) for i in range(lax.axis_size("band"))])


def cross_swap(block):
    count = lax.axis_size("band")
    pairs = [(i, (i + 1) % count) for i in range(1, count, 2)]
    return lax.ppermute(block, "band", pairs + [(b, a) for a, b in pairs])


def along_level(block, step):
    count = lax.axis_size("level")
    return lax.ppermute(block, "level", [(i, (i + step) % count) for i in range(count)])


def across_bands(blocks):
    partner, cross, own = blocks
    return [core_swap(partner), cross_swap(cross), own]


def along_levels(blocks, sign):
    return blocks + [along_level(jnp.stack([b[d] for b in blocks]), sign * d) for d in (1, 2, 3)]


def chip_axis(block, stride, step):
    count = lax.axis_size("band")
    pairs = []
    for i in range(count):
        at = (i // stride) % 4
        pairs.append((i, i + (((at + step) % 4) - at) * stride))
    return lax.ppermute(block, "band", pairs)


def rounded(values):
    return lax.reduce_precision(values, 8, 7)


def sum_of_four(values, first, second, third):
    return (values + second.astype(F32)) + (first.astype(F32) + third.astype(F32))


def sum_along(values, stride):
    own = rounded(values)
    sent = own.astype(B16)
    return sum_of_four(own, *(chip_axis(sent, stride, d) for d in (1, 2, 3)))


def shards(
    lower_nodes, latent, up_feat, down_feat, up_send, up_counts, up_senders, up_targets,
    down_send, down_counts, down_senders, down_targets,
    edge_w1, edge_w2, node_w1, node_w2, biases, norm_gains, lower_cot, upper_cot,
):
    lower, upper = lower_nodes.T, latent.T
    feat_up, feat_down = up_feat.T, down_feat.T
    cot_lower, cot_upper = lower_cot.T, upper_cot.T
    w1, wn1 = edge_w1.transpose(0, 2, 1), node_w1.transpose(0, 2, 1)
    w2, wn2 = edge_w2, node_w2
    edges, lower_rows, upper_rows = up_feat.shape[0], lower_nodes.shape[0], latent.shape[0]
    dense = (edges // 128, 128)
    senders_up, targets_up, senders_down, targets_down = (
        x.reshape(dense) for x in (up_senders, up_targets, down_senders, down_targets))
    bias_rows = biases.transpose(1, 0, 2)
    ids = jnp.stack([lax.axis_index("level"), lax.axis_index("band") & 1]).astype(jnp.int32)
    ids = jnp.concatenate([ids, up_counts.reshape(-1), down_counts.reshape(-1)])

    lower_groups, lower_n = groups_of(lower_rows)
    upper_groups, upper_n = groups_of(upper_rows)
    lower_table, upper_table = (lower_groups * D, lower_n), (upper_groups * D, upper_n)
    slots = pltpu.VMEM((SLOT_GROUPS * D, SLOT_COLS), B16)
    block, four = shape((4, D, 128), B16), shape((4, D, 128))
    wide32, wide16, row = shape((D, edges)), shape((D, edges), B16), shape((1, edges))
    steps = edges // EDGE_BLOCK
    half = edges // 2

    early = (up_send, lower, senders_up, targets_up, senders_down, targets_down, upper, w1, bias_rows, norm_gains,
             down_send, w2, wn1, wn2)
    count = len(early)
    (*sent, up_send, lower, senders_up, targets_up, senders_down, targets_down, upper, w1, bias_rows,
     norm_gains, down_send, w2, wn1, wn2) = call(
        functools.partial(send_kernel, count), "send_lower", [block] * 3 + [shape(x.shape, x.dtype) for x in early],
        [pltpu.VMEM(lower_table, B16), pltpu.SemaphoreType.DMA((count,))], 1, raw=range(1, count + 1),
    )(ids, *early)
    index, lives = shape((4, *dense), jnp.int32), shape((1, *dense))
    index_up, alive_up, index_down, alive_down = call(
        functools.partial(tables_kernel, upper_rows, lower_rows), "edge_tables", [index, lives, index, lives], [], 1,
    )(ids, senders_up, targets_up, senders_down, targets_down)

    def part(k, start, size, name, table, index, feat, local, after):
        return call(
            functools.partial(part_kernel, k, start), name, [shape((D, size)), shape((D, size), B16)],
            [pltpu.VMEM(table, B16), pltpu.SemaphoreType.DMA], 0, raw=(1,),
        )(index, feat, local, w1, bias_rows, norm_gains, after=after)

    sent = across_bands(sent)
    part_up, feat_up = part(0, 0, edges, "part_up", upper_table, index_up, feat_up, upper, ())
    sent, part_up = lax.optimization_barrier((sent, part_up))
    up_slots = along_levels(sent, 1)
    part_a, feat_a = part(1, 0, half, "part_down_a", lower_table, index_down, feat_down, lower, (sent[1],))
    up_slots, part_a = lax.optimization_barrier((up_slots, part_a))
    (upper_new, summed_up, s0, s1, s2, slope, normed, hidden, factor) = call(
        up_forward_kernel, "up_forward",
        [shape((D, upper_rows)), shape((D, upper_rows), B16)] + [block] * 3 + [wide32, wide32, wide16, row],
        [slots, pltpu.VMEM(upper_table, F32), pltpu.VMEM(upper_table, B16), pltpu.VMEM((D, upper_rows), F32),
         pltpu.SemaphoreType.DMA], 1, (0,),
    )(ids, part_up, alive_up, index_up, *up_slots, upper, down_send, w1, w2, wn1, wn2, bias_rows, norm_gains)
    sent = across_bands([s0, s1, s2])
    part_b, feat_b = part(1, half, half, "part_down_b", lower_table, index_down, feat_down, lower, (s0,))
    sent, part_b = lax.optimization_barrier((sent, part_b))
    down_slots = along_levels(sent, 1)
    sums_shape = shape((SLOT_GROUPS * D, SLOT_COLS))
    (lower_new, g0, g1, g2, first_down, second_down, hidden_down, start_lower, sums_down, edge_sums, node_sums, wn1_grad, wn2_grad) = call(
        down_kernel, "down_sweep",
        [shape((D, lower_rows))] + [block] * 3 + [wide16] * 3 + [shape((D, lower_rows)), sums_shape, four, four,
         shape((D, 2 * D)), shape((D, D))],
        [slots, pltpu.VMEM(lower_table, F32), pltpu.VMEM(lower_table, B16), pltpu.VMEM((D, edges), F32),
         pltpu.VMEM((D, edges), F32), pltpu.VMEM((1, edges), F32),
         pltpu.VMEM((D, lower_rows), F32), pltpu.SemaphoreType.DMA], 0, (0,),
    )(part_a, part_b, alive_down, index_down, *down_slots, lower, cot_lower, w1, w2, wn1, wn2, bias_rows, norm_gains)
    back = across_bands([g0, g1, g2])
    start_lower, local_grads = call(
        down_targets_kernel, "down_targets", [shape((D, lower_rows)), shape((D, D))], [pltpu.VMEM(lower_table, F32)],
    )(index_down, first_down, lower, start_lower, w1)
    back, local_grads = lax.optimization_barrier((back, local_grads))
    down_back = along_levels(back, -1)
    feat_grad_down, packed_down = call(
        down_rest_kernel, "down_rest", [wide32, four],
        [slots, pltpu.VMEM((D, D), F32), pltpu.VMEM((D, D), F32)], 0, (), (steps, (), (0,)),
    )(feat_a, feat_b, first_down, second_down, hidden_down, *down_slots, sums_down, local_grads,
      edge_sums, node_sums, wn1_grad, wn2_grad, w1, after=(back[1],))
    (partner, cross, own, first_up, grad_latent, keep) = call(
        up_backward_kernel, "up_backward",
        [shape((8, D, 128), B16), block, block, wide16, shape((D, upper_rows)), four],
        [slots, pltpu.VMEM(upper_table, B16), pltpu.VMEM(upper_table, F32), pltpu.VMEM(upper_table, F32),
         pltpu.VMEM((SLOT_GROUPS * D, SLOT_COLS), F32), pltpu.VMEM((D, upper_rows), F32),
         pltpu.VMEM((D, D), F32), pltpu.VMEM((D, D), F32), pltpu.VMEM((4, D, 128), F32), pltpu.VMEM((4, D, 128), F32),
         pltpu.VMEM((D, 2 * D), F32), pltpu.VMEM((D, D), F32), pltpu.VMEM((8, D, 128), F32)], 1, (), None, (4,),
    )(ids, index_up, feat_up, *down_back, down_send, cot_upper, upper, summed_up, *up_slots,
      slope, normed, hidden, factor, alive_up, packed_down, w1, w2, wn1, wn2, bias_rows, norm_gains)

    (feat_grad_up,) = call(feat_grad_kernel, "feat_grad_up", [wide32], [], 0, (), (steps, (0,), (0,)))(first_up, w1)
    partner, cross = core_swap(partner), cross_swap(cross)
    partner, cross, feat_grad_up = lax.optimization_barrier((partner, cross, feat_grad_up))
    total = rounded(rounded(keep) + partner[4:].astype(F32))
    blocks = (partner, cross, own)
    levels = [
        along_level(jnp.concatenate([jnp.stack([b[d] for b in blocks]), total.astype(B16)]), -d) for d in (1, 2, 3)
    ]
    total = sum_of_four(total, *(b[3:] for b in levels))
    (grad_lower,) = call(lower_grad_kernel, "lower_grad", [shape((D, lower_rows))], [pltpu.VMEM(lower_table, F32)], 1, (), None, (0,))(
        ids, *blocks, *levels, up_send, start_lower)
    total = sum_along(total, 2)
    total, grad_lower = lax.optimization_barrier((total, grad_lower))
    total = rounded(sum_along(total, 8)).astype(B16)
    w1_grad, w2_grad, wn1_grad, wn2_grad, bias_grad, gain_grad = call(
        unpack_kernel, "unpack",
        [shape((2, D, 3 * D)), shape((2, D, D)), shape((2, D, 2 * D)), shape((2, D, D)), shape((6, 2, D)), shape((2, 2, D))],
        [pltpu.VMEM((8, D, 128), F32)], 1, (), None, range(6))(ids, total, core_swap(total))
    return (
        lower_new.T, upper_new.T, grad_lower.T, grad_latent.T, feat_grad_up.T, feat_grad_down.T,
        w1_grad.transpose(0, 2, 1), w2_grad, wn1_grad.transpose(0, 2, 1), wn2_grad, bias_grad.transpose(1, 0, 2), gain_grad,
    )


def solution(mesh):
    rows, index, whole = P(("band", "level"), None), P(("band", "level")), P()
    placed = (rows,) * 6 + (index, index) + (rows,) * 2 + (index, index) + (whole,) * 6 + (rows,) * 2
    return jax.shard_map(
        shards,
        mesh=mesh,
        in_specs=placed,
        out_specs=(rows,) * 6 + (whole,) * 6,
        check_vma=False,
    )
```

```python
import functools

import jax
import jax.numpy as jnp
from jax import lax
from jax.experimental import pallas as pl
from jax.experimental.pallas import tpu as pltpu
from jax.sharding import PartitionSpec as P

EPSILON = 1e-05
F32 = jnp.float32
B16 = jnp.bfloat16
D = 64
SLOT_GROUPS, SLOT_COLS = 6, 256
EDGE_BLOCK = 3072
CHUNK = 1024
VMEM_BYTES = 24 * 1024 * 1024


def groups_of(rows):
    return (4, rows // 4) if rows > 1024 else (rows // 256, 256)


def dot(a, b):
    return jnp.dot(a, b, preferred_element_type=F32)


def dot_rows(a, b):
    return lax.dot_general(a, b, (((1,), (1,)), ((), ())), preferred_element_type=F32)


def halves(x):
    high = x.astype(B16)
    return high, (x - high.astype(F32)).astype(B16)


def one_hot(column, n):
    rows = lax.broadcasted_iota(jnp.int16, (n, column.shape[1]), 0)
    return jnp.where(rows == column.astype(jnp.int16), jnp.ones((), B16), jnp.zeros((), B16))


def place(index, groups, n):
    group = jnp.zeros_like(index)
    for j in range(1, groups):
        group = group + (index >= j * n).astype(jnp.int32)
    return group, index - group * n


def level_and_core():
    return lax.axis_index("level").astype(jnp.int32), lax.axis_index("band").astype(jnp.int32) & 1


def slot_place(senders):
    level, core = level_and_core()
    distance = (level - ((senders >> 7) & 3)) & 3
    offset = senders >> 9
    source = jnp.where(offset == 1, 2, jnp.where(offset == 2 - 2 * core, 0, 1))
    block = distance * 3 + source
    return block >> 1, ((block & 1) << 7) | (senders & 127)


def live(senders, counts_ref):
    peer = senders >> 7
    limit = jnp.zeros_like(senders)
    for j in range(12):
        limit = jnp.where(peer == j, counts_ref[0, j], limit)
    return ((senders & 127) < limit).astype(F32)


def choose(stacked, group, groups):
    picked = stacked[0:D]
    for j in range(1, groups):
        picked = jnp.where(group == j, stacked[j * D : (j + 1) * D], picked)
    return picked


def row_of(ref, k, start, size):
    rows = size // 128
    if not isinstance(start, int):
        start = pl.multiple_of(start // 128, rows)
        return jnp.concatenate([ref[k, pl.ds(start + r, 1), :] for r in range(rows)], axis=1)
    return jnp.concatenate([ref[k, r : r + 1, :] for r in range(start // 128, start // 128 + rows)], axis=1)


def pick(table, group, column, groups, n):
    return choose(dot(table[...], one_hot(column, n)), group, groups).astype(B16)


def spread(values, group, groups):
    wide = jnp.broadcast_to(group.astype(jnp.int16), values.shape)
    nothing = jnp.zeros_like(values)
    return jnp.concatenate([jnp.where(wide == j, values, nothing) for j in range(groups)], axis=0)


def add_at(total, values, group, column, groups, n):
    total[...] += dot_rows(spread(values, group, groups), one_hot(column, n))


def pack_table(table, source, groups, n):
    for j in range(groups):
        table[j * D : (j + 1) * D, :] = source[:, j * n : (j + 1) * n]


def columns_of(biases_ref, gains_ref, k):
    rows = [biases_ref[i, k : k + 1] for i in range(6)] + [gains_ref[k]]
    return jnp.concatenate(rows, axis=0).T


def fold(values):
    total = values[:, 0:128]
    for i in range(128, values.shape[1], 128):
        total = total + values[:, i : i + 128]
    return total


def norm_parts(values):
    centre = values - jnp.sum(values, axis=0, keepdims=True) * (1.0 / D)
    spread_sum = jnp.sum(centre * centre, axis=0, keepdims=True) * (1.0 / D)
    factor = lax.rsqrt(spread_sum + EPSILON)
    return centre * factor, factor


def norm_back(grad, normed, factor, gain):
    scaled = grad * gain
    first = jnp.sum(scaled, axis=0, keepdims=True) * (1.0 / D)
    second = jnp.sum(scaled * normed, axis=0, keepdims=True) * (1.0 / D)
    return factor * (scaled - first - normed * second)


def sigmoid(values):
    return 0.5 * jnp.tanh(0.5 * values) + 0.5


def send_rows(send_ref, source):
    level, core = level_and_core()
    offset = (2 - 2 * core, 2 * core, 1)[source]
    return jnp.concatenate(
        [send_ref[pl.ds(offset * 4 + ((level + d) & 3), 1), :] for d in range(4)], axis=1
    )


def send_blocks(outs, table, send_ref, groups, n):
    for j in range(3):
        group, column = place(send_rows(send_ref, j), groups, n)
        rows = pick(table, group, column, groups, n)
        for d in range(4):
            outs[j][d] = rows[:, d * 128 : (d + 1) * 128]


def add_back(total, blocks, send_ref, groups, n):
    for j in range(3):
        group, column = place(send_rows(send_ref, j), groups, n)
        values = jnp.concatenate([block_at(blocks, d, j) for d in range(4)], axis=1)
        add_at(total, values, group, column, groups, n)


def block_at(received, d, j):
    return received[j][0] if d == 0 else received[2 + d][j]


def slot_table(table, received):
    for t in range(12):
        table[(t >> 1) * D : ((t >> 1) + 1) * D, (t & 1) * 128 : ((t & 1) + 1) * 128] = block_at(received, t // 3, t % 3)


def slot_gradients(outs, sums, weight):
    for j in range(SLOT_GROUPS):
        high, low = halves(sums[j * D : (j + 1) * D, :])
        grads = (dot(weight, high) + dot(weight, low)).astype(B16)
        for t in (2 * j, 2 * j + 1):
            outs[t % 3][t // 3] = grads[:, (t & 1) * 128 : ((t & 1) + 1) * 128]


def over_blocks(total, block, body):
    block = min(block, total)
    if block == total:
        body(pl.ds(0, block))
        return

    def step(i, carry):
        body(pl.ds(pl.multiple_of(i * block, block), block))
        return carry

    lax.fori_loop(0, total // block, step, 0)


def pipelined(stages, spans):
    held = [None] * len(spans)
    for t in range(len(spans) + len(stages) - 1):
        for k in reversed(range(len(stages))):
            i = t - k
            if 0 <= i < len(spans):
                held[i] = stages[k](spans[i], held[i])


def spans_of(parts, chunk):
    spans, start = [], 0
    for which, ref in enumerate(parts):
        size = min(chunk, ref.shape[1])
        for at in range(0, ref.shape[1], size):
            spans.append((which, pl.ds(at, size), pl.ds(start + at, size)))
        start += ref.shape[1]
    return spans


def tables_kernel(upper_rows, lower_rows, counts_up, counts_down, senders_up, targets_up, senders_down, targets_down,
                  index_up, alive_up, index_down, alive_down, limits_up, limits_down, sems):
    copies = [pltpu.make_async_copy(counts_up, limits_up, sems.at[0]), pltpu.make_async_copy(counts_down, limits_down, sems.at[1])]
    for copy in copies:
        copy.start()
    sweeps = ((index_up, senders_up, targets_up, upper_rows), (index_down, senders_down, targets_down, lower_rows))
    for index_ref, senders_ref, targets_ref, rows in sweeps:
        index_ref[0], index_ref[1] = place(targets_ref[...], *groups_of(rows))
        index_ref[2], index_ref[3] = slot_place(senders_ref[...])
    for copy in copies:
        copy.wait()
    alive_up[0] = live(senders_up[...], limits_up)
    alive_down[0] = live(senders_down[...], limits_down)


def send_kernel(count, *refs):
    sources, refs = refs[:count], refs[count:]
    sent, held, table, sems = refs[:3], refs[3:-2], refs[-2], refs[-1]
    copies = [pltpu.make_async_copy(a, b, sems.at[i]) for i, (a, b) in enumerate(zip(sources, held))]
    for copy in copies:
        copy.start()
    for copy in copies[:2]:
        copy.wait()
    send_ref, source_ref = held[:2]
    groups, n = groups_of(source_ref.shape[1])
    pack_table(table, source_ref, groups, n)
    send_blocks(sent, table, send_ref, groups, n)
    for copy in copies[2:]:
        copy.wait()


def part_kernel(k, block, index_ref, feat_ref, local_ref, w1_ref, biases_ref, gains_ref, *rest):
    part_ref, held_ref, table, picked, sem = rest[-5:]
    copy = pltpu.make_async_copy(feat_ref, held_ref, sem)
    copy.start()
    groups, n = groups_of(local_ref.shape[1])
    pack_table(table, local_ref, groups, n)
    columns = columns_of(biases_ref, gains_ref, k)
    weight = jnp.concatenate([w1_ref[k, :, 0:D], w1_ref[k, :, 2 * D : 3 * D]], axis=1)

    def body(s):
        picked[:, s] = pick(table, row_of(index_ref, 0, s.start, s.size), row_of(index_ref, 1, s.start, s.size), groups, n)

    over_blocks(feat_ref.shape[1], block, body)
    copy.wait()
    part_ref[...] = dot(weight, jnp.concatenate([held_ref[...], picked[...]], axis=0)) + columns[:, 0:1]


def edges_forward(k, parts, alive_ref, index_ref, table, w1_ref, w2_ref, columns, total, groups, n,
                  slope_ref, normed_ref, hidden_ref, factor_ref):
    weight_slot = w1_ref[k, :, D : 2 * D]
    weight_two = w2_ref[k].astype(F32).T.astype(B16)
    total[...] = jnp.zeros_like(total)

    def slot_rows(span, unused):
        a, size = span[2].start, span[2].size
        return pick(table, row_of(index_ref, 2, a, size), row_of(index_ref, 3, a, size), SLOT_GROUPS, SLOT_COLS)

    def first_layer(span, picked):
        which, t, s = span
        first = parts[which][:, t] + dot(weight_slot, picked)
        gate = sigmoid(first)
        hidden = (first * gate).astype(B16)
        slope_ref[:, s] = gate * (1.0 + first * (1.0 - gate))
        hidden_ref[:, s] = hidden
        return hidden

    def second_layer(span, hidden):
        s = span[2]
        normed, factor = norm_parts(dot(weight_two, hidden) + columns[:, 1:2])
        alive = row_of(alive_ref, 0, s.start, s.size)
        normed_ref[:, s] = normed
        factor_ref[:, s] = factor
        return ((normed * columns[:, 6:7] + columns[:, 2:3]) * alive).astype(B16)

    def sum_messages(span, messages):
        a, size = span[2].start, span[2].size
        add_at(total, messages, row_of(index_ref, 0, a, size), row_of(index_ref, 1, a, size), groups, n)

    pipelined((slot_rows, first_layer, second_layer, sum_messages), spans_of(parts, CHUNK))


def node_first(k, inputs, wn1_ref, columns):
    first = dot(wn1_ref[k], inputs) + columns[:, 3:4]
    gate = sigmoid(first)
    return (first * gate).astype(B16), gate * (1.0 + first * (1.0 - gate))


def node_second(hidden, weight_two, columns):
    return norm_parts(dot(weight_two, hidden) + columns[:, 4:5])


def node_second_grad(grad, normed, factor, hidden, columns, two_ref, sums_ref):
    second = norm_back(grad, normed, factor, columns[:, 7:8]).astype(B16)
    sums_ref[1] += fold(second.astype(F32))
    sums_ref[2] += fold(grad)
    sums_ref[3] += fold(grad * normed)
    two_ref[...] += dot_rows(hidden, second)
    return second


def node_first_grad(second, slope, inputs, wn2, one_ref, sums_ref):
    first = (dot(wn2, second) * slope).astype(B16)
    sums_ref[0] += fold(first.astype(F32))
    one_ref[...] += dot_rows(first, inputs)
    return first


def clear(refs):
    for ref in refs:
        ref[...] = jnp.zeros_like(ref)


def transposed(weight):
    return weight.astype(F32).T.astype(B16)


def edge_second(grad_rows, s, columns, weight_sum, alive_ref, normed_ref, factor_ref, sums_ref):
    grad = dot(weight_sum, grad_rows) * row_of(alive_ref, 0, s.start, s.size)
    normed = normed_ref[:, s]
    second = norm_back(grad, normed, factor_ref[:, s], columns[:, 6:7]).astype(B16)
    sums_ref[1] += fold(second.astype(F32))
    sums_ref[2] += fold(grad)
    sums_ref[3] += fold(grad * normed)
    return second


def edge_first(second, s, weight_two, slope_ref, sums_ref):
    first = (dot(weight_two, second) * slope_ref[:, s]).astype(B16)
    sums_ref[0] += fold(first.astype(F32))
    return first


def pack_columns(edge_sums, node_sums):
    order = (edge_sums[0], edge_sums[1], edge_sums[2], node_sums[0], node_sums[1], node_sums[2], edge_sums[3], node_sums[3])
    columns = [jnp.sum(v, axis=1, keepdims=True) for v in order]
    lanes = lax.broadcasted_iota(jnp.int32, (D, D), 1)
    packed = jnp.zeros((D, D), F32)
    for i, column in enumerate(columns):
        packed = jnp.where(lanes == i, column, packed)
    return packed


def slot_weight_grads(sums, table):
    total = jnp.zeros((D, D), F32)
    for j in range(SLOT_GROUPS):
        high, low = halves(sums[j * D : (j + 1) * D, :])
        rows = table[j * D : (j + 1) * D, :]
        total = total + dot_rows(high, rows) + dot_rows(low, rows)
    return total


def target_grads(total, local_ref, weight, start_ref, out_ref, groups, n):
    grads = jnp.zeros((D, D), F32)
    for j in range(groups):
        high, low = halves(total[j * D : (j + 1) * D, :])
        s = slice(j * n, (j + 1) * n)
        rows = local_ref[:, s]
        grads = grads + dot_rows(high, rows) + dot_rows(low, rows)
        out_ref[:, s] = start_ref[:, s] + dot(weight, high) + dot(weight, low)
    return grads


def up_forward_kernel(part_ref, alive_ref, index_ref, r0, r1, r2, r3, r4, r5, local_ref, send_ref,
                      w1_ref, w2_ref, wn1_ref, wn2_ref, biases_ref, gains_ref,
                      out_ref, summed_ref, s0, s1, s2, slope_ref, normed_ref, hidden_ref, factor_ref,
                      slots, total, table, out, sem):
    groups, n = groups_of(local_ref.shape[1])
    columns = columns_of(biases_ref, gains_ref, 0)
    slot_table(slots, (r0, r1, r2, r3, r4, r5))
    edges_forward(0, (part_ref,), alive_ref, index_ref, slots, w1_ref, w2_ref, columns, total, groups, n,
                  slope_ref, normed_ref, hidden_ref, factor_ref)
    weight_two = transposed(wn2_ref[0])

    def first_layer(j, unused):
        s = slice(j * n, (j + 1) * n)
        summed = total[j * D : (j + 1) * D, :].astype(B16)
        summed_ref[:, s] = summed
        return node_first(0, jnp.concatenate([local_ref[:, s], summed], axis=0), wn1_ref, columns)

    def second_layer(j, held):
        s = slice(j * n, (j + 1) * n)
        normed, unused = node_second(held[0], weight_two, columns)
        result = local_ref[:, s].astype(F32) + normed * columns[:, 7:8] + columns[:, 5:6]
        out[:, s] = result
        table[j * D : (j + 1) * D, :] = result.astype(B16)

    pipelined((first_layer, second_layer), range(groups))
    copy = pltpu.make_async_copy(out, out_ref, sem)
    copy.start()
    send_blocks((s0, s1, s2), table, send_ref, groups, n)
    copy.wait()


def down_kernel(part_ref, alive_ref, index_ref, r0, r1, r2, r3, r4, r5, local_ref, cot_ref,
                w1_ref, w2_ref, wn1_ref, wn2_ref, biases_ref, gains_ref,
                out_ref, g0, g1, g2, first_ref, second_ref, hidden_ref, grad_ref, sums_ref, edge_sums, node_sums, wn1_grad, wn2_grad,
                slots, total, table, slope_ref, normed_ref, factor_ref, out, sem):
    groups, n = groups_of(local_ref.shape[1])
    columns = columns_of(biases_ref, gains_ref, 1)
    slot_table(slots, (r0, r1, r2, r3, r4, r5))
    parts = (part_ref,)
    edges_forward(1, parts, alive_ref, index_ref, slots, w1_ref, w2_ref, columns, total, groups, n,
                  slope_ref, normed_ref, hidden_ref, factor_ref)
    clear((wn1_grad, wn2_grad, node_sums, edge_sums, sums_ref))
    wn2 = wn2_ref[1]
    wn2_t = transposed(wn2)
    wn1 = transposed(wn1_ref[1])

    def first_layer(j, unused):
        local = local_ref[:, j * n : (j + 1) * n]
        inputs = jnp.concatenate([local, total[j * D : (j + 1) * D, :].astype(B16)], axis=0)
        return inputs, *node_first(1, inputs, wn1_ref, columns)

    def second_layer(j, held):
        inputs, hidden, slope = held
        s = slice(j * n, (j + 1) * n)
        normed, factor = node_second(hidden, wn2_t, columns)
        out[:, s] = local_ref[:, s].astype(F32) + normed * columns[:, 7:8] + columns[:, 5:6]
        return inputs, slope, node_second_grad(cot_ref[:, s], normed, factor, hidden, columns, wn2_grad, node_sums)

    def node_grads(j, held):
        inputs, slope, second = held
        s = slice(j * n, (j + 1) * n)
        first = node_first_grad(second, slope, inputs, wn2, wn1_grad, node_sums)
        table[j * D : (j + 1) * D, :] = first
        grad_ref[:, s] = cot_ref[:, s] + dot(wn1[0:D], first)

    pipelined((first_layer, second_layer, node_grads), range(groups))
    copy = pltpu.make_async_copy(out, out_ref, sem)
    copy.start()
    weight_two = w2_ref[1]
    weight_slot = transposed(w1_ref[1, :, D : 2 * D])

    def grad_rows(span, unused):
        a, size = span[2].start, span[2].size
        return pick(table, row_of(index_ref, 0, a, size), row_of(index_ref, 1, a, size), groups, n)

    def second_grad(span, rows):
        return edge_second(rows, span[2], columns, wn1[D : 2 * D], alive_ref, normed_ref, factor_ref, edge_sums)

    def first_grad(span, second):
        s = span[2]
        first = edge_first(second, s, weight_two, slope_ref, edge_sums)
        first_ref[:, s] = first
        second_ref[:, s] = second
        return first

    def sum_slots(span, first):
        a, size = span[2].start, span[2].size
        add_at(sums_ref, first, row_of(index_ref, 2, a, size), row_of(index_ref, 3, a, size), SLOT_GROUPS, SLOT_COLS)

    pipelined((grad_rows, second_grad, first_grad, sum_slots), spans_of(parts, CHUNK))
    slot_gradients((g0, g1, g2), sums_ref, weight_slot)
    copy.wait()


def down_targets_kernel(index_ref, first_ref, local_ref, start_ref, w1_ref, grad_ref, weight_grad_ref, total):
    groups, n = groups_of(local_ref.shape[1])
    weight = transposed(w1_ref[1, :, 2 * D : 3 * D])
    total[...] = jnp.zeros_like(total)

    def body(s):
        group, column = row_of(index_ref, 0, s.start, s.size), row_of(index_ref, 1, s.start, s.size)
        add_at(total, first_ref[:, s], group, column, groups, n)

    over_blocks(first_ref.shape[1], EDGE_BLOCK, body)
    weight_grad_ref[...] = target_grads(total, local_ref, weight, start_ref, grad_ref, groups, n)


def down_rest_kernel(feat_ref, first_ref, second_ref, hidden_ref, r0, r1, r2, r3, r4, r5, sums_ref, local_grads_ref,
                     edge_sums, node_sums, wn1_grad, wn2_grad, w1_ref, *rest):
    feat_grad_ref, packed_ref, slots, one_ref, two_ref = rest[-5:]
    step = pl.program_id(0)
    weight = transposed(w1_ref[1, :, 0:D])

    @pl.when(step == 0)
    def _():
        clear((one_ref, two_ref))

    s = pl.ds(pl.multiple_of(step * EDGE_BLOCK, EDGE_BLOCK), EDGE_BLOCK)
    first = first_ref[:, s]
    feat_grad_ref[...] = dot(weight, first)
    one_ref[...] += dot_rows(first, feat_ref[:, s])
    two_ref[...] += dot_rows(hidden_ref[:, s], second_ref[:, s])

    @pl.when(step == pl.num_programs(0) - 1)
    def _():
        slot_table(slots, (r0, r1, r2, r3, r4, r5))
        slot_grads = slot_weight_grads(sums_ref, slots)
        write_packed(packed_ref, one_ref[...], slot_grads, local_grads_ref[...], two_ref[...], wn1_grad[...], wn2_grad[...],
                     pack_columns(edge_sums, node_sums))


def write_packed(packed_ref, one, slot_grads, local_grads, two, wn1_grad, wn2_grad, columns):
    packed_ref[0] = jnp.concatenate([one, slot_grads], axis=1)
    packed_ref[1] = jnp.concatenate([local_grads, two], axis=1)
    packed_ref[2] = wn1_grad
    packed_ref[3] = jnp.concatenate([wn2_grad, columns], axis=1)


def up_backward_kernel(index_ref, feat_ref, h0, h1, h2, h3, h4, h5,
                       send_ref, cot_ref, local_ref, summed_ref, r0, r1, r2, r3, r4, r5, slope_ref, normed_ref, hidden_ref, factor_ref, alive_ref, packed_down_ref,
                       w1_ref, w2_ref, wn1_ref, wn2_ref, biases_ref, gains_ref,
                       g0, g1, g2, first_ref, grad_ref, keep_ref,
                       slots, table, back, total, sums, start, one_ref, two_ref, edge_sums, node_sums, wn1_grad, wn2_grad, pieces):
    groups, n = groups_of(local_ref.shape[1])
    columns = columns_of(biases_ref, gains_ref, 0)
    clear((back, total, sums, one_ref, two_ref, edge_sums, node_sums, wn1_grad, wn2_grad))
    slot_table(slots, (r0, r1, r2, r3, r4, r5))
    add_back(back, (h0, h1, h2, h3, h4, h5), send_ref, groups, n)
    wn2 = wn2_ref[0]
    wn2_t = transposed(wn2)
    wn1 = transposed(wn1_ref[0])
    w1 = transposed(w1_ref[0])

    def first_layer(j, unused):
        s = slice(j * n, (j + 1) * n)
        inputs = jnp.concatenate([local_ref[:, s], summed_ref[:, s]], axis=0)
        return inputs, *node_first(0, inputs, wn1_ref, columns)

    def second_layer(j, held):
        inputs, hidden, slope = held
        grad = cot_ref[:, j * n : (j + 1) * n] + back[j * D : (j + 1) * D, :]
        normed, factor = node_second(hidden, wn2_t, columns)
        return inputs, slope, grad, node_second_grad(grad, normed, factor, hidden, columns, wn2_grad, node_sums)

    def node_grads(j, held):
        inputs, slope, grad, second = held
        first = node_first_grad(second, slope, inputs, wn2, wn1_grad, node_sums)
        table[j * D : (j + 1) * D, :] = first
        start[:, j * n : (j + 1) * n] = grad + dot(wn1[0:D], first)

    pipelined((first_layer, second_layer, node_grads), range(groups))
    weight_two = w2_ref[0]

    def grad_rows(span, unused):
        a, size = span[2].start, span[2].size
        return pick(table, row_of(index_ref, 0, a, size), row_of(index_ref, 1, a, size), groups, n)

    def second_grad(span, rows):
        return edge_second(rows, span[2], columns, wn1[D : 2 * D], alive_ref, normed_ref, factor_ref, edge_sums)

    def first_grad(span, second):
        s = span[2]
        first = edge_first(second, s, weight_two, slope_ref, edge_sums)
        first_ref[:, s] = first
        two_ref[...] += dot_rows(hidden_ref[:, s], second)
        return first

    def sum_rows(span, first):
        s = span[2]
        rows = [row_of(index_ref, i, s.start, s.size) for i in range(4)]
        add_at(total, first, rows[0], rows[1], groups, n)
        add_at(sums, first, rows[2], rows[3], SLOT_GROUPS, SLOT_COLS)
        one_ref[...] += dot_rows(first, feat_ref[:, s])

    pipelined((grad_rows, second_grad, first_grad, sum_rows), spans_of((first_ref,), CHUNK))
    slot_gradients((g0, g1, g2), sums, w1[D : 2 * D])
    local_grads = target_grads(total, local_ref, w1[2 * D : 3 * D], start, grad_ref, groups, n)
    slot_grads = slot_weight_grads(sums, slots)
    write_packed(pieces, one_ref[...], slot_grads, local_grads, two_ref[...], wn1_grad[...], wn2_grad[...],
                 pack_columns(edge_sums, node_sums))
    unused, core = level_and_core()
    for p in range(4):
        pieces[4 + p] = packed_down_ref[p]
    for p in range(4):
        keep_ref[p] = pieces[core * 4 + p]
        g0[4 + p] = pieces[(1 - core) * 4 + p].astype(B16)


def feat_grad_kernel(first_ref, w1_ref, out_ref):
    out_ref[...] = dot(transposed(w1_ref[0, :, 0:D]), first_ref[...])


def lower_grad_kernel(h0, h1, h2, h3, h4, h5, send_ref, start_ref, out_ref, total):
    groups, n = groups_of(start_ref.shape[1])
    clear((total,))
    add_back(total, (h0, h1, h2, h3, h4, h5), send_ref, groups, n)
    for j in range(groups):
        s = slice(j * n, (j + 1) * n)
        out_ref[:, s] = start_ref[:, s] + total[j * D : (j + 1) * D, :]


def unpack_kernel(own_ref, other_ref, w1_ref, w2_ref, wn1_ref, wn2_ref, biases_ref, gains_ref, pieces):
    unused, core = level_and_core()
    for p in range(4):
        pieces[core * 4 + p] = own_ref[p].astype(F32)
        pieces[(1 - core) * 4 + p] = other_ref[p].astype(F32)
    for k in range(2):
        w1_ref[k] = jnp.concatenate([pieces[4 * k], pieces[4 * k + 1, :, 0:D]], axis=1)
        w2_ref[k] = pieces[4 * k + 1, :, D : 2 * D]
        wn1_ref[k] = pieces[4 * k + 2]
        wn2_ref[k] = pieces[4 * k + 3, :, 0:D]
        rows = pieces[4 * k + 3].T
        for i in range(6):
            biases_ref[i, k : k + 1] = rows[D + i : D + i + 1]
        gains_ref[k] = rows[D + 6 : D + 8]


def shape(dims, dtype=F32):
    return jax.ShapeDtypeStruct(dims, dtype)


def call(kernel, name, outs, scratch, scalars=0, stored=(), streamed=None, final=(), raw=()):
    steps, stream_in, stream_out = streamed if streamed else (1, (), ())

    def run(*operands, after=()):
        def whole(space):
            return pl.BlockSpec(memory_space=space)

        def cut(x):
            return pl.BlockSpec((x.shape[0], x.shape[1] // steps), lambda i: (0, i))

        in_specs, placed = [], []
        for i, x in enumerate(operands):
            if i < scalars:
                in_specs.append(whole(pltpu.SMEM))
            elif i in stream_in:
                in_specs.append(cut(x))
            elif i in raw:
                in_specs.append(whole(pltpu.HBM))
                x = pltpu.with_memory_space_constraint(x, pltpu.HBM)
            else:
                in_specs.append(whole(pltpu.VMEM))
                x = pltpu.with_memory_space_constraint(x, pltpu.VMEM)
            placed.append(x)
        in_specs += [whole(pl.ANY) for _ in after]
        out_specs, out_shape = [], []
        for i, x in enumerate(outs):
            if i in stream_out:
                out_specs.append(cut(x))
                out_shape.append(x)
            elif i in stored:
                out_specs.append(whole(pl.ANY))
                out_shape.append(x)
            elif i in final:
                out_specs.append(whole(pltpu.VMEM))
                out_shape.append(x)
            else:
                out_specs.append(whole(pltpu.VMEM))
                out_shape.append(pltpu.VMEM(x.shape, x.dtype))
        return pl.pallas_call(
            kernel,
            name=name,
            grid=(steps,) if streamed else (),
            in_specs=in_specs,
            out_specs=out_specs,
            out_shape=out_shape,
            scratch_shapes=scratch,
            compiler_params=pltpu.CompilerParams(vmem_limit_bytes=VMEM_BYTES),
        )(*placed, *after)

    return run


def core_swap(block):
    return lax.ppermute(block, "band", [(i, i ^ 1) for i in range(lax.axis_size("band"))])


def cross_swap(block):
    last = lax.axis_size("band") - 1
    pairs = [(i, i + 1) for i in range(1, last, 2)]
    return lax.ppermute(block, "band", pairs + [(b, a) for a, b in pairs] + [(0, 0), (last, last)])


def along_level(block, step):
    count = lax.axis_size("level")
    return lax.ppermute(block, "level", [(i, (i + step) % count) for i in range(count)])


def across_bands(blocks):
    partner, cross, own = blocks
    return [core_swap(partner), cross_swap(cross), own]


def along_levels(blocks, sign):
    return blocks + [along_level(jnp.stack([b[d] for b in blocks]), sign * d) for d in (1, 2, 3)]


def chip_axis(block, stride, step):
    count = lax.axis_size("band")
    pairs = []
    for i in range(count):
        at = (i // stride) % 4
        pairs.append((i, i + (((at + step) % 4) - at) * stride))
    return lax.ppermute(block, "band", pairs)


def rounded(values):
    return lax.reduce_precision(values, 8, 7)


def sum_of_four(values, first, second, third):
    return (values + second.astype(F32)) + (first.astype(F32) + third.astype(F32))


def sum_along(values, stride):
    own = rounded(values)
    sent = own.astype(B16)
    return sum_of_four(own, *(chip_axis(sent, stride, d) for d in (1, 2, 3)))


def shards(
    lower_nodes, latent, up_feat, down_feat, up_send, up_counts, up_senders, up_targets,
    down_send, down_counts, down_senders, down_targets,
    edge_w1, edge_w2, node_w1, node_w2, biases, norm_gains, lower_cot, upper_cot,
):
    lower, upper = lower_nodes.T, latent.T
    feat_up, feat_down = up_feat.T, down_feat.T
    cot_lower, cot_upper = lower_cot.T, upper_cot.T
    w1, wn1 = edge_w1.transpose(0, 2, 1), node_w1.transpose(0, 2, 1)
    w2, wn2 = edge_w2, node_w2
    edges, lower_rows, upper_rows = up_feat.shape[0], lower_nodes.shape[0], latent.shape[0]
    dense = (edges // 128, 128)
    senders_up, targets_up, senders_down, targets_down = (
        x.reshape(dense) for x in (up_senders, up_targets, down_senders, down_targets))
    bias_rows = biases.transpose(1, 0, 2)

    lower_groups, lower_n = groups_of(lower_rows)
    upper_groups, upper_n = groups_of(upper_rows)
    lower_table, upper_table = (lower_groups * D, lower_n), (upper_groups * D, upper_n)
    slots = pltpu.VMEM((SLOT_GROUPS * D, SLOT_COLS), B16)
    block, four = shape((4, D, 128), B16), shape((4, D, 128))
    wide32, wide16, row = shape((D, edges)), shape((D, edges), B16), shape((1, edges))
    steps = edges // EDGE_BLOCK

    early = (up_send, lower, senders_up, targets_up, senders_down, targets_down, upper, w1, bias_rows, norm_gains,
             down_send, w2, wn1, wn2)
    count = len(early)
    (*sent, up_send, lower, senders_up, targets_up, senders_down, targets_down, upper, w1, bias_rows,
     norm_gains, down_send, w2, wn1, wn2) = call(
        functools.partial(send_kernel, count), "send_lower", [block] * 3 + [shape(x.shape, x.dtype) for x in early],
        [pltpu.VMEM(lower_table, B16), pltpu.SemaphoreType.DMA((count,))], 0, raw=range(count),
    )(*early)
    index, lives = shape((4, *dense), jnp.int32), shape((1, *dense))
    index_up, alive_up, index_down, alive_down = call(
        functools.partial(tables_kernel, upper_rows, lower_rows), "edge_tables", [index, lives, index, lives],
        [pltpu.SMEM((1, 12), jnp.int32), pltpu.SMEM((1, 12), jnp.int32), pltpu.SemaphoreType.DMA((2,))], 0, raw=(0, 1),
    )(up_counts, down_counts, senders_up, targets_up, senders_down, targets_down)

    def part(k, block, name, table, index, feat, local, after):
        return call(
            functools.partial(part_kernel, k, block), name, [wide32, wide16],
            [pltpu.VMEM(table, B16), pltpu.VMEM((D, edges), B16), pltpu.SemaphoreType.DMA], 0, raw=(1,),
        )(index, feat, local, w1, bias_rows, norm_gains, after=after)

    sent = across_bands(sent)
    part_up, feat_up = part(0, EDGE_BLOCK, "part_up", upper_table, index_up, feat_up, upper, ())
    sent, part_up = lax.optimization_barrier((sent, part_up))
    up_slots = along_levels(sent, 1)
    (upper_new, summed_up, s0, s1, s2, slope, normed, hidden, factor) = call(
        up_forward_kernel, "up_forward",
        [shape((D, upper_rows)), shape((D, upper_rows), B16)] + [block] * 3 + [wide32, wide32, wide16, row],
        [slots, pltpu.VMEM(upper_table, F32), pltpu.VMEM(upper_table, B16), pltpu.VMEM((D, upper_rows), F32),
         pltpu.SemaphoreType.DMA], 0, (0,),
    )(part_up, alive_up, index_up, *up_slots, upper, down_send, w1, w2, wn1, wn2, bias_rows, norm_gains)
    sent = across_bands([s0, s1, s2])
    part_down, feat_down = part(1, EDGE_BLOCK, "part_down", lower_table, index_down, feat_down, lower, (s0,))
    sent, part_down = lax.optimization_barrier((sent, part_down))
    down_slots = along_levels(sent, 1)
    sums_shape = shape((SLOT_GROUPS * D, SLOT_COLS))
    (lower_new, g0, g1, g2, first_down, second_down, hidden_down, start_lower, sums_down, edge_sums, node_sums, wn1_grad, wn2_grad) = call(
        down_kernel, "down_sweep",
        [shape((D, lower_rows))] + [block] * 3 + [wide16] * 3 + [shape((D, lower_rows)), sums_shape, four, four,
         shape((D, 2 * D)), shape((D, D))],
        [slots, pltpu.VMEM(lower_table, F32), pltpu.VMEM(lower_table, B16), pltpu.VMEM((D, edges), F32),
         pltpu.VMEM((D, edges), F32), pltpu.VMEM((1, edges), F32),
         pltpu.VMEM((D, lower_rows), F32), pltpu.SemaphoreType.DMA], 0, (0,),
    )(part_down, alive_down, index_down, *down_slots, lower, cot_lower, w1, w2, wn1, wn2, bias_rows, norm_gains)
    back = across_bands([g0, g1, g2])
    start_lower, local_grads = call(
        down_targets_kernel, "down_targets", [shape((D, lower_rows)), shape((D, D))], [pltpu.VMEM(lower_table, F32)],
    )(index_down, first_down, lower, start_lower, w1)
    back, local_grads = lax.optimization_barrier((back, local_grads))
    down_back = along_levels(back, -1)
    feat_grad_down, packed_down = call(
        down_rest_kernel, "down_rest", [wide32, four],
        [slots, pltpu.VMEM((D, D), F32), pltpu.VMEM((D, D), F32)], 0, (), (steps, (), (0,)),
    )(feat_down, first_down, second_down, hidden_down, *down_slots, sums_down, local_grads,
      edge_sums, node_sums, wn1_grad, wn2_grad, w1, after=(back[1],))
    (partner, cross, own, first_up, grad_latent, keep) = call(
        up_backward_kernel, "up_backward",
        [shape((8, D, 128), B16), block, block, wide16, shape((D, upper_rows)), four],
        [slots, pltpu.VMEM(upper_table, B16), pltpu.VMEM(upper_table, F32), pltpu.VMEM(upper_table, F32),
         pltpu.VMEM((SLOT_GROUPS * D, SLOT_COLS), F32), pltpu.VMEM((D, upper_rows), F32),
         pltpu.VMEM((D, D), F32), pltpu.VMEM((D, D), F32), pltpu.VMEM((4, D, 128), F32), pltpu.VMEM((4, D, 128), F32),
         pltpu.VMEM((D, 2 * D), F32), pltpu.VMEM((D, D), F32), pltpu.VMEM((8, D, 128), F32)], 0, (), None, (4,),
    )(index_up, feat_up, *down_back, down_send, cot_upper, upper, summed_up, *up_slots,
      slope, normed, hidden, factor, alive_up, packed_down, w1, w2, wn1, wn2, bias_rows, norm_gains)

    (feat_grad_up,) = call(feat_grad_kernel, "feat_grad_up", [wide32], [], 0, (), (steps, (0,), (0,)))(first_up, w1)
    partner, cross = core_swap(partner), cross_swap(cross)
    partner, cross, feat_grad_up = lax.optimization_barrier((partner, cross, feat_grad_up))
    total = rounded(rounded(keep) + partner[4:].astype(F32))
    blocks = (partner, cross, own)
    levels = [
        along_level(jnp.concatenate([jnp.stack([b[d] for b in blocks]), total.astype(B16)]), -d) for d in (1, 2, 3)
    ]
    total = sum_of_four(total, *(b[3:] for b in levels))
    (grad_lower,) = call(lower_grad_kernel, "lower_grad", [shape((D, lower_rows))], [pltpu.VMEM(lower_table, F32)], 0, (), None, (0,))(
        *blocks, *levels, up_send, start_lower)
    total = sum_along(total, 2)
    total, grad_lower = lax.optimization_barrier((total, grad_lower))
    total = rounded(sum_along(total, 8)).astype(B16)
    w1_grad, w2_grad, wn1_grad, wn2_grad, bias_grad, gain_grad = call(
        unpack_kernel, "unpack",
        [shape((2, D, 3 * D)), shape((2, D, D)), shape((2, D, 2 * D)), shape((2, D, D)), shape((6, 2, D)), shape((2, 2, D))],
        [pltpu.VMEM((8, D, 128), F32)], 0, (), None, range(6))(total, core_swap(total))
    return (
        lower_new.T, upper_new.T, grad_lower.T, grad_latent.T, feat_grad_up.T, feat_grad_down.T,
        w1_grad.transpose(0, 2, 1), w2_grad, wn1_grad.transpose(0, 2, 1), wn2_grad, bias_grad.transpose(1, 0, 2), gain_grad,
    )


def solution(mesh):
    rows, index, whole = P(("band", "level"), None), P(("band", "level")), P()
    placed = (rows,) * 6 + (index, index) + (rows,) * 2 + (index, index) + (whole,) * 6 + (rows,) * 2
    return jax.shard_map(
        shards,
        mesh=mesh,
        in_specs=placed,
        out_specs=(rows,) * 6 + (whole,) * 6,
        check_vma=False,
    )
```

```python
import functools

import jax
import jax.numpy as jnp
from jax import lax
from jax.experimental import pallas as pl
from jax.experimental.pallas import tpu as pltpu
from jax.sharding import PartitionSpec as P

EPSILON = 1e-05
F32 = jnp.float32
B16 = jnp.bfloat16
D = 64
SLOT_GROUPS, SLOT_COLS = 6, 256
EDGE_BLOCK = 3072
CHUNK = 1024
VMEM_BYTES = 24 * 1024 * 1024


def groups_of(rows):
    return (4, rows // 4) if rows > 1024 else (rows // 256, 256)


def dot(a, b):
    return jnp.dot(a, b, preferred_element_type=F32)


def dot_rows(a, b):
    return lax.dot_general(a, b, (((1,), (1,)), ((), ())), preferred_element_type=F32)


def halves(x):
    high = x.astype(B16)
    return high, (x - high.astype(F32)).astype(B16)


def one_hot(column, n):
    rows = lax.broadcasted_iota(jnp.int16, (n, column.shape[1]), 0)
    return jnp.where(rows == column.astype(jnp.int16), jnp.ones((), B16), jnp.zeros((), B16))


def place(index, groups, n):
    group = jnp.zeros_like(index)
    for j in range(1, groups):
        group = group + (index >= j * n).astype(jnp.int32)
    return group, index - group * n


def level_and_core():
    return lax.axis_index("level").astype(jnp.int32), lax.axis_index("band").astype(jnp.int32) & 1


def slot_place(senders):
    level, core = level_and_core()
    distance = (level - ((senders >> 7) & 3)) & 3
    offset = senders >> 9
    source = jnp.where(offset == 1, 2, jnp.where(offset == 2 - 2 * core, 0, 1))
    block = distance * 3 + source
    return block >> 1, ((block & 1) << 7) | (senders & 127)


def live(senders, counts_ref):
    peer = senders >> 7
    limit = jnp.zeros_like(senders)
    for j in range(12):
        limit = jnp.where(peer == j, counts_ref[0, j], limit)
    return ((senders & 127) < limit).astype(F32)


def choose(stacked, group, groups):
    picked = stacked[0:D]
    for j in range(1, groups):
        picked = jnp.where(group == j, stacked[j * D : (j + 1) * D], picked)
    return picked


def row_of(ref, k, start, size):
    rows = size // 128
    if not isinstance(start, int):
        start = pl.multiple_of(start // 128, rows)
        return jnp.concatenate([ref[k, pl.ds(start + r, 1), :] for r in range(rows)], axis=1)
    return jnp.concatenate([ref[k, r : r + 1, :] for r in range(start // 128, start // 128 + rows)], axis=1)


def pick(table, group, column, groups, n):
    return choose(dot(table[...], one_hot(column, n)), group, groups).astype(B16)


def spread(values, group, groups):
    wide = jnp.broadcast_to(group.astype(jnp.int16), values.shape)
    nothing = jnp.zeros_like(values)
    return jnp.concatenate([jnp.where(wide == j, values, nothing) for j in range(groups)], axis=0)


def add_at(total, values, group, column, groups, n):
    total[...] += dot_rows(spread(values, group, groups), one_hot(column, n))


def pack_table(table, source, groups, n):
    for j in range(groups):
        table[j * D : (j + 1) * D, :] = source[:, j * n : (j + 1) * n]


def columns_of(biases_ref, gains_ref, k):
    rows = [biases_ref[i, k : k + 1] for i in range(6)] + [gains_ref[k]]
    return jnp.concatenate(rows, axis=0).T


def fold(values):
    total = values[:, 0:128]
    for i in range(128, values.shape[1], 128):
        total = total + values[:, i : i + 128]
    return total


def norm_parts(values):
    centre = values - jnp.sum(values, axis=0, keepdims=True) * (1.0 / D)
    spread_sum = jnp.sum(centre * centre, axis=0, keepdims=True) * (1.0 / D)
    factor = lax.rsqrt(spread_sum + EPSILON)
    return centre * factor, factor


def norm_back(grad, normed, factor, gain):
    scaled = grad * gain
    first = jnp.sum(scaled, axis=0, keepdims=True) * (1.0 / D)
    second = jnp.sum(scaled * normed, axis=0, keepdims=True) * (1.0 / D)
    return factor * (scaled - first - normed * second)


def sigmoid(values):
    return 0.5 * jnp.tanh(0.5 * values) + 0.5


def send_rows(send_ref, source):
    level, core = level_and_core()
    offset = (2 - 2 * core, 2 * core, 1)[source]
    return jnp.concatenate(
        [send_ref[pl.ds(offset * 4 + ((level + d) & 3), 1), :] for d in range(4)], axis=1
    )


def send_blocks(outs, table, send_ref, groups, n):
    for j in range(3):
        group, column = place(send_rows(send_ref, j), groups, n)
        rows = pick(table, group, column, groups, n)
        for d in range(4):
            outs[j][d] = rows[:, d * 128 : (d + 1) * 128]


def add_back(total, blocks, send_ref, groups, n):
    for j in range(3):
        group, column = place(send_rows(send_ref, j), groups, n)
        values = jnp.concatenate([block_at(blocks, d, j) for d in range(4)], axis=1)
        add_at(total, values, group, column, groups, n)


def block_at(received, d, j):
    return received[j][0] if d == 0 else received[2 + d][j]


def slot_table(table, received):
    for t in range(12):
        table[(t >> 1) * D : ((t >> 1) + 1) * D, (t & 1) * 128 : ((t & 1) + 1) * 128] = block_at(received, t // 3, t % 3)


def slot_gradients(outs, sums, weight):
    for j in range(SLOT_GROUPS):
        high, low = halves(sums[j * D : (j + 1) * D, :])
        grads = (dot(weight, high) + dot(weight, low)).astype(B16)
        for t in (2 * j, 2 * j + 1):
            outs[t % 3][t // 3] = grads[:, (t & 1) * 128 : ((t & 1) + 1) * 128]


def over_blocks(total, block, body):
    block = min(block, total)
    if block == total:
        body(pl.ds(0, block))
        return

    def step(i, carry):
        body(pl.ds(pl.multiple_of(i * block, block), block))
        return carry

    lax.fori_loop(0, total // block, step, 0)


def pipelined(stages, spans):
    held = [None] * len(spans)
    for t in range(len(spans) + len(stages) - 1):
        for k in reversed(range(len(stages))):
            i = t - k
            if 0 <= i < len(spans):
                held[i] = stages[k](spans[i], held[i])


def spans_of(parts, chunk):
    spans, start = [], 0
    for which, ref in enumerate(parts):
        size = min(chunk, ref.shape[1])
        for at in range(0, ref.shape[1], size):
            spans.append((which, pl.ds(at, size), pl.ds(start + at, size)))
        start += ref.shape[1]
    return spans


def tables_kernel(upper_rows, lower_rows, counts_up, counts_down, senders_up, targets_up, senders_down, targets_down,
                  index_up, alive_up, index_down, alive_down, limits_up, limits_down, sems):
    copies = [pltpu.make_async_copy(counts_up, limits_up, sems.at[0]), pltpu.make_async_copy(counts_down, limits_down, sems.at[1])]
    for copy in copies:
        copy.start()
    sweeps = ((index_up, senders_up, targets_up, upper_rows), (index_down, senders_down, targets_down, lower_rows))
    for index_ref, senders_ref, targets_ref, rows in sweeps:
        index_ref[0], index_ref[1] = place(targets_ref[...], *groups_of(rows))
        index_ref[2], index_ref[3] = slot_place(senders_ref[...])
    for copy in copies:
        copy.wait()
    alive_up[0] = live(senders_up[...], limits_up)
    alive_down[0] = live(senders_down[...], limits_down)


def send_kernel(count, *refs):
    sources, refs = refs[:count], refs[count:]
    sent, held, table, sems = refs[:3], refs[3:-2], refs[-2], refs[-1]
    copies = [pltpu.make_async_copy(a, b, sems.at[i]) for i, (a, b) in enumerate(zip(sources, held))]
    for copy in copies:
        copy.start()
    for copy in copies[:2]:
        copy.wait()
    send_ref, source_ref = held[:2]
    groups, n = groups_of(source_ref.shape[1])
    pack_table(table, source_ref, groups, n)
    send_blocks(sent, table, send_ref, groups, n)
    for copy in copies[2:]:
        copy.wait()


def part_kernel(k, block, index_ref, feat_ref, local_ref, w1_ref, biases_ref, gains_ref, *rest):
    part_ref, held_ref, table, picked, sem = rest[-5:]
    copy = pltpu.make_async_copy(feat_ref, held_ref, sem)
    copy.start()
    groups, n = groups_of(local_ref.shape[1])
    pack_table(table, local_ref, groups, n)
    columns = columns_of(biases_ref, gains_ref, k)
    weight = jnp.concatenate([w1_ref[k, :, 0:D], w1_ref[k, :, 2 * D : 3 * D]], axis=1)

    def body(s):
        picked[:, s] = pick(table, row_of(index_ref, 0, s.start, s.size), row_of(index_ref, 1, s.start, s.size), groups, n)

    over_blocks(feat_ref.shape[1], block, body)
    copy.wait()
    part_ref[...] = dot(weight, jnp.concatenate([held_ref[...], picked[...]], axis=0)) + columns[:, 0:1]


def edges_forward(k, parts, alive_ref, index_ref, table, w1_ref, w2_ref, columns, total, groups, n,
                  slope_ref, normed_ref, hidden_ref, factor_ref):
    weight_slot = w1_ref[k, :, D : 2 * D]
    weight_two = w2_ref[k].astype(F32).T.astype(B16)
    total[...] = jnp.zeros_like(total)

    def slot_rows(span, unused):
        a, size = span[2].start, span[2].size
        return pick(table, row_of(index_ref, 2, a, size), row_of(index_ref, 3, a, size), SLOT_GROUPS, SLOT_COLS)

    def first_layer(span, picked):
        which, t, s = span
        first = parts[which][:, t] + dot(weight_slot, picked)
        gate = sigmoid(first)
        hidden = (first * gate).astype(B16)
        slope_ref[:, s] = gate * (1.0 + first * (1.0 - gate))
        hidden_ref[:, s] = hidden
        return hidden

    def second_layer(span, hidden):
        s = span[2]
        normed, factor = norm_parts(dot(weight_two, hidden) + columns[:, 1:2])
        alive = row_of(alive_ref, 0, s.start, s.size)
        normed_ref[:, s] = normed
        factor_ref[:, s] = factor
        return ((normed * columns[:, 6:7] + columns[:, 2:3]) * alive).astype(B16)

    def sum_messages(span, messages):
        a, size = span[2].start, span[2].size
        add_at(total, messages, row_of(index_ref, 0, a, size), row_of(index_ref, 1, a, size), groups, n)

    pipelined((slot_rows, first_layer, second_layer, sum_messages), spans_of(parts, CHUNK))


def node_first(k, inputs, wn1_ref, columns):
    first = dot(wn1_ref[k], inputs) + columns[:, 3:4]
    gate = sigmoid(first)
    return (first * gate).astype(B16), gate * (1.0 + first * (1.0 - gate))


def node_second(hidden, weight_two, columns):
    return norm_parts(dot(weight_two, hidden) + columns[:, 4:5])


def node_second_grad(grad, normed, factor, columns, sums_ref):
    sums_ref[2] += fold(grad)
    sums_ref[3] += fold(grad * normed)
    return norm_back(grad, normed, factor, columns[:, 7:8]).astype(B16)


def node_weight_grads(first, second, inputs, hidden, one_ref, two_ref, sums_ref):
    sums_ref[0] += fold(first.astype(F32))
    sums_ref[1] += fold(second.astype(F32))
    one_ref[...] += dot_rows(first, inputs)
    two_ref[...] += dot_rows(hidden, second)


def clear(refs):
    for ref in refs:
        ref[...] = jnp.zeros_like(ref)


def transposed(weight):
    return weight.astype(F32).T.astype(B16)


def edge_second(grad_rows, s, columns, weight_sum, alive_ref, normed_ref, factor_ref, sums_ref):
    grad = dot(weight_sum, grad_rows) * row_of(alive_ref, 0, s.start, s.size)
    normed = normed_ref[:, s]
    sums_ref[2] += fold(grad)
    sums_ref[3] += fold(grad * normed)
    return norm_back(grad, normed, factor_ref[:, s], columns[:, 6:7]).astype(B16)


def edge_first(second, s, weight_two, slope_ref):
    return (dot(weight_two, second) * slope_ref[:, s]).astype(B16)


def edge_weight_grads(first, second, feat, hidden, one_ref, two_ref, sums_ref):
    sums_ref[0] += fold(first.astype(F32))
    sums_ref[1] += fold(second.astype(F32))
    one_ref[...] += dot_rows(first, feat)
    two_ref[...] += dot_rows(hidden, second)


def pack_columns(edge_sums, node_sums):
    order = (edge_sums[0], edge_sums[1], edge_sums[2], node_sums[0], node_sums[1], node_sums[2], edge_sums[3], node_sums[3])
    columns = [jnp.sum(v, axis=1, keepdims=True) for v in order]
    lanes = lax.broadcasted_iota(jnp.int32, (D, D), 1)
    packed = jnp.zeros((D, D), F32)
    for i, column in enumerate(columns):
        packed = jnp.where(lanes == i, column, packed)
    return packed


def slot_weight_grads(sums, table):
    total = jnp.zeros((D, D), F32)
    for j in range(SLOT_GROUPS):
        high, low = halves(sums[j * D : (j + 1) * D, :])
        rows = table[j * D : (j + 1) * D, :]
        total = total + dot_rows(high, rows) + dot_rows(low, rows)
    return total


def target_grads(total, local_ref, weight, start, out_ref, groups, n):
    grads = jnp.zeros((D, D), F32)
    for j in range(groups):
        high, low = halves(total[j * D : (j + 1) * D, :])
        s = slice(j * n, (j + 1) * n)
        rows = local_ref[:, s]
        grads = grads + dot_rows(high, rows) + dot_rows(low, rows)
        out_ref[:, s] = start(j) + dot(weight, high) + dot(weight, low)
    return grads


def up_forward_kernel(part_ref, alive_ref, index_ref, r0, r1, r2, r3, r4, r5, local_ref, send_ref,
                      w1_ref, w2_ref, wn1_ref, wn2_ref, biases_ref, gains_ref,
                      out_ref, summed_ref, s0, s1, s2, slope_ref, normed_ref, hidden_ref, factor_ref,
                      slots, total, table, out, sem):
    groups, n = groups_of(local_ref.shape[1])
    columns = columns_of(biases_ref, gains_ref, 0)
    slot_table(slots, (r0, r1, r2, r3, r4, r5))
    edges_forward(0, (part_ref,), alive_ref, index_ref, slots, w1_ref, w2_ref, columns, total, groups, n,
                  slope_ref, normed_ref, hidden_ref, factor_ref)
    weight_two = transposed(wn2_ref[0])

    def first_layer(j, unused):
        s = slice(j * n, (j + 1) * n)
        summed = total[j * D : (j + 1) * D, :].astype(B16)
        summed_ref[:, s] = summed
        return node_first(0, jnp.concatenate([local_ref[:, s], summed], axis=0), wn1_ref, columns)

    def second_layer(j, held):
        s = slice(j * n, (j + 1) * n)
        normed, unused = node_second(held[0], weight_two, columns)
        result = local_ref[:, s].astype(F32) + normed * columns[:, 7:8] + columns[:, 5:6]
        out[:, s] = result
        table[j * D : (j + 1) * D, :] = result.astype(B16)

    pipelined((first_layer, second_layer), range(groups))
    copy = pltpu.make_async_copy(out, out_ref, sem)
    copy.start()
    send_blocks((s0, s1, s2), table, send_ref, groups, n)
    copy.wait()


def down_kernel(part_ref, alive_ref, index_ref, r0, r1, r2, r3, r4, r5, local_ref, cot_ref,
                w1_ref, w2_ref, wn1_ref, wn2_ref, biases_ref, gains_ref,
                out_ref, g0, g1, g2, first_ref, second_ref, hidden_ref, sums_ref, edge_sums, node_sums,
                table, summed_ref, node_hidden_ref, node_second_ref,
                slots, total, slope_ref, normed_ref, factor_ref, out, sem):
    groups, n = groups_of(local_ref.shape[1])
    columns = columns_of(biases_ref, gains_ref, 1)
    slot_table(slots, (r0, r1, r2, r3, r4, r5))
    parts = (part_ref,)
    edges_forward(1, parts, alive_ref, index_ref, slots, w1_ref, w2_ref, columns, total, groups, n,
                  slope_ref, normed_ref, hidden_ref, factor_ref)
    clear((node_sums, edge_sums, sums_ref))
    wn2 = wn2_ref[1]
    wn2_t = transposed(wn2)
    wn1 = transposed(wn1_ref[1])

    def first_layer(j, unused):
        summed = total[j * D : (j + 1) * D, :].astype(B16)
        summed_ref[j * D : (j + 1) * D, :] = summed
        inputs = jnp.concatenate([local_ref[:, j * n : (j + 1) * n], summed], axis=0)
        return node_first(1, inputs, wn1_ref, columns)

    def second_layer(j, held):
        hidden, slope = held
        s = slice(j * n, (j + 1) * n)
        normed, factor = node_second(hidden, wn2_t, columns)
        out[:, s] = local_ref[:, s].astype(F32) + normed * columns[:, 7:8] + columns[:, 5:6]
        second = node_second_grad(cot_ref[:, s], normed, factor, columns, node_sums)
        node_hidden_ref[:, s] = hidden
        node_second_ref[:, s] = second
        return slope, second

    def node_grads(j, held):
        slope, second = held
        table[j * D : (j + 1) * D, :] = (dot(wn2, second) * slope).astype(B16)

    pipelined((first_layer, second_layer, node_grads), range(groups))
    copy = pltpu.make_async_copy(out, out_ref, sem)
    copy.start()
    weight_two = w2_ref[1]
    weight_slot = transposed(w1_ref[1, :, D : 2 * D])

    def grad_rows(span, unused):
        a, size = span[2].start, span[2].size
        return pick(table, row_of(index_ref, 0, a, size), row_of(index_ref, 1, a, size), groups, n)

    def second_grad(span, rows):
        return edge_second(rows, span[2], columns, wn1[D : 2 * D], alive_ref, normed_ref, factor_ref, edge_sums)

    def first_grad(span, second):
        s = span[2]
        first = edge_first(second, s, weight_two, slope_ref)
        first_ref[:, s] = first
        second_ref[:, s] = second
        return first

    def sum_slots(span, first):
        a, size = span[2].start, span[2].size
        add_at(sums_ref, first, row_of(index_ref, 2, a, size), row_of(index_ref, 3, a, size), SLOT_GROUPS, SLOT_COLS)

    pipelined((grad_rows, second_grad, first_grad, sum_slots), spans_of(parts, CHUNK))
    slot_gradients((g0, g1, g2), sums_ref, weight_slot)
    copy.wait()


def down_targets_kernel(index_ref, first_ref, local_ref, cot_ref, table, w1_ref, wn1_ref, *rest):
    grad_ref, weight_grad_ref, total = rest[-3:]
    groups, n = groups_of(local_ref.shape[1])
    weight = transposed(w1_ref[1, :, 2 * D : 3 * D])
    total[...] = jnp.zeros_like(total)

    def body(s):
        group, column = row_of(index_ref, 0, s.start, s.size), row_of(index_ref, 1, s.start, s.size)
        add_at(total, first_ref[:, s], group, column, groups, n)

    over_blocks(first_ref.shape[1], EDGE_BLOCK, body)
    weight_node = transposed(wn1_ref[1, :, 0:D])

    def start(j):
        return cot_ref[:, j * n : (j + 1) * n] + dot(weight_node, table[j * D : (j + 1) * D, :])

    weight_grad_ref[...] = target_grads(total, local_ref, weight, start, grad_ref, groups, n)


def down_rest_kernel(feat_ref, first_ref, second_ref, hidden_ref, r0, r1, r2, r3, r4, r5, sums_ref, edge_in, node_in,
                     table, summed_ref, node_hidden_ref, node_second_ref, local_ref, w1_ref,
                     feat_grad_ref, packed_ref, slots, one_ref, two_ref, wn1_grad, wn2_grad, edge_sums, node_sums):
    step = pl.program_id(0)
    weight = transposed(w1_ref[1, :, 0:D])

    @pl.when(step == 0)
    def _():
        clear((one_ref, two_ref, wn1_grad, wn2_grad))
        edge_sums[...] = edge_in[...]
        node_sums[...] = node_in[...]

    s = pl.ds(pl.multiple_of(step * EDGE_BLOCK, EDGE_BLOCK), EDGE_BLOCK)
    first = first_ref[:, s]
    feat_grad_ref[...] = dot(weight, first)
    edge_weight_grads(first, second_ref[:, s], feat_ref[:, s], hidden_ref[:, s], one_ref, two_ref, edge_sums)

    @pl.when(step == pl.num_programs(0) - 1)
    def _():
        groups, n = groups_of(local_ref.shape[1])
        for j in range(groups):
            t, rows = slice(j * n, (j + 1) * n), slice(j * D, (j + 1) * D)
            inputs = jnp.concatenate([local_ref[:, t], summed_ref[rows, :]], axis=0)
            node_weight_grads(table[rows, :], node_second_ref[:, t], inputs, node_hidden_ref[:, t], wn1_grad, wn2_grad, node_sums)
        slot_table(slots, (r0, r1, r2, r3, r4, r5))
        write_packed(packed_ref, one_ref[...], slot_weight_grads(sums_ref, slots), jnp.zeros((D, D), F32), two_ref[...],
                     wn1_grad[...], wn2_grad[...], pack_columns(edge_sums, node_sums))


def write_packed(packed_ref, one, slot_grads, local_grads, two, wn1_grad, wn2_grad, columns):
    packed_ref[0] = jnp.concatenate([one, slot_grads], axis=1)
    packed_ref[1] = jnp.concatenate([local_grads, two], axis=1)
    packed_ref[2] = wn1_grad
    packed_ref[3] = jnp.concatenate([wn2_grad, columns], axis=1)


def up_backward_kernel(index_ref, feat_ref, h0, h1, h2, h3, h4, h5,
                       send_ref, cot_ref, local_ref, summed_ref, r0, r1, r2, r3, r4, r5, slope_ref, normed_ref, hidden_ref, factor_ref, alive_ref, packed_down_ref, local_down_ref,
                       w1_ref, w2_ref, wn1_ref, wn2_ref, biases_ref, gains_ref,
                       g0, g1, g2, first_ref, grad_ref, keep_ref,
                       slots, table, back, total, sums, start, one_ref, two_ref, edge_sums, node_sums, wn1_grad, wn2_grad, pieces):
    groups, n = groups_of(local_ref.shape[1])
    columns = columns_of(biases_ref, gains_ref, 0)
    clear((back, total, sums, one_ref, two_ref, edge_sums, node_sums, wn1_grad, wn2_grad))
    slot_table(slots, (r0, r1, r2, r3, r4, r5))
    add_back(back, (h0, h1, h2, h3, h4, h5), send_ref, groups, n)
    wn2 = wn2_ref[0]
    wn2_t = transposed(wn2)
    wn1 = transposed(wn1_ref[0])
    w1 = transposed(w1_ref[0])

    def first_layer(j, unused):
        s = slice(j * n, (j + 1) * n)
        inputs = jnp.concatenate([local_ref[:, s], summed_ref[:, s]], axis=0)
        return inputs, *node_first(0, inputs, wn1_ref, columns)

    def second_layer(j, held):
        inputs, hidden, slope = held
        grad = cot_ref[:, j * n : (j + 1) * n] + back[j * D : (j + 1) * D, :]
        normed, factor = node_second(hidden, wn2_t, columns)
        return inputs, hidden, slope, grad, node_second_grad(grad, normed, factor, columns, node_sums)

    def node_grads(j, held):
        inputs, hidden, slope, grad, second = held
        first = (dot(wn2, second) * slope).astype(B16)
        node_weight_grads(first, second, inputs, hidden, wn1_grad, wn2_grad, node_sums)
        table[j * D : (j + 1) * D, :] = first
        start[:, j * n : (j + 1) * n] = grad + dot(wn1[0:D], first)

    pipelined((first_layer, second_layer, node_grads), range(groups))
    weight_two = w2_ref[0]

    def grad_rows(span, unused):
        a, size = span[2].start, span[2].size
        return pick(table, row_of(index_ref, 0, a, size), row_of(index_ref, 1, a, size), groups, n)

    def second_grad(span, rows):
        return edge_second(rows, span[2], columns, wn1[D : 2 * D], alive_ref, normed_ref, factor_ref, edge_sums)

    def first_grad(span, second):
        s = span[2]
        first = edge_first(second, s, weight_two, slope_ref)
        first_ref[:, s] = first
        edge_weight_grads(first, second, feat_ref[:, s], hidden_ref[:, s], one_ref, two_ref, edge_sums)
        return first

    def sum_rows(span, first):
        s = span[2]
        rows = [row_of(index_ref, i, s.start, s.size) for i in range(4)]
        add_at(total, first, rows[0], rows[1], groups, n)
        add_at(sums, first, rows[2], rows[3], SLOT_GROUPS, SLOT_COLS)

    pipelined((grad_rows, second_grad, first_grad, sum_rows), spans_of((first_ref,), CHUNK))
    slot_gradients((g0, g1, g2), sums, w1[D : 2 * D])
    local_grads = target_grads(total, local_ref, w1[2 * D : 3 * D], lambda j: start[:, j * n : (j + 1) * n], grad_ref, groups, n)
    slot_grads = slot_weight_grads(sums, slots)
    write_packed(pieces, one_ref[...], slot_grads, local_grads, two_ref[...], wn1_grad[...], wn2_grad[...],
                 pack_columns(edge_sums, node_sums))
    unused, core = level_and_core()
    for p in range(4):
        pieces[4 + p] = packed_down_ref[p]
    pieces[5, :, 0:D] = local_down_ref[...]
    for p in range(4):
        keep_ref[p] = pieces[core * 4 + p]
        g0[4 + p] = pieces[(1 - core) * 4 + p].astype(B16)


def feat_grad_kernel(first_ref, w1_ref, *rest):
    out_ref = rest[-1]
    out_ref[...] = dot(transposed(w1_ref[0, :, 0:D]), first_ref[...])


def lower_grad_kernel(h0, h1, h2, h3, h4, h5, send_ref, start_ref, out_ref, total):
    groups, n = groups_of(start_ref.shape[1])
    clear((total,))
    add_back(total, (h0, h1, h2, h3, h4, h5), send_ref, groups, n)
    for j in range(groups):
        s = slice(j * n, (j + 1) * n)
        out_ref[:, s] = start_ref[:, s] + total[j * D : (j + 1) * D, :]


def unpack_kernel(own_ref, other_ref, w1_ref, w2_ref, wn1_ref, wn2_ref, biases_ref, gains_ref, pieces):
    unused, core = level_and_core()
    for p in range(4):
        pieces[core * 4 + p] = own_ref[p].astype(F32)
        pieces[(1 - core) * 4 + p] = other_ref[p].astype(F32)
    for k in range(2):
        w1_ref[k] = jnp.concatenate([pieces[4 * k], pieces[4 * k + 1, :, 0:D]], axis=1)
        w2_ref[k] = pieces[4 * k + 1, :, D : 2 * D]
        wn1_ref[k] = pieces[4 * k + 2]
        wn2_ref[k] = pieces[4 * k + 3, :, 0:D]
        rows = pieces[4 * k + 3].T
        for i in range(6):
            biases_ref[i, k : k + 1] = rows[D + i : D + i + 1]
        gains_ref[k] = rows[D + 6 : D + 8]


def shape(dims, dtype=F32):
    return jax.ShapeDtypeStruct(dims, dtype)


def call(kernel, name, outs, scratch, scalars=0, stored=(), streamed=None, final=(), raw=()):
    steps, stream_in, stream_out = streamed if streamed else (1, (), ())

    def run(*operands, after=()):
        def whole(space):
            return pl.BlockSpec(memory_space=space)

        def cut(x):
            return pl.BlockSpec((x.shape[0], x.shape[1] // steps), lambda i: (0, i))

        in_specs, placed = [], []
        for i, x in enumerate(operands):
            if i < scalars:
                in_specs.append(whole(pltpu.SMEM))
            elif i in stream_in:
                in_specs.append(cut(x))
            elif i in raw:
                in_specs.append(whole(pltpu.HBM))
                x = pltpu.with_memory_space_constraint(x, pltpu.HBM)
            else:
                in_specs.append(whole(pltpu.VMEM))
                x = pltpu.with_memory_space_constraint(x, pltpu.VMEM)
            placed.append(x)
        in_specs += [whole(pl.ANY) for _ in after]
        out_specs, out_shape = [], []
        for i, x in enumerate(outs):
            if i in stream_out:
                out_specs.append(cut(x))
                out_shape.append(x)
            elif i in stored:
                out_specs.append(whole(pl.ANY))
                out_shape.append(x)
            elif i in final:
                out_specs.append(whole(pltpu.VMEM))
                out_shape.append(x)
            else:
                out_specs.append(whole(pltpu.VMEM))
                out_shape.append(pltpu.VMEM(x.shape, x.dtype))
        return pl.pallas_call(
            kernel,
            name=name,
            grid=(steps,) if streamed else (),
            in_specs=in_specs,
            out_specs=out_specs,
            out_shape=out_shape,
            scratch_shapes=scratch,
            compiler_params=pltpu.CompilerParams(vmem_limit_bytes=VMEM_BYTES),
        )(*placed, *after)

    return run


def core_swap(block):
    return lax.ppermute(block, "band", [(i, i ^ 1) for i in range(lax.axis_size("band"))])


def cross_swap(block):
    last = lax.axis_size("band") - 1
    pairs = [(i, i + 1) for i in range(1, last, 2)]
    return lax.ppermute(block, "band", pairs + [(b, a) for a, b in pairs] + [(0, 0), (last, last)])


def along_level(block, step):
    count = lax.axis_size("level")
    return lax.ppermute(block, "level", [(i, (i + step) % count) for i in range(count)])


def across_bands(blocks):
    partner, cross, own = blocks
    return [core_swap(partner), cross_swap(cross), own]


def along_levels(blocks, sign):
    return blocks + [along_level(jnp.stack([b[d] for b in blocks]), sign * d) for d in (1, 2, 3)]


def chip_axis(block, stride, step):
    count = lax.axis_size("band")
    pairs = []
    for i in range(count):
        at = (i // stride) % 4
        pairs.append((i, i + (((at + step) % 4) - at) * stride))
    return lax.ppermute(block, "band", pairs)


def rounded(values):
    return lax.reduce_precision(values, 8, 7)


def sum_of_four(values, first, second, third):
    return (values + second.astype(F32)) + (first.astype(F32) + third.astype(F32))


def sum_along(values, stride):
    own = rounded(values)
    sent = own.astype(B16)
    return sum_of_four(own, *(chip_axis(sent, stride, d) for d in (1, 2, 3)))


def shards(
    lower_nodes, latent, up_feat, down_feat, up_send, up_counts, up_senders, up_targets,
    down_send, down_counts, down_senders, down_targets,
    edge_w1, edge_w2, node_w1, node_w2, biases, norm_gains, lower_cot, upper_cot,
):
    lower, upper = lower_nodes.T, latent.T
    feat_up, feat_down = up_feat.T, down_feat.T
    cot_lower, cot_upper = lower_cot.T, upper_cot.T
    w1, wn1 = edge_w1.transpose(0, 2, 1), node_w1.transpose(0, 2, 1)
    w2, wn2 = edge_w2, node_w2
    edges, lower_rows, upper_rows = up_feat.shape[0], lower_nodes.shape[0], latent.shape[0]
    dense = (edges // 128, 128)
    senders_up, targets_up, senders_down, targets_down = (
        x.reshape(dense) for x in (up_senders, up_targets, down_senders, down_targets))
    bias_rows = biases.transpose(1, 0, 2)

    lower_groups, lower_n = groups_of(lower_rows)
    upper_groups, upper_n = groups_of(upper_rows)
    lower_table, upper_table = (lower_groups * D, lower_n), (upper_groups * D, upper_n)
    slots = pltpu.VMEM((SLOT_GROUPS * D, SLOT_COLS), B16)
    block, four = shape((4, D, 128), B16), shape((4, D, 128))
    wide32, wide16, row = shape((D, edges)), shape((D, edges), B16), shape((1, edges))
    steps = edges // EDGE_BLOCK

    early = (up_send, lower, senders_up, targets_up, senders_down, targets_down, upper, w1, bias_rows, norm_gains,
             down_send, w2, wn1, wn2)
    count = len(early)
    (*sent, up_send, lower, senders_up, targets_up, senders_down, targets_down, upper, w1, bias_rows,
     norm_gains, down_send, w2, wn1, wn2) = call(
        functools.partial(send_kernel, count), "send_lower", [block] * 3 + [shape(x.shape, x.dtype) for x in early],
        [pltpu.VMEM(lower_table, B16), pltpu.SemaphoreType.DMA((count,))], 0, raw=range(count),
    )(*early)
    index, lives = shape((4, *dense), jnp.int32), shape((1, *dense))
    index_up, alive_up, index_down, alive_down = call(
        functools.partial(tables_kernel, upper_rows, lower_rows), "edge_tables", [index, lives, index, lives],
        [pltpu.SMEM((1, 12), jnp.int32), pltpu.SMEM((1, 12), jnp.int32), pltpu.SemaphoreType.DMA((2,))], 0, raw=(0, 1),
    )(up_counts, down_counts, senders_up, targets_up, senders_down, targets_down)

    def part(k, block, name, table, index, feat, local, after):
        return call(
            functools.partial(part_kernel, k, block), name, [wide32, wide16],
            [pltpu.VMEM(table, B16), pltpu.VMEM((D, edges), B16), pltpu.SemaphoreType.DMA], 0, raw=(1,),
        )(index, feat, local, w1, bias_rows, norm_gains, after=after)

    sent = across_bands(sent)
    sent, alive_up = lax.optimization_barrier((sent, alive_up))
    part_up, feat_up = part(0, EDGE_BLOCK, "part_up", upper_table, index_up, feat_up, upper, (sent[0], sent[1]))
    up_slots = along_levels(sent, 1)
    up_slots, part_up = lax.optimization_barrier((up_slots, part_up))
    (upper_new, summed_up, s0, s1, s2, slope, normed, hidden, factor) = call(
        up_forward_kernel, "up_forward",
        [shape((D, upper_rows)), shape((D, upper_rows), B16)] + [block] * 3 + [wide32, wide32, wide16, row],
        [slots, pltpu.VMEM(upper_table, F32), pltpu.VMEM(upper_table, B16), pltpu.VMEM((D, upper_rows), F32),
         pltpu.SemaphoreType.DMA], 0, (0,),
    )(part_up, alive_up, index_up, *up_slots, upper, down_send, w1, w2, wn1, wn2, bias_rows, norm_gains)
    sent = across_bands([s0, s1, s2])
    part_down, feat_down = part(1, EDGE_BLOCK, "part_down", lower_table, index_down, feat_down, lower, (sent[0], sent[1]))
    down_slots = along_levels(sent, 1)
    down_slots, part_down = lax.optimization_barrier((down_slots, part_down))
    sums_shape = shape((SLOT_GROUPS * D, SLOT_COLS))
    node16 = shape((D, lower_rows), B16)
    (lower_new, g0, g1, g2, first_down, second_down, hidden_down, sums_down, edge_sums, node_sums, *nodes) = call(
        down_kernel, "down_sweep",
        [shape((D, lower_rows))] + [block] * 3 + [wide16] * 3 + [sums_shape, four, four, shape(lower_table, B16),
         shape(lower_table, B16), node16, node16],
        [slots, pltpu.VMEM(lower_table, F32), pltpu.VMEM((D, edges), F32),
         pltpu.VMEM((D, edges), F32), pltpu.VMEM((1, edges), F32),
         pltpu.VMEM((D, lower_rows), F32), pltpu.SemaphoreType.DMA], 0, (0,),
    )(part_down, alive_down, index_down, *down_slots, lower, cot_lower, w1, w2, wn1, wn2, bias_rows, norm_gains)
    back = across_bands([g0, g1, g2])
    feat_grad_down, packed_down = call(
        down_rest_kernel, "down_rest", [wide32, four],
        [slots, pltpu.VMEM((D, D), F32), pltpu.VMEM((D, D), F32), pltpu.VMEM((D, 2 * D), F32), pltpu.VMEM((D, D), F32),
         pltpu.VMEM((4, D, 128), F32), pltpu.VMEM((4, D, 128), F32)], 0, (), (steps, (), (0,)),
    )(feat_down, first_down, second_down, hidden_down, *down_slots, sums_down, edge_sums, node_sums, *nodes, lower, w1)
    back, packed_down = lax.optimization_barrier((back, packed_down))
    start_lower, local_down = call(
        down_targets_kernel, "down_targets", [shape((D, lower_rows)), shape((D, D))], [pltpu.VMEM(lower_table, F32)],
    )(index_down, first_down, lower, cot_lower, nodes[0], w1, wn1, after=(back[0], back[1]))
    down_back = along_levels(back, -1)
    down_back, local_down = lax.optimization_barrier((down_back, local_down))
    (partner, cross, own, first_up, grad_latent, keep) = call(
        up_backward_kernel, "up_backward",
        [shape((8, D, 128), B16), block, block, wide16, shape((D, upper_rows)), four],
        [slots, pltpu.VMEM(upper_table, B16), pltpu.VMEM(upper_table, F32), pltpu.VMEM(upper_table, F32),
         pltpu.VMEM((SLOT_GROUPS * D, SLOT_COLS), F32), pltpu.VMEM((D, upper_rows), F32),
         pltpu.VMEM((D, D), F32), pltpu.VMEM((D, D), F32), pltpu.VMEM((4, D, 128), F32), pltpu.VMEM((4, D, 128), F32),
         pltpu.VMEM((D, 2 * D), F32), pltpu.VMEM((D, D), F32), pltpu.VMEM((8, D, 128), F32)], 0, (), None, (4,),
    )(index_up, feat_up, *down_back, down_send, cot_upper, upper, summed_up, *up_slots,
      slope, normed, hidden, factor, alive_up, packed_down, local_down, w1, w2, wn1, wn2, bias_rows, norm_gains)

    partner, cross = core_swap(partner), cross_swap(cross)
    (feat_grad_up,) = call(feat_grad_kernel, "feat_grad_up", [wide32], [], 0, (), (steps, (0,), (0,)))(
        first_up, w1, after=(partner, cross))
    total = rounded(rounded(keep) + partner[4:].astype(F32))
    blocks = (partner, cross, own)
    levels = [
        along_level(jnp.concatenate([jnp.stack([b[d] for b in blocks]), total.astype(B16)]), -d) for d in (1, 2, 3)
    ]
    levels, feat_grad_up = lax.optimization_barrier((levels, feat_grad_up))
    total = sum_of_four(total, *(b[3:] for b in levels))
    (grad_lower,) = call(lower_grad_kernel, "lower_grad", [shape((D, lower_rows))], [pltpu.VMEM(lower_table, F32)], 0, (), None, (0,))(
        *blocks, *levels, up_send, start_lower)
    total = sum_along(total, 2)
    total, grad_lower = lax.optimization_barrier((total, grad_lower))
    total = rounded(sum_along(total, 8)).astype(B16)
    w1_grad, w2_grad, wn1_grad, wn2_grad, bias_grad, gain_grad = call(
        unpack_kernel, "unpack",
        [shape((2, D, 3 * D)), shape((2, D, D)), shape((2, D, 2 * D)), shape((2, D, D)), shape((6, 2, D)), shape((2, 2, D))],
        [pltpu.VMEM((8, D, 128), F32)], 0, (), None, range(6))(total, core_swap(total))
    return (
        lower_new.T, upper_new.T, grad_lower.T, grad_latent.T, feat_grad_up.T, feat_grad_down.T,
        w1_grad.transpose(0, 2, 1), w2_grad, wn1_grad.transpose(0, 2, 1), wn2_grad, bias_grad.transpose(1, 0, 2), gain_grad,
    )


def solution(mesh):
    rows, index, whole = P(("band", "level"), None), P(("band", "level")), P()
    placed = (rows,) * 6 + (index, index) + (rows,) * 2 + (index, index) + (whole,) * 6 + (rows,) * 2
    return jax.shard_map(
        shards,
        mesh=mesh,
        in_specs=placed,
        out_specs=(rows,) * 6 + (whole,) * 6,
        check_vma=False,
    )
```

```python
import functools

import jax
import jax.numpy as jnp
from jax import lax
from jax.experimental import pallas as pl
from jax.experimental.pallas import tpu as pltpu
from jax.sharding import PartitionSpec as P

EPSILON = 1e-05
F32 = jnp.float32
B16 = jnp.bfloat16
D = 64
SLOT_GROUPS, SLOT_COLS = 6, 256
EDGE_BLOCK = 3072
CHUNK = 1024
VMEM_BYTES = 24 * 1024 * 1024


def groups_of(rows):
    return (4, rows // 4) if rows > 1024 else (rows // 256, 256)


def dot(a, b):
    return jnp.dot(a, b, preferred_element_type=F32)


def dot_rows(a, b):
    return lax.dot_general(a, b, (((1,), (1,)), ((), ())), preferred_element_type=F32)


def halves(x):
    high = x.astype(B16)
    return high, (x - high.astype(F32)).astype(B16)


def one_hot(column, n):
    rows = lax.broadcasted_iota(jnp.int16, (n, column.shape[1]), 0)
    return jnp.where(rows == column.astype(jnp.int16), jnp.ones((), B16), jnp.zeros((), B16))


def place(index, groups, n):
    group = jnp.zeros_like(index)
    for j in range(1, groups):
        group = group + (index >= j * n).astype(jnp.int32)
    return group, index - group * n


def level_and_core():
    return lax.axis_index("level").astype(jnp.int32), lax.axis_index("band").astype(jnp.int32) & 1


def slot_place(senders):
    level, unused = level_and_core()
    distance = (level - ((senders >> 7) & 3)) & 3
    offset = senders >> 9
    source = jnp.where(offset == 0, 0, 3 - offset)
    block = distance * 3 + source
    return block >> 1, ((block & 1) << 7) | (senders & 127)


def live(senders, counts_ref):
    peer = senders >> 7
    limit = jnp.zeros_like(senders)
    for j in range(12):
        limit = jnp.where(peer == j, counts_ref[0, j], limit)
    return ((senders & 127) < limit).astype(F32)


def choose(stacked, group, groups):
    picked = stacked[0:D]
    for j in range(1, groups):
        picked = jnp.where(group == j, stacked[j * D : (j + 1) * D], picked)
    return picked


def row_of(ref, k, start, size):
    rows = size // 128
    if not isinstance(start, int):
        start = pl.multiple_of(start // 128, rows)
        return jnp.concatenate([ref[k, pl.ds(start + r, 1), :] for r in range(rows)], axis=1)
    return jnp.concatenate([ref[k, r : r + 1, :] for r in range(start // 128, start // 128 + rows)], axis=1)


def pick(table, group, column, groups, n):
    return choose(dot(table[...], one_hot(column, n)), group, groups).astype(B16)


def spread(values, group, groups):
    wide = jnp.broadcast_to(group.astype(jnp.int16), values.shape)
    nothing = jnp.zeros_like(values)
    return jnp.concatenate([jnp.where(wide == j, values, nothing) for j in range(groups)], axis=0)


def add_at(total, values, group, column, groups, n):
    total[...] += dot_rows(spread(values, group, groups), one_hot(column, n))


def pack_table(table, source, groups, n):
    for j in range(groups):
        table[j * D : (j + 1) * D, :] = source[:, j * n : (j + 1) * n]


def columns_of(biases_ref, gains_ref, k):
    rows = [biases_ref[i, k : k + 1] for i in range(6)] + [gains_ref[k]]
    return jnp.concatenate(rows, axis=0).T


def fold(values):
    total = values[:, 0:128]
    for i in range(128, values.shape[1], 128):
        total = total + values[:, i : i + 128]
    return total


def norm_parts(values):
    centre = values - jnp.sum(values, axis=0, keepdims=True) * (1.0 / D)
    spread_sum = jnp.sum(centre * centre, axis=0, keepdims=True) * (1.0 / D)
    factor = lax.rsqrt(spread_sum + EPSILON)
    return centre * factor, factor


def norm_back(grad, normed, factor, gain):
    scaled = grad * gain
    first = jnp.sum(scaled, axis=0, keepdims=True) * (1.0 / D)
    second = jnp.sum(scaled * normed, axis=0, keepdims=True) * (1.0 / D)
    return factor * (scaled - first - normed * second)


def sigmoid(values):
    return 0.5 * jnp.tanh(0.5 * values) + 0.5


def send_rows(send_ref, offset):
    level, unused = level_and_core()
    return jnp.concatenate(
        [send_ref[pl.ds(offset * 4 + ((level + d) & 3), 1), :] for d in range(4)], axis=1
    )


def send_blocks(outs, table, send_ref, groups, n):
    for j, offset in enumerate((0, 2, 1)):
        group, column = place(send_rows(send_ref, offset), groups, n)
        rows = pick(table, group, column, groups, n)
        for d in range(4):
            outs[j][d] = rows[:, d * 128 : (d + 1) * 128]


def add_back(total, blocks, offsets, send_ref, groups, n):
    for j, offset in enumerate(offsets):
        group, column = place(send_rows(send_ref, offset), groups, n)
        values = jnp.concatenate([block_at(blocks, d, j) for d in range(4)], axis=1)
        add_at(total, values, group, column, groups, n)


def block_at(received, d, j):
    return received[j][0] if d == 0 else received[2 + d][j]


def slot_table(table, received):
    for t in range(12):
        table[(t >> 1) * D : ((t >> 1) + 1) * D, (t & 1) * 128 : ((t & 1) + 1) * 128] = block_at(received, t // 3, t % 3)


def slot_gradients(outs, sums, weight):
    for j in range(SLOT_GROUPS):
        high, low = halves(sums[j * D : (j + 1) * D, :])
        grads = (dot(weight, high) + dot(weight, low)).astype(B16)
        for t in (2 * j, 2 * j + 1):
            outs[t % 3][t // 3] = grads[:, (t & 1) * 128 : ((t & 1) + 1) * 128]


def over_blocks(total, block, body):
    block = min(block, total)
    if block == total:
        body(pl.ds(0, block))
        return

    def step(i, carry):
        body(pl.ds(pl.multiple_of(i * block, block), block))
        return carry

    lax.fori_loop(0, total // block, step, 0)


def pipelined(stages, spans):
    held = [None] * len(spans)
    for t in range(len(spans) + len(stages) - 1):
        for k in reversed(range(len(stages))):
            i = t - k
            if 0 <= i < len(spans):
                held[i] = stages[k](spans[i], held[i])


def spans_of(parts, chunk):
    spans, start = [], 0
    for which, ref in enumerate(parts):
        size = min(chunk, ref.shape[1])
        for at in range(0, ref.shape[1], size):
            spans.append((which, pl.ds(at, size), pl.ds(start + at, size)))
        start += ref.shape[1]
    return spans


def tables_kernel(upper_rows, lower_rows, counts_up, counts_down, senders_up, targets_up, senders_down, targets_down,
                  index_up, alive_up, index_down, alive_down, limits_up, limits_down, sems):
    copies = [pltpu.make_async_copy(counts_up, limits_up, sems.at[0]), pltpu.make_async_copy(counts_down, limits_down, sems.at[1])]
    for copy in copies:
        copy.start()
    sweeps = ((index_up, senders_up, targets_up, upper_rows), (index_down, senders_down, targets_down, lower_rows))
    for index_ref, senders_ref, targets_ref, rows in sweeps:
        index_ref[0], index_ref[1] = place(targets_ref[...], *groups_of(rows))
        index_ref[2], index_ref[3] = slot_place(senders_ref[...])
    for copy in copies:
        copy.wait()
    alive_up[0] = live(senders_up[...], limits_up)
    alive_down[0] = live(senders_down[...], limits_down)


def send_kernel(count, *refs):
    sources, refs = refs[:count], refs[count:]
    sent, held, table, sems = refs[:3], refs[3:-2], refs[-2], refs[-1]
    copies = [pltpu.make_async_copy(a, b, sems.at[i]) for i, (a, b) in enumerate(zip(sources, held))]
    for copy in copies:
        copy.start()
    for copy in copies[:2]:
        copy.wait()
    send_ref, source_ref = held[:2]
    groups, n = groups_of(source_ref.shape[1])
    pack_table(table, source_ref, groups, n)
    send_blocks(sent, table, send_ref, groups, n)
    for copy in copies[2:]:
        copy.wait()


def part_kernel(k, block, index_ref, feat_ref, local_ref, w1_ref, biases_ref, gains_ref, *rest):
    part_ref, held_ref, table, picked, sem = rest[-5:]
    copy = pltpu.make_async_copy(feat_ref, held_ref, sem)
    copy.start()
    groups, n = groups_of(local_ref.shape[1])
    pack_table(table, local_ref, groups, n)
    columns = columns_of(biases_ref, gains_ref, k)
    weight = jnp.concatenate([w1_ref[k, :, 0:D], w1_ref[k, :, 2 * D : 3 * D]], axis=1)

    def body(s):
        picked[:, s] = pick(table, row_of(index_ref, 0, s.start, s.size), row_of(index_ref, 1, s.start, s.size), groups, n)

    over_blocks(feat_ref.shape[1], block, body)
    copy.wait()
    part_ref[...] = dot(weight, jnp.concatenate([held_ref[...], picked[...]], axis=0)) + columns[:, 0:1]


def edges_forward(k, parts, alive_ref, index_ref, table, w1_ref, w2_ref, columns, total, groups, n,
                  slope_ref, normed_ref, hidden_ref, factor_ref):
    weight_slot = w1_ref[k, :, D : 2 * D]
    weight_two = w2_ref[k].astype(F32).T.astype(B16)
    total[...] = jnp.zeros_like(total)

    def slot_rows(span, unused):
        a, size = span[2].start, span[2].size
        return pick(table, row_of(index_ref, 2, a, size), row_of(index_ref, 3, a, size), SLOT_GROUPS, SLOT_COLS)

    def first_layer(span, picked):
        which, t, s = span
        first = parts[which][:, t] + dot(weight_slot, picked)
        gate = sigmoid(first)
        hidden = (first * gate).astype(B16)
        slope_ref[:, s] = gate * (1.0 + first * (1.0 - gate))
        hidden_ref[:, s] = hidden
        return hidden

    def second_layer(span, hidden):
        s = span[2]
        normed, factor = norm_parts(dot(weight_two, hidden) + columns[:, 1:2])
        alive = row_of(alive_ref, 0, s.start, s.size)
        normed_ref[:, s] = normed
        factor_ref[:, s] = factor
        return ((normed * columns[:, 6:7] + columns[:, 2:3]) * alive).astype(B16)

    def sum_messages(span, messages):
        a, size = span[2].start, span[2].size
        add_at(total, messages, row_of(index_ref, 0, a, size), row_of(index_ref, 1, a, size), groups, n)

    pipelined((slot_rows, first_layer, second_layer, sum_messages), spans_of(parts, CHUNK))


def node_first(k, inputs, wn1_ref, columns):
    first = dot(wn1_ref[k], inputs) + columns[:, 3:4]
    gate = sigmoid(first)
    return (first * gate).astype(B16), gate * (1.0 + first * (1.0 - gate))


def node_second(hidden, weight_two, columns):
    return norm_parts(dot(weight_two, hidden) + columns[:, 4:5])


def node_second_grad(grad, normed, factor, columns, sums_ref):
    sums_ref[2] += fold(grad)
    sums_ref[3] += fold(grad * normed)
    return norm_back(grad, normed, factor, columns[:, 7:8]).astype(B16)


def node_weight_grads(first, second, inputs, hidden, one_ref, two_ref, sums_ref):
    sums_ref[0] += fold(first.astype(F32))
    sums_ref[1] += fold(second.astype(F32))
    one_ref[...] += dot_rows(first, inputs)
    two_ref[...] += dot_rows(hidden, second)


def clear(refs):
    for ref in refs:
        ref[...] = jnp.zeros_like(ref)


def transposed(weight):
    return weight.astype(F32).T.astype(B16)


def edge_second(grad_rows, s, columns, weight_sum, alive_ref, normed_ref, factor_ref, sums_ref):
    grad = dot(weight_sum, grad_rows) * row_of(alive_ref, 0, s.start, s.size)
    normed = normed_ref[:, s]
    sums_ref[2] += fold(grad)
    sums_ref[3] += fold(grad * normed)
    return norm_back(grad, normed, factor_ref[:, s], columns[:, 6:7]).astype(B16)


def edge_first(second, s, weight_two, slope_ref):
    return (dot(weight_two, second) * slope_ref[:, s]).astype(B16)


def edge_weight_grads(first, second, feat, hidden, one_ref, two_ref, sums_ref):
    sums_ref[0] += fold(first.astype(F32))
    sums_ref[1] += fold(second.astype(F32))
    one_ref[...] += dot_rows(first, feat)
    two_ref[...] += dot_rows(hidden, second)


def pack_columns(edge_sums, node_sums):
    order = (edge_sums[0], edge_sums[1], edge_sums[2], node_sums[0], node_sums[1], node_sums[2], edge_sums[3], node_sums[3])
    columns = [jnp.sum(v, axis=1, keepdims=True) for v in order]
    lanes = lax.broadcasted_iota(jnp.int32, (D, D), 1)
    packed = jnp.zeros((D, D), F32)
    for i, column in enumerate(columns):
        packed = jnp.where(lanes == i, column, packed)
    return packed


def slot_weight_grads(sums, table):
    total = jnp.zeros((D, D), F32)
    for j in range(SLOT_GROUPS):
        high, low = halves(sums[j * D : (j + 1) * D, :])
        rows = table[j * D : (j + 1) * D, :]
        total = total + dot_rows(high, rows) + dot_rows(low, rows)
    return total


def target_grads(total, local_ref, weight, start, out_ref, groups, n):
    grads = jnp.zeros((D, D), F32)
    for j in range(groups):
        high, low = halves(total[j * D : (j + 1) * D, :])
        s = slice(j * n, (j + 1) * n)
        rows = local_ref[:, s]
        grads = grads + dot_rows(high, rows) + dot_rows(low, rows)
        out_ref[:, s] = start(j) + dot(weight, high) + dot(weight, low)
    return grads


def up_forward_kernel(part_ref, alive_ref, index_ref, r0, r1, r2, r3, r4, r5, local_ref, send_ref,
                      w1_ref, w2_ref, wn1_ref, wn2_ref, biases_ref, gains_ref,
                      out_ref, summed_ref, s0, s1, s2, slope_ref, normed_ref, hidden_ref, factor_ref,
                      slots, total, table, out, sem):
    groups, n = groups_of(local_ref.shape[1])
    columns = columns_of(biases_ref, gains_ref, 0)
    slot_table(slots, (r0, r1, r2, r3, r4, r5))
    edges_forward(0, (part_ref,), alive_ref, index_ref, slots, w1_ref, w2_ref, columns, total, groups, n,
                  slope_ref, normed_ref, hidden_ref, factor_ref)
    weight_two = transposed(wn2_ref[0])

    def first_layer(j, unused):
        s = slice(j * n, (j + 1) * n)
        summed = total[j * D : (j + 1) * D, :].astype(B16)
        summed_ref[:, s] = summed
        return node_first(0, jnp.concatenate([local_ref[:, s], summed], axis=0), wn1_ref, columns)

    def second_layer(j, held):
        s = slice(j * n, (j + 1) * n)
        normed, unused = node_second(held[0], weight_two, columns)
        result = local_ref[:, s].astype(F32) + normed * columns[:, 7:8] + columns[:, 5:6]
        out[:, s] = result
        table[j * D : (j + 1) * D, :] = result.astype(B16)

    pipelined((first_layer, second_layer), range(groups))
    copy = pltpu.make_async_copy(out, out_ref, sem)
    copy.start()
    send_blocks((s0, s1, s2), table, send_ref, groups, n)
    copy.wait()


def down_kernel(part_ref, alive_ref, index_ref, r0, r1, r2, r3, r4, r5, local_ref, cot_ref,
                w1_ref, w2_ref, wn1_ref, wn2_ref, biases_ref, gains_ref,
                out_ref, g0, g1, g2, first_ref, second_ref, hidden_ref, sums_ref, edge_sums, node_sums,
                table, summed_ref, node_hidden_ref, node_second_ref,
                slots, total, slope_ref, normed_ref, factor_ref, out, sem):
    groups, n = groups_of(local_ref.shape[1])
    columns = columns_of(biases_ref, gains_ref, 1)
    slot_table(slots, (r0, r1, r2, r3, r4, r5))
    parts = (part_ref,)
    edges_forward(1, parts, alive_ref, index_ref, slots, w1_ref, w2_ref, columns, total, groups, n,
                  slope_ref, normed_ref, hidden_ref, factor_ref)
    clear((node_sums, edge_sums, sums_ref))
    wn2 = wn2_ref[1]
    wn2_t = transposed(wn2)
    wn1 = transposed(wn1_ref[1])

    def first_layer(j, unused):
        summed = total[j * D : (j + 1) * D, :].astype(B16)
        summed_ref[j * D : (j + 1) * D, :] = summed
        inputs = jnp.concatenate([local_ref[:, j * n : (j + 1) * n], summed], axis=0)
        return node_first(1, inputs, wn1_ref, columns)

    def second_layer(j, held):
        hidden, slope = held
        s = slice(j * n, (j + 1) * n)
        normed, factor = node_second(hidden, wn2_t, columns)
        out[:, s] = local_ref[:, s].astype(F32) + normed * columns[:, 7:8] + columns[:, 5:6]
        second = node_second_grad(cot_ref[:, s], normed, factor, columns, node_sums)
        node_hidden_ref[:, s] = hidden
        node_second_ref[:, s] = second
        return slope, second

    def node_grads(j, held):
        slope, second = held
        table[j * D : (j + 1) * D, :] = (dot(wn2, second) * slope).astype(B16)

    pipelined((first_layer, second_layer, node_grads), range(groups))
    copy = pltpu.make_async_copy(out, out_ref, sem)
    copy.start()
    weight_two = w2_ref[1]
    weight_slot = transposed(w1_ref[1, :, D : 2 * D])

    def grad_rows(span, unused):
        a, size = span[2].start, span[2].size
        return pick(table, row_of(index_ref, 0, a, size), row_of(index_ref, 1, a, size), groups, n)

    def second_grad(span, rows):
        return edge_second(rows, span[2], columns, wn1[D : 2 * D], alive_ref, normed_ref, factor_ref, edge_sums)

    def first_grad(span, second):
        s = span[2]
        first = edge_first(second, s, weight_two, slope_ref)
        first_ref[:, s] = first
        second_ref[:, s] = second
        return first

    def sum_slots(span, first):
        a, size = span[2].start, span[2].size
        add_at(sums_ref, first, row_of(index_ref, 2, a, size), row_of(index_ref, 3, a, size), SLOT_GROUPS, SLOT_COLS)

    pipelined((grad_rows, second_grad, first_grad, sum_slots), spans_of(parts, CHUNK))
    slot_gradients((g0, g1, g2), sums_ref, weight_slot)
    copy.wait()


def down_targets_kernel(index_ref, first_ref, local_ref, cot_ref, table, w1_ref, wn1_ref, *rest):
    grad_ref, weight_grad_ref, total = rest[-3:]
    groups, n = groups_of(local_ref.shape[1])
    weight = transposed(w1_ref[1, :, 2 * D : 3 * D])
    total[...] = jnp.zeros_like(total)

    def body(s):
        group, column = row_of(index_ref, 0, s.start, s.size), row_of(index_ref, 1, s.start, s.size)
        add_at(total, first_ref[:, s], group, column, groups, n)

    over_blocks(first_ref.shape[1], EDGE_BLOCK, body)
    weight_node = transposed(wn1_ref[1, :, 0:D])

    def start(j):
        return cot_ref[:, j * n : (j + 1) * n] + dot(weight_node, table[j * D : (j + 1) * D, :])

    weight_grad_ref[...] = target_grads(total, local_ref, weight, start, grad_ref, groups, n)


def down_rest_kernel(feat_ref, first_ref, second_ref, hidden_ref, r0, r1, r2, r3, r4, r5, sums_ref, edge_in, node_in,
                     table, summed_ref, node_hidden_ref, node_second_ref, local_ref, w1_ref,
                     feat_grad_ref, packed_ref, slots, one_ref, two_ref, wn1_grad, wn2_grad, edge_sums, node_sums):
    step = pl.program_id(0)
    weight = transposed(w1_ref[1, :, 0:D])

    @pl.when(step == 0)
    def _():
        clear((one_ref, two_ref, wn1_grad, wn2_grad))
        edge_sums[...] = edge_in[...]
        node_sums[...] = node_in[...]

    s = pl.ds(pl.multiple_of(step * EDGE_BLOCK, EDGE_BLOCK), EDGE_BLOCK)
    first = first_ref[:, s]
    feat_grad_ref[...] = dot(weight, first)
    edge_weight_grads(first, second_ref[:, s], feat_ref[:, s], hidden_ref[:, s], one_ref, two_ref, edge_sums)

    @pl.when(step == pl.num_programs(0) - 1)
    def _():
        groups, n = groups_of(local_ref.shape[1])
        for j in range(groups):
            t, rows = slice(j * n, (j + 1) * n), slice(j * D, (j + 1) * D)
            inputs = jnp.concatenate([local_ref[:, t], summed_ref[rows, :]], axis=0)
            node_weight_grads(table[rows, :], node_second_ref[:, t], inputs, node_hidden_ref[:, t], wn1_grad, wn2_grad, node_sums)
        slot_table(slots, (r0, r1, r2, r3, r4, r5))
        write_packed(packed_ref, one_ref[...], slot_weight_grads(sums_ref, slots), jnp.zeros((D, D), F32), two_ref[...],
                     wn1_grad[...], wn2_grad[...], pack_columns(edge_sums, node_sums))


def write_packed(packed_ref, one, slot_grads, local_grads, two, wn1_grad, wn2_grad, columns):
    packed_ref[0] = jnp.concatenate([one, slot_grads], axis=1)
    packed_ref[1] = jnp.concatenate([local_grads, two], axis=1)
    packed_ref[2] = wn1_grad
    packed_ref[3] = jnp.concatenate([wn2_grad, columns], axis=1)


def up_backward_kernel(index_ref, feat_ref, h0, h1, h2, h3, h4, h5,
                       send_ref, cot_ref, local_ref, summed_ref, r0, r1, r2, r3, r4, r5, slope_ref, normed_ref, hidden_ref, factor_ref, alive_ref, packed_down_ref, local_down_ref,
                       w1_ref, w2_ref, wn1_ref, wn2_ref, biases_ref, gains_ref,
                       partner_ref, cross_ref, own_ref, first_ref, grad_ref, keep_ref,
                       slots, table, back, total, sums, start, one_ref, two_ref, edge_sums, node_sums, wn1_grad, wn2_grad, pieces, below, above):
    groups, n = groups_of(local_ref.shape[1])
    columns = columns_of(biases_ref, gains_ref, 0)
    clear((back, total, sums, one_ref, two_ref, edge_sums, node_sums, wn1_grad, wn2_grad))
    slot_table(slots, (r0, r1, r2, r3, r4, r5))
    add_back(back, (h0, h1, h2, h3, h4, h5), (0, 2, 1), send_ref, groups, n)
    wn2 = wn2_ref[0]
    wn2_t = transposed(wn2)
    wn1 = transposed(wn1_ref[0])
    w1 = transposed(w1_ref[0])

    def first_layer(j, unused):
        s = slice(j * n, (j + 1) * n)
        inputs = jnp.concatenate([local_ref[:, s], summed_ref[:, s]], axis=0)
        return inputs, *node_first(0, inputs, wn1_ref, columns)

    def second_layer(j, held):
        inputs, hidden, slope = held
        grad = cot_ref[:, j * n : (j + 1) * n] + back[j * D : (j + 1) * D, :]
        normed, factor = node_second(hidden, wn2_t, columns)
        return inputs, hidden, slope, grad, node_second_grad(grad, normed, factor, columns, node_sums)

    def node_grads(j, held):
        inputs, hidden, slope, grad, second = held
        first = (dot(wn2, second) * slope).astype(B16)
        node_weight_grads(first, second, inputs, hidden, wn1_grad, wn2_grad, node_sums)
        table[j * D : (j + 1) * D, :] = first
        start[:, j * n : (j + 1) * n] = grad + dot(wn1[0:D], first)

    pipelined((first_layer, second_layer, node_grads), range(groups))
    weight_two = w2_ref[0]

    def grad_rows(span, unused):
        a, size = span[2].start, span[2].size
        return pick(table, row_of(index_ref, 0, a, size), row_of(index_ref, 1, a, size), groups, n)

    def second_grad(span, rows):
        return edge_second(rows, span[2], columns, wn1[D : 2 * D], alive_ref, normed_ref, factor_ref, edge_sums)

    def first_grad(span, second):
        s = span[2]
        first = edge_first(second, s, weight_two, slope_ref)
        first_ref[:, s] = first
        edge_weight_grads(first, second, feat_ref[:, s], hidden_ref[:, s], one_ref, two_ref, edge_sums)
        return first

    def sum_rows(span, first):
        s = span[2]
        rows = [row_of(index_ref, i, s.start, s.size) for i in range(4)]
        add_at(total, first, rows[0], rows[1], groups, n)
        add_at(sums, first, rows[2], rows[3], SLOT_GROUPS, SLOT_COLS)

    pipelined((grad_rows, second_grad, first_grad, sum_rows), spans_of((first_ref,), CHUNK))
    slot_gradients((below, above, own_ref), sums, w1[D : 2 * D])
    unused, core = level_and_core()
    for d in range(4):
        partner_ref[d] = jnp.where(core == 0, above[d], below[d])
        cross_ref[d] = jnp.where(core == 0, below[d], above[d])
    local_grads = target_grads(total, local_ref, w1[2 * D : 3 * D], lambda j: start[:, j * n : (j + 1) * n], grad_ref, groups, n)
    slot_grads = slot_weight_grads(sums, slots)
    write_packed(pieces, one_ref[...], slot_grads, local_grads, two_ref[...], wn1_grad[...], wn2_grad[...],
                 pack_columns(edge_sums, node_sums))
    for p in range(4):
        pieces[4 + p] = packed_down_ref[p]
    pieces[5, :, 0:D] = local_down_ref[...]
    for p in range(4):
        keep_ref[p] = pieces[core * 4 + p]
        partner_ref[4 + p] = pieces[(1 - core) * 4 + p].astype(B16)


def feat_grad_kernel(first_ref, w1_ref, *rest):
    out_ref = rest[-1]
    out_ref[...] = dot(transposed(w1_ref[0, :, 0:D]), first_ref[...])


def lower_grad_kernel(h0, h1, h2, h3, h4, h5, send_ref, start_ref, out_ref, total):
    groups, n = groups_of(start_ref.shape[1])
    clear((total,))
    unused, core = level_and_core()
    add_back(total, (h0, h1, h2, h3, h4, h5), (2 - 2 * core, 2 * core, 1), send_ref, groups, n)
    for j in range(groups):
        s = slice(j * n, (j + 1) * n)
        out_ref[:, s] = start_ref[:, s] + total[j * D : (j + 1) * D, :]


def unpack_kernel(own_ref, other_ref, w1_ref, w2_ref, wn1_ref, wn2_ref, biases_ref, gains_ref, pieces):
    unused, core = level_and_core()
    for p in range(4):
        pieces[core * 4 + p] = own_ref[p].astype(F32)
        pieces[(1 - core) * 4 + p] = other_ref[p].astype(F32)
    for k in range(2):
        w1_ref[k] = jnp.concatenate([pieces[4 * k], pieces[4 * k + 1, :, 0:D]], axis=1)
        w2_ref[k] = pieces[4 * k + 1, :, D : 2 * D]
        wn1_ref[k] = pieces[4 * k + 2]
        wn2_ref[k] = pieces[4 * k + 3, :, 0:D]
        rows = pieces[4 * k + 3].T
        for i in range(6):
            biases_ref[i, k : k + 1] = rows[D + i : D + i + 1]
        gains_ref[k] = rows[D + 6 : D + 8]


def shape(dims, dtype=F32):
    return jax.ShapeDtypeStruct(dims, dtype)


def call(kernel, name, outs, scratch, scalars=0, stored=(), streamed=None, final=(), raw=()):
    steps, stream_in, stream_out = streamed if streamed else (1, (), ())

    def run(*operands, after=()):
        def whole(space):
            return pl.BlockSpec(memory_space=space)

        def cut(x):
            return pl.BlockSpec((x.shape[0], x.shape[1] // steps), lambda i: (0, i))

        in_specs, placed = [], []
        for i, x in enumerate(operands):
            if i < scalars:
                in_specs.append(whole(pltpu.SMEM))
            elif i in stream_in:
                in_specs.append(cut(x))
            elif i in raw:
                in_specs.append(whole(pltpu.HBM))
                x = pltpu.with_memory_space_constraint(x, pltpu.HBM)
            else:
                in_specs.append(whole(pltpu.VMEM))
                x = pltpu.with_memory_space_constraint(x, pltpu.VMEM)
            placed.append(x)
        in_specs += [whole(pl.ANY) for _ in after]
        out_specs, out_shape = [], []
        for i, x in enumerate(outs):
            if i in stream_out:
                out_specs.append(cut(x))
                out_shape.append(x)
            elif i in stored:
                out_specs.append(whole(pl.ANY))
                out_shape.append(x)
            elif i in final:
                out_specs.append(whole(pltpu.VMEM))
                out_shape.append(x)
            else:
                out_specs.append(whole(pltpu.VMEM))
                out_shape.append(pltpu.VMEM(x.shape, x.dtype))
        return pl.pallas_call(
            kernel,
            name=name,
            grid=(steps,) if streamed else (),
            in_specs=in_specs,
            out_specs=out_specs,
            out_shape=out_shape,
            scratch_shapes=scratch,
            compiler_params=pltpu.CompilerParams(vmem_limit_bytes=VMEM_BYTES),
        )(*placed, *after)

    return run


def core_swap(block):
    return lax.ppermute(block, "band", [(i, i ^ 1) for i in range(lax.axis_size("band"))])


def cross_swap(block):
    last = lax.axis_size("band") - 1
    pairs = [(i, i + 1) for i in range(1, last, 2)]
    return lax.ppermute(block, "band", pairs + [(b, a) for a, b in pairs] + [(0, 0), (last, last)])


def along_level(block, step):
    count = lax.axis_size("level")
    return lax.ppermute(block, "level", [(i, (i + step) % count) for i in range(count)])


def along_band(block, step):
    count = lax.axis_size("band")
    return lax.ppermute(block, "band", [(i, (i + step) % count) for i in range(count)])


def across_bands(blocks):
    below, above, own = blocks
    return [along_band(above, 1), along_band(below, -1), own]


def along_levels(blocks, sign):
    return blocks + [along_level(jnp.stack([b[d] for b in blocks]), sign * d) for d in (1, 2, 3)]


def chip_ring(block, step, core_strides):
    count = lax.axis_size("band")
    pairs = []
    for i in range(count):
        stride = core_strides[i % 2]
        at = (i // stride) % 4
        pairs.append((i, i + (((at + step) % 4) - at) * stride))
    return lax.ppermute(block, "band", pairs)


def rounded(values):
    return lax.reduce_precision(values, 8, 7)


def sum_of_four(values, first, second, third):
    return (values + second.astype(F32)) + (first.astype(F32) + third.astype(F32))


def sum_along(values, core_strides):
    own = rounded(values)
    sent = own.astype(B16)
    return sum_of_four(own, *(chip_ring(sent, d, core_strides) for d in (1, 2, 3)))


def shards(
    lower_nodes, latent, up_feat, down_feat, up_send, up_counts, up_senders, up_targets,
    down_send, down_counts, down_senders, down_targets,
    edge_w1, edge_w2, node_w1, node_w2, biases, norm_gains, lower_cot, upper_cot,
):
    lower, upper = lower_nodes.T, latent.T
    feat_up, feat_down = up_feat.T, down_feat.T
    cot_lower, cot_upper = lower_cot.T, upper_cot.T
    w1, wn1 = edge_w1.transpose(0, 2, 1), node_w1.transpose(0, 2, 1)
    w2, wn2 = edge_w2, node_w2
    edges, lower_rows, upper_rows = up_feat.shape[0], lower_nodes.shape[0], latent.shape[0]
    dense = (edges // 128, 128)
    senders_up, targets_up, senders_down, targets_down = (
        x.reshape(dense) for x in (up_senders, up_targets, down_senders, down_targets))
    bias_rows = biases.transpose(1, 0, 2)

    lower_groups, lower_n = groups_of(lower_rows)
    upper_groups, upper_n = groups_of(upper_rows)
    lower_table, upper_table = (lower_groups * D, lower_n), (upper_groups * D, upper_n)
    slots = pltpu.VMEM((SLOT_GROUPS * D, SLOT_COLS), B16)
    block, four = shape((4, D, 128), B16), shape((4, D, 128))
    wide32, wide16, row = shape((D, edges)), shape((D, edges), B16), shape((1, edges))
    steps = edges // EDGE_BLOCK

    early = (up_send, lower, senders_up, targets_up, senders_down, targets_down, upper, w1, bias_rows, norm_gains,
             down_send, w2, wn1, wn2)
    count = len(early)
    (*sent, up_send, lower, senders_up, targets_up, senders_down, targets_down, upper, w1, bias_rows,
     norm_gains, down_send, w2, wn1, wn2) = call(
        functools.partial(send_kernel, count), "send_lower", [block] * 3 + [shape(x.shape, x.dtype) for x in early],
        [pltpu.VMEM(lower_table, B16), pltpu.SemaphoreType.DMA((count,))], 0, raw=range(count),
    )(*early)
    index, lives = shape((4, *dense), jnp.int32), shape((1, *dense))
    index_up, alive_up, index_down, alive_down = call(
        functools.partial(tables_kernel, upper_rows, lower_rows), "edge_tables", [index, lives, index, lives],
        [pltpu.SMEM((1, 12), jnp.int32), pltpu.SMEM((1, 12), jnp.int32), pltpu.SemaphoreType.DMA((2,))], 0, raw=(0, 1),
    )(up_counts, down_counts, senders_up, targets_up, senders_down, targets_down)

    def part(k, block, name, table, index, feat, local, after):
        return call(
            functools.partial(part_kernel, k, block), name, [wide32, wide16],
            [pltpu.VMEM(table, B16), pltpu.VMEM((D, edges), B16), pltpu.SemaphoreType.DMA], 0, raw=(1,),
        )(index, feat, local, w1, bias_rows, norm_gains, after=after)

    sent = across_bands(sent)
    sent, alive_up = lax.optimization_barrier((sent, alive_up))
    part_up, feat_up = part(0, EDGE_BLOCK, "part_up", upper_table, index_up, feat_up, upper, (sent[0], sent[1]))
    up_slots = along_levels(sent, 1)
    up_slots, part_up = lax.optimization_barrier((up_slots, part_up))
    (upper_new, summed_up, s0, s1, s2, slope, normed, hidden, factor) = call(
        up_forward_kernel, "up_forward",
        [shape((D, upper_rows)), shape((D, upper_rows), B16)] + [block] * 3 + [wide32, wide32, wide16, row],
        [slots, pltpu.VMEM(upper_table, F32), pltpu.VMEM(upper_table, B16), pltpu.VMEM((D, upper_rows), F32),
         pltpu.SemaphoreType.DMA], 0, (0,),
    )(part_up, alive_up, index_up, *up_slots, upper, down_send, w1, w2, wn1, wn2, bias_rows, norm_gains)
    sent = across_bands([s0, s1, s2])
    part_down, feat_down = part(1, EDGE_BLOCK, "part_down", lower_table, index_down, feat_down, lower, (sent[0], sent[1]))
    down_slots = along_levels(sent, 1)
    down_slots, part_down = lax.optimization_barrier((down_slots, part_down))
    sums_shape = shape((SLOT_GROUPS * D, SLOT_COLS))
    node16 = shape((D, lower_rows), B16)
    (lower_new, g0, g1, g2, first_down, second_down, hidden_down, sums_down, edge_sums, node_sums, *nodes) = call(
        down_kernel, "down_sweep",
        [shape((D, lower_rows))] + [block] * 3 + [wide16] * 3 + [sums_shape, four, four, shape(lower_table, B16),
         shape(lower_table, B16), node16, node16],
        [slots, pltpu.VMEM(lower_table, F32), pltpu.VMEM((D, edges), F32),
         pltpu.VMEM((D, edges), F32), pltpu.VMEM((1, edges), F32),
         pltpu.VMEM((D, lower_rows), F32), pltpu.SemaphoreType.DMA], 0, (0,),
    )(part_down, alive_down, index_down, *down_slots, lower, cot_lower, w1, w2, wn1, wn2, bias_rows, norm_gains)
    back = across_bands([g0, g1, g2])
    feat_grad_down, packed_down = call(
        down_rest_kernel, "down_rest", [wide32, four],
        [slots, pltpu.VMEM((D, D), F32), pltpu.VMEM((D, D), F32), pltpu.VMEM((D, 2 * D), F32), pltpu.VMEM((D, D), F32),
         pltpu.VMEM((4, D, 128), F32), pltpu.VMEM((4, D, 128), F32)], 0, (), (steps, (), (0,)),
    )(feat_down, first_down, second_down, hidden_down, *down_slots, sums_down, edge_sums, node_sums, *nodes, lower, w1)
    back, packed_down = lax.optimization_barrier((back, packed_down))
    start_lower, local_down = call(
        down_targets_kernel, "down_targets", [shape((D, lower_rows)), shape((D, D))], [pltpu.VMEM(lower_table, F32)],
    )(index_down, first_down, lower, cot_lower, nodes[0], w1, wn1, after=(back[0], back[1]))
    down_back = along_levels(back, -1)
    down_back, local_down = lax.optimization_barrier((down_back, local_down))
    (partner, cross, own, first_up, grad_latent, keep) = call(
        up_backward_kernel, "up_backward",
        [shape((8, D, 128), B16), block, block, wide16, shape((D, upper_rows)), four],
        [slots, pltpu.VMEM(upper_table, B16), pltpu.VMEM(upper_table, F32), pltpu.VMEM(upper_table, F32),
         pltpu.VMEM((SLOT_GROUPS * D, SLOT_COLS), F32), pltpu.VMEM((D, upper_rows), F32),
         pltpu.VMEM((D, D), F32), pltpu.VMEM((D, D), F32), pltpu.VMEM((4, D, 128), F32), pltpu.VMEM((4, D, 128), F32),
         pltpu.VMEM((D, 2 * D), F32), pltpu.VMEM((D, D), F32), pltpu.VMEM((8, D, 128), F32), pltpu.VMEM((4, D, 128), B16),
         pltpu.VMEM((4, D, 128), B16)], 0, (), None, (4,),
    )(index_up, feat_up, *down_back, down_send, cot_upper, upper, summed_up, *up_slots,
      slope, normed, hidden, factor, alive_up, packed_down, local_down, w1, w2, wn1, wn2, bias_rows, norm_gains)

    partner = core_swap(partner)
    total = rounded(rounded(keep) + partner[4:].astype(F32))
    cross, keep = lax.optimization_barrier((cross, total))
    cross = cross_swap(cross)
    total = sum_along(total, (2, 8))
    (feat_grad_up,) = call(feat_grad_kernel, "feat_grad_up", [wide32], [], 0, (), (steps, (0,), (0,)))(
        first_up, w1, after=(partner,))
    total, cross, feat_grad_up = lax.optimization_barrier((total, cross, feat_grad_up))
    blocks = (partner, cross, own)
    total = rounded(total)
    levels = [
        along_level(jnp.concatenate([jnp.stack([b[d] for b in blocks]), total.astype(B16)]), -d) for d in (1, 2, 3)
    ]
    total = sum_of_four(total, *(b[3:] for b in levels))
    (grad_lower,) = call(lower_grad_kernel, "lower_grad", [shape((D, lower_rows))], [pltpu.VMEM(lower_table, F32)], 0, (), None, (0,))(
        *blocks, *levels, up_send, start_lower)
    total = sum_along(total, (8, 2))
    total, grad_lower = lax.optimization_barrier((total, grad_lower))
    total = rounded(total).astype(B16)
    w1_grad, w2_grad, wn1_grad, wn2_grad, bias_grad, gain_grad = call(
        unpack_kernel, "unpack",
        [shape((2, D, 3 * D)), shape((2, D, D)), shape((2, D, 2 * D)), shape((2, D, D)), shape((6, 2, D)), shape((2, 2, D))],
        [pltpu.VMEM((8, D, 128), F32)], 0, (), None, range(6))(total, core_swap(total))
    return (
        lower_new.T, upper_new.T, grad_lower.T, grad_latent.T, feat_grad_up.T, feat_grad_down.T,
        w1_grad.transpose(0, 2, 1), w2_grad, wn1_grad.transpose(0, 2, 1), wn2_grad, bias_grad.transpose(1, 0, 2), gain_grad,
    )


def solution(mesh):
    rows, index, whole = P(("band", "level"), None), P(("band", "level")), P()
    placed = (rows,) * 6 + (index, index) + (rows,) * 2 + (index, index) + (whole,) * 6 + (rows,) * 2
    return jax.shard_map(
        shards,
        mesh=mesh,
        in_specs=placed,
        out_specs=(rows,) * 6 + (whole,) * 6,
        check_vma=False,
    )
```

```python
import functools

import jax
import jax.numpy as jnp
from jax import lax
from jax.experimental import pallas as pl
from jax.experimental.pallas import tpu as pltpu
from jax.sharding import PartitionSpec as P

EPSILON = 1e-05
F32 = jnp.float32
B16 = jnp.bfloat16
D = 64
SLOT_GROUPS, SLOT_COLS = 6, 256
EDGE_BLOCK = 3072
CHUNK = 1024
VMEM_BYTES = 24 * 1024 * 1024


def groups_of(rows):
    return (4, rows // 4) if rows > 1024 else (rows // 256, 256)


def dot(a, b):
    return jnp.dot(a, b, preferred_element_type=F32)


def dot_rows(a, b):
    return lax.dot_general(a, b, (((1,), (1,)), ((), ())), preferred_element_type=F32)


def halves(x):
    high = x.astype(B16)
    return high, (x - high.astype(F32)).astype(B16)


def one_hot(column, n):
    rows = lax.broadcasted_iota(jnp.int16, (n, column.shape[1]), 0)
    return jnp.where(rows == column.astype(jnp.int16), jnp.ones((), B16), jnp.zeros((), B16))


def place(index, groups, n):
    group = jnp.zeros_like(index)
    for j in range(1, groups):
        group = group + (index >= j * n).astype(jnp.int32)
    return group, index - group * n


def level_and_core():
    return lax.axis_index("level").astype(jnp.int32), lax.axis_index("band").astype(jnp.int32) & 1


def band_offsets(swapped):
    unused, core = level_and_core()
    return (2 - 2 * core, 2 * core, 1) if swapped else (0, 2, 1)


def slot_place(senders, swapped):
    level, unused = level_and_core()
    distance = (level - ((senders >> 7) & 3)) & 3
    offset = senders >> 9
    source = jnp.where(offset == 1, 2, jnp.where(offset == band_offsets(swapped)[0], 0, 1))
    block = distance * 3 + source
    return block >> 1, ((block & 1) << 7) | (senders & 127)


def live(senders, counts_ref):
    peer = senders >> 7
    limit = jnp.zeros_like(senders)
    for j in range(12):
        limit = jnp.where(peer == j, counts_ref[0, j], limit)
    return ((senders & 127) < limit).astype(F32)


def choose(stacked, group, groups):
    picked = stacked[0:D]
    for j in range(1, groups):
        picked = jnp.where(group == j, stacked[j * D : (j + 1) * D], picked)
    return picked


def row_of(ref, k, start, size):
    rows = size // 128
    if not isinstance(start, int):
        start = pl.multiple_of(start // 128, rows)
        return jnp.concatenate([ref[k, pl.ds(start + r, 1), :] for r in range(rows)], axis=1)
    return jnp.concatenate([ref[k, r : r + 1, :] for r in range(start // 128, start // 128 + rows)], axis=1)


def pick(table, group, column, groups, n):
    return choose(dot(table[...], one_hot(column, n)), group, groups).astype(B16)


def spread(values, group, groups):
    wide = jnp.broadcast_to(group.astype(jnp.int16), values.shape)
    nothing = jnp.zeros_like(values)
    return jnp.concatenate([jnp.where(wide == j, values, nothing) for j in range(groups)], axis=0)


def add_at(total, values, group, column, groups, n):
    total[...] += dot_rows(spread(values, group, groups), one_hot(column, n))


def pack_table(table, source, groups, n):
    for j in range(groups):
        table[j * D : (j + 1) * D, :] = source[:, j * n : (j + 1) * n]


def columns_of(biases_ref, gains_ref, k):
    rows = [biases_ref[i, k : k + 1] for i in range(6)] + [gains_ref[k]]
    return jnp.concatenate(rows, axis=0).T


def fold(values):
    total = values[:, 0:128]
    for i in range(128, values.shape[1], 128):
        total = total + values[:, i : i + 128]
    return total


def norm_parts(values):
    centre = values - jnp.sum(values, axis=0, keepdims=True) * (1.0 / D)
    spread_sum = jnp.sum(centre * centre, axis=0, keepdims=True) * (1.0 / D)
    factor = lax.rsqrt(spread_sum + EPSILON)
    return centre * factor, factor


def norm_back(grad, normed, factor, gain):
    scaled = grad * gain
    first = jnp.sum(scaled, axis=0, keepdims=True) * (1.0 / D)
    second = jnp.sum(scaled * normed, axis=0, keepdims=True) * (1.0 / D)
    return factor * (scaled - first - normed * second)


def sigmoid(values):
    return 0.5 * jnp.tanh(0.5 * values) + 0.5


def send_rows(send_ref, offset):
    level, unused = level_and_core()
    return jnp.concatenate(
        [send_ref[pl.ds(offset * 4 + ((level + d) & 3), 1), :] for d in range(4)], axis=1
    )


def send_blocks(outs, table, send_ref, groups, n, swapped):
    for j, offset in enumerate(band_offsets(swapped)):
        group, column = place(send_rows(send_ref, offset), groups, n)
        rows = pick(table, group, column, groups, n)
        for d in range(4):
            outs[j][d] = rows[:, d * 128 : (d + 1) * 128]


def add_back(total, blocks, send_ref, groups, n, swapped):
    for j, offset in enumerate(band_offsets(swapped)):
        group, column = place(send_rows(send_ref, offset), groups, n)
        values = jnp.concatenate([block_at(blocks, d, j) for d in range(4)], axis=1)
        add_at(total, values, group, column, groups, n)


def block_at(received, d, j):
    return received[j][0] if d == 0 else received[2 + d][j]


def slot_table(table, received):
    for t in range(12):
        table[(t >> 1) * D : ((t >> 1) + 1) * D, (t & 1) * 128 : ((t & 1) + 1) * 128] = block_at(received, t // 3, t % 3)


def slot_gradients(outs, sums, weight):
    for j in range(SLOT_GROUPS):
        high, low = halves(sums[j * D : (j + 1) * D, :])
        grads = (dot(weight, high) + dot(weight, low)).astype(B16)
        for t in (2 * j, 2 * j + 1):
            outs[t % 3][t // 3] = grads[:, (t & 1) * 128 : ((t & 1) + 1) * 128]


def over_blocks(total, block, body):
    block = min(block, total)
    if block == total:
        body(pl.ds(0, block))
        return

    def step(i, carry):
        body(pl.ds(pl.multiple_of(i * block, block), block))
        return carry

    lax.fori_loop(0, total // block, step, 0)


def pipelined(stages, spans):
    held = [None] * len(spans)
    for t in range(len(spans) + len(stages) - 1):
        for k in reversed(range(len(stages))):
            i = t - k
            if 0 <= i < len(spans):
                held[i] = stages[k](spans[i], held[i])


def spans_of(parts, chunk):
    spans, start = [], 0
    for which, ref in enumerate(parts):
        size = min(chunk, ref.shape[1])
        for at in range(0, ref.shape[1], size):
            spans.append((which, pl.ds(at, size), pl.ds(start + at, size)))
        start += ref.shape[1]
    return spans


def tables_kernel(upper_rows, lower_rows, counts_up, counts_down, senders_up, targets_up, senders_down, targets_down,
                  index_up, alive_up, index_down, alive_down, limits_up, limits_down, sems):
    copies = [pltpu.make_async_copy(counts_up, limits_up, sems.at[0]), pltpu.make_async_copy(counts_down, limits_down, sems.at[1])]
    for copy in copies:
        copy.start()
    sweeps = ((index_up, senders_up, targets_up, upper_rows, True), (index_down, senders_down, targets_down, lower_rows, False))
    for index_ref, senders_ref, targets_ref, rows, swapped in sweeps:
        index_ref[0], index_ref[1] = place(targets_ref[...], *groups_of(rows))
        index_ref[2], index_ref[3] = slot_place(senders_ref[...], swapped)
    for copy in copies:
        copy.wait()
    alive_up[0] = live(senders_up[...], limits_up)
    alive_down[0] = live(senders_down[...], limits_down)


def send_kernel(count, *refs):
    sources, refs = refs[:count], refs[count:]
    sent, held, table, sems = refs[:3], refs[3:-2], refs[-2], refs[-1]
    copies = [pltpu.make_async_copy(a, b, sems.at[i]) for i, (a, b) in enumerate(zip(sources, held))]
    for copy in copies:
        copy.start()
    for copy in copies[:2]:
        copy.wait()
    send_ref, source_ref = held[:2]
    groups, n = groups_of(source_ref.shape[1])
    pack_table(table, source_ref, groups, n)
    send_blocks(sent, table, send_ref, groups, n, True)
    for copy in copies[2:]:
        copy.wait()


def part_kernel(k, block, index_ref, feat_ref, local_ref, w1_ref, biases_ref, gains_ref, *rest):
    part_ref, held_ref, table, picked, sem = rest[-5:]
    copy = pltpu.make_async_copy(feat_ref, held_ref, sem)
    copy.start()
    groups, n = groups_of(local_ref.shape[1])
    pack_table(table, local_ref, groups, n)
    columns = columns_of(biases_ref, gains_ref, k)
    weight = jnp.concatenate([w1_ref[k, :, 0:D], w1_ref[k, :, 2 * D : 3 * D]], axis=1)

    def body(s):
        picked[:, s] = pick(table, row_of(index_ref, 0, s.start, s.size), row_of(index_ref, 1, s.start, s.size), groups, n)

    over_blocks(feat_ref.shape[1], block, body)
    copy.wait()
    part_ref[...] = dot(weight, jnp.concatenate([held_ref[...], picked[...]], axis=0)) + columns[:, 0:1]


def edges_forward(k, parts, alive_ref, index_ref, table, w1_ref, w2_ref, columns, total, groups, n,
                  slope_ref, normed_ref, hidden_ref, factor_ref):
    weight_slot = w1_ref[k, :, D : 2 * D]
    weight_two = w2_ref[k].astype(F32).T.astype(B16)
    total[...] = jnp.zeros_like(total)

    def slot_rows(span, unused):
        a, size = span[2].start, span[2].size
        return pick(table, row_of(index_ref, 2, a, size), row_of(index_ref, 3, a, size), SLOT_GROUPS, SLOT_COLS)

    def first_layer(span, picked):
        which, t, s = span
        first = parts[which][:, t] + dot(weight_slot, picked)
        gate = sigmoid(first)
        hidden = (first * gate).astype(B16)
        slope_ref[:, s] = gate * (1.0 + first * (1.0 - gate))
        hidden_ref[:, s] = hidden
        return hidden

    def second_layer(span, hidden):
        s = span[2]
        normed, factor = norm_parts(dot(weight_two, hidden) + columns[:, 1:2])
        alive = row_of(alive_ref, 0, s.start, s.size)
        normed_ref[:, s] = normed
        factor_ref[:, s] = factor
        return ((normed * columns[:, 6:7] + columns[:, 2:3]) * alive).astype(B16)

    def sum_messages(span, messages):
        a, size = span[2].start, span[2].size
        add_at(total, messages, row_of(index_ref, 0, a, size), row_of(index_ref, 1, a, size), groups, n)

    pipelined((slot_rows, first_layer, second_layer, sum_messages), spans_of(parts, CHUNK))


def node_first(k, inputs, wn1_ref, columns):
    first = dot(wn1_ref[k], inputs) + columns[:, 3:4]
    gate = sigmoid(first)
    return (first * gate).astype(B16), gate * (1.0 + first * (1.0 - gate))


def node_second(hidden, weight_two, columns):
    return norm_parts(dot(weight_two, hidden) + columns[:, 4:5])


def node_second_grad(grad, normed, factor, columns, sums_ref):
    sums_ref[2] += fold(grad)
    sums_ref[3] += fold(grad * normed)
    return norm_back(grad, normed, factor, columns[:, 7:8]).astype(B16)


def node_weight_grads(first, second, inputs, hidden, one_ref, two_ref, sums_ref):
    sums_ref[0] += fold(first.astype(F32))
    sums_ref[1] += fold(second.astype(F32))
    one_ref[...] += dot_rows(first, inputs)
    two_ref[...] += dot_rows(hidden, second)


def clear(refs):
    for ref in refs:
        ref[...] = jnp.zeros_like(ref)


def transposed(weight):
    return weight.astype(F32).T.astype(B16)


def edge_second(grad_rows, s, columns, weight_sum, alive_ref, normed_ref, factor_ref, sums_ref):
    grad = dot(weight_sum, grad_rows) * row_of(alive_ref, 0, s.start, s.size)
    normed = normed_ref[:, s]
    sums_ref[2] += fold(grad)
    sums_ref[3] += fold(grad * normed)
    return norm_back(grad, normed, factor_ref[:, s], columns[:, 6:7]).astype(B16)


def edge_first(second, s, weight_two, slope_ref):
    return (dot(weight_two, second) * slope_ref[:, s]).astype(B16)


def edge_weight_grads(first, second, feat, hidden, one_ref, two_ref, sums_ref):
    sums_ref[0] += fold(first.astype(F32))
    sums_ref[1] += fold(second.astype(F32))
    one_ref[...] += dot_rows(first, feat)
    two_ref[...] += dot_rows(hidden, second)


def pack_columns(edge_sums, node_sums):
    order = (edge_sums[0], edge_sums[1], edge_sums[2], node_sums[0], node_sums[1], node_sums[2], edge_sums[3], node_sums[3])
    columns = [jnp.sum(v, axis=1, keepdims=True) for v in order]
    lanes = lax.broadcasted_iota(jnp.int32, (D, D), 1)
    packed = jnp.zeros((D, D), F32)
    for i, column in enumerate(columns):
        packed = jnp.where(lanes == i, column, packed)
    return packed


def slot_weight_grads(sums, table):
    total = jnp.zeros((D, D), F32)
    for j in range(SLOT_GROUPS):
        high, low = halves(sums[j * D : (j + 1) * D, :])
        rows = table[j * D : (j + 1) * D, :]
        total = total + dot_rows(high, rows) + dot_rows(low, rows)
    return total


def target_grads(total, local_ref, weight, start, out_ref, groups, n):
    grads = jnp.zeros((D, D), F32)
    for j in range(groups):
        high, low = halves(total[j * D : (j + 1) * D, :])
        s = slice(j * n, (j + 1) * n)
        rows = local_ref[:, s]
        grads = grads + dot_rows(high, rows) + dot_rows(low, rows)
        out_ref[:, s] = start(j) + dot(weight, high) + dot(weight, low)
    return grads


def up_forward_kernel(part_ref, alive_ref, index_ref, r0, r1, r2, r3, r4, r5, local_ref, send_ref,
                      w1_ref, w2_ref, wn1_ref, wn2_ref, biases_ref, gains_ref,
                      out_ref, summed_ref, s0, s1, s2, slope_ref, normed_ref, hidden_ref, factor_ref,
                      slots, total, table, out, sem):
    groups, n = groups_of(local_ref.shape[1])
    columns = columns_of(biases_ref, gains_ref, 0)
    slot_table(slots, (r0, r1, r2, r3, r4, r5))
    edges_forward(0, (part_ref,), alive_ref, index_ref, slots, w1_ref, w2_ref, columns, total, groups, n,
                  slope_ref, normed_ref, hidden_ref, factor_ref)
    weight_two = transposed(wn2_ref[0])

    def first_layer(j, unused):
        s = slice(j * n, (j + 1) * n)
        summed = total[j * D : (j + 1) * D, :].astype(B16)
        summed_ref[:, s] = summed
        return node_first(0, jnp.concatenate([local_ref[:, s], summed], axis=0), wn1_ref, columns)

    def second_layer(j, held):
        s = slice(j * n, (j + 1) * n)
        normed, unused = node_second(held[0], weight_two, columns)
        result = local_ref[:, s].astype(F32) + normed * columns[:, 7:8] + columns[:, 5:6]
        out[:, s] = result
        table[j * D : (j + 1) * D, :] = result.astype(B16)

    pipelined((first_layer, second_layer), range(groups))
    copy = pltpu.make_async_copy(out, out_ref, sem)
    copy.start()
    send_blocks((s0, s1, s2), table, send_ref, groups, n, False)
    copy.wait()


def down_kernel(part_ref, alive_ref, index_ref, r0, r1, r2, r3, r4, r5, local_ref, cot_ref,
                w1_ref, w2_ref, wn1_ref, wn2_ref, biases_ref, gains_ref,
                out_ref, g0, g1, g2, first_ref, second_ref, hidden_ref, sums_ref, edge_sums, node_sums,
                table, summed_ref, node_hidden_ref, node_second_ref,
                slots, total, slope_ref, normed_ref, factor_ref, out, sem):
    groups, n = groups_of(local_ref.shape[1])
    columns = columns_of(biases_ref, gains_ref, 1)
    slot_table(slots, (r0, r1, r2, r3, r4, r5))
    parts = (part_ref,)
    edges_forward(1, parts, alive_ref, index_ref, slots, w1_ref, w2_ref, columns, total, groups, n,
                  slope_ref, normed_ref, hidden_ref, factor_ref)
    clear((node_sums, edge_sums, sums_ref))
    wn2 = wn2_ref[1]
    wn2_t = transposed(wn2)
    wn1 = transposed(wn1_ref[1])

    def first_layer(j, unused):
        summed = total[j * D : (j + 1) * D, :].astype(B16)
        summed_ref[j * D : (j + 1) * D, :] = summed
        inputs = jnp.concatenate([local_ref[:, j * n : (j + 1) * n], summed], axis=0)
        return node_first(1, inputs, wn1_ref, columns)

    def second_layer(j, held):
        hidden, slope = held
        s = slice(j * n, (j + 1) * n)
        normed, factor = node_second(hidden, wn2_t, columns)
        out[:, s] = local_ref[:, s].astype(F32) + normed * columns[:, 7:8] + columns[:, 5:6]
        second = node_second_grad(cot_ref[:, s], normed, factor, columns, node_sums)
        node_hidden_ref[:, s] = hidden
        node_second_ref[:, s] = second
        return slope, second

    def node_grads(j, held):
        slope, second = held
        table[j * D : (j + 1) * D, :] = (dot(wn2, second) * slope).astype(B16)

    pipelined((first_layer, second_layer, node_grads), range(groups))
    copy = pltpu.make_async_copy(out, out_ref, sem)
    copy.start()
    weight_two = w2_ref[1]
    weight_slot = transposed(w1_ref[1, :, D : 2 * D])

    def grad_rows(span, unused):
        a, size = span[2].start, span[2].size
        return pick(table, row_of(index_ref, 0, a, size), row_of(index_ref, 1, a, size), groups, n)

    def second_grad(span, rows):
        return edge_second(rows, span[2], columns, wn1[D : 2 * D], alive_ref, normed_ref, factor_ref, edge_sums)

    def first_grad(span, second):
        s = span[2]
        first = edge_first(second, s, weight_two, slope_ref)
        first_ref[:, s] = first
        second_ref[:, s] = second
        return first

    def sum_slots(span, first):
        a, size = span[2].start, span[2].size
        add_at(sums_ref, first, row_of(index_ref, 2, a, size), row_of(index_ref, 3, a, size), SLOT_GROUPS, SLOT_COLS)

    pipelined((grad_rows, second_grad, first_grad, sum_slots), spans_of(parts, CHUNK))
    slot_gradients((g0, g1, g2), sums_ref, weight_slot)
    copy.wait()


def down_targets_kernel(index_ref, first_ref, local_ref, cot_ref, table, w1_ref, wn1_ref, *rest):
    grad_ref, weight_grad_ref, total = rest[-3:]
    groups, n = groups_of(local_ref.shape[1])
    weight = transposed(w1_ref[1, :, 2 * D : 3 * D])
    total[...] = jnp.zeros_like(total)

    def body(s):
        group, column = row_of(index_ref, 0, s.start, s.size), row_of(index_ref, 1, s.start, s.size)
        add_at(total, first_ref[:, s], group, column, groups, n)

    over_blocks(first_ref.shape[1], EDGE_BLOCK, body)
    weight_node = transposed(wn1_ref[1, :, 0:D])

    def start(j):
        return cot_ref[:, j * n : (j + 1) * n] + dot(weight_node, table[j * D : (j + 1) * D, :])

    weight_grad_ref[...] = target_grads(total, local_ref, weight, start, grad_ref, groups, n)


def down_rest_kernel(feat_ref, first_ref, second_ref, hidden_ref, r0, r1, r2, r3, r4, r5, sums_ref, edge_in, node_in,
                     table, summed_ref, node_hidden_ref, node_second_ref, local_ref, w1_ref,
                     feat_grad_ref, packed_ref, slots, one_ref, two_ref, wn1_grad, wn2_grad, edge_sums, node_sums):
    step = pl.program_id(0)
    weight = transposed(w1_ref[1, :, 0:D])

    @pl.when(step == 0)
    def _():
        clear((one_ref, two_ref, wn1_grad, wn2_grad))
        edge_sums[...] = edge_in[...]
        node_sums[...] = node_in[...]

    s = pl.ds(pl.multiple_of(step * EDGE_BLOCK, EDGE_BLOCK), EDGE_BLOCK)
    first = first_ref[:, s]
    feat_grad_ref[...] = dot(weight, first)
    edge_weight_grads(first, second_ref[:, s], feat_ref[:, s], hidden_ref[:, s], one_ref, two_ref, edge_sums)

    @pl.when(step == pl.num_programs(0) - 1)
    def _():
        groups, n = groups_of(local_ref.shape[1])
        for j in range(groups):
            t, rows = slice(j * n, (j + 1) * n), slice(j * D, (j + 1) * D)
            inputs = jnp.concatenate([local_ref[:, t], summed_ref[rows, :]], axis=0)
            node_weight_grads(table[rows, :], node_second_ref[:, t], inputs, node_hidden_ref[:, t], wn1_grad, wn2_grad, node_sums)
        slot_table(slots, (r0, r1, r2, r3, r4, r5))
        write_packed(packed_ref, one_ref[...], slot_weight_grads(sums_ref, slots), jnp.zeros((D, D), F32), two_ref[...],
                     wn1_grad[...], wn2_grad[...], pack_columns(edge_sums, node_sums))


def write_packed(packed_ref, one, slot_grads, local_grads, two, wn1_grad, wn2_grad, columns):
    packed_ref[0] = jnp.concatenate([one, slot_grads], axis=1)
    packed_ref[1] = jnp.concatenate([local_grads, two], axis=1)
    packed_ref[2] = wn1_grad
    packed_ref[3] = jnp.concatenate([wn2_grad, columns], axis=1)


def up_backward_kernel(index_ref, feat_ref, h0, h1, h2, h3, h4, h5,
                       send_ref, cot_ref, local_ref, summed_ref, r0, r1, r2, r3, r4, r5, slope_ref, normed_ref, hidden_ref, factor_ref, alive_ref, packed_down_ref, local_down_ref,
                       w1_ref, w2_ref, wn1_ref, wn2_ref, biases_ref, gains_ref,
                       partner_ref, cross_ref, own_ref, first_ref, grad_ref, keep_ref,
                       slots, table, back, total, sums, start, one_ref, two_ref, edge_sums, node_sums, wn1_grad, wn2_grad, pieces):
    groups, n = groups_of(local_ref.shape[1])
    columns = columns_of(biases_ref, gains_ref, 0)
    clear((back, total, sums, one_ref, two_ref, edge_sums, node_sums, wn1_grad, wn2_grad))
    slot_table(slots, (r0, r1, r2, r3, r4, r5))
    add_back(back, (h0, h1, h2, h3, h4, h5), send_ref, groups, n, False)
    wn2 = wn2_ref[0]
    wn2_t = transposed(wn2)
    wn1 = transposed(wn1_ref[0])
    w1 = transposed(w1_ref[0])

    def first_layer(j, unused):
        s = slice(j * n, (j + 1) * n)
        inputs = jnp.concatenate([local_ref[:, s], summed_ref[:, s]], axis=0)
        return inputs, *node_first(0, inputs, wn1_ref, columns)

    def second_layer(j, held):
        inputs, hidden, slope = held
        grad = cot_ref[:, j * n : (j + 1) * n] + back[j * D : (j + 1) * D, :]
        normed, factor = node_second(hidden, wn2_t, columns)
        return inputs, hidden, slope, grad, node_second_grad(grad, normed, factor, columns, node_sums)

    def node_grads(j, held):
        inputs, hidden, slope, grad, second = held
        first = (dot(wn2, second) * slope).astype(B16)
        node_weight_grads(first, second, inputs, hidden, wn1_grad, wn2_grad, node_sums)
        table[j * D : (j + 1) * D, :] = first
        start[:, j * n : (j + 1) * n] = grad + dot(wn1[0:D], first)

    pipelined((first_layer, second_layer, node_grads), range(groups))
    weight_two = w2_ref[0]

    def grad_rows(span, unused):
        a, size = span[2].start, span[2].size
        return pick(table, row_of(index_ref, 0, a, size), row_of(index_ref, 1, a, size), groups, n)

    def second_grad(span, rows):
        return edge_second(rows, span[2], columns, wn1[D : 2 * D], alive_ref, normed_ref, factor_ref, edge_sums)

    def first_grad(span, second):
        s = span[2]
        first = edge_first(second, s, weight_two, slope_ref)
        first_ref[:, s] = first
        edge_weight_grads(first, second, feat_ref[:, s], hidden_ref[:, s], one_ref, two_ref, edge_sums)
        return first

    def sum_rows(span, first):
        s = span[2]
        rows = [row_of(index_ref, i, s.start, s.size) for i in range(4)]
        add_at(total, first, rows[0], rows[1], groups, n)
        add_at(sums, first, rows[2], rows[3], SLOT_GROUPS, SLOT_COLS)

    pipelined((grad_rows, second_grad, first_grad, sum_rows), spans_of((first_ref,), CHUNK))
    slot_gradients((partner_ref, cross_ref, own_ref), sums, w1[D : 2 * D])
    local_grads = target_grads(total, local_ref, w1[2 * D : 3 * D], lambda j: start[:, j * n : (j + 1) * n], grad_ref, groups, n)
    slot_grads = slot_weight_grads(sums, slots)
    write_packed(pieces, one_ref[...], slot_grads, local_grads, two_ref[...], wn1_grad[...], wn2_grad[...],
                 pack_columns(edge_sums, node_sums))
    unused, core = level_and_core()
    for p in range(4):
        pieces[4 + p] = packed_down_ref[p]
    pieces[5, :, 0:D] = local_down_ref[...]
    for p in range(4):
        keep_ref[p] = pieces[core * 4 + p]
        partner_ref[4 + p] = pieces[(1 - core) * 4 + p].astype(B16)


def feat_grad_kernel(first_ref, w1_ref, *rest):
    out_ref = rest[-1]
    out_ref[...] = dot(transposed(w1_ref[0, :, 0:D]), first_ref[...])


def lower_grad_kernel(h0, h1, h2, h3, h4, h5, send_ref, start_ref, out_ref, total):
    groups, n = groups_of(start_ref.shape[1])
    clear((total,))
    add_back(total, (h0, h1, h2, h3, h4, h5), send_ref, groups, n, True)
    for j in range(groups):
        s = slice(j * n, (j + 1) * n)
        out_ref[:, s] = start_ref[:, s] + total[j * D : (j + 1) * D, :]


def unpack_kernel(own_ref, other_ref, w1_ref, w2_ref, wn1_ref, wn2_ref, biases_ref, gains_ref, pieces):
    unused, core = level_and_core()
    for p in range(4):
        pieces[core * 4 + p] = own_ref[p].astype(F32)
        pieces[(1 - core) * 4 + p] = other_ref[p].astype(F32)
    for k in range(2):
        w1_ref[k] = jnp.concatenate([pieces[4 * k], pieces[4 * k + 1, :, 0:D]], axis=1)
        w2_ref[k] = pieces[4 * k + 1, :, D : 2 * D]
        wn1_ref[k] = pieces[4 * k + 2]
        wn2_ref[k] = pieces[4 * k + 3, :, 0:D]
        rows = pieces[4 * k + 3].T
        for i in range(6):
            biases_ref[i, k : k + 1] = rows[D + i : D + i + 1]
        gains_ref[k] = rows[D + 6 : D + 8]


def shape(dims, dtype=F32):
    return jax.ShapeDtypeStruct(dims, dtype)


def call(kernel, name, outs, scratch, scalars=0, stored=(), streamed=None, final=(), raw=()):
    steps, stream_in, stream_out = streamed if streamed else (1, (), ())

    def run(*operands, after=()):
        def whole(space):
            return pl.BlockSpec(memory_space=space)

        def cut(x):
            return pl.BlockSpec((x.shape[0], x.shape[1] // steps), lambda i: (0, i))

        in_specs, placed = [], []
        for i, x in enumerate(operands):
            if i < scalars:
                in_specs.append(whole(pltpu.SMEM))
            elif i in stream_in:
                in_specs.append(cut(x))
            elif i in raw:
                in_specs.append(whole(pltpu.HBM))
                x = pltpu.with_memory_space_constraint(x, pltpu.HBM)
            else:
                in_specs.append(whole(pltpu.VMEM))
                x = pltpu.with_memory_space_constraint(x, pltpu.VMEM)
            placed.append(x)
        in_specs += [whole(pl.ANY) for _ in after]
        out_specs, out_shape = [], []
        for i, x in enumerate(outs):
            if i in stream_out:
                out_specs.append(cut(x))
                out_shape.append(x)
            elif i in stored:
                out_specs.append(whole(pl.ANY))
                out_shape.append(x)
            elif i in final:
                out_specs.append(whole(pltpu.VMEM))
                out_shape.append(x)
            else:
                out_specs.append(whole(pltpu.VMEM))
                out_shape.append(pltpu.VMEM(x.shape, x.dtype))
        return pl.pallas_call(
            kernel,
            name=name,
            grid=(steps,) if streamed else (),
            in_specs=in_specs,
            out_specs=out_specs,
            out_shape=out_shape,
            scratch_shapes=scratch,
            compiler_params=pltpu.CompilerParams(vmem_limit_bytes=VMEM_BYTES),
        )(*placed, *after)

    return run


def core_swap(block):
    return lax.ppermute(block, "band", [(i, i ^ 1) for i in range(lax.axis_size("band"))])


def cross_swap(block):
    last = lax.axis_size("band") - 1
    pairs = [(i, i + 1) for i in range(1, last, 2)]
    return lax.ppermute(block, "band", pairs + [(b, a) for a, b in pairs] + [(0, 0), (last, last)])


def along_level(block, step):
    count = lax.axis_size("level")
    return lax.ppermute(block, "level", [(i, (i + step) % count) for i in range(count)])


def along_band(block, step):
    count = lax.axis_size("band")
    return lax.ppermute(block, "band", [(i, (i + step) % count) for i in range(count)])


def across_bands(blocks):
    below, above, own = blocks
    return [along_band(above, 1), along_band(below, -1), own]


def along_levels(blocks, sign):
    return blocks + [along_level(jnp.stack([b[d] for b in blocks]), sign * d) for d in (1, 2, 3)]


def chip_ring(block, step, core_strides):
    count = lax.axis_size("band")
    pairs = []
    for i in range(count):
        stride = core_strides[i % 2]
        at = (i // stride) % 4
        pairs.append((i, i + (((at + step) % 4) - at) * stride))
    return lax.ppermute(block, "band", pairs)


def rounded(values):
    return lax.reduce_precision(values, 8, 7)


def sum_of_four(values, first, second, third):
    return (values + second.astype(F32)) + (first.astype(F32) + third.astype(F32))


def sum_along(values, core_strides):
    own = rounded(values)
    sent = own.astype(B16)
    return sum_of_four(own, *(chip_ring(sent, d, core_strides) for d in (1, 2, 3)))


def shards(
    lower_nodes, latent, up_feat, down_feat, up_send, up_counts, up_senders, up_targets,
    down_send, down_counts, down_senders, down_targets,
    edge_w1, edge_w2, node_w1, node_w2, biases, norm_gains, lower_cot, upper_cot,
):
    lower, upper = lower_nodes.T, latent.T
    feat_up, feat_down = up_feat.T, down_feat.T
    cot_lower, cot_upper = lower_cot.T, upper_cot.T
    w1, wn1 = edge_w1.transpose(0, 2, 1), node_w1.transpose(0, 2, 1)
    w2, wn2 = edge_w2, node_w2
    edges, lower_rows, upper_rows = up_feat.shape[0], lower_nodes.shape[0], latent.shape[0]
    dense = (edges // 128, 128)
    senders_up, targets_up, senders_down, targets_down = (
        x.reshape(dense) for x in (up_senders, up_targets, down_senders, down_targets))
    bias_rows = biases.transpose(1, 0, 2)

    lower_groups, lower_n = groups_of(lower_rows)
    upper_groups, upper_n = groups_of(upper_rows)
    lower_table, upper_table = (lower_groups * D, lower_n), (upper_groups * D, upper_n)
    slots = pltpu.VMEM((SLOT_GROUPS * D, SLOT_COLS), B16)
    block, four = shape((4, D, 128), B16), shape((4, D, 128))
    wide32, wide16, row = shape((D, edges)), shape((D, edges), B16), shape((1, edges))
    steps = edges // EDGE_BLOCK

    early = (up_send, lower, senders_up, targets_up, senders_down, targets_down, upper, w1, bias_rows, norm_gains,
             down_send, w2, wn1, wn2)
    count = len(early)
    (*sent, up_send, lower, senders_up, targets_up, senders_down, targets_down, upper, w1, bias_rows,
     norm_gains, down_send, w2, wn1, wn2) = call(
        functools.partial(send_kernel, count), "send_lower", [block] * 3 + [shape(x.shape, x.dtype) for x in early],
        [pltpu.VMEM(lower_table, B16), pltpu.SemaphoreType.DMA((count,))], 0, raw=range(count),
    )(*early)
    index, lives = shape((4, *dense), jnp.int32), shape((1, *dense))
    index_up, alive_up, index_down, alive_down = call(
        functools.partial(tables_kernel, upper_rows, lower_rows), "edge_tables", [index, lives, index, lives],
        [pltpu.SMEM((1, 12), jnp.int32), pltpu.SMEM((1, 12), jnp.int32), pltpu.SemaphoreType.DMA((2,))], 0, raw=(0, 1),
    )(up_counts, down_counts, senders_up, targets_up, senders_down, targets_down)

    def part(k, block, name, table, index, feat, local, after):
        return call(
            functools.partial(part_kernel, k, block), name, [wide32, wide16],
            [pltpu.VMEM(table, B16), pltpu.VMEM((D, edges), B16), pltpu.SemaphoreType.DMA], 0, raw=(1,),
        )(index, feat, local, w1, bias_rows, norm_gains, after=after)

    sent = [core_swap(sent[0]), cross_swap(sent[1]), sent[2]]
    sent, alive_up = lax.optimization_barrier((sent, alive_up))
    part_up, feat_up = part(0, EDGE_BLOCK, "part_up", upper_table, index_up, feat_up, upper, (sent[0], sent[1]))
    up_slots = along_levels(sent, 1)
    up_slots, part_up = lax.optimization_barrier((up_slots, part_up))
    (upper_new, summed_up, s0, s1, s2, slope, normed, hidden, factor) = call(
        up_forward_kernel, "up_forward",
        [shape((D, upper_rows)), shape((D, upper_rows), B16)] + [block] * 3 + [wide32, wide32, wide16, row],
        [slots, pltpu.VMEM(upper_table, F32), pltpu.VMEM(upper_table, B16), pltpu.VMEM((D, upper_rows), F32),
         pltpu.SemaphoreType.DMA], 0, (0,),
    )(part_up, alive_up, index_up, *up_slots, upper, down_send, w1, w2, wn1, wn2, bias_rows, norm_gains)
    sent = across_bands([s0, s1, s2])
    part_down, feat_down = part(1, EDGE_BLOCK, "part_down", lower_table, index_down, feat_down, lower, (sent[0], sent[1]))
    down_slots = along_levels(sent, 1)
    down_slots, part_down = lax.optimization_barrier((down_slots, part_down))
    sums_shape = shape((SLOT_GROUPS * D, SLOT_COLS))
    node16 = shape((D, lower_rows), B16)
    (lower_new, g0, g1, g2, first_down, second_down, hidden_down, sums_down, edge_sums, node_sums, *nodes) = call(
        down_kernel, "down_sweep",
        [shape((D, lower_rows))] + [block] * 3 + [wide16] * 3 + [sums_shape, four, four, shape(lower_table, B16),
         shape(lower_table, B16), node16, node16],
        [slots, pltpu.VMEM(lower_table, F32), pltpu.VMEM((D, edges), F32),
         pltpu.VMEM((D, edges), F32), pltpu.VMEM((1, edges), F32),
         pltpu.VMEM((D, lower_rows), F32), pltpu.SemaphoreType.DMA], 0, (0,),
    )(part_down, alive_down, index_down, *down_slots, lower, cot_lower, w1, w2, wn1, wn2, bias_rows, norm_gains)
    back = across_bands([g0, g1, g2])
    feat_grad_down, packed_down = call(
        down_rest_kernel, "down_rest", [wide32, four],
        [slots, pltpu.VMEM((D, D), F32), pltpu.VMEM((D, D), F32), pltpu.VMEM((D, 2 * D), F32), pltpu.VMEM((D, D), F32),
         pltpu.VMEM((4, D, 128), F32), pltpu.VMEM((4, D, 128), F32)], 0, (), (steps, (), (0,)),
    )(feat_down, first_down, second_down, hidden_down, *down_slots, sums_down, edge_sums, node_sums, *nodes, lower, w1)
    back, packed_down = lax.optimization_barrier((back, packed_down))
    start_lower, local_down = call(
        down_targets_kernel, "down_targets", [shape((D, lower_rows)), shape((D, D))], [pltpu.VMEM(lower_table, F32)],
    )(index_down, first_down, lower, cot_lower, nodes[0], w1, wn1, after=(back[0], back[1]))
    down_back = along_levels(back, -1)
    down_back, local_down = lax.optimization_barrier((down_back, local_down))
    (partner, cross, own, first_up, grad_latent, keep) = call(
        up_backward_kernel, "up_backward",
        [shape((8, D, 128), B16), block, block, wide16, shape((D, upper_rows)), four],
        [slots, pltpu.VMEM(upper_table, B16), pltpu.VMEM(upper_table, F32), pltpu.VMEM(upper_table, F32),
         pltpu.VMEM((SLOT_GROUPS * D, SLOT_COLS), F32), pltpu.VMEM((D, upper_rows), F32),
         pltpu.VMEM((D, D), F32), pltpu.VMEM((D, D), F32), pltpu.VMEM((4, D, 128), F32), pltpu.VMEM((4, D, 128), F32),
         pltpu.VMEM((D, 2 * D), F32), pltpu.VMEM((D, D), F32), pltpu.VMEM((8, D, 128), F32)], 0, (), None, (4,),
    )(index_up, feat_up, *down_back, down_send, cot_upper, upper, summed_up, *up_slots,
      slope, normed, hidden, factor, alive_up, packed_down, local_down, w1, w2, wn1, wn2, bias_rows, norm_gains)

    partner = core_swap(partner)
    total = rounded(rounded(keep) + partner[4:].astype(F32))
    cross, keep = lax.optimization_barrier((cross, total))
    cross = cross_swap(cross)
    total = sum_along(total, (2, 8))
    (feat_grad_up,) = call(feat_grad_kernel, "feat_grad_up", [wide32], [], 0, (), (steps, (0,), (0,)))(
        first_up, w1, after=(partner,))
    total, cross, feat_grad_up = lax.optimization_barrier((total, cross, feat_grad_up))
    blocks = (partner, cross, own)
    total = rounded(total)
    levels = [
        along_level(jnp.concatenate([jnp.stack([b[d] for b in blocks]), total.astype(B16)]), -d) for d in (1, 2, 3)
    ]
    total = sum_of_four(total, *(b[3:] for b in levels))
    (grad_lower,) = call(lower_grad_kernel, "lower_grad", [shape((D, lower_rows))], [pltpu.VMEM(lower_table, F32)], 0, (), None, (0,))(
        *blocks, *levels, up_send, start_lower)
    total = sum_along(total, (8, 2))
    total, grad_lower = lax.optimization_barrier((total, grad_lower))
    total = rounded(total).astype(B16)
    w1_grad, w2_grad, wn1_grad, wn2_grad, bias_grad, gain_grad = call(
        unpack_kernel, "unpack",
        [shape((2, D, 3 * D)), shape((2, D, D)), shape((2, D, 2 * D)), shape((2, D, D)), shape((6, 2, D)), shape((2, 2, D))],
        [pltpu.VMEM((8, D, 128), F32)], 0, (), None, range(6))(total, core_swap(total))
    return (
        lower_new.T, upper_new.T, grad_lower.T, grad_latent.T, feat_grad_up.T, feat_grad_down.T,
        w1_grad.transpose(0, 2, 1), w2_grad, wn1_grad.transpose(0, 2, 1), wn2_grad, bias_grad.transpose(1, 0, 2), gain_grad,
    )


def solution(mesh):
    rows, index, whole = P(("band", "level"), None), P(("band", "level")), P()
    placed = (rows,) * 6 + (index, index) + (rows,) * 2 + (index, index) + (whole,) * 6 + (rows,) * 2
    return jax.shard_map(
        shards,
        mesh=mesh,
        in_specs=placed,
        out_specs=(rows,) * 6 + (whole,) * 6,
        check_vma=False,
    )
```

```python
import functools

import jax
import jax.numpy as jnp
from jax import lax
from jax.experimental import pallas as pl
from jax.experimental.pallas import tpu as pltpu
from jax.sharding import PartitionSpec as P

EPSILON = 1e-05
F32 = jnp.float32
B16 = jnp.bfloat16
D = 64
SLOT_GROUPS, SLOT_COLS = 6, 256
EDGE_BLOCK = 3072
CHUNK = 1024
VMEM_BYTES = 24 * 1024 * 1024


def groups_of(rows):
    return (4, rows // 4) if rows > 1024 else (rows // 256, 256)


def dot(a, b):
    return jnp.dot(a, b, preferred_element_type=F32)


def dot_rows(a, b):
    return lax.dot_general(a, b, (((1,), (1,)), ((), ())), preferred_element_type=F32)


def halves(x):
    high = x.astype(B16)
    return high, (x - high.astype(F32)).astype(B16)


def one_hot(column, n):
    rows = lax.broadcasted_iota(jnp.int16, (n, column.shape[1]), 0)
    return jnp.where(rows == column.astype(jnp.int16), jnp.ones((), B16), jnp.zeros((), B16))


def place(index, groups, n):
    group = jnp.zeros_like(index)
    for j in range(1, groups):
        group = group + (index >= j * n).astype(jnp.int32)
    return group, index - group * n


def level_and_core():
    return lax.axis_index("level").astype(jnp.int32), lax.axis_index("band").astype(jnp.int32) & 1


def band_offsets(swapped):
    unused, core = level_and_core()
    return (2 - 2 * core, 2 * core, 1) if swapped else (0, 2, 1)


def slot_place(senders, swapped):
    level, unused = level_and_core()
    distance = (level - ((senders >> 7) & 3)) & 3
    offset = senders >> 9
    source = jnp.where(offset == 1, 2, jnp.where(offset == band_offsets(swapped)[0], 0, 1))
    block = distance * 3 + source
    return block >> 1, ((block & 1) << 7) | (senders & 127)


def live(senders, counts_ref):
    peer = senders >> 7
    limit = jnp.zeros_like(senders)
    for j in range(12):
        limit = jnp.where(peer == j, counts_ref[0, j], limit)
    return ((senders & 127) < limit).astype(F32)


def choose(stacked, group, groups):
    picked = stacked[0:D]
    for j in range(1, groups):
        picked = jnp.where(group == j, stacked[j * D : (j + 1) * D], picked)
    return picked


def row_of(ref, k, start, size):
    rows = size // 128
    if not isinstance(start, int):
        start = pl.multiple_of(start // 128, rows)
        return jnp.concatenate([ref[k, pl.ds(start + r, 1), :] for r in range(rows)], axis=1)
    return jnp.concatenate([ref[k, r : r + 1, :] for r in range(start // 128, start // 128 + rows)], axis=1)


def pick(table, group, column, groups, n):
    return choose(dot(table[...], one_hot(column, n)), group, groups).astype(B16)


def spread(values, group, groups):
    wide = jnp.broadcast_to(group.astype(jnp.int16), values.shape)
    nothing = jnp.zeros_like(values)
    return jnp.concatenate([jnp.where(wide == j, values, nothing) for j in range(groups)], axis=0)


def add_at(total, values, group, column, groups, n):
    total[...] += dot_rows(spread(values, group, groups), one_hot(column, n))


def pack_table(table, source, groups, n):
    for j in range(groups):
        table[j * D : (j + 1) * D, :] = source[:, j * n : (j + 1) * n]


def columns_of(biases_ref, gains_ref, k):
    rows = [biases_ref[i, k : k + 1] for i in range(6)] + [gains_ref[k]]
    return jnp.concatenate(rows, axis=0).T


def fold(values):
    total = values[:, 0:128]
    for i in range(128, values.shape[1], 128):
        total = total + values[:, i : i + 128]
    return total


def norm_parts(values):
    centre = values - jnp.sum(values, axis=0, keepdims=True) * (1.0 / D)
    spread_sum = jnp.sum(centre * centre, axis=0, keepdims=True) * (1.0 / D)
    factor = lax.rsqrt(spread_sum + EPSILON)
    return centre * factor, factor


def norm_back(grad, normed, factor, gain):
    scaled = grad * gain
    first = jnp.sum(scaled, axis=0, keepdims=True) * (1.0 / D)
    second = jnp.sum(scaled * normed, axis=0, keepdims=True) * (1.0 / D)
    return factor * (scaled - first - normed * second)


def sigmoid(values):
    return 0.5 * jnp.tanh(0.5 * values) + 0.5


def send_rows(send_ref, offset):
    level, unused = level_and_core()
    return jnp.concatenate(
        [send_ref[pl.ds(offset * 4 + ((level + d) & 3), 1), :] for d in range(4)], axis=1
    )


def send_blocks(outs, table, send_ref, groups, n, swapped):
    for j, offset in enumerate(band_offsets(swapped)):
        group, column = place(send_rows(send_ref, offset), groups, n)
        rows = pick(table, group, column, groups, n)
        for d in range(4):
            outs[j][d] = rows[:, d * 128 : (d + 1) * 128]


def add_back(total, blocks, send_ref, groups, n, swapped):
    for j, offset in enumerate(band_offsets(swapped)):
        group, column = place(send_rows(send_ref, offset), groups, n)
        values = jnp.concatenate([block_at(blocks, d, j) for d in range(4)], axis=1)
        add_at(total, values, group, column, groups, n)


def block_at(received, d, j):
    return received[j][0] if d == 0 else received[2 + d][j]


def slot_table(table, received):
    for t in range(12):
        table[(t >> 1) * D : ((t >> 1) + 1) * D, (t & 1) * 128 : ((t & 1) + 1) * 128] = block_at(received, t // 3, t % 3)


def slot_gradients(outs, sums, weight):
    for j in range(SLOT_GROUPS):
        high, low = halves(sums[j * D : (j + 1) * D, :])
        grads = (dot(weight, high) + dot(weight, low)).astype(B16)
        for t in (2 * j, 2 * j + 1):
            outs[t % 3][t // 3] = grads[:, (t & 1) * 128 : ((t & 1) + 1) * 128]


def over_blocks(total, block, body):
    block = min(block, total)
    if block == total:
        body(pl.ds(0, block))
        return

    def step(i, carry):
        body(pl.ds(pl.multiple_of(i * block, block), block))
        return carry

    lax.fori_loop(0, total // block, step, 0)


def pipelined(stages, spans):
    held = [None] * len(spans)
    for t in range(len(spans) + len(stages) - 1):
        for k in reversed(range(len(stages))):
            i = t - k
            if 0 <= i < len(spans):
                held[i] = stages[k](spans[i], held[i])


def spans_of(parts, chunk):
    spans, start = [], 0
    for which, ref in enumerate(parts):
        size = min(chunk, ref.shape[1])
        for at in range(0, ref.shape[1], size):
            spans.append((which, pl.ds(at, size), pl.ds(start + at, size)))
        start += ref.shape[1]
    return spans


def tables_kernel(upper_rows, lower_rows, counts_up, counts_down, senders_up, targets_up, senders_down, targets_down,
                  index_up, alive_up, index_down, alive_down, limits_up, limits_down, sems):
    copies = [pltpu.make_async_copy(counts_up, limits_up, sems.at[0]), pltpu.make_async_copy(counts_down, limits_down, sems.at[1])]
    for copy in copies:
        copy.start()
    sweeps = ((index_up, senders_up, targets_up, upper_rows, True), (index_down, senders_down, targets_down, lower_rows, False))
    for index_ref, senders_ref, targets_ref, rows, swapped in sweeps:
        index_ref[0], index_ref[1] = place(targets_ref[...], *groups_of(rows))
        index_ref[2], index_ref[3] = slot_place(senders_ref[...], swapped)
    for copy in copies:
        copy.wait()
    alive_up[0] = live(senders_up[...], limits_up)
    alive_down[0] = live(senders_down[...], limits_down)


def send_kernel(count, *refs):
    sources, refs = refs[:count], refs[count:]
    sent, held, table, sems = refs[:3], refs[3:-2], refs[-2], refs[-1]
    copies = [pltpu.make_async_copy(a, b, sems.at[i]) for i, (a, b) in enumerate(zip(sources, held))]
    for copy in copies:
        copy.start()
    for copy in copies[:2]:
        copy.wait()
    send_ref, source_ref = held[:2]
    groups, n = groups_of(source_ref.shape[1])
    pack_table(table, source_ref, groups, n)
    send_blocks(sent, table, send_ref, groups, n, True)
    for copy in copies[2:]:
        copy.wait()


def part_kernel(k, block, index_ref, feat_ref, local_ref, w1_ref, biases_ref, gains_ref, *rest):
    part_ref, rows_ref, table, sem = rest[-4:]
    copy = pltpu.make_async_copy(feat_ref, rows_ref.at[0:D], sem)
    copy.start()
    groups, n = groups_of(local_ref.shape[1])
    pack_table(table, local_ref, groups, n)
    columns = columns_of(biases_ref, gains_ref, k)
    weight = jnp.concatenate([w1_ref[k, :, 0:D], w1_ref[k, :, 2 * D : 3 * D]], axis=1)

    def body(s):
        rows_ref[D : 2 * D, s] = pick(table, row_of(index_ref, 0, s.start, s.size), row_of(index_ref, 1, s.start, s.size), groups, n)

    over_blocks(feat_ref.shape[1], block, body)
    copy.wait()
    part_ref[...] = dot(weight, rows_ref[...]) + columns[:, 0:1]


def edges_forward(k, parts, alive_ref, index_ref, table, w1_ref, w2_ref, columns, total, groups, n,
                  slope_ref, normed_ref, hidden_ref, factor_ref):
    weight_slot = w1_ref[k, :, D : 2 * D]
    weight_two = w2_ref[k].astype(F32).T.astype(B16)
    total[...] = jnp.zeros_like(total)

    def slot_rows(span, unused):
        a, size = span[2].start, span[2].size
        return pick(table, row_of(index_ref, 2, a, size), row_of(index_ref, 3, a, size), SLOT_GROUPS, SLOT_COLS)

    def first_layer(span, picked):
        which, t, s = span
        first = parts[which][:, t] + dot(weight_slot, picked)
        gate = sigmoid(first)
        hidden = (first * gate).astype(B16)
        slope_ref[:, s] = gate * (1.0 + first * (1.0 - gate))
        hidden_ref[:, s] = hidden
        return hidden

    def second_layer(span, hidden):
        s = span[2]
        normed, factor = norm_parts(dot(weight_two, hidden) + columns[:, 1:2])
        alive = row_of(alive_ref, 0, s.start, s.size)
        normed_ref[:, s] = normed
        factor_ref[:, s] = factor
        return ((normed * columns[:, 6:7] + columns[:, 2:3]) * alive).astype(B16)

    def sum_messages(span, messages):
        a, size = span[2].start, span[2].size
        add_at(total, messages, row_of(index_ref, 0, a, size), row_of(index_ref, 1, a, size), groups, n)

    pipelined((slot_rows, first_layer, second_layer, sum_messages), spans_of(parts, CHUNK))


def node_first(k, inputs, wn1_ref, columns):
    first = dot(wn1_ref[k], inputs) + columns[:, 3:4]
    gate = sigmoid(first)
    return (first * gate).astype(B16), gate * (1.0 + first * (1.0 - gate))


def node_second(hidden, weight_two, columns):
    return norm_parts(dot(weight_two, hidden) + columns[:, 4:5])


def node_second_grad(grad, normed, factor, columns, sums_ref):
    sums_ref[2] += fold(grad)
    sums_ref[3] += fold(grad * normed)
    return norm_back(grad, normed, factor, columns[:, 7:8]).astype(B16)


def node_weight_grads(first, second, inputs, hidden, one_ref, two_ref, sums_ref):
    sums_ref[0] += fold(first.astype(F32))
    sums_ref[1] += fold(second.astype(F32))
    one_ref[...] += dot_rows(first, inputs)
    two_ref[...] += dot_rows(hidden, second)


def clear(refs):
    for ref in refs:
        ref[...] = jnp.zeros_like(ref)


def transposed(weight):
    return weight.astype(F32).T.astype(B16)


def edge_second(grad_rows, s, columns, weight_sum, alive_ref, normed_ref, factor_ref, sums_ref):
    grad = dot(weight_sum, grad_rows) * row_of(alive_ref, 0, s.start, s.size)
    normed = normed_ref[:, s]
    sums_ref[2] += fold(grad)
    sums_ref[3] += fold(grad * normed)
    return norm_back(grad, normed, factor_ref[:, s], columns[:, 6:7]).astype(B16)


def edge_first(second, s, weight_two, slope_ref):
    return (dot(weight_two, second) * slope_ref[:, s]).astype(B16)


def edge_weight_grads(first, second, rows, hidden, one_ref, two_ref, sums_ref):
    sums_ref[0] += fold(first.astype(F32))
    sums_ref[1] += fold(second.astype(F32))
    one_ref[...] += dot_rows(first, rows)
    two_ref[...] += dot_rows(hidden, second)


def pack_columns(edge_sums, node_sums):
    order = (edge_sums[0], edge_sums[1], edge_sums[2], node_sums[0], node_sums[1], node_sums[2], edge_sums[3], node_sums[3])
    columns = [jnp.sum(v, axis=1, keepdims=True) for v in order]
    lanes = lax.broadcasted_iota(jnp.int32, (D, D), 1)
    packed = jnp.zeros((D, D), F32)
    for i, column in enumerate(columns):
        packed = jnp.where(lanes == i, column, packed)
    return packed


def slot_weight_grads(sums, table):
    total = jnp.zeros((D, D), F32)
    for j in range(SLOT_GROUPS):
        high, low = halves(sums[j * D : (j + 1) * D, :])
        rows = table[j * D : (j + 1) * D, :]
        total = total + dot_rows(high, rows) + dot_rows(low, rows)
    return total


def target_grads(total, weight, start, out_ref, groups, n):
    for j in range(groups):
        high, low = halves(total[j * D : (j + 1) * D, :])
        out_ref[:, j * n : (j + 1) * n] = start(j) + dot(weight, high) + dot(weight, low)


def up_forward_kernel(part_ref, alive_ref, index_ref, r0, r1, r2, r3, r4, r5, local_ref, send_ref,
                      w1_ref, w2_ref, wn1_ref, wn2_ref, biases_ref, gains_ref,
                      out_ref, summed_ref, s0, s1, s2, slope_ref, normed_ref, hidden_ref, factor_ref,
                      slots, total, table, out, sem):
    groups, n = groups_of(local_ref.shape[1])
    columns = columns_of(biases_ref, gains_ref, 0)
    slot_table(slots, (r0, r1, r2, r3, r4, r5))
    edges_forward(0, (part_ref,), alive_ref, index_ref, slots, w1_ref, w2_ref, columns, total, groups, n,
                  slope_ref, normed_ref, hidden_ref, factor_ref)
    weight_two = transposed(wn2_ref[0])

    def first_layer(j, unused):
        s = slice(j * n, (j + 1) * n)
        summed = total[j * D : (j + 1) * D, :].astype(B16)
        summed_ref[:, s] = summed
        return node_first(0, jnp.concatenate([local_ref[:, s], summed], axis=0), wn1_ref, columns)

    def second_layer(j, held):
        s = slice(j * n, (j + 1) * n)
        normed, unused = node_second(held[0], weight_two, columns)
        result = local_ref[:, s].astype(F32) + normed * columns[:, 7:8] + columns[:, 5:6]
        out[:, s] = result
        table[j * D : (j + 1) * D, :] = result.astype(B16)

    pipelined((first_layer, second_layer), range(groups))
    copy = pltpu.make_async_copy(out, out_ref, sem)
    copy.start()
    send_blocks((s0, s1, s2), table, send_ref, groups, n, False)
    copy.wait()


def down_kernel(part_ref, alive_ref, index_ref, r0, r1, r2, r3, r4, r5, local_ref, cot_ref,
                w1_ref, w2_ref, wn1_ref, wn2_ref, biases_ref, gains_ref,
                out_ref, g0, g1, g2, first_ref, second_ref, hidden_ref, sums_ref, edge_sums, node_sums,
                table, summed_ref, node_hidden_ref, node_second_ref,
                slots, total, slope_ref, normed_ref, factor_ref, out, sem):
    groups, n = groups_of(local_ref.shape[1])
    columns = columns_of(biases_ref, gains_ref, 1)
    slot_table(slots, (r0, r1, r2, r3, r4, r5))
    parts = (part_ref,)
    edges_forward(1, parts, alive_ref, index_ref, slots, w1_ref, w2_ref, columns, total, groups, n,
                  slope_ref, normed_ref, hidden_ref, factor_ref)
    clear((node_sums, edge_sums, sums_ref))
    wn2 = wn2_ref[1]
    wn2_t = transposed(wn2)
    wn1 = transposed(wn1_ref[1])

    def first_layer(j, unused):
        summed = total[j * D : (j + 1) * D, :].astype(B16)
        summed_ref[j * D : (j + 1) * D, :] = summed
        inputs = jnp.concatenate([local_ref[:, j * n : (j + 1) * n], summed], axis=0)
        return node_first(1, inputs, wn1_ref, columns)

    def second_layer(j, held):
        hidden, slope = held
        s = slice(j * n, (j + 1) * n)
        normed, factor = node_second(hidden, wn2_t, columns)
        out[:, s] = local_ref[:, s].astype(F32) + normed * columns[:, 7:8] + columns[:, 5:6]
        second = node_second_grad(cot_ref[:, s], normed, factor, columns, node_sums)
        node_hidden_ref[:, s] = hidden
        node_second_ref[:, s] = second
        return slope, second

    def node_grads(j, held):
        slope, second = held
        table[j * D : (j + 1) * D, :] = (dot(wn2, second) * slope).astype(B16)

    pipelined((first_layer, second_layer, node_grads), range(groups))
    copy = pltpu.make_async_copy(out, out_ref, sem)
    copy.start()
    weight_two = w2_ref[1]
    weight_slot = transposed(w1_ref[1, :, D : 2 * D])

    def grad_rows(span, unused):
        a, size = span[2].start, span[2].size
        return pick(table, row_of(index_ref, 0, a, size), row_of(index_ref, 1, a, size), groups, n)

    def second_grad(span, rows):
        return edge_second(rows, span[2], columns, wn1[D : 2 * D], alive_ref, normed_ref, factor_ref, edge_sums)

    def first_grad(span, second):
        s = span[2]
        first = edge_first(second, s, weight_two, slope_ref)
        first_ref[:, s] = first
        second_ref[:, s] = second
        return first

    def sum_slots(span, first):
        a, size = span[2].start, span[2].size
        add_at(sums_ref, first, row_of(index_ref, 2, a, size), row_of(index_ref, 3, a, size), SLOT_GROUPS, SLOT_COLS)

    pipelined((grad_rows, second_grad, first_grad, sum_slots), spans_of(parts, CHUNK))
    slot_gradients((g0, g1, g2), sums_ref, weight_slot)
    copy.wait()


def down_targets_kernel(index_ref, first_ref, cot_ref, table, w1_ref, wn1_ref, *rest):
    grad_ref, total = rest[-2:]
    groups, n = groups_of(cot_ref.shape[1])
    weight = transposed(w1_ref[1, :, 2 * D : 3 * D])
    total[...] = jnp.zeros_like(total)

    def body(s):
        group, column = row_of(index_ref, 0, s.start, s.size), row_of(index_ref, 1, s.start, s.size)
        add_at(total, first_ref[:, s], group, column, groups, n)

    over_blocks(first_ref.shape[1], EDGE_BLOCK, body)
    weight_node = transposed(wn1_ref[1, :, 0:D])

    def start(j):
        return cot_ref[:, j * n : (j + 1) * n] + dot(weight_node, table[j * D : (j + 1) * D, :])

    target_grads(total, weight, start, grad_ref, groups, n)


def down_rest_kernel(rows_ref, first_ref, second_ref, hidden_ref, r0, r1, r2, r3, r4, r5, sums_ref, edge_in, node_in,
                     table, summed_ref, node_hidden_ref, node_second_ref, local_ref, w1_ref, *rest):
    feat_grad_ref, packed_ref, slots, one_ref, two_ref, wn1_grad, wn2_grad, edge_sums, node_sums = rest[-9:]
    step = pl.program_id(0)
    weight = transposed(w1_ref[1, :, 0:D])

    @pl.when(step == 0)
    def _():
        clear((one_ref, two_ref, wn1_grad, wn2_grad))
        edge_sums[...] = edge_in[...]
        node_sums[...] = node_in[...]

    s = pl.ds(pl.multiple_of(step * EDGE_BLOCK, EDGE_BLOCK), EDGE_BLOCK)
    first = first_ref[:, s]
    feat_grad_ref[...] = dot(weight, first)
    edge_weight_grads(first, second_ref[:, s], rows_ref[:, s], hidden_ref[:, s], one_ref, two_ref, edge_sums)

    @pl.when(step == pl.num_programs(0) - 1)
    def _():
        groups, n = groups_of(local_ref.shape[1])
        for j in range(groups):
            t, rows = slice(j * n, (j + 1) * n), slice(j * D, (j + 1) * D)
            inputs = jnp.concatenate([local_ref[:, t], summed_ref[rows, :]], axis=0)
            node_weight_grads(table[rows, :], node_second_ref[:, t], inputs, node_hidden_ref[:, t], wn1_grad, wn2_grad, node_sums)
        slot_table(slots, (r0, r1, r2, r3, r4, r5))
        write_packed(packed_ref, one_ref[...], slot_weight_grads(sums_ref, slots), two_ref[...],
                     wn1_grad[...], wn2_grad[...], pack_columns(edge_sums, node_sums))


def write_packed(packed_ref, one, slot_grads, two, wn1_grad, wn2_grad, columns):
    packed_ref[0] = jnp.concatenate([one[:, 0:D], slot_grads], axis=1)
    packed_ref[1] = jnp.concatenate([one[:, D : 2 * D], two], axis=1)
    packed_ref[2] = wn1_grad
    packed_ref[3] = jnp.concatenate([wn2_grad, columns], axis=1)


def up_backward_kernel(index_ref, rows_ref, h0, h1, h2, h3, h4, h5,
                       send_ref, cot_ref, local_ref, summed_ref, r0, r1, r2, r3, r4, r5, slope_ref, normed_ref, hidden_ref, factor_ref, alive_ref, packed_down_ref,
                       w1_ref, w2_ref, wn1_ref, wn2_ref, biases_ref, gains_ref,
                       partner_ref, cross_ref, own_ref, first_ref, grad_ref, keep_ref,
                       slots, table, back, total, sums, start, one_ref, two_ref, edge_sums, node_sums, wn1_grad, wn2_grad, pieces):
    groups, n = groups_of(local_ref.shape[1])
    columns = columns_of(biases_ref, gains_ref, 0)
    clear((back, total, sums, one_ref, two_ref, edge_sums, node_sums, wn1_grad, wn2_grad))
    slot_table(slots, (r0, r1, r2, r3, r4, r5))
    add_back(back, (h0, h1, h2, h3, h4, h5), send_ref, groups, n, False)
    wn2 = wn2_ref[0]
    wn2_t = transposed(wn2)
    wn1 = transposed(wn1_ref[0])
    w1 = transposed(w1_ref[0])

    def first_layer(j, unused):
        s = slice(j * n, (j + 1) * n)
        inputs = jnp.concatenate([local_ref[:, s], summed_ref[:, s]], axis=0)
        return inputs, *node_first(0, inputs, wn1_ref, columns)

    def second_layer(j, held):
        inputs, hidden, slope = held
        grad = cot_ref[:, j * n : (j + 1) * n] + back[j * D : (j + 1) * D, :]
        normed, factor = node_second(hidden, wn2_t, columns)
        return inputs, hidden, slope, grad, node_second_grad(grad, normed, factor, columns, node_sums)

    def node_grads(j, held):
        inputs, hidden, slope, grad, second = held
        first = (dot(wn2, second) * slope).astype(B16)
        node_weight_grads(first, second, inputs, hidden, wn1_grad, wn2_grad, node_sums)
        table[j * D : (j + 1) * D, :] = first
        start[:, j * n : (j + 1) * n] = grad + dot(wn1[0:D], first)

    pipelined((first_layer, second_layer, node_grads), range(groups))
    weight_two = w2_ref[0]

    def grad_rows(span, unused):
        a, size = span[2].start, span[2].size
        return pick(table, row_of(index_ref, 0, a, size), row_of(index_ref, 1, a, size), groups, n)

    def second_grad(span, rows):
        return edge_second(rows, span[2], columns, wn1[D : 2 * D], alive_ref, normed_ref, factor_ref, edge_sums)

    def first_grad(span, second):
        s = span[2]
        first = edge_first(second, s, weight_two, slope_ref)
        first_ref[:, s] = first
        edge_weight_grads(first, second, rows_ref[:, s], hidden_ref[:, s], one_ref, two_ref, edge_sums)
        return first

    def sum_rows(span, first):
        s = span[2]
        rows = [row_of(index_ref, i, s.start, s.size) for i in range(4)]
        add_at(total, first, rows[0], rows[1], groups, n)
        add_at(sums, first, rows[2], rows[3], SLOT_GROUPS, SLOT_COLS)

    pipelined((grad_rows, second_grad, first_grad, sum_rows), spans_of((first_ref,), CHUNK))
    slot_gradients((partner_ref, cross_ref, own_ref), sums, w1[D : 2 * D])
    target_grads(total, w1[2 * D : 3 * D], lambda j: start[:, j * n : (j + 1) * n], grad_ref, groups, n)
    slot_grads = slot_weight_grads(sums, slots)
    write_packed(pieces, one_ref[...], slot_grads, two_ref[...], wn1_grad[...], wn2_grad[...],
                 pack_columns(edge_sums, node_sums))
    unused, core = level_and_core()
    for p in range(4):
        pieces[4 + p] = packed_down_ref[p]
    for p in range(4):
        keep_ref[p] = pieces[core * 4 + p]
        partner_ref[4 + p] = pieces[(1 - core) * 4 + p].astype(B16)


def feat_grad_kernel(first_ref, w1_ref, *rest):
    out_ref = rest[-1]
    out_ref[...] = dot(transposed(w1_ref[0, :, 0:D]), first_ref[...])


def lower_grad_kernel(h0, h1, h2, h3, h4, h5, send_ref, start_ref, out_ref, total):
    groups, n = groups_of(start_ref.shape[1])
    clear((total,))
    add_back(total, (h0, h1, h2, h3, h4, h5), send_ref, groups, n, True)
    for j in range(groups):
        s = slice(j * n, (j + 1) * n)
        out_ref[:, s] = start_ref[:, s] + total[j * D : (j + 1) * D, :]


def unpack_kernel(own_ref, other_ref, w1_ref, w2_ref, wn1_ref, wn2_ref, biases_ref, gains_ref, pieces):
    unused, core = level_and_core()
    for p in range(4):
        pieces[core * 4 + p] = own_ref[p].astype(F32)
        pieces[(1 - core) * 4 + p] = other_ref[p].astype(F32)
    for k in range(2):
        w1_ref[k] = jnp.concatenate([pieces[4 * k], pieces[4 * k + 1, :, 0:D]], axis=1)
        w2_ref[k] = pieces[4 * k + 1, :, D : 2 * D]
        wn1_ref[k] = pieces[4 * k + 2]
        wn2_ref[k] = pieces[4 * k + 3, :, 0:D]
        rows = pieces[4 * k + 3].T
        for i in range(6):
            biases_ref[i, k : k + 1] = rows[D + i : D + i + 1]
        gains_ref[k] = rows[D + 6 : D + 8]


def shape(dims, dtype=F32):
    return jax.ShapeDtypeStruct(dims, dtype)


def call(kernel, name, outs, scratch, scalars=0, stored=(), streamed=None, final=(), raw=()):
    steps, stream_in, stream_out = streamed if streamed else (1, (), ())

    def run(*operands, after=()):
        def whole(space):
            return pl.BlockSpec(memory_space=space)

        def cut(x):
            return pl.BlockSpec((x.shape[0], x.shape[1] // steps), lambda i: (0, i))

        in_specs, placed = [], []
        for i, x in enumerate(operands):
            if i < scalars:
                in_specs.append(whole(pltpu.SMEM))
            elif i in stream_in:
                in_specs.append(cut(x))
            elif i in raw:
                in_specs.append(whole(pltpu.HBM))
                x = pltpu.with_memory_space_constraint(x, pltpu.HBM)
            else:
                in_specs.append(whole(pltpu.VMEM))
                x = pltpu.with_memory_space_constraint(x, pltpu.VMEM)
            placed.append(x)
        in_specs += [whole(pl.ANY) for _ in after]
        out_specs, out_shape = [], []
        for i, x in enumerate(outs):
            if i in stream_out:
                out_specs.append(cut(x))
                out_shape.append(x)
            elif i in stored:
                out_specs.append(whole(pl.ANY))
                out_shape.append(x)
            elif i in final:
                out_specs.append(whole(pltpu.VMEM))
                out_shape.append(x)
            else:
                out_specs.append(whole(pltpu.VMEM))
                out_shape.append(pltpu.VMEM(x.shape, x.dtype))
        return pl.pallas_call(
            kernel,
            name=name,
            grid=(steps,) if streamed else (),
            in_specs=in_specs,
            out_specs=out_specs,
            out_shape=out_shape,
            scratch_shapes=scratch,
            compiler_params=pltpu.CompilerParams(vmem_limit_bytes=VMEM_BYTES),
        )(*placed, *after)

    return run


def core_swap(block):
    return lax.ppermute(block, "band", [(i, i ^ 1) for i in range(lax.axis_size("band"))])


def cross_swap(block):
    last = lax.axis_size("band") - 1
    pairs = [(i, i + 1) for i in range(1, last, 2)]
    return lax.ppermute(block, "band", pairs + [(b, a) for a, b in pairs] + [(0, 0), (last, last)])


def along_level(block, step):
    count = lax.axis_size("level")
    return lax.ppermute(block, "level", [(i, (i + step) % count) for i in range(count)])


def along_band(block, step):
    count = lax.axis_size("band")
    return lax.ppermute(block, "band", [(i, (i + step) % count) for i in range(count)])


def across_bands(blocks):
    below, above, own = blocks
    return [along_band(above, 1), along_band(below, -1), own]


def along_levels(blocks, sign):
    return blocks + [along_level(jnp.stack([b[d] for b in blocks]), sign * d) for d in (1, 2, 3)]


def chip_ring(block, step, core_strides):
    count = lax.axis_size("band")
    pairs = []
    for i in range(count):
        stride = core_strides[i % 2]
        at = (i // stride) % 4
        pairs.append((i, i + (((at + step) % 4) - at) * stride))
    return lax.ppermute(block, "band", pairs)


def rounded(values):
    return lax.reduce_precision(values, 8, 7)


def sum_of_four(values, first, second, third):
    return (values + second.astype(F32)) + (first.astype(F32) + third.astype(F32))


def sum_along(values, core_strides):
    own = rounded(values)
    sent = own.astype(B16)
    return sum_of_four(own, *(chip_ring(sent, d, core_strides) for d in (1, 2, 3)))


def shards(
    lower_nodes, latent, up_feat, down_feat, up_send, up_counts, up_senders, up_targets,
    down_send, down_counts, down_senders, down_targets,
    edge_w1, edge_w2, node_w1, node_w2, biases, norm_gains, lower_cot, upper_cot,
):
    lower, upper = lower_nodes.T, latent.T
    feat_up, feat_down = up_feat.T, down_feat.T
    cot_lower, cot_upper = lower_cot.T, upper_cot.T
    w1, wn1 = edge_w1.transpose(0, 2, 1), node_w1.transpose(0, 2, 1)
    w2, wn2 = edge_w2, node_w2
    edges, lower_rows, upper_rows = up_feat.shape[0], lower_nodes.shape[0], latent.shape[0]
    dense = (edges // 128, 128)
    senders_up, targets_up, senders_down, targets_down = (
        x.reshape(dense) for x in (up_senders, up_targets, down_senders, down_targets))
    bias_rows = biases.transpose(1, 0, 2)

    lower_groups, lower_n = groups_of(lower_rows)
    upper_groups, upper_n = groups_of(upper_rows)
    lower_table, upper_table = (lower_groups * D, lower_n), (upper_groups * D, upper_n)
    slots = pltpu.VMEM((SLOT_GROUPS * D, SLOT_COLS), B16)
    block, four = shape((4, D, 128), B16), shape((4, D, 128))
    wide32, wide16, row = shape((D, edges)), shape((D, edges), B16), shape((1, edges))
    steps = edges // EDGE_BLOCK

    early = (up_send, lower, senders_up, targets_up, senders_down, targets_down, upper, w1, bias_rows, norm_gains,
             down_send, w2, wn1, wn2)
    count = len(early)
    (*sent, up_send, lower, senders_up, targets_up, senders_down, targets_down, upper, w1, bias_rows,
     norm_gains, down_send, w2, wn1, wn2) = call(
        functools.partial(send_kernel, count), "send_lower", [block] * 3 + [shape(x.shape, x.dtype) for x in early],
        [pltpu.VMEM(lower_table, B16), pltpu.SemaphoreType.DMA((count,))], 0, raw=range(count),
    )(*early)
    index, lives = shape((4, *dense), jnp.int32), shape((1, *dense))
    index_up, alive_up, index_down, alive_down = call(
        functools.partial(tables_kernel, upper_rows, lower_rows), "edge_tables", [index, lives, index, lives],
        [pltpu.SMEM((1, 12), jnp.int32), pltpu.SMEM((1, 12), jnp.int32), pltpu.SemaphoreType.DMA((2,))], 0, raw=(0, 1),
    )(up_counts, down_counts, senders_up, targets_up, senders_down, targets_down)

    def part(k, block, name, table, index, feat, local, after):
        return call(
            functools.partial(part_kernel, k, block), name, [wide32, shape((2 * D, edges), B16)],
            [pltpu.VMEM(table, B16), pltpu.SemaphoreType.DMA], 0, raw=(1,),
        )(index, feat, local, w1, bias_rows, norm_gains, after=after)

    sent = [core_swap(sent[0]), cross_swap(sent[1]), sent[2]]
    sent, alive_up = lax.optimization_barrier((sent, alive_up))
    part_up, rows_up = part(0, EDGE_BLOCK, "part_up", upper_table, index_up, feat_up, upper, (sent[0], sent[1]))
    up_slots = along_levels(sent, 1)
    up_slots, part_up = lax.optimization_barrier((up_slots, part_up))
    (upper_new, summed_up, s0, s1, s2, slope, normed, hidden, factor) = call(
        up_forward_kernel, "up_forward",
        [shape((D, upper_rows)), shape((D, upper_rows), B16)] + [block] * 3 + [wide32, wide32, wide16, row],
        [slots, pltpu.VMEM(upper_table, F32), pltpu.VMEM(upper_table, B16), pltpu.VMEM((D, upper_rows), F32),
         pltpu.SemaphoreType.DMA], 0, (0,),
    )(part_up, alive_up, index_up, *up_slots, upper, down_send, w1, w2, wn1, wn2, bias_rows, norm_gains)
    sent = across_bands([s0, s1, s2])
    part_down, rows_down = part(1, EDGE_BLOCK, "part_down", lower_table, index_down, feat_down, lower, (sent[0], sent[1]))
    down_slots = along_levels(sent, 1)
    down_slots, part_down = lax.optimization_barrier((down_slots, part_down))
    sums_shape = shape((SLOT_GROUPS * D, SLOT_COLS))
    node16 = shape((D, lower_rows), B16)
    (lower_new, g0, g1, g2, first_down, second_down, hidden_down, sums_down, edge_sums, node_sums, *nodes) = call(
        down_kernel, "down_sweep",
        [shape((D, lower_rows))] + [block] * 3 + [wide16] * 3 + [sums_shape, four, four, shape(lower_table, B16),
         shape(lower_table, B16), node16, node16],
        [slots, pltpu.VMEM(lower_table, F32), pltpu.VMEM((D, edges), F32),
         pltpu.VMEM((D, edges), F32), pltpu.VMEM((1, edges), F32),
         pltpu.VMEM((D, lower_rows), F32), pltpu.SemaphoreType.DMA], 0, (0,),
    )(part_down, alive_down, index_down, *down_slots, lower, cot_lower, w1, w2, wn1, wn2, bias_rows, norm_gains)
    back = across_bands([g0, g1, g2])
    feat_grad_down, packed_down = call(
        down_rest_kernel, "down_rest", [wide32, four],
        [slots, pltpu.VMEM((D, 2 * D), F32), pltpu.VMEM((D, D), F32), pltpu.VMEM((D, 2 * D), F32), pltpu.VMEM((D, D), F32),
         pltpu.VMEM((4, D, 128), F32), pltpu.VMEM((4, D, 128), F32)], 0, (), (steps, (), (0,)),
    )(rows_down, first_down, second_down, hidden_down, *down_slots, sums_down, edge_sums, node_sums, *nodes, lower, w1,
      after=(back[0], back[1]))
    down_back = along_levels(back, -1)
    down_back, packed_down = lax.optimization_barrier((down_back, packed_down))
    (partner, cross, own, first_up, grad_latent, keep) = call(
        up_backward_kernel, "up_backward",
        [shape((8, D, 128), B16), block, block, wide16, shape((D, upper_rows)), four],
        [slots, pltpu.VMEM(upper_table, B16), pltpu.VMEM(upper_table, F32), pltpu.VMEM(upper_table, F32),
         pltpu.VMEM((SLOT_GROUPS * D, SLOT_COLS), F32), pltpu.VMEM((D, upper_rows), F32),
         pltpu.VMEM((D, 2 * D), F32), pltpu.VMEM((D, D), F32), pltpu.VMEM((4, D, 128), F32), pltpu.VMEM((4, D, 128), F32),
         pltpu.VMEM((D, 2 * D), F32), pltpu.VMEM((D, D), F32), pltpu.VMEM((8, D, 128), F32)], 0, (), None, (4,),
    )(index_up, rows_up, *down_back, down_send, cot_upper, upper, summed_up, *up_slots,
      slope, normed, hidden, factor, alive_up, packed_down, w1, w2, wn1, wn2, bias_rows, norm_gains)

    partner = core_swap(partner)
    total = rounded(rounded(keep) + partner[4:].astype(F32))
    cross, keep = lax.optimization_barrier((cross, total))
    cross = cross_swap(cross)
    total = sum_along(total, (2, 8))
    (feat_grad_up,) = call(feat_grad_kernel, "feat_grad_up", [wide32], [], 0, (), (steps, (0,), (0,)))(
        first_up, w1, after=(partner,))
    total, cross, feat_grad_up = lax.optimization_barrier((total, cross, feat_grad_up))
    blocks = (partner, cross, own)
    total = rounded(total)
    levels = [
        along_level(jnp.concatenate([jnp.stack([b[d] for b in blocks]), total.astype(B16)]), -d) for d in (1, 2, 3)
    ]
    (start_lower,) = call(
        down_targets_kernel, "down_targets", [shape((D, lower_rows))], [pltpu.VMEM(lower_table, F32)],
    )(index_down, first_down, cot_lower, nodes[0], w1, wn1, after=(total,))
    levels, start_lower = lax.optimization_barrier((levels, start_lower))
    total = sum_of_four(total, *(b[3:] for b in levels))
    (grad_lower,) = call(lower_grad_kernel, "lower_grad", [shape((D, lower_rows))], [pltpu.VMEM(lower_table, F32)], 0, (), None, (0,))(
        *blocks, *levels, up_send, start_lower)
    total = sum_along(total, (8, 2))
    total, grad_lower = lax.optimization_barrier((total, grad_lower))
    total = rounded(total).astype(B16)
    w1_grad, w2_grad, wn1_grad, wn2_grad, bias_grad, gain_grad = call(
        unpack_kernel, "unpack",
        [shape((2, D, 3 * D)), shape((2, D, D)), shape((2, D, 2 * D)), shape((2, D, D)), shape((6, 2, D)), shape((2, 2, D))],
        [pltpu.VMEM((8, D, 128), F32)], 0, (), None, range(6))(total, core_swap(total))
    return (
        lower_new.T, upper_new.T, grad_lower.T, grad_latent.T, feat_grad_up.T, feat_grad_down.T,
        w1_grad.transpose(0, 2, 1), w2_grad, wn1_grad.transpose(0, 2, 1), wn2_grad, bias_grad.transpose(1, 0, 2), gain_grad,
    )


def solution(mesh):
    rows, index, whole = P(("band", "level"), None), P(("band", "level")), P()
    placed = (rows,) * 6 + (index, index) + (rows,) * 2 + (index, index) + (whole,) * 6 + (rows,) * 2
    return jax.shard_map(
        shards,
        mesh=mesh,
        in_specs=placed,
        out_specs=(rows,) * 6 + (whole,) * 6,
        check_vma=False,
    )
```

```python
import functools

import jax
import jax.numpy as jnp
from jax import lax
from jax.experimental import pallas as pl
from jax.experimental.pallas import tpu as pltpu
from jax.sharding import PartitionSpec as P

EPSILON = 1e-05
F32 = jnp.float32
B16 = jnp.bfloat16
D = 64
SLOT_GROUPS, SLOT_COLS = 6, 256
EDGE_BLOCK = 3072
CHUNK = 1024
VMEM_BYTES = 24 * 1024 * 1024


def groups_of(rows):
    return (4, rows // 4) if rows > 1024 else (rows // 256, 256)


def dot(a, b):
    return jnp.dot(a, b, preferred_element_type=F32)


def dot_rows(a, b):
    return lax.dot_general(a, b, (((1,), (1,)), ((), ())), preferred_element_type=F32)


def halves(x):
    high = x.astype(B16)
    return high, (x - high.astype(F32)).astype(B16)


def one_hot(column, n):
    rows = lax.broadcasted_iota(jnp.int16, (n, column.shape[1]), 0)
    return jnp.where(rows == column.astype(jnp.int16), jnp.ones((), B16), jnp.zeros((), B16))


def place(index, groups, n):
    group = jnp.zeros_like(index)
    for j in range(1, groups):
        group = group + (index >= j * n).astype(jnp.int32)
    return group, index - group * n


def level_and_core():
    return lax.axis_index("level").astype(jnp.int32), lax.axis_index("band").astype(jnp.int32) & 1


def band_offsets(swapped):
    unused, core = level_and_core()
    return (2 - 2 * core, 2 * core, 1) if swapped else (0, 2, 1)


def slot_place(senders, swapped):
    level, unused = level_and_core()
    distance = (level - ((senders >> 7) & 3)) & 3
    offset = senders >> 9
    source = jnp.where(offset == 1, 2, jnp.where(offset == band_offsets(swapped)[0], 0, 1))
    block = distance * 3 + source
    return block >> 1, ((block & 1) << 7) | (senders & 127)


def live(senders, counts_ref):
    peer = senders >> 7
    limit = jnp.zeros_like(senders)
    for j in range(12):
        limit = jnp.where(peer == j, counts_ref[0, j], limit)
    return ((senders & 127) < limit).astype(F32)


def choose(stacked, group, groups):
    picked = stacked[0:D]
    for j in range(1, groups):
        picked = jnp.where(group == j, stacked[j * D : (j + 1) * D], picked)
    return picked


def row_of(ref, k, start, size):
    rows = size // 128
    if not isinstance(start, int):
        start = start // 128
        return jnp.concatenate([ref[k, pl.ds(start + r, 1), :] for r in range(rows)], axis=1)
    return jnp.concatenate([ref[k, r : r + 1, :] for r in range(start // 128, start // 128 + rows)], axis=1)


def pick(table, group, column, groups, n):
    return choose(dot(table[...], one_hot(column, n)), group, groups).astype(B16)


def spread(values, group, groups):
    wide = jnp.broadcast_to(group.astype(jnp.int16), values.shape)
    nothing = jnp.zeros_like(values)
    return jnp.concatenate([jnp.where(wide == j, values, nothing) for j in range(groups)], axis=0)


def add_at(total, values, group, column, groups, n):
    total[...] += dot_rows(spread(values, group, groups), one_hot(column, n))


def pack_table(table, source, groups, n):
    for j in range(groups):
        table[j * D : (j + 1) * D, :] = source[:, j * n : (j + 1) * n]


def columns_of(biases_ref, gains_ref, k):
    rows = [biases_ref[i, k : k + 1] for i in range(6)] + [gains_ref[k]]
    return jnp.concatenate(rows, axis=0).T


def fold(values):
    total = values[:, 0:128]
    for i in range(128, values.shape[1], 128):
        total = total + values[:, i : i + 128]
    return total


def norm_parts(values):
    centre = values - jnp.sum(values, axis=0, keepdims=True) * (1.0 / D)
    spread_sum = jnp.sum(centre * centre, axis=0, keepdims=True) * (1.0 / D)
    factor = lax.rsqrt(spread_sum + EPSILON)
    return centre * factor, factor


def norm_back(grad, normed, factor, gain):
    scaled = grad * gain
    first = jnp.sum(scaled, axis=0, keepdims=True) * (1.0 / D)
    second = jnp.sum(scaled * normed, axis=0, keepdims=True) * (1.0 / D)
    return factor * (scaled - first - normed * second)


def sigmoid(values):
    return 0.5 * jnp.tanh(0.5 * values) + 0.5


def send_rows(send_ref, offset):
    level, unused = level_and_core()
    return jnp.concatenate(
        [send_ref[pl.ds(offset * 4 + ((level + d) & 3), 1), :] for d in range(4)], axis=1
    )


def send_blocks(outs, table, send_ref, groups, n, swapped):
    for j, offset in enumerate(band_offsets(swapped)):
        group, column = place(send_rows(send_ref, offset), groups, n)
        rows = pick(table, group, column, groups, n)
        for d in range(4):
            outs[j][d] = rows[:, d * 128 : (d + 1) * 128]


def add_back(total, blocks, send_ref, groups, n, swapped):
    for j, offset in enumerate(band_offsets(swapped)):
        group, column = place(send_rows(send_ref, offset), groups, n)
        values = jnp.concatenate([block_at(blocks, d, j) for d in range(4)], axis=1)
        add_at(total, values, group, column, groups, n)


def block_at(received, d, j):
    return received[j][0] if d == 0 else received[2 + d][j]


def slot_table(table, received):
    for t in range(12):
        table[(t >> 1) * D : ((t >> 1) + 1) * D, (t & 1) * 128 : ((t & 1) + 1) * 128] = block_at(received, t // 3, t % 3)


def slot_gradients(outs, sums, weight):
    for j in range(SLOT_GROUPS):
        high, low = halves(sums[j * D : (j + 1) * D, :])
        grads = (dot(weight, high) + dot(weight, low)).astype(B16)
        for t in (2 * j, 2 * j + 1):
            outs[t % 3][t // 3] = grads[:, (t & 1) * 128 : ((t & 1) + 1) * 128]


def over_blocks(total, block, body):
    block = min(block, total)
    if block == total:
        body(pl.ds(0, block))
        return

    def step(i, carry):
        body(pl.ds(pl.multiple_of(i * block, block), block))
        return carry

    lax.fori_loop(0, total // block, step, 0)


def pipelined(stages, spans):
    held = [None] * len(spans)
    for t in range(len(spans) + len(stages) - 1):
        for k in reversed(range(len(stages))):
            i = t - k
            if 0 <= i < len(spans):
                held[i] = stages[k](spans[i], held[i])


def spans_of(parts, chunk):
    spans, start = [], 0
    for which, ref in enumerate(parts):
        size = min(chunk, ref.shape[1])
        for at in range(0, ref.shape[1], size):
            spans.append((which, pl.ds(at, size), pl.ds(start + at, size)))
        start += ref.shape[1]
    return spans


def tables_kernel(upper_rows, lower_rows, counts_up, counts_down, senders_up, targets_up, senders_down, targets_down,
                  w1_ref, w2_ref, wn1_ref, wn2_ref, biases_ref, gains_ref, index_up, alive_up, index_down, alive_down, columns_ref, w1t_ref, w2t_ref, wn1t_ref, wn2t_ref, limits_up, limits_down, sems):
    copies = [pltpu.make_async_copy(counts_up, limits_up, sems.at[0]), pltpu.make_async_copy(counts_down, limits_down, sems.at[1])]
    for copy in copies:
        copy.start()
    sweeps = ((index_up, senders_up, targets_up, upper_rows, True), (index_down, senders_down, targets_down, lower_rows, False))
    for index_ref, senders_ref, targets_ref, rows, swapped in sweeps:
        index_ref[0], index_ref[1] = place(targets_ref[...], *groups_of(rows))
        index_ref[2], index_ref[3] = slot_place(senders_ref[...], swapped)
    for k in range(2):
        columns_ref[k] = columns_of(biases_ref, gains_ref, k)
        for turned, ref in ((w1t_ref, w1_ref), (w2t_ref, w2_ref), (wn1t_ref, wn1_ref), (wn2t_ref, wn2_ref)):
            turned[k] = transposed(ref[k])
    for copy in copies:
        copy.wait()
    alive_up[0] = live(senders_up[...], limits_up)
    alive_down[0] = live(senders_down[...], limits_down)


def send_kernel(count, *refs):
    sources, refs = refs[:count], refs[count:]
    sent, held, table, sems = refs[:3], refs[3:-2], refs[-2], refs[-1]
    copies = [pltpu.make_async_copy(a, b, sems.at[i]) for i, (a, b) in enumerate(zip(sources, held))]
    for copy in copies:
        copy.start()
    for copy in copies[:2]:
        copy.wait()
    send_ref, source_ref = held[:2]
    groups, n = groups_of(source_ref.shape[1])
    pack_table(table, source_ref, groups, n)
    send_blocks(sent, table, send_ref, groups, n, True)
    for copy in copies[2:]:
        copy.wait()


def part_kernel(k, block, first, index_ref, feat_ref, local_ref, w1_ref, columns_ref, *rest):
    part_ref, rows_ref, table, sem = rest[-4:]
    size = part_ref.shape[1]
    copy = pltpu.make_async_copy(feat_ref.at[:, pl.ds(first, size)], rows_ref.at[0:D], sem)
    copy.start()
    groups, n = groups_of(local_ref.shape[1])
    pack_table(table, local_ref, groups, n)
    columns = columns_ref[k]
    weight = jnp.concatenate([w1_ref[k, :, 0:D], w1_ref[k, :, 2 * D : 3 * D]], axis=1)

    def body(s):
        a = first + s.start
        rows_ref[D : 2 * D, s] = pick(table, row_of(index_ref, 0, a, s.size), row_of(index_ref, 1, a, s.size), groups, n)

    over_blocks(size, block, body)
    copy.wait()
    part_ref[...] = dot(weight, rows_ref[...]) + columns[:, 0:1]


def edges_forward(k, parts, alive_ref, index_ref, table, w1_ref, w2t_ref, columns, total, groups, n,
                  slope_ref, normed_ref, hidden_ref, factor_ref):
    weight_slot = w1_ref[k, :, D : 2 * D]
    weight_two = w2t_ref[k]
    total[...] = jnp.zeros_like(total)

    def slot_rows(span, unused):
        a, size = span[2].start, span[2].size
        return pick(table, row_of(index_ref, 2, a, size), row_of(index_ref, 3, a, size), SLOT_GROUPS, SLOT_COLS)

    def first_layer(span, picked):
        which, t, s = span
        first = parts[which][:, t] + dot(weight_slot, picked)
        gate = sigmoid(first)
        hidden = (first * gate).astype(B16)
        slope_ref[:, s] = gate * (1.0 + first * (1.0 - gate))
        hidden_ref[:, s] = hidden
        return hidden

    def second_layer(span, hidden):
        s = span[2]
        normed, factor = norm_parts(dot(weight_two, hidden) + columns[:, 1:2])
        alive = row_of(alive_ref, 0, s.start, s.size)
        normed_ref[:, s] = normed
        factor_ref[:, s] = factor
        return ((normed * columns[:, 6:7] + columns[:, 2:3]) * alive).astype(B16)

    def sum_messages(span, messages):
        a, size = span[2].start, span[2].size
        add_at(total, messages, row_of(index_ref, 0, a, size), row_of(index_ref, 1, a, size), groups, n)

    pipelined((slot_rows, first_layer, second_layer, sum_messages), spans_of(parts, CHUNK))


def node_first(k, inputs, wn1_ref, columns):
    first = dot(wn1_ref[k], inputs) + columns[:, 3:4]
    gate = sigmoid(first)
    return (first * gate).astype(B16), gate * (1.0 + first * (1.0 - gate))


def node_second(hidden, weight_two, columns):
    return norm_parts(dot(weight_two, hidden) + columns[:, 4:5])


def node_second_grad(grad, normed, factor, columns, sums_ref):
    sums_ref[2] += fold(grad)
    sums_ref[3] += fold(grad * normed)
    return norm_back(grad, normed, factor, columns[:, 7:8]).astype(B16)


def node_weight_grads(first, second, inputs, hidden, one_ref, two_ref, sums_ref):
    sums_ref[0] += fold(first.astype(F32))
    sums_ref[1] += fold(second.astype(F32))
    one_ref[...] += dot_rows(first, inputs)
    two_ref[...] += dot_rows(hidden, second)


def clear(refs):
    for ref in refs:
        ref[...] = jnp.zeros_like(ref)


def transposed(weight):
    return weight.astype(F32).T.astype(B16)


def edge_second(grad_rows, s, columns, weight_sum, alive_ref, normed_ref, factor_ref, sums_ref):
    grad = dot(weight_sum, grad_rows) * row_of(alive_ref, 0, s.start, s.size)
    normed = normed_ref[:, s]
    sums_ref[2] += fold(grad)
    sums_ref[3] += fold(grad * normed)
    return norm_back(grad, normed, factor_ref[:, s], columns[:, 6:7]).astype(B16)


def edge_first(second, s, weight_two, slope_ref):
    return (dot(weight_two, second) * slope_ref[:, s]).astype(B16)


def edge_weight_grads(first, second, rows, hidden, one_ref, two_ref, sums_ref):
    sums_ref[0] += fold(first.astype(F32))
    sums_ref[1] += fold(second.astype(F32))
    one_ref[...] += dot_rows(first, rows)
    two_ref[...] += dot_rows(hidden, second)


def pack_columns(edge_sums, node_sums):
    order = (edge_sums[0], edge_sums[1], edge_sums[2], node_sums[0], node_sums[1], node_sums[2], edge_sums[3], node_sums[3])
    columns = [jnp.sum(v, axis=1, keepdims=True) for v in order]
    lanes = lax.broadcasted_iota(jnp.int32, (D, D), 1)
    packed = jnp.zeros((D, D), F32)
    for i, column in enumerate(columns):
        packed = jnp.where(lanes == i, column, packed)
    return packed


def slot_weight_grads(sums, table):
    total = jnp.zeros((D, D), F32)
    for j in range(SLOT_GROUPS):
        high, low = halves(sums[j * D : (j + 1) * D, :])
        rows = table[j * D : (j + 1) * D, :]
        total = total + dot_rows(high, rows) + dot_rows(low, rows)
    return total


def target_grads(total, weight, start, out_ref, groups, n):
    for j in range(groups):
        high, low = halves(total[j * D : (j + 1) * D, :])
        out_ref[:, j * n : (j + 1) * n] = start(j) + dot(weight, high) + dot(weight, low)


def up_forward_kernel(part_ref, alive_ref, index_ref, r0, r1, r2, r3, r4, r5, local_ref, send_ref,
                      w1_ref, w2t_ref, wn1_ref, wn2t_ref, columns_ref,
                      out_ref, summed_ref, s0, s1, s2, slope_ref, normed_ref, hidden_ref, factor_ref,
                      node_hidden_ref, node_slope_ref, node_normed_ref, node_factor_ref, slots, total, table, out, sem):
    groups, n = groups_of(local_ref.shape[1])
    columns = columns_ref[0]
    slot_table(slots, (r0, r1, r2, r3, r4, r5))
    edges_forward(0, (part_ref,), alive_ref, index_ref, slots, w1_ref, w2t_ref, columns, total, groups, n,
                  slope_ref, normed_ref, hidden_ref, factor_ref)
    weight_two = wn2t_ref[0]

    def first_layer(j, unused):
        s = slice(j * n, (j + 1) * n)
        summed = total[j * D : (j + 1) * D, :].astype(B16)
        summed_ref[:, s] = summed
        return node_first(0, jnp.concatenate([local_ref[:, s], summed], axis=0), wn1_ref, columns)

    def second_layer(j, held):
        s = slice(j * n, (j + 1) * n)
        hidden, slope = held
        normed, factor = node_second(hidden, weight_two, columns)
        node_hidden_ref[:, s] = hidden
        node_slope_ref[:, s] = slope
        node_normed_ref[:, s] = normed
        node_factor_ref[:, s] = factor
        result = local_ref[:, s].astype(F32) + normed * columns[:, 7:8] + columns[:, 5:6]
        out[:, s] = result
        table[j * D : (j + 1) * D, :] = result.astype(B16)

    pipelined((first_layer, second_layer), range(groups))
    copy = pltpu.make_async_copy(out, out_ref, sem)
    copy.start()
    send_blocks((s0, s1, s2), table, send_ref, groups, n, False)
    copy.wait()


def down_kernel(part_a, part_b, alive_ref, index_ref, r0, r1, r2, r3, r4, r5, local_ref, cot_ref,
                w1_ref, w1t_ref, w2_ref, w2t_ref, wn1_ref, wn1t_ref, wn2_ref, wn2t_ref, columns_ref,
                out_ref, g0, g1, g2, first_ref, second_ref, hidden_ref, sums_ref, edge_sums, node_sums,
                table, summed_ref, node_hidden_ref, node_second_ref,
                slots, total, slope_ref, normed_ref, factor_ref, out, sem):
    groups, n = groups_of(local_ref.shape[1])
    columns = columns_ref[1]
    slot_table(slots, (r0, r1, r2, r3, r4, r5))
    parts = (part_a, part_b)
    edges_forward(1, parts, alive_ref, index_ref, slots, w1_ref, w2t_ref, columns, total, groups, n,
                  slope_ref, normed_ref, hidden_ref, factor_ref)
    clear((node_sums, edge_sums, sums_ref))
    wn2 = wn2_ref[1]
    wn2_t = wn2t_ref[1]
    wn1 = wn1t_ref[1]

    def first_layer(j, unused):
        summed = total[j * D : (j + 1) * D, :].astype(B16)
        summed_ref[j * D : (j + 1) * D, :] = summed
        inputs = jnp.concatenate([local_ref[:, j * n : (j + 1) * n], summed], axis=0)
        return node_first(1, inputs, wn1_ref, columns)

    def second_layer(j, held):
        hidden, slope = held
        s = slice(j * n, (j + 1) * n)
        normed, factor = node_second(hidden, wn2_t, columns)
        out[:, s] = local_ref[:, s].astype(F32) + normed * columns[:, 7:8] + columns[:, 5:6]
        second = node_second_grad(cot_ref[:, s], normed, factor, columns, node_sums)
        node_hidden_ref[:, s] = hidden
        node_second_ref[:, s] = second
        return slope, second

    def node_grads(j, held):
        slope, second = held
        table[j * D : (j + 1) * D, :] = (dot(wn2, second) * slope).astype(B16)

    pipelined((first_layer, second_layer, node_grads), range(groups))
    copy = pltpu.make_async_copy(out, out_ref, sem)
    copy.start()
    weight_two = w2_ref[1]
    weight_slot = w1t_ref[1, D : 2 * D]

    def grad_rows(span, unused):
        a, size = span[2].start, span[2].size
        return pick(table, row_of(index_ref, 0, a, size), row_of(index_ref, 1, a, size), groups, n)

    def second_grad(span, rows):
        return edge_second(rows, span[2], columns, wn1[D : 2 * D], alive_ref, normed_ref, factor_ref, edge_sums)

    def first_grad(span, second):
        s = span[2]
        first = edge_first(second, s, weight_two, slope_ref)
        first_ref[:, s] = first
        second_ref[:, s] = second
        return first

    def sum_slots(span, first):
        a, size = span[2].start, span[2].size
        add_at(sums_ref, first, row_of(index_ref, 2, a, size), row_of(index_ref, 3, a, size), SLOT_GROUPS, SLOT_COLS)

    pipelined((grad_rows, second_grad, first_grad, sum_slots), spans_of(parts, CHUNK))
    slot_gradients((g0, g1, g2), sums_ref, weight_slot)
    copy.wait()


def down_targets_kernel(index_ref, first_ref, cot_ref, table, w1t_ref, wn1t_ref, *rest):
    grad_ref, total = rest[-2:]
    groups, n = groups_of(cot_ref.shape[1])
    weight = w1t_ref[1, 2 * D : 3 * D]
    total[...] = jnp.zeros_like(total)

    def body(s):
        group, column = row_of(index_ref, 0, s.start, s.size), row_of(index_ref, 1, s.start, s.size)
        add_at(total, first_ref[:, s], group, column, groups, n)

    over_blocks(first_ref.shape[1], EDGE_BLOCK, body)
    weight_node = wn1t_ref[1, 0:D]

    def start(j):
        return cot_ref[:, j * n : (j + 1) * n] + dot(weight_node, table[j * D : (j + 1) * D, :])

    target_grads(total, weight, start, grad_ref, groups, n)


def down_rest_kernel(rows_a, rows_b, first_ref, second_ref, hidden_ref, r0, r1, r2, r3, r4, r5, sums_ref, edge_in, node_in,
                     table, summed_ref, node_hidden_ref, node_second_ref, local_ref, *rest):
    packed_ref, slots, one_ref, two_ref, wn1_grad, wn2_grad, edge_sums, node_sums = rest[-8:]
    step = pl.program_id(0)

    @pl.when(step == 0)
    def _():
        clear((one_ref, two_ref, wn1_grad, wn2_grad))
        edge_sums[...] = edge_in[...]
        node_sums[...] = node_in[...]

    s = pl.ds(pl.multiple_of(step * EDGE_BLOCK, EDGE_BLOCK), EDGE_BLOCK)
    first = first_ref[:, s]
    rows = jnp.where(step == 0, rows_a[...], rows_b[...])
    edge_weight_grads(first, second_ref[:, s], rows, hidden_ref[:, s], one_ref, two_ref, edge_sums)

    @pl.when(step == pl.num_programs(0) - 1)
    def _():
        groups, n = groups_of(local_ref.shape[1])
        for j in range(groups):
            t, rows = slice(j * n, (j + 1) * n), slice(j * D, (j + 1) * D)
            inputs = jnp.concatenate([local_ref[:, t], summed_ref[rows, :]], axis=0)
            node_weight_grads(table[rows, :], node_second_ref[:, t], inputs, node_hidden_ref[:, t], wn1_grad, wn2_grad, node_sums)
        slot_table(slots, (r0, r1, r2, r3, r4, r5))
        write_packed(packed_ref, one_ref[...], slot_weight_grads(sums_ref, slots), two_ref[...],
                     wn1_grad[...], wn2_grad[...], pack_columns(edge_sums, node_sums))


def write_packed(packed_ref, one, slot_grads, two, wn1_grad, wn2_grad, columns):
    packed_ref[0] = jnp.concatenate([one[:, 0:D], slot_grads], axis=1)
    packed_ref[1] = jnp.concatenate([one[:, D : 2 * D], two], axis=1)
    packed_ref[2] = wn1_grad
    packed_ref[3] = jnp.concatenate([wn2_grad, columns], axis=1)


def up_backward_kernel(index_ref, rows_ref, h0, h1, h2, h3, h4, h5,
                       send_ref, cot_ref, local_ref, summed_ref, r0, r1, r2, r3, r4, r5, slope_ref, normed_ref, hidden_ref, factor_ref, alive_ref, packed_down_ref,
                       node_hidden_ref, node_slope_ref, node_normed_ref, node_factor_ref, w1t_ref, w2_ref, wn1t_ref, wn2_ref, columns_ref,
                       partner_ref, cross_ref, own_ref, first_ref, grad_ref, keep_ref,
                       slots, table, back, total, sums, start, one_ref, two_ref, edge_sums, node_sums, wn1_grad, wn2_grad, pieces):
    groups, n = groups_of(local_ref.shape[1])
    columns = columns_ref[0]
    clear((back, total, sums, one_ref, two_ref, edge_sums, node_sums, wn1_grad, wn2_grad))
    slot_table(slots, (r0, r1, r2, r3, r4, r5))
    add_back(back, (h0, h1, h2, h3, h4, h5), send_ref, groups, n, False)
    wn2 = wn2_ref[0]
    wn1 = wn1t_ref[0]
    w1 = w1t_ref[0]

    def second_layer(j, unused):
        s = slice(j * n, (j + 1) * n)
        grad = cot_ref[:, s] + back[j * D : (j + 1) * D, :]
        return grad, node_second_grad(grad, node_normed_ref[:, s], node_factor_ref[:, s], columns, node_sums)

    def node_grads(j, held):
        grad, second = held
        s = slice(j * n, (j + 1) * n)
        inputs = jnp.concatenate([local_ref[:, s], summed_ref[:, s]], axis=0)
        first = (dot(wn2, second) * node_slope_ref[:, s]).astype(B16)
        node_weight_grads(first, second, inputs, node_hidden_ref[:, s], wn1_grad, wn2_grad, node_sums)
        table[j * D : (j + 1) * D, :] = first
        start[:, j * n : (j + 1) * n] = grad + dot(wn1[0:D], first)

    pipelined((second_layer, node_grads), range(groups))
    weight_two = w2_ref[0]

    def grad_rows(span, unused):
        a, size = span[2].start, span[2].size
        return pick(table, row_of(index_ref, 0, a, size), row_of(index_ref, 1, a, size), groups, n)

    def second_grad(span, rows):
        return edge_second(rows, span[2], columns, wn1[D : 2 * D], alive_ref, normed_ref, factor_ref, edge_sums)

    def first_grad(span, second):
        s = span[2]
        first = edge_first(second, s, weight_two, slope_ref)
        first_ref[:, s] = first
        edge_weight_grads(first, second, rows_ref[:, s], hidden_ref[:, s], one_ref, two_ref, edge_sums)
        return first

    def sum_rows(span, first):
        s = span[2]
        rows = [row_of(index_ref, i, s.start, s.size) for i in range(4)]
        add_at(total, first, rows[0], rows[1], groups, n)
        add_at(sums, first, rows[2], rows[3], SLOT_GROUPS, SLOT_COLS)

    pipelined((grad_rows, second_grad, first_grad, sum_rows), spans_of((first_ref,), CHUNK))
    slot_gradients((partner_ref, cross_ref, own_ref), sums, w1[D : 2 * D])
    target_grads(total, w1[2 * D : 3 * D], lambda j: start[:, j * n : (j + 1) * n], grad_ref, groups, n)
    slot_grads = slot_weight_grads(sums, slots)
    write_packed(pieces, one_ref[...], slot_grads, two_ref[...], wn1_grad[...], wn2_grad[...],
                 pack_columns(edge_sums, node_sums))
    unused, core = level_and_core()
    for p in range(4):
        pieces[4 + p] = packed_down_ref[p]
    for p in range(4):
        keep_ref[p] = pieces[core * 4 + p]
        partner_ref[4 + p] = pieces[(1 - core) * 4 + p].astype(B16)


def feat_grad_kernel(up_ref, down_ref, w1t_ref, *rest):
    out_up, out_down = rest[-2:]
    out_up[...] = dot(w1t_ref[0, 0:D], up_ref[...])
    out_down[...] = dot(w1t_ref[1, 0:D], down_ref[...])


def lower_grad_kernel(h0, h1, h2, h3, h4, h5, send_ref, start_ref, out_ref, total):
    groups, n = groups_of(start_ref.shape[1])
    clear((total,))
    add_back(total, (h0, h1, h2, h3, h4, h5), send_ref, groups, n, True)
    for j in range(groups):
        s = slice(j * n, (j + 1) * n)
        out_ref[:, s] = start_ref[:, s] + total[j * D : (j + 1) * D, :]


def unpack_kernel(own_ref, other_ref, w1_ref, w2_ref, wn1_ref, wn2_ref, biases_ref, gains_ref, pieces):
    unused, core = level_and_core()
    for p in range(4):
        pieces[core * 4 + p] = own_ref[p].astype(F32)
        pieces[(1 - core) * 4 + p] = other_ref[p].astype(F32)
    for k in range(2):
        w1_ref[k] = jnp.concatenate([pieces[4 * k], pieces[4 * k + 1, :, 0:D]], axis=1)
        w2_ref[k] = pieces[4 * k + 1, :, D : 2 * D]
        wn1_ref[k] = pieces[4 * k + 2]
        wn2_ref[k] = pieces[4 * k + 3, :, 0:D]
        rows = pieces[4 * k + 3].T
        for i in range(6):
            biases_ref[i, k : k + 1] = rows[D + i : D + i + 1]
        gains_ref[k] = rows[D + 6 : D + 8]


def shape(dims, dtype=F32):
    return jax.ShapeDtypeStruct(dims, dtype)


def call(kernel, name, outs, scratch, scalars=0, stored=(), streamed=None, final=(), raw=()):
    steps, stream_in, stream_out = streamed if streamed else (1, (), ())

    def run(*operands, after=()):
        def whole(space):
            return pl.BlockSpec(memory_space=space)

        def cut(x):
            return pl.BlockSpec((x.shape[0], x.shape[1] // steps), lambda i: (0, i))

        in_specs, placed = [], []
        for i, x in enumerate(operands):
            if i < scalars:
                in_specs.append(whole(pltpu.SMEM))
            elif i in stream_in:
                in_specs.append(cut(x))
            elif i in raw:
                in_specs.append(whole(pltpu.HBM))
                x = pltpu.with_memory_space_constraint(x, pltpu.HBM)
            else:
                in_specs.append(whole(pltpu.VMEM))
                x = pltpu.with_memory_space_constraint(x, pltpu.VMEM)
            placed.append(x)
        in_specs += [whole(pl.ANY) for _ in after]
        out_specs, out_shape = [], []
        for i, x in enumerate(outs):
            if i in stream_out:
                out_specs.append(cut(x))
                out_shape.append(x)
            elif i in stored:
                out_specs.append(whole(pl.ANY))
                out_shape.append(x)
            elif i in final:
                out_specs.append(whole(pltpu.VMEM))
                out_shape.append(x)
            else:
                out_specs.append(whole(pltpu.VMEM))
                out_shape.append(pltpu.VMEM(x.shape, x.dtype))
        return pl.pallas_call(
            kernel,
            name=name,
            grid=(steps,) if streamed else (),
            in_specs=in_specs,
            out_specs=out_specs,
            out_shape=out_shape,
            scratch_shapes=scratch,
            compiler_params=pltpu.CompilerParams(vmem_limit_bytes=VMEM_BYTES),
        )(*placed, *after)

    return run


def core_swap(block):
    return lax.ppermute(block, "band", [(i, i ^ 1) for i in range(lax.axis_size("band"))])


def cross_swap(block):
    last = lax.axis_size("band") - 1
    pairs = [(i, i + 1) for i in range(1, last, 2)]
    return lax.ppermute(block, "band", pairs + [(b, a) for a, b in pairs] + [(0, 0), (last, last)])


def along_level(block, step):
    count = lax.axis_size("level")
    return lax.ppermute(block, "level", [(i, (i + step) % count) for i in range(count)])


def along_band(block, step):
    count = lax.axis_size("band")
    return lax.ppermute(block, "band", [(i, (i + step) % count) for i in range(count)])


def across_bands(blocks):
    below, above, own = blocks
    return [along_band(above, 1), along_band(below, -1), own]


def along_levels(blocks, sign):
    return blocks + [along_level(jnp.stack([b[d] for b in blocks]), sign * d) for d in (1, 2, 3)]


def chip_ring(block, step, core_strides):
    count = lax.axis_size("band")
    pairs = []
    for i in range(count):
        stride = core_strides[i % 2]
        at = (i // stride) % 4
        pairs.append((i, i + (((at + step) % 4) - at) * stride))
    return lax.ppermute(block, "band", pairs)


def rounded(values):
    return lax.reduce_precision(values, 8, 7)


def sum_of_four(values, first, second, third):
    return (values + second.astype(F32)) + (first.astype(F32) + third.astype(F32))


def sum_along(values, core_strides):
    own = rounded(values)
    sent = own.astype(B16)
    return sum_of_four(own, *(chip_ring(sent, d, core_strides) for d in (1, 2, 3)))


def shards(
    lower_nodes, latent, up_feat, down_feat, up_send, up_counts, up_senders, up_targets,
    down_send, down_counts, down_senders, down_targets,
    edge_w1, edge_w2, node_w1, node_w2, biases, norm_gains, lower_cot, upper_cot,
):
    lower, upper = lower_nodes.T, latent.T
    feat_up, feat_down = up_feat.T, down_feat.T
    cot_lower, cot_upper = lower_cot.T, upper_cot.T
    w1, wn1 = edge_w1.transpose(0, 2, 1), node_w1.transpose(0, 2, 1)
    w2, wn2 = edge_w2, node_w2
    edges, lower_rows, upper_rows = up_feat.shape[0], lower_nodes.shape[0], latent.shape[0]
    dense = (edges // 128, 128)
    senders_up, targets_up, senders_down, targets_down = (
        x.reshape(dense) for x in (up_senders, up_targets, down_senders, down_targets))
    bias_rows = biases.transpose(1, 0, 2)

    lower_groups, lower_n = groups_of(lower_rows)
    upper_groups, upper_n = groups_of(upper_rows)
    lower_table, upper_table = (lower_groups * D, lower_n), (upper_groups * D, upper_n)
    slots = pltpu.VMEM((SLOT_GROUPS * D, SLOT_COLS), B16)
    block, four = shape((4, D, 128), B16), shape((4, D, 128))
    wide32, wide16, row = shape((D, edges)), shape((D, edges), B16), shape((1, edges))
    steps = edges // EDGE_BLOCK

    early = (up_send, lower, senders_up, targets_up, senders_down, targets_down, upper, w1, bias_rows, norm_gains,
             down_send, w2, wn1, wn2)
    count = len(early)
    (*sent, up_send, lower, senders_up, targets_up, senders_down, targets_down, upper, w1, bias_rows,
     norm_gains, down_send, w2, wn1, wn2) = call(
        functools.partial(send_kernel, count), "send_lower", [block] * 3 + [shape(x.shape, x.dtype) for x in early],
        [pltpu.VMEM(lower_table, B16), pltpu.SemaphoreType.DMA((count,))], 0, raw=range(count),
    )(*early)
    index, lives = shape((4, *dense), jnp.int32), shape((1, *dense))
    turned = [shape((2, D, 8)), shape((2, 3 * D, D), B16), shape((2, D, D), B16), shape((2, 2 * D, D), B16), shape((2, D, D), B16)]
    index_up, alive_up, index_down, alive_down, columns, w1t, w2t, wn1t, wn2t = call(
        functools.partial(tables_kernel, upper_rows, lower_rows), "edge_tables", [index, lives, index, lives] + turned,
        [pltpu.SMEM((1, 12), jnp.int32), pltpu.SMEM((1, 12), jnp.int32), pltpu.SemaphoreType.DMA((2,))], 0, raw=(0, 1),
    )(up_counts, down_counts, senders_up, targets_up, senders_down, targets_down, w1, w2, wn1, wn2, bias_rows, norm_gains)

    def part(k, block, first, size, name, table, index, feat, local, after):
        return call(
            functools.partial(part_kernel, k, block, first), name, [shape((D, size)), shape((2 * D, size), B16)],
            [pltpu.VMEM(table, B16), pltpu.SemaphoreType.DMA], 0, raw=(1,),
        )(index, feat, local, w1, columns, after=after)

    sent = [core_swap(sent[0]), cross_swap(sent[1]), sent[2]]
    half = edges // 2
    part_a, rows_a = part(1, half // 2, 0, half, "part_down_a", lower_table, index_down, feat_down, lower, ())
    sent, part_a = lax.optimization_barrier((sent, part_a))
    part_up, rows_up = part(0, EDGE_BLOCK, 0, edges, "part_up", upper_table, index_up, feat_up, upper, (sent[0], sent[1]))
    up_slots = along_levels(sent, 1)
    up_slots, part_up = lax.optimization_barrier((up_slots, part_up))
    (upper_new, summed_up, s0, s1, s2, slope, normed, hidden, factor, *nodes_up) = call(
        up_forward_kernel, "up_forward",
        [shape((D, upper_rows)), shape((D, upper_rows), B16)] + [block] * 3 + [wide32, wide32, wide16, row,
         shape((D, upper_rows), B16), shape((D, upper_rows)), shape((D, upper_rows)), shape((1, upper_rows))],
        [slots, pltpu.VMEM(upper_table, F32), pltpu.VMEM(upper_table, B16), pltpu.VMEM((D, upper_rows), F32),
         pltpu.SemaphoreType.DMA], 0, (0,),
    )(part_up, alive_up, index_up, *up_slots, upper, down_send, w1, w2t, wn1, wn2t, columns)
    sent = across_bands([s0, s1, s2])
    part_b, rows_b = part(1, half // 2, half, half, "part_down_b", lower_table, index_down, feat_down, lower, (sent[0], sent[1]))
    down_slots = along_levels(sent, 1)
    down_slots, part_b = lax.optimization_barrier((down_slots, part_b))
    sums_shape = shape((SLOT_GROUPS * D, SLOT_COLS))
    node16 = shape((D, lower_rows), B16)
    (lower_new, g0, g1, g2, first_down, second_down, hidden_down, sums_down, edge_sums, node_sums, *nodes) = call(
        down_kernel, "down_sweep",
        [shape((D, lower_rows))] + [block] * 3 + [wide16] * 3 + [sums_shape, four, four, shape(lower_table, B16),
         shape(lower_table, B16), node16, node16],
        [slots, pltpu.VMEM(lower_table, F32), pltpu.VMEM((D, edges), F32),
         pltpu.VMEM((D, edges), F32), pltpu.VMEM((1, edges), F32),
         pltpu.VMEM((D, lower_rows), F32), pltpu.SemaphoreType.DMA], 0, (0,),
    )(part_a, part_b, alive_down, index_down, *down_slots, lower, cot_lower, w1, w1t, w2, w2t, wn1, wn1t, wn2, wn2t, columns)
    back = across_bands([g0, g1, g2])
    (packed_down,) = call(
        down_rest_kernel, "down_rest", [four],
        [slots, pltpu.VMEM((D, 2 * D), F32), pltpu.VMEM((D, D), F32), pltpu.VMEM((D, 2 * D), F32), pltpu.VMEM((D, D), F32),
         pltpu.VMEM((4, D, 128), F32), pltpu.VMEM((4, D, 128), F32)], 0, (), (steps, (), ()),
    )(rows_a, rows_b, first_down, second_down, hidden_down, *down_slots, sums_down, edge_sums, node_sums, *nodes, lower,
      after=(back[0], back[1]))
    down_back = along_levels(back, -1)
    down_back, packed_down = lax.optimization_barrier((down_back, packed_down))
    (partner, cross, own, first_up, grad_latent, keep) = call(
        up_backward_kernel, "up_backward",
        [shape((8, D, 128), B16), block, block, wide16, shape((D, upper_rows)), four],
        [slots, pltpu.VMEM(upper_table, B16), pltpu.VMEM(upper_table, F32), pltpu.VMEM(upper_table, F32),
         pltpu.VMEM((SLOT_GROUPS * D, SLOT_COLS), F32), pltpu.VMEM((D, upper_rows), F32),
         pltpu.VMEM((D, 2 * D), F32), pltpu.VMEM((D, D), F32), pltpu.VMEM((4, D, 128), F32), pltpu.VMEM((4, D, 128), F32),
         pltpu.VMEM((D, 2 * D), F32), pltpu.VMEM((D, D), F32), pltpu.VMEM((8, D, 128), F32)], 0, (), None, (4,),
    )(index_up, rows_up, *down_back, down_send, cot_upper, upper, summed_up, *up_slots,
      slope, normed, hidden, factor, alive_up, packed_down, *nodes_up, w1t, w2, wn1t, wn2, columns)

    partner = core_swap(partner)
    total = rounded(rounded(keep) + partner[4:].astype(F32))
    cross, keep = lax.optimization_barrier((cross, total))
    cross = cross_swap(cross)
    total = sum_along(total, (2, 8))
    feat_grad_up, feat_grad_down = call(
        feat_grad_kernel, "feat_grads", [wide32, wide32], [], 0, (), (steps, (0, 1), (0, 1)),
    )(first_up, first_down, w1t, after=(partner,))
    total, cross, feat_grad_up = lax.optimization_barrier((total, cross, feat_grad_up))
    blocks = (partner, cross, own)
    total = rounded(total)
    levels = [
        along_level(jnp.concatenate([jnp.stack([b[d] for b in blocks]), total.astype(B16)]), -d) for d in (1, 2, 3)
    ]
    (start_lower,) = call(
        down_targets_kernel, "down_targets", [shape((D, lower_rows))], [pltpu.VMEM(lower_table, F32)],
    )(index_down, first_down, cot_lower, nodes[0], w1t, wn1t, after=(total,))
    levels, start_lower = lax.optimization_barrier((levels, start_lower))
    total = sum_of_four(total, *(b[3:] for b in levels))
    (grad_lower,) = call(lower_grad_kernel, "lower_grad", [shape((D, lower_rows))], [pltpu.VMEM(lower_table, F32)], 0, (), None, (0,))(
        *blocks, *levels, up_send, start_lower)
    total = sum_along(total, (8, 2))
    total, grad_lower = lax.optimization_barrier((total, grad_lower))
    total = rounded(total).astype(B16)
    w1_grad, w2_grad, wn1_grad, wn2_grad, bias_grad, gain_grad = call(
        unpack_kernel, "unpack",
        [shape((2, D, 3 * D)), shape((2, D, D)), shape((2, D, 2 * D)), shape((2, D, D)), shape((6, 2, D)), shape((2, 2, D))],
        [pltpu.VMEM((8, D, 128), F32)], 0, (), None, range(6))(total, core_swap(total))
    return (
        lower_new.T, upper_new.T, grad_lower.T, grad_latent.T, feat_grad_up.T, feat_grad_down.T,
        w1_grad.transpose(0, 2, 1), w2_grad, wn1_grad.transpose(0, 2, 1), wn2_grad, bias_grad.transpose(1, 0, 2), gain_grad,
    )


def solution(mesh):
    rows, index, whole = P(("band", "level"), None), P(("band", "level")), P()
    placed = (rows,) * 6 + (index, index) + (rows,) * 2 + (index, index) + (whole,) * 6 + (rows,) * 2
    return jax.shard_map(
        shards,
        mesh=mesh,
        in_specs=placed,
        out_specs=(rows,) * 6 + (whole,) * 6,
        check_vma=False,
    )
```

```python
import functools

import jax
import jax.numpy as jnp
from jax import lax
from jax.experimental import pallas as pl
from jax.experimental.pallas import tpu as pltpu
from jax.sharding import PartitionSpec as P

EPSILON = 1e-05
F32 = jnp.float32
B16 = jnp.bfloat16
D = 64
SLOT_GROUPS, SLOT_COLS = 6, 256
EDGE_BLOCK = 3072
CHUNK = 1024
VMEM_BYTES = 24 * 1024 * 1024


def groups_of(rows):
    return (4, rows // 4) if rows > 1024 else (rows // 256, 256)


def dot(a, b):
    return jnp.dot(a, b, preferred_element_type=F32)


def dot_rows(a, b):
    return lax.dot_general(a, b, (((1,), (1,)), ((), ())), preferred_element_type=F32)


def halves(x):
    high = x.astype(B16)
    return high, (x - high.astype(F32)).astype(B16)


def one_hot(column, n):
    rows = lax.broadcasted_iota(jnp.int16, (n, column.shape[1]), 0)
    return jnp.where(rows == column.astype(jnp.int16), jnp.ones((), B16), jnp.zeros((), B16))


def place(index, groups, n):
    group = jnp.zeros_like(index)
    for j in range(1, groups):
        group = group + (index >= j * n).astype(jnp.int32)
    return group, index - group * n


def level_and_core():
    return lax.axis_index("level").astype(jnp.int32), lax.axis_index("band").astype(jnp.int32) & 1


def band_offsets(swapped):
    unused, core = level_and_core()
    return (2 - 2 * core, 2 * core, 1) if swapped else (0, 2, 1)


def slot_place(senders, swapped):
    level, unused = level_and_core()
    distance = (level - ((senders >> 7) & 3)) & 3
    offset = senders >> 9
    source = jnp.where(offset == 1, 2, jnp.where(offset == band_offsets(swapped)[0], 0, 1))
    block = distance * 3 + source
    return block >> 1, ((block & 1) << 7) | (senders & 127)


def live(senders, counts_ref):
    peer = senders >> 7
    limit = jnp.zeros_like(senders)
    for j in range(12):
        limit = jnp.where(peer == j, counts_ref[0, j], limit)
    return ((senders & 127) < limit).astype(F32)


def choose(stacked, group, groups):
    picked = stacked[0:D]
    for j in range(1, groups):
        picked = jnp.where(group == j, stacked[j * D : (j + 1) * D], picked)
    return picked


def row_of(ref, k, start, size):
    rows = size // 128
    if not isinstance(start, int):
        start = start // 128
        return jnp.concatenate([ref[k, pl.ds(start + r, 1), :] for r in range(rows)], axis=1)
    return jnp.concatenate([ref[k, r : r + 1, :] for r in range(start // 128, start // 128 + rows)], axis=1)


def pick(table, group, column, groups, n):
    return choose(dot(table[...], one_hot(column, n)), group, groups).astype(B16)


def spread(values, group, groups):
    wide = jnp.broadcast_to(group.astype(jnp.int16), values.shape)
    nothing = jnp.zeros_like(values)
    return jnp.concatenate([jnp.where(wide == j, values, nothing) for j in range(groups)], axis=0)


def add_at(total, values, group, column, groups, n):
    total[...] += dot_rows(spread(values, group, groups), one_hot(column, n))


def pack_table(table, source, groups, n):
    for j in range(groups):
        table[j * D : (j + 1) * D, :] = source[:, j * n : (j + 1) * n]


def columns_of(biases_ref, gains_ref, k):
    rows = [biases_ref[i, k : k + 1] for i in range(6)] + [gains_ref[k]]
    return jnp.concatenate(rows, axis=0).T


def fold(values):
    total = values[:, 0:128]
    for i in range(128, values.shape[1], 128):
        total = total + values[:, i : i + 128]
    return total


def norm_parts(values):
    centre = values - jnp.sum(values, axis=0, keepdims=True) * (1.0 / D)
    spread_sum = jnp.sum(centre * centre, axis=0, keepdims=True) * (1.0 / D)
    factor = lax.rsqrt(spread_sum + EPSILON)
    return centre * factor, factor


def norm_back(grad, normed, factor, gain):
    scaled = grad * gain
    first = jnp.sum(scaled, axis=0, keepdims=True) * (1.0 / D)
    second = jnp.sum(scaled * normed, axis=0, keepdims=True) * (1.0 / D)
    return factor * (scaled - first - normed * second)


def sigmoid(values):
    return 0.5 * jnp.tanh(0.5 * values) + 0.5


def send_rows(send_ref, offset):
    level, unused = level_and_core()
    return jnp.concatenate(
        [send_ref[pl.ds(offset * 4 + ((level + d) & 3), 1), :] for d in range(4)], axis=1
    )


def send_blocks(outs, table, send_ref, groups, n, swapped):
    for j, offset in enumerate(band_offsets(swapped)):
        group, column = place(send_rows(send_ref, offset), groups, n)
        rows = pick(table, group, column, groups, n)
        for d in range(4):
            outs[j][d] = rows[:, d * 128 : (d + 1) * 128]


def add_back(total, blocks, send_ref, groups, n, swapped):
    for j, offset in enumerate(band_offsets(swapped)):
        group, column = place(send_rows(send_ref, offset), groups, n)
        values = jnp.concatenate([block_at(blocks, d, j) for d in range(4)], axis=1)
        add_at(total, values, group, column, groups, n)


def block_at(received, d, j):
    return received[j][0] if d == 0 else received[2 + d][j]


def slot_table(table, received):
    for t in range(12):
        table[(t >> 1) * D : ((t >> 1) + 1) * D, (t & 1) * 128 : ((t & 1) + 1) * 128] = block_at(received, t // 3, t % 3)


def slot_gradients(outs, sums, weight):
    for j in range(SLOT_GROUPS):
        high, low = halves(sums[j * D : (j + 1) * D, :])
        grads = (dot(weight, high) + dot(weight, low)).astype(B16)
        for t in (2 * j, 2 * j + 1):
            outs[t % 3][t // 3] = grads[:, (t & 1) * 128 : ((t & 1) + 1) * 128]


def over_blocks(total, block, body):
    block = min(block, total)
    if block == total:
        body(pl.ds(0, block))
        return

    def step(i, carry):
        body(pl.ds(pl.multiple_of(i * block, block), block))
        return carry

    lax.fori_loop(0, total // block, step, 0)


def pipelined(stages, spans):
    held = [None] * len(spans)
    for t in range(len(spans) + len(stages) - 1):
        for k in reversed(range(len(stages))):
            i = t - k
            if 0 <= i < len(spans):
                held[i] = stages[k](spans[i], held[i])


def spans_of(parts, chunk):
    spans, start = [], 0
    for which, ref in enumerate(parts):
        size = min(chunk, ref.shape[1])
        for at in range(0, ref.shape[1], size):
            spans.append((which, pl.ds(at, size), pl.ds(start + at, size)))
        start += ref.shape[1]
    return spans


def tables_kernel(upper_rows, lower_rows, counts_up, counts_down, senders_up, targets_up, senders_down, targets_down,
                  w1_ref, w2_ref, wn1_ref, wn2_ref, biases_ref, gains_ref, index_up, alive_up, index_down, alive_down, columns_ref, w1t_ref, w2t_ref, wn1t_ref, wn2t_ref, limits_up, limits_down, sems):
    copies = [pltpu.make_async_copy(counts_up, limits_up, sems.at[0]), pltpu.make_async_copy(counts_down, limits_down, sems.at[1])]
    for copy in copies:
        copy.start()
    sweeps = ((index_up, senders_up, targets_up, upper_rows, True), (index_down, senders_down, targets_down, lower_rows, False))
    for index_ref, senders_ref, targets_ref, rows, swapped in sweeps:
        index_ref[0], index_ref[1] = place(targets_ref[...], *groups_of(rows))
        index_ref[2], index_ref[3] = slot_place(senders_ref[...], swapped)
    for k in range(2):
        columns_ref[k] = columns_of(biases_ref, gains_ref, k)
        for turned, ref in ((w1t_ref, w1_ref), (w2t_ref, w2_ref), (wn1t_ref, wn1_ref), (wn2t_ref, wn2_ref)):
            turned[k] = transposed(ref[k])
    for copy in copies:
        copy.wait()
    alive_up[0] = live(senders_up[...], limits_up)
    alive_down[0] = live(senders_down[...], limits_down)


def send_kernel(count, *refs):
    sources, refs = refs[:count], refs[count:]
    sent, held, table, sems = refs[:3], refs[3:-2], refs[-2], refs[-1]
    copies = [pltpu.make_async_copy(a, b, sems.at[i]) for i, (a, b) in enumerate(zip(sources, held))]
    for copy in copies:
        copy.start()
    for copy in copies[:2]:
        copy.wait()
    send_ref, source_ref = held[:2]
    groups, n = groups_of(source_ref.shape[1])
    pack_table(table, source_ref, groups, n)
    send_blocks(sent, table, send_ref, groups, n, True)
    for copy in copies[2:]:
        copy.wait()


def part_kernel(k, block, first, index_ref, feat_ref, local_ref, w1_ref, columns_ref, *rest):
    part_ref, rows_ref, table, sem = rest[-4:]
    size = part_ref.shape[1]
    copy = pltpu.make_async_copy(feat_ref.at[:, pl.ds(first, size)], rows_ref.at[0:D], sem)
    copy.start()
    groups, n = groups_of(local_ref.shape[1])
    pack_table(table, local_ref, groups, n)
    columns = columns_ref[k]
    weight = jnp.concatenate([w1_ref[k, :, 0:D], w1_ref[k, :, 2 * D : 3 * D]], axis=1)

    def body(s):
        a = first + s.start
        rows_ref[D : 2 * D, s] = pick(table, row_of(index_ref, 0, a, s.size), row_of(index_ref, 1, a, s.size), groups, n)

    over_blocks(size, block, body)
    copy.wait()
    part_ref[...] = dot(weight, rows_ref[...]) + columns[:, 0:1]


def edges_forward(k, parts, alive_ref, index_ref, table, w1_ref, w2t_ref, columns, total, groups, n,
                  slope_ref, normed_ref, hidden_ref, factor_ref):
    weight_slot = w1_ref[k, :, D : 2 * D]
    weight_two = w2t_ref[k]
    total[...] = jnp.zeros_like(total)

    def slot_rows(span, unused):
        a, size = span[2].start, span[2].size
        return pick(table, row_of(index_ref, 2, a, size), row_of(index_ref, 3, a, size), SLOT_GROUPS, SLOT_COLS)

    def first_layer(span, picked):
        which, t, s = span
        first = parts[which][:, t] + dot(weight_slot, picked)
        gate = sigmoid(first)
        hidden = (first * gate).astype(B16)
        slope_ref[:, s] = gate * (1.0 + first * (1.0 - gate))
        hidden_ref[:, s] = hidden
        return hidden

    def second_layer(span, hidden):
        s = span[2]
        normed, factor = norm_parts(dot(weight_two, hidden) + columns[:, 1:2])
        alive = row_of(alive_ref, 0, s.start, s.size)
        normed_ref[:, s] = normed
        factor_ref[:, s] = factor
        return ((normed * columns[:, 6:7] + columns[:, 2:3]) * alive).astype(B16)

    def sum_messages(span, messages):
        a, size = span[2].start, span[2].size
        add_at(total, messages, row_of(index_ref, 0, a, size), row_of(index_ref, 1, a, size), groups, n)

    pipelined((slot_rows, first_layer, second_layer, sum_messages), spans_of(parts, CHUNK))


def node_first(k, inputs, wn1_ref, columns):
    first = dot(wn1_ref[k], inputs) + columns[:, 3:4]
    gate = sigmoid(first)
    return (first * gate).astype(B16), gate * (1.0 + first * (1.0 - gate))


def node_second(hidden, weight_two, columns):
    return norm_parts(dot(weight_two, hidden) + columns[:, 4:5])


def node_second_grad(grad, normed, factor, columns, sums_ref):
    sums_ref[2] += fold(grad)
    sums_ref[3] += fold(grad * normed)
    return norm_back(grad, normed, factor, columns[:, 7:8]).astype(B16)


def node_weight_grads(first, second, inputs, hidden, one_ref, two_ref, sums_ref):
    sums_ref[0] += fold(first.astype(F32))
    sums_ref[1] += fold(second.astype(F32))
    one_ref[...] += dot_rows(first, inputs)
    two_ref[...] += dot_rows(hidden, second)


def clear(refs):
    for ref in refs:
        ref[...] = jnp.zeros_like(ref)


def transposed(weight):
    return weight.astype(F32).T.astype(B16)


def edge_second(grad_rows, s, columns, weight_sum, alive_ref, normed_ref, factor_ref, sums_ref):
    grad = dot(weight_sum, grad_rows) * row_of(alive_ref, 0, s.start, s.size)
    normed = normed_ref[:, s]
    sums_ref[2] += fold(grad)
    sums_ref[3] += fold(grad * normed)
    return norm_back(grad, normed, factor_ref[:, s], columns[:, 6:7]).astype(B16)


def edge_first(second, s, weight_two, slope_ref):
    return (dot(weight_two, second) * slope_ref[:, s]).astype(B16)


def edge_weight_grads(first, second, rows, hidden, one_ref, two_ref, sums_ref):
    sums_ref[0] += fold(first.astype(F32))
    sums_ref[1] += fold(second.astype(F32))
    one_ref[...] += dot_rows(first, rows)
    two_ref[...] += dot_rows(hidden, second)


def pack_columns(edge_sums, node_sums):
    order = (edge_sums[0], edge_sums[1], edge_sums[2], node_sums[0], node_sums[1], node_sums[2], edge_sums[3], node_sums[3])
    columns = [jnp.sum(v, axis=1, keepdims=True) for v in order]
    lanes = lax.broadcasted_iota(jnp.int32, (D, D), 1)
    packed = jnp.zeros((D, D), F32)
    for i, column in enumerate(columns):
        packed = jnp.where(lanes == i, column, packed)
    return packed


def slot_weight_grads(sums, table):
    total = jnp.zeros((D, D), F32)
    for j in range(SLOT_GROUPS):
        high, low = halves(sums[j * D : (j + 1) * D, :])
        rows = table[j * D : (j + 1) * D, :]
        total = total + dot_rows(high, rows) + dot_rows(low, rows)
    return total


def target_grads(total, weight, start, out_ref, groups, n):
    for j in range(groups):
        high, low = halves(total[j * D : (j + 1) * D, :])
        out_ref[:, j * n : (j + 1) * n] = start(j) + dot(weight, high) + dot(weight, low)


def up_forward_kernel(part_ref, alive_ref, index_ref, r0, r1, r2, r3, r4, r5, local_ref, send_ref,
                      w1_ref, w2t_ref, wn1_ref, wn2t_ref, columns_ref,
                      out_ref, summed_ref, s0, s1, s2, slope_ref, normed_ref, hidden_ref, factor_ref,
                      node_hidden_ref, node_slope_ref, node_normed_ref, node_factor_ref, slots, total, table, out, sem):
    groups, n = groups_of(local_ref.shape[1])
    columns = columns_ref[0]
    slot_table(slots, (r0, r1, r2, r3, r4, r5))
    edges_forward(0, (part_ref,), alive_ref, index_ref, slots, w1_ref, w2t_ref, columns, total, groups, n,
                  slope_ref, normed_ref, hidden_ref, factor_ref)
    weight_two = wn2t_ref[0]

    def first_layer(j, unused):
        s = slice(j * n, (j + 1) * n)
        summed = total[j * D : (j + 1) * D, :].astype(B16)
        summed_ref[:, s] = summed
        return node_first(0, jnp.concatenate([local_ref[:, s], summed], axis=0), wn1_ref, columns)

    def second_layer(j, held):
        s = slice(j * n, (j + 1) * n)
        hidden, slope = held
        normed, factor = node_second(hidden, weight_two, columns)
        node_hidden_ref[:, s] = hidden
        node_slope_ref[:, s] = slope
        node_normed_ref[:, s] = normed
        node_factor_ref[:, s] = factor
        result = local_ref[:, s].astype(F32) + normed * columns[:, 7:8] + columns[:, 5:6]
        out[:, s] = result
        table[j * D : (j + 1) * D, :] = result.astype(B16)

    pipelined((first_layer, second_layer), range(groups))
    copy = pltpu.make_async_copy(out, out_ref, sem)
    copy.start()
    send_blocks((s0, s1, s2), table, send_ref, groups, n, False)
    copy.wait()


def down_kernel(part_a, part_b, alive_ref, index_ref, r0, r1, r2, r3, r4, r5, local_ref, cot_ref,
                w1_ref, w1t_ref, w2_ref, w2t_ref, wn1_ref, wn1t_ref, wn2_ref, wn2t_ref, columns_ref,
                out_ref, g0, g1, g2, first_ref, second_ref, hidden_ref, sums_ref, edge_sums, node_sums,
                table, summed_ref, node_hidden_ref, node_second_ref,
                slots, total, slope_ref, normed_ref, factor_ref, out, sem):
    groups, n = groups_of(local_ref.shape[1])
    columns = columns_ref[1]
    slot_table(slots, (r0, r1, r2, r3, r4, r5))
    parts = (part_a, part_b)
    edges_forward(1, parts, alive_ref, index_ref, slots, w1_ref, w2t_ref, columns, total, groups, n,
                  slope_ref, normed_ref, hidden_ref, factor_ref)
    clear((node_sums, edge_sums, sums_ref))
    wn2 = wn2_ref[1]
    wn2_t = wn2t_ref[1]
    wn1 = wn1t_ref[1]

    def first_layer(j, unused):
        summed = total[j * D : (j + 1) * D, :].astype(B16)
        summed_ref[j * D : (j + 1) * D, :] = summed
        inputs = jnp.concatenate([local_ref[:, j * n : (j + 1) * n], summed], axis=0)
        return node_first(1, inputs, wn1_ref, columns)

    def second_layer(j, held):
        hidden, slope = held
        s = slice(j * n, (j + 1) * n)
        normed, factor = node_second(hidden, wn2_t, columns)
        out[:, s] = local_ref[:, s].astype(F32) + normed * columns[:, 7:8] + columns[:, 5:6]
        second = node_second_grad(cot_ref[:, s], normed, factor, columns, node_sums)
        node_hidden_ref[:, s] = hidden
        node_second_ref[:, s] = second
        return slope, second

    def node_grads(j, held):
        slope, second = held
        table[j * D : (j + 1) * D, :] = (dot(wn2, second) * slope).astype(B16)

    pipelined((first_layer, second_layer, node_grads), range(groups))
    copy = pltpu.make_async_copy(out, out_ref, sem)
    copy.start()
    weight_two = w2_ref[1]
    weight_slot = w1t_ref[1, D : 2 * D]

    def grad_rows(span, unused):
        a, size = span[2].start, span[2].size
        return pick(table, row_of(index_ref, 0, a, size), row_of(index_ref, 1, a, size), groups, n)

    def second_grad(span, rows):
        return edge_second(rows, span[2], columns, wn1[D : 2 * D], alive_ref, normed_ref, factor_ref, edge_sums)

    def first_grad(span, second):
        s = span[2]
        first = edge_first(second, s, weight_two, slope_ref)
        first_ref[:, s] = first
        second_ref[:, s] = second
        return first

    def sum_slots(span, first):
        a, size = span[2].start, span[2].size
        add_at(sums_ref, first, row_of(index_ref, 2, a, size), row_of(index_ref, 3, a, size), SLOT_GROUPS, SLOT_COLS)

    pipelined((grad_rows, second_grad, first_grad, sum_slots), spans_of(parts, CHUNK))
    slot_gradients((g0, g1, g2), sums_ref, weight_slot)
    copy.wait()


def down_targets_kernel(index_ref, first_ref, cot_ref, table, w1t_ref, wn1t_ref, *rest):
    grad_ref, total = rest[-2:]
    groups, n = groups_of(cot_ref.shape[1])
    weight = w1t_ref[1, 2 * D : 3 * D]
    total[...] = jnp.zeros_like(total)

    def body(s):
        group, column = row_of(index_ref, 0, s.start, s.size), row_of(index_ref, 1, s.start, s.size)
        add_at(total, first_ref[:, s], group, column, groups, n)

    over_blocks(first_ref.shape[1], EDGE_BLOCK, body)
    weight_node = wn1t_ref[1, 0:D]

    def start(j):
        return cot_ref[:, j * n : (j + 1) * n] + dot(weight_node, table[j * D : (j + 1) * D, :])

    target_grads(total, weight, start, grad_ref, groups, n)


def down_rest_kernel(rows_a, rows_b, first_ref, second_ref, hidden_ref, r0, r1, r2, r3, r4, r5, sums_ref, edge_in, node_in,
                     table, summed_ref, node_hidden_ref, node_second_ref, local_ref, *rest):
    packed_ref, slots, one_ref, two_ref, wn1_grad, wn2_grad, edge_sums, node_sums = rest[-8:]
    step = pl.program_id(0)

    @pl.when(step == 0)
    def _():
        clear((one_ref, two_ref, wn1_grad, wn2_grad))
        edge_sums[...] = edge_in[...]
        node_sums[...] = node_in[...]

    s = pl.ds(pl.multiple_of(step * EDGE_BLOCK, EDGE_BLOCK), EDGE_BLOCK)
    first = first_ref[:, s]
    rows = jnp.where(step == 0, rows_a[...], rows_b[...])
    edge_weight_grads(first, second_ref[:, s], rows, hidden_ref[:, s], one_ref, two_ref, edge_sums)

    @pl.when(step == pl.num_programs(0) - 1)
    def _():
        groups, n = groups_of(local_ref.shape[1])
        for j in range(groups):
            t, rows = slice(j * n, (j + 1) * n), slice(j * D, (j + 1) * D)
            inputs = jnp.concatenate([local_ref[:, t], summed_ref[rows, :]], axis=0)
            node_weight_grads(table[rows, :], node_second_ref[:, t], inputs, node_hidden_ref[:, t], wn1_grad, wn2_grad, node_sums)
        slot_table(slots, (r0, r1, r2, r3, r4, r5))
        write_packed(packed_ref, one_ref[...], slot_weight_grads(sums_ref, slots), two_ref[...],
                     wn1_grad[...], wn2_grad[...], pack_columns(edge_sums, node_sums))


def write_packed(packed_ref, one, slot_grads, two, wn1_grad, wn2_grad, columns):
    packed_ref[0] = jnp.concatenate([one[:, 0:D], slot_grads], axis=1)
    packed_ref[1] = jnp.concatenate([one[:, D : 2 * D], two], axis=1)
    packed_ref[2] = wn1_grad
    packed_ref[3] = jnp.concatenate([wn2_grad, columns], axis=1)


def up_backward_kernel(index_ref, rows_ref, h0, h1, h2, h3, h4, h5,
                       send_ref, cot_ref, local_ref, summed_ref, r0, r1, r2, r3, r4, r5, slope_ref, normed_ref, hidden_ref, factor_ref, alive_ref, packed_down_ref,
                       node_hidden_ref, node_slope_ref, node_normed_ref, node_factor_ref, w1t_ref, w2_ref, wn1t_ref, wn2_ref, columns_ref,
                       partner_ref, cross_ref, own_ref, first_ref, grad_ref, keep_ref,
                       slots, table, back, total, sums, start, one_ref, two_ref, edge_sums, node_sums, wn1_grad, wn2_grad, pieces):
    groups, n = groups_of(local_ref.shape[1])
    columns = columns_ref[0]
    clear((back, total, sums, one_ref, two_ref, edge_sums, node_sums, wn1_grad, wn2_grad))
    slot_table(slots, (r0, r1, r2, r3, r4, r5))
    add_back(back, (h0, h1, h2, h3, h4, h5), send_ref, groups, n, False)
    wn2 = wn2_ref[0]
    wn1 = wn1t_ref[0]
    w1 = w1t_ref[0]

    def second_layer(j, unused):
        s = slice(j * n, (j + 1) * n)
        grad = cot_ref[:, s] + back[j * D : (j + 1) * D, :]
        return grad, node_second_grad(grad, node_normed_ref[:, s], node_factor_ref[:, s], columns, node_sums)

    def node_grads(j, held):
        grad, second = held
        s = slice(j * n, (j + 1) * n)
        inputs = jnp.concatenate([local_ref[:, s], summed_ref[:, s]], axis=0)
        first = (dot(wn2, second) * node_slope_ref[:, s]).astype(B16)
        node_weight_grads(first, second, inputs, node_hidden_ref[:, s], wn1_grad, wn2_grad, node_sums)
        table[j * D : (j + 1) * D, :] = first
        start[:, j * n : (j + 1) * n] = grad + dot(wn1[0:D], first)

    pipelined((second_layer, node_grads), range(groups))
    weight_two = w2_ref[0]

    def grad_rows(span, unused):
        a, size = span[2].start, span[2].size
        return pick(table, row_of(index_ref, 0, a, size), row_of(index_ref, 1, a, size), groups, n)

    def second_grad(span, rows):
        return edge_second(rows, span[2], columns, wn1[D : 2 * D], alive_ref, normed_ref, factor_ref, edge_sums)

    def first_grad(span, second):
        s = span[2]
        first = edge_first(second, s, weight_two, slope_ref)
        first_ref[:, s] = first
        edge_weight_grads(first, second, rows_ref[:, s], hidden_ref[:, s], one_ref, two_ref, edge_sums)
        return first

    def sum_rows(span, first):
        s = span[2]
        rows = [row_of(index_ref, i, s.start, s.size) for i in range(4)]
        add_at(total, first, rows[0], rows[1], groups, n)
        add_at(sums, first, rows[2], rows[3], SLOT_GROUPS, SLOT_COLS)

    pipelined((grad_rows, second_grad, first_grad, sum_rows), spans_of((first_ref,), CHUNK))
    slot_gradients((partner_ref, cross_ref, own_ref), sums, w1[D : 2 * D])
    target_grads(total, w1[2 * D : 3 * D], lambda j: start[:, j * n : (j + 1) * n], grad_ref, groups, n)
    slot_grads = slot_weight_grads(sums, slots)
    write_packed(pieces, one_ref[...], slot_grads, two_ref[...], wn1_grad[...], wn2_grad[...],
                 pack_columns(edge_sums, node_sums))
    unused, core = level_and_core()
    for p in range(4):
        pieces[4 + p] = packed_down_ref[p]
    for p in range(4):
        keep_ref[p] = pieces[core * 4 + p]
        partner_ref[4 + p] = pieces[(1 - core) * 4 + p].astype(B16)


def feat_grad_kernel(up_ref, down_ref, w1t_ref, *rest):
    out_up, out_down = rest[-2:]
    out_up[...] = dot(w1t_ref[0, 0:D], up_ref[...])
    out_down[...] = dot(w1t_ref[1, 0:D], down_ref[...])


def lower_grad_kernel(h0, h1, h2, h3, h4, h5, send_ref, start_ref, out_ref, total):
    groups, n = groups_of(start_ref.shape[1])
    clear((total,))
    add_back(total, (h0, h1, h2, h3, h4, h5), send_ref, groups, n, True)
    for j in range(groups):
        s = slice(j * n, (j + 1) * n)
        out_ref[:, s] = start_ref[:, s] + total[j * D : (j + 1) * D, :]


def unpack_kernel(own_ref, other_ref, w1_ref, w2_ref, wn1_ref, wn2_ref, biases_ref, gains_ref, pieces):
    unused, core = level_and_core()
    for p in range(4):
        pieces[core * 4 + p] = own_ref[p].astype(F32)
        pieces[(1 - core) * 4 + p] = other_ref[p].astype(F32)
    for k in range(2):
        w1_ref[k] = jnp.concatenate([pieces[4 * k], pieces[4 * k + 1, :, 0:D]], axis=1)
        w2_ref[k] = pieces[4 * k + 1, :, D : 2 * D]
        wn1_ref[k] = pieces[4 * k + 2]
        wn2_ref[k] = pieces[4 * k + 3, :, 0:D]
        rows = pieces[4 * k + 3].T
        for i in range(6):
            biases_ref[i, k : k + 1] = rows[D + i : D + i + 1]
        gains_ref[k] = rows[D + 6 : D + 8]


def shape(dims, dtype=F32):
    return jax.ShapeDtypeStruct(dims, dtype)


def call(kernel, name, outs, scratch, scalars=0, stored=(), streamed=None, final=(), raw=()):
    steps, stream_in, stream_out = streamed if streamed else (1, (), ())

    def run(*operands, after=()):
        def whole(space):
            return pl.BlockSpec(memory_space=space)

        def cut(x):
            return pl.BlockSpec((x.shape[0], x.shape[1] // steps), lambda i: (0, i))

        in_specs, placed = [], []
        for i, x in enumerate(operands):
            if i < scalars:
                in_specs.append(whole(pltpu.SMEM))
            elif i in stream_in:
                in_specs.append(cut(x))
            elif i in raw:
                in_specs.append(whole(pltpu.HBM))
                x = pltpu.with_memory_space_constraint(x, pltpu.HBM)
            else:
                in_specs.append(whole(pltpu.VMEM))
                x = pltpu.with_memory_space_constraint(x, pltpu.VMEM)
            placed.append(x)
        in_specs += [whole(pl.ANY) for _ in after]
        out_specs, out_shape = [], []
        for i, x in enumerate(outs):
            if i in stream_out:
                out_specs.append(cut(x))
                out_shape.append(x)
            elif i in stored:
                out_specs.append(whole(pl.ANY))
                out_shape.append(x)
            elif i in final:
                out_specs.append(whole(pltpu.VMEM))
                out_shape.append(x)
            else:
                out_specs.append(whole(pltpu.VMEM))
                out_shape.append(pltpu.VMEM(x.shape, x.dtype))
        return pl.pallas_call(
            kernel,
            name=name,
            grid=(steps,) if streamed else (),
            in_specs=in_specs,
            out_specs=out_specs,
            out_shape=out_shape,
            scratch_shapes=scratch,
            compiler_params=pltpu.CompilerParams(vmem_limit_bytes=VMEM_BYTES),
        )(*placed, *after)

    return run


def core_swap(block):
    return lax.ppermute(block, "band", [(i, i ^ 1) for i in range(lax.axis_size("band"))])


def cross_swap(block):
    last = lax.axis_size("band") - 1
    pairs = [(i, i + 1) for i in range(1, last, 2)]
    return lax.ppermute(block, "band", pairs + [(b, a) for a, b in pairs] + [(0, 0), (last, last)])


def along_level(block, step):
    count = lax.axis_size("level")
    return lax.ppermute(block, "level", [(i, (i + step) % count) for i in range(count)])


def along_band(block, step):
    count = lax.axis_size("band")
    return lax.ppermute(block, "band", [(i, (i + step) % count) for i in range(count)])


def across_bands(blocks):
    below, above, own = blocks
    return [along_band(above, 1), along_band(below, -1), own]


def along_levels(blocks, sign):
    return blocks + [along_level(jnp.stack([b[d] for b in blocks]), sign * d) for d in (1, 2, 3)]


def chip_ring(block, step, core_strides):
    count = lax.axis_size("band")
    pairs = []
    for i in range(count):
        stride = core_strides[i % 2]
        at = (i // stride) % 4
        pairs.append((i, i + (((at + step) % 4) - at) * stride))
    return lax.ppermute(block, "band", pairs)


def rounded(values):
    return lax.reduce_precision(values, 8, 7)


def sum_of_four(values, first, second, third):
    return (values + second.astype(F32)) + (first.astype(F32) + third.astype(F32))


def sum_along(values, core_strides):
    own = rounded(values)
    sent = own.astype(B16)
    return sum_of_four(own, *(chip_ring(sent, d, core_strides) for d in (1, 2, 3)))


def shards(
    lower_nodes, latent, up_feat, down_feat, up_send, up_counts, up_senders, up_targets,
    down_send, down_counts, down_senders, down_targets,
    edge_w1, edge_w2, node_w1, node_w2, biases, norm_gains, lower_cot, upper_cot,
):
    lower, upper = lower_nodes.T, latent.T
    feat_up, feat_down = up_feat.T, down_feat.T
    cot_lower, cot_upper = lower_cot.T, upper_cot.T
    w1, wn1 = edge_w1.transpose(0, 2, 1), node_w1.transpose(0, 2, 1)
    w2, wn2 = edge_w2, node_w2
    edges, lower_rows, upper_rows = up_feat.shape[0], lower_nodes.shape[0], latent.shape[0]
    dense = (edges // 128, 128)
    senders_up, targets_up, senders_down, targets_down = (
        x.reshape(dense) for x in (up_senders, up_targets, down_senders, down_targets))
    bias_rows = biases.transpose(1, 0, 2)

    lower_groups, lower_n = groups_of(lower_rows)
    upper_groups, upper_n = groups_of(upper_rows)
    lower_table, upper_table = (lower_groups * D, lower_n), (upper_groups * D, upper_n)
    slots = pltpu.VMEM((SLOT_GROUPS * D, SLOT_COLS), B16)
    block, four = shape((4, D, 128), B16), shape((4, D, 128))
    wide32, wide16, row = shape((D, edges)), shape((D, edges), B16), shape((1, edges))
    steps = edges // EDGE_BLOCK

    early = (up_send, lower, senders_up, targets_up, senders_down, targets_down, upper, w1, bias_rows, norm_gains,
             down_send, w2, wn1, wn2)
    count = len(early)
    (*sent, up_send, lower, senders_up, targets_up, senders_down, targets_down, upper, w1, bias_rows,
     norm_gains, down_send, w2, wn1, wn2) = call(
        functools.partial(send_kernel, count), "send_lower", [block] * 3 + [shape(x.shape, x.dtype) for x in early],
        [pltpu.VMEM(lower_table, B16), pltpu.SemaphoreType.DMA((count,))], 0, raw=range(count),
    )(*early)
    index, lives = shape((4, *dense), jnp.int32), shape((1, *dense))
    turned = [shape((2, D, 8)), shape((2, 3 * D, D), B16), shape((2, D, D), B16), shape((2, 2 * D, D), B16), shape((2, D, D), B16)]
    index_up, alive_up, index_down, alive_down, columns, w1t, w2t, wn1t, wn2t = call(
        functools.partial(tables_kernel, upper_rows, lower_rows), "edge_tables", [index, lives, index, lives] + turned,
        [pltpu.SMEM((1, 12), jnp.int32), pltpu.SMEM((1, 12), jnp.int32), pltpu.SemaphoreType.DMA((2,))], 0, raw=(0, 1),
    )(up_counts, down_counts, senders_up, targets_up, senders_down, targets_down, w1, w2, wn1, wn2, bias_rows, norm_gains)

    def part(k, block, first, size, name, table, index, feat, local, after):
        return call(
            functools.partial(part_kernel, k, block, first), name, [shape((D, size)), shape((2 * D, size), B16)],
            [pltpu.VMEM(table, B16), pltpu.SemaphoreType.DMA], 0, raw=(1,),
        )(index, feat, local, w1, columns, after=after)

    sent = [core_swap(sent[0]), cross_swap(sent[1]), sent[2]]
    half = edges // 2
    part_a, rows_a = part(1, half // 2, 0, half, "part_down_a", lower_table, index_down, feat_down, lower, ())
    sent, part_a = lax.optimization_barrier((sent, part_a))
    part_up, rows_up = part(0, EDGE_BLOCK, 0, edges, "part_up", upper_table, index_up, feat_up, upper, (sent[0], sent[1]))
    up_slots = along_levels(sent, 1)
    up_slots, part_up = lax.optimization_barrier((up_slots, part_up))
    (upper_new, summed_up, s0, s1, s2, slope, normed, hidden, factor, *nodes_up) = call(
        up_forward_kernel, "up_forward",
        [shape((D, upper_rows)), shape((D, upper_rows), B16)] + [block] * 3 + [wide32, wide32, wide16, row,
         shape((D, upper_rows), B16), shape((D, upper_rows)), shape((D, upper_rows)), shape((1, upper_rows))],
        [slots, pltpu.VMEM(upper_table, F32), pltpu.VMEM(upper_table, B16), pltpu.VMEM((D, upper_rows), F32),
         pltpu.SemaphoreType.DMA], 0, (0,),
    )(part_up, alive_up, index_up, *up_slots, upper, down_send, w1, w2t, wn1, wn2t, columns)
    sent = across_bands([s0, s1, s2])
    part_b, rows_b = part(1, half // 2, half, half, "part_down_b", lower_table, index_down, feat_down, lower, (sent[0], sent[1]))
    down_slots = along_levels(sent, 1)
    down_slots, part_b = lax.optimization_barrier((down_slots, part_b))
    sums_shape = shape((SLOT_GROUPS * D, SLOT_COLS))
    node16 = shape((D, lower_rows), B16)
    (lower_new, g0, g1, g2, first_down, second_down, hidden_down, sums_down, edge_sums, node_sums, *nodes) = call(
        down_kernel, "down_sweep",
        [shape((D, lower_rows))] + [block] * 3 + [wide16] * 3 + [sums_shape, four, four, shape(lower_table, B16),
         shape(lower_table, B16), node16, node16],
        [slots, pltpu.VMEM(lower_table, F32), pltpu.VMEM((D, edges), F32),
         pltpu.VMEM((D, edges), F32), pltpu.VMEM((1, edges), F32),
         pltpu.VMEM((D, lower_rows), F32), pltpu.SemaphoreType.DMA], 0, (0,),
    )(part_a, part_b, alive_down, index_down, *down_slots, lower, cot_lower, w1, w1t, w2, w2t, wn1, wn1t, wn2, wn2t, columns)
    back = across_bands([g0, g1, g2])
    (packed_down,) = call(
        down_rest_kernel, "down_rest", [four],
        [slots, pltpu.VMEM((D, 2 * D), F32), pltpu.VMEM((D, D), F32), pltpu.VMEM((D, 2 * D), F32), pltpu.VMEM((D, D), F32),
         pltpu.VMEM((4, D, 128), F32), pltpu.VMEM((4, D, 128), F32)], 0, (), (steps, (), ()),
    )(rows_a, rows_b, first_down, second_down, hidden_down, *down_slots, sums_down, edge_sums, node_sums, *nodes, lower,
      after=(back[0], back[1]))
    down_back = along_levels(back, -1)
    down_back, packed_down = lax.optimization_barrier((down_back, packed_down))
    (partner, cross, own, first_up, grad_latent, keep) = call(
        up_backward_kernel, "up_backward",
        [shape((8, D, 128), B16), block, block, wide16, shape((D, upper_rows)), four],
        [slots, pltpu.VMEM(upper_table, B16), pltpu.VMEM(upper_table, F32), pltpu.VMEM(upper_table, F32),
         pltpu.VMEM((SLOT_GROUPS * D, SLOT_COLS), F32), pltpu.VMEM((D, upper_rows), F32),
         pltpu.VMEM((D, 2 * D), F32), pltpu.VMEM((D, D), F32), pltpu.VMEM((4, D, 128), F32), pltpu.VMEM((4, D, 128), F32),
         pltpu.VMEM((D, 2 * D), F32), pltpu.VMEM((D, D), F32), pltpu.VMEM((8, D, 128), F32)], 0, (), None, (4,),
    )(index_up, rows_up, *down_back, down_send, cot_upper, upper, summed_up, *up_slots,
      slope, normed, hidden, factor, alive_up, packed_down, *nodes_up, w1t, w2, wn1t, wn2, columns)

    partner = core_swap(partner)
    total = rounded(rounded(keep) + partner[4:].astype(F32))
    cross = cross_swap(cross)
    total = sum_along(total, (2, 8))
    feat_grad_up, feat_grad_down = call(
        feat_grad_kernel, "feat_grads", [wide32, wide32], [], 0, (), (steps, (0, 1), (0, 1)),
    )(first_up, first_down, w1t, after=(partner,))
    total, cross, feat_grad_up = lax.optimization_barrier((total, cross, feat_grad_up))
    blocks = (partner, cross, own)
    total = rounded(total)
    levels = [
        along_level(jnp.concatenate([jnp.stack([b[d] for b in blocks]), total.astype(B16)]), -d) for d in (1, 2, 3)
    ]
    (start_lower,) = call(
        down_targets_kernel, "down_targets", [shape((D, lower_rows))], [pltpu.VMEM(lower_table, F32)],
    )(index_down, first_down, cot_lower, nodes[0], w1t, wn1t, after=(total,))
    levels, start_lower = lax.optimization_barrier((levels, start_lower))
    total = sum_of_four(total, *(b[3:] for b in levels))
    (grad_lower,) = call(lower_grad_kernel, "lower_grad", [shape((D, lower_rows))], [pltpu.VMEM(lower_table, F32)], 0, (), None, (0,))(
        *blocks, *levels, up_send, start_lower)
    total = sum_along(total, (8, 2))
    total, grad_lower = lax.optimization_barrier((total, grad_lower))
    total = rounded(total).astype(B16)
    w1_grad, w2_grad, wn1_grad, wn2_grad, bias_grad, gain_grad = call(
        unpack_kernel, "unpack",
        [shape((2, D, 3 * D)), shape((2, D, D)), shape((2, D, 2 * D)), shape((2, D, D)), shape((6, 2, D)), shape((2, 2, D))],
        [pltpu.VMEM((8, D, 128), F32)], 0, (), None, range(6))(total, core_swap(total))
    return (
        lower_new.T, upper_new.T, grad_lower.T, grad_latent.T, feat_grad_up.T, feat_grad_down.T,
        w1_grad.transpose(0, 2, 1), w2_grad, wn1_grad.transpose(0, 2, 1), wn2_grad, bias_grad.transpose(1, 0, 2), gain_grad,
    )


def solution(mesh):
    rows, index, whole = P(("band", "level"), None), P(("band", "level")), P()
    placed = (rows,) * 6 + (index, index) + (rows,) * 2 + (index, index) + (whole,) * 6 + (rows,) * 2
    return jax.shard_map(
        shards,
        mesh=mesh,
        in_specs=placed,
        out_specs=(rows,) * 6 + (whole,) * 6,
        check_vma=False,
    )
```

```python
import functools

import jax
import jax.numpy as jnp
from jax import lax
from jax.experimental import pallas as pl
from jax.experimental.pallas import tpu as pltpu
from jax.sharding import PartitionSpec as P

EPSILON = 1e-05
F32 = jnp.float32
B16 = jnp.bfloat16
D = 64
SLOT_GROUPS, SLOT_COLS = 6, 256
EDGE_BLOCK = 3072
CHUNK = 1024
VMEM_BYTES = 24 * 1024 * 1024


def groups_of(rows):
    return (4, rows // 4) if rows > 1024 else (rows // 256, 256)


def dot(a, b):
    return jnp.dot(a, b, preferred_element_type=F32)


def dot_rows(a, b):
    return lax.dot_general(a, b, (((1,), (1,)), ((), ())), preferred_element_type=F32)


def halves(x):
    high = x.astype(B16)
    return high, (x - high.astype(F32)).astype(B16)


def one_hot(column, n):
    rows = lax.broadcasted_iota(jnp.int16, (n, column.shape[1]), 0)
    return jnp.where(rows == column.astype(jnp.int16), jnp.ones((), B16), jnp.zeros((), B16))


def place(index, groups, n):
    group = jnp.zeros_like(index)
    for j in range(1, groups):
        group = group + (index >= j * n).astype(jnp.int32)
    return group, index - group * n


def level_and_core():
    return lax.axis_index("level").astype(jnp.int32), lax.axis_index("band").astype(jnp.int32) & 1


def band_offsets(swapped):
    unused, core = level_and_core()
    return (2 - 2 * core, 2 * core, 1) if swapped else (0, 2, 1)


def slot_place(senders, swapped):
    level, unused = level_and_core()
    distance = (level - ((senders >> 7) & 3)) & 3
    offset = senders >> 9
    source = jnp.where(offset == 1, 2, jnp.where(offset == band_offsets(swapped)[0], 0, 1))
    block = distance * 3 + source
    return block >> 1, ((block & 1) << 7) | (senders & 127)


def live(senders, counts_ref):
    peer = senders >> 7
    limit = jnp.zeros_like(senders)
    for j in range(12):
        limit = jnp.where(peer == j, counts_ref[0, j], limit)
    return ((senders & 127) < limit).astype(F32)


def choose(stacked, group, groups):
    picked = stacked[0:D]
    for j in range(1, groups):
        picked = jnp.where(group == j, stacked[j * D : (j + 1) * D], picked)
    return picked


def row_of(ref, k, start, size):
    rows = size // 128
    if not isinstance(start, int):
        start = start // 128
        return jnp.concatenate([ref[k, pl.ds(start + r, 1), :] for r in range(rows)], axis=1)
    return jnp.concatenate([ref[k, r : r + 1, :] for r in range(start // 128, start // 128 + rows)], axis=1)


def pick(table, group, column, groups, n):
    return choose(dot(table[...], one_hot(column, n)), group, groups).astype(B16)


def spread(values, group, groups):
    wide = jnp.broadcast_to(group.astype(jnp.int16), values.shape)
    nothing = jnp.zeros_like(values)
    return jnp.concatenate([jnp.where(wide == j, values, nothing) for j in range(groups)], axis=0)


def add_at(total, values, group, column, groups, n):
    total[...] += dot_rows(spread(values, group, groups), one_hot(column, n))


def pack_table(table, source, groups, n):
    for j in range(groups):
        table[j * D : (j + 1) * D, :] = source[:, j * n : (j + 1) * n]


def columns_of(biases_ref, gains_ref, k):
    rows = [biases_ref[i, k : k + 1] for i in range(6)] + [gains_ref[k]]
    return jnp.concatenate(rows, axis=0).T


def fold(values):
    total = values[:, 0:128]
    for i in range(128, values.shape[1], 128):
        total = total + values[:, i : i + 128]
    return total


def norm_parts(values):
    centre = values - jnp.sum(values, axis=0, keepdims=True) * (1.0 / D)
    spread_sum = jnp.sum(centre * centre, axis=0, keepdims=True) * (1.0 / D)
    factor = lax.rsqrt(spread_sum + EPSILON)
    return centre * factor, factor


def norm_back(grad, normed, factor, gain):
    scaled = grad * gain
    first = jnp.sum(scaled, axis=0, keepdims=True) * (1.0 / D)
    second = jnp.sum(scaled * normed, axis=0, keepdims=True) * (1.0 / D)
    return factor * (scaled - first - normed * second)


def sigmoid(values):
    return 0.5 * jnp.tanh(0.5 * values) + 0.5


def send_rows(send_ref, offset):
    level, unused = level_and_core()
    return jnp.concatenate(
        [send_ref[pl.ds(offset * 4 + ((level + d) & 3), 1), :] for d in range(4)], axis=1
    )


def send_blocks(outs, table, send_ref, groups, n, swapped):
    for j, offset in enumerate(band_offsets(swapped)):
        group, column = place(send_rows(send_ref, offset), groups, n)
        rows = pick(table, group, column, groups, n)
        for d in range(4):
            outs[j][d] = rows[:, d * 128 : (d + 1) * 128]


def add_back(total, blocks, send_ref, groups, n, swapped):
    for j, offset in enumerate(band_offsets(swapped)):
        group, column = place(send_rows(send_ref, offset), groups, n)
        values = jnp.concatenate([block_at(blocks, d, j) for d in range(4)], axis=1)
        add_at(total, values, group, column, groups, n)


def block_at(received, d, j):
    return received[j][0] if d == 0 else received[2 + d][j]


def slot_table(table, received):
    for t in range(12):
        table[(t >> 1) * D : ((t >> 1) + 1) * D, (t & 1) * 128 : ((t & 1) + 1) * 128] = block_at(received, t // 3, t % 3)


def slot_gradients(outs, sums, weight):
    for j in range(SLOT_GROUPS):
        high, low = halves(sums[j * D : (j + 1) * D, :])
        grads = (dot(weight, high) + dot(weight, low)).astype(B16)
        for t in (2 * j, 2 * j + 1):
            outs[t % 3][t // 3] = grads[:, (t & 1) * 128 : ((t & 1) + 1) * 128]


def over_blocks(total, block, body):
    block = min(block, total)
    if block == total:
        body(pl.ds(0, block))
        return

    def step(i, carry):
        body(pl.ds(pl.multiple_of(i * block, block), block))
        return carry

    lax.fori_loop(0, total // block, step, 0)


def pipelined(stages, spans):
    held = [None] * len(spans)
    for t in range(len(spans) + len(stages) - 1):
        for k in reversed(range(len(stages))):
            i = t - k
            if 0 <= i < len(spans):
                held[i] = stages[k](spans[i], held[i])


def spans_of(parts, chunk):
    spans, start = [], 0
    for which, ref in enumerate(parts):
        size = min(chunk, ref.shape[1])
        for at in range(0, ref.shape[1], size):
            spans.append((which, pl.ds(at, size), pl.ds(start + at, size)))
        start += ref.shape[1]
    return spans


def tables_kernel(upper_rows, lower_rows, counts_up, counts_down, senders_up, targets_up, senders_down, targets_down,
                  w1_ref, w2_ref, wn1_ref, wn2_ref, biases_ref, gains_ref, index_up, alive_up, index_down, alive_down, columns_ref, w1t_ref, w2t_ref, wn1t_ref, wn2t_ref, limits_up, limits_down, sems):
    copies = [pltpu.make_async_copy(counts_up, limits_up, sems.at[0]), pltpu.make_async_copy(counts_down, limits_down, sems.at[1])]
    for copy in copies:
        copy.start()
    sweeps = ((index_up, senders_up, targets_up, upper_rows, True), (index_down, senders_down, targets_down, lower_rows, False))
    for index_ref, senders_ref, targets_ref, rows, swapped in sweeps:
        index_ref[0], index_ref[1] = place(targets_ref[...], *groups_of(rows))
        index_ref[2], index_ref[3] = slot_place(senders_ref[...], swapped)
    for k in range(2):
        columns_ref[k] = columns_of(biases_ref, gains_ref, k)
        for turned, ref in ((w1t_ref, w1_ref), (w2t_ref, w2_ref), (wn1t_ref, wn1_ref), (wn2t_ref, wn2_ref)):
            turned[k] = transposed(ref[k])
    for copy in copies:
        copy.wait()
    alive_up[0] = live(senders_up[...], limits_up)
    alive_down[0] = live(senders_down[...], limits_down)


def send_kernel(count, *refs):
    sources, refs = refs[:count], refs[count:]
    sent, held, table, sems = refs[:3], refs[3:-2], refs[-2], refs[-1]
    copies = [pltpu.make_async_copy(a, b, sems.at[i]) for i, (a, b) in enumerate(zip(sources, held))]
    for copy in copies:
        copy.start()
    for copy in copies[:2]:
        copy.wait()
    send_ref, source_ref = held[:2]
    groups, n = groups_of(source_ref.shape[1])
    pack_table(table, source_ref, groups, n)
    send_blocks(sent, table, send_ref, groups, n, True)
    for copy in copies[2:]:
        copy.wait()


def part_kernel(k, block, first, index_ref, feat_ref, local_ref, w1_ref, columns_ref, *rest):
    part_ref, rows_ref, table, sem = rest[-4:]
    size = part_ref.shape[1]
    copy = pltpu.make_async_copy(feat_ref.at[:, pl.ds(first, size)], rows_ref.at[0:D], sem)
    copy.start()
    groups, n = groups_of(local_ref.shape[1])
    pack_table(table, local_ref, groups, n)
    columns = columns_ref[k]
    weight = jnp.concatenate([w1_ref[k, :, 0:D], w1_ref[k, :, 2 * D : 3 * D]], axis=1)

    def body(s):
        a = first + s.start
        rows_ref[D : 2 * D, s] = pick(table, row_of(index_ref, 0, a, s.size), row_of(index_ref, 1, a, s.size), groups, n)

    over_blocks(size, block, body)
    copy.wait()
    part_ref[...] = dot(weight, rows_ref[...]) + columns[:, 0:1]


def edges_forward(k, parts, alive_ref, index_ref, table, w1_ref, w2t_ref, columns, total, groups, n,
                  slope_ref, normed_ref, hidden_ref, factor_ref):
    weight_slot = w1_ref[k, :, D : 2 * D]
    weight_two = w2t_ref[k]
    total[...] = jnp.zeros_like(total)

    def slot_rows(span, unused):
        a, size = span[2].start, span[2].size
        return pick(table, row_of(index_ref, 2, a, size), row_of(index_ref, 3, a, size), SLOT_GROUPS, SLOT_COLS)

    def first_layer(span, picked):
        which, t, s = span
        first = parts[which][:, t] + dot(weight_slot, picked)
        gate = sigmoid(first)
        hidden = (first * gate).astype(B16)
        slope_ref[:, s] = gate * (1.0 + first * (1.0 - gate))
        hidden_ref[:, s] = hidden
        return hidden

    def second_layer(span, hidden):
        s = span[2]
        normed, factor = norm_parts(dot(weight_two, hidden) + columns[:, 1:2])
        alive = row_of(alive_ref, 0, s.start, s.size)
        normed_ref[:, s] = normed
        factor_ref[:, s] = factor
        return ((normed * columns[:, 6:7] + columns[:, 2:3]) * alive).astype(B16)

    def sum_messages(span, messages):
        a, size = span[2].start, span[2].size
        add_at(total, messages, row_of(index_ref, 0, a, size), row_of(index_ref, 1, a, size), groups, n)

    pipelined((slot_rows, first_layer, second_layer, sum_messages), spans_of(parts, CHUNK))


def node_first(k, inputs, wn1_ref, columns):
    first = dot(wn1_ref[k], inputs) + columns[:, 3:4]
    gate = sigmoid(first)
    return (first * gate).astype(B16), gate * (1.0 + first * (1.0 - gate))


def node_second(hidden, weight_two, columns):
    return norm_parts(dot(weight_two, hidden) + columns[:, 4:5])


def node_second_grad(grad, normed, factor, columns, sums_ref):
    sums_ref[2] += fold(grad)
    sums_ref[3] += fold(grad * normed)
    return norm_back(grad, normed, factor, columns[:, 7:8]).astype(B16)


def node_weight_grads(first, second, inputs, hidden, one_ref, two_ref, sums_ref):
    sums_ref[0] += fold(first.astype(F32))
    sums_ref[1] += fold(second.astype(F32))
    one_ref[...] += dot_rows(first, inputs)
    two_ref[...] += dot_rows(hidden, second)


def clear(refs):
    for ref in refs:
        ref[...] = jnp.zeros_like(ref)


def transposed(weight):
    return weight.astype(F32).T.astype(B16)


def edge_second(grad_rows, s, columns, weight_sum, alive_ref, normed_ref, factor_ref, sums_ref):
    grad = dot(weight_sum, grad_rows) * row_of(alive_ref, 0, s.start, s.size)
    normed = normed_ref[:, s]
    sums_ref[2] += fold(grad)
    sums_ref[3] += fold(grad * normed)
    return norm_back(grad, normed, factor_ref[:, s], columns[:, 6:7]).astype(B16)


def edge_first(second, s, weight_two, slope_ref):
    return (dot(weight_two, second) * slope_ref[:, s]).astype(B16)


def edge_weight_grads(first, second, rows, hidden, one_ref, two_ref, sums_ref):
    sums_ref[0] += fold(first.astype(F32))
    sums_ref[1] += fold(second.astype(F32))
    one_ref[...] += dot_rows(first, rows)
    two_ref[...] += dot_rows(hidden, second)


def pack_columns(edge_sums, node_sums):
    order = (edge_sums[0], edge_sums[1], edge_sums[2], node_sums[0], node_sums[1], node_sums[2], edge_sums[3], node_sums[3])
    columns = [jnp.sum(v, axis=1, keepdims=True) for v in order]
    lanes = lax.broadcasted_iota(jnp.int32, (D, D), 1)
    packed = jnp.zeros((D, D), F32)
    for i, column in enumerate(columns):
        packed = jnp.where(lanes == i, column, packed)
    return packed


def slot_weight_grads(sums, table):
    total = jnp.zeros((D, D), F32)
    for j in range(SLOT_GROUPS):
        high, low = halves(sums[j * D : (j + 1) * D, :])
        rows = table[j * D : (j + 1) * D, :]
        total = total + dot_rows(high, rows) + dot_rows(low, rows)
    return total


def target_grads(total, weight, start, out_ref, groups, n):
    for j in range(groups):
        high, low = halves(total[j * D : (j + 1) * D, :])
        out_ref[:, j * n : (j + 1) * n] = start(j) + dot(weight, high) + dot(weight, low)


def up_forward_kernel(part_ref, alive_ref, index_ref, r0, r1, r2, r3, r4, r5, local_ref, send_ref,
                      w1_ref, w2t_ref, wn1_ref, wn2t_ref, columns_ref,
                      out_ref, summed_ref, s0, s1, s2, slope_ref, normed_ref, hidden_ref, factor_ref,
                      node_hidden_ref, node_slope_ref, node_normed_ref, node_factor_ref, slots, total, table, out, sem):
    groups, n = groups_of(local_ref.shape[1])
    columns = columns_ref[0]
    slot_table(slots, (r0, r1, r2, r3, r4, r5))
    edges_forward(0, (part_ref,), alive_ref, index_ref, slots, w1_ref, w2t_ref, columns, total, groups, n,
                  slope_ref, normed_ref, hidden_ref, factor_ref)
    weight_two = wn2t_ref[0]

    def first_layer(j, unused):
        s = slice(j * n, (j + 1) * n)
        summed = total[j * D : (j + 1) * D, :].astype(B16)
        summed_ref[:, s] = summed
        return node_first(0, jnp.concatenate([local_ref[:, s], summed], axis=0), wn1_ref, columns)

    def second_layer(j, held):
        s = slice(j * n, (j + 1) * n)
        hidden, slope = held
        normed, factor = node_second(hidden, weight_two, columns)
        node_hidden_ref[:, s] = hidden
        node_slope_ref[:, s] = slope
        node_normed_ref[:, s] = normed
        node_factor_ref[:, s] = factor
        result = local_ref[:, s].astype(F32) + normed * columns[:, 7:8] + columns[:, 5:6]
        out[:, s] = result
        table[j * D : (j + 1) * D, :] = result.astype(B16)

    pipelined((first_layer, second_layer), range(groups))
    copy = pltpu.make_async_copy(out, out_ref, sem)
    copy.start()
    send_blocks((s0, s1, s2), table, send_ref, groups, n, False)
    copy.wait()


def down_kernel(part_a, part_b, alive_ref, index_ref, r0, r1, r2, r3, r4, r5, local_ref, cot_ref,
                w1_ref, w1t_ref, w2_ref, w2t_ref, wn1_ref, wn1t_ref, wn2_ref, wn2t_ref, columns_ref,
                out_ref, g0, g1, g2, first_ref, second_ref, hidden_ref, sums_ref, edge_sums, node_sums,
                table, summed_ref, node_hidden_ref, node_second_ref,
                slots, total, slope_ref, normed_ref, factor_ref, out, sem):
    groups, n = groups_of(local_ref.shape[1])
    columns = columns_ref[1]
    slot_table(slots, (r0, r1, r2, r3, r4, r5))
    parts = (part_a, part_b)
    edges_forward(1, parts, alive_ref, index_ref, slots, w1_ref, w2t_ref, columns, total, groups, n,
                  slope_ref, normed_ref, hidden_ref, factor_ref)
    clear((node_sums, edge_sums, sums_ref))
    wn2 = wn2_ref[1]
    wn2_t = wn2t_ref[1]
    wn1 = wn1t_ref[1]

    def first_layer(j, unused):
        summed = total[j * D : (j + 1) * D, :].astype(B16)
        summed_ref[j * D : (j + 1) * D, :] = summed
        inputs = jnp.concatenate([local_ref[:, j * n : (j + 1) * n], summed], axis=0)
        return node_first(1, inputs, wn1_ref, columns)

    def second_layer(j, held):
        hidden, slope = held
        s = slice(j * n, (j + 1) * n)
        normed, factor = node_second(hidden, wn2_t, columns)
        out[:, s] = local_ref[:, s].astype(F32) + normed * columns[:, 7:8] + columns[:, 5:6]
        second = node_second_grad(cot_ref[:, s], normed, factor, columns, node_sums)
        node_hidden_ref[:, s] = hidden
        node_second_ref[:, s] = second
        return slope, second

    def node_grads(j, held):
        slope, second = held
        table[j * D : (j + 1) * D, :] = (dot(wn2, second) * slope).astype(B16)

    pipelined((first_layer, second_layer, node_grads), range(groups))
    copy = pltpu.make_async_copy(out, out_ref, sem)
    copy.start()
    weight_two = w2_ref[1]
    weight_slot = w1t_ref[1, D : 2 * D]

    def grad_rows(span, unused):
        a, size = span[2].start, span[2].size
        return pick(table, row_of(index_ref, 0, a, size), row_of(index_ref, 1, a, size), groups, n)

    def second_grad(span, rows):
        return edge_second(rows, span[2], columns, wn1[D : 2 * D], alive_ref, normed_ref, factor_ref, edge_sums)

    def first_grad(span, second):
        s = span[2]
        first = edge_first(second, s, weight_two, slope_ref)
        first_ref[:, s] = first
        second_ref[:, s] = second
        return first

    def sum_slots(span, first):
        a, size = span[2].start, span[2].size
        add_at(sums_ref, first, row_of(index_ref, 2, a, size), row_of(index_ref, 3, a, size), SLOT_GROUPS, SLOT_COLS)

    pipelined((grad_rows, second_grad, first_grad, sum_slots), spans_of(parts, CHUNK))
    slot_gradients((g0, g1, g2), sums_ref, weight_slot)
    copy.wait()


def down_targets_kernel(index_ref, first_ref, cot_ref, table, w1t_ref, wn1t_ref, *rest):
    grad_ref, total = rest[-2:]
    groups, n = groups_of(cot_ref.shape[1])
    weight = w1t_ref[1, 2 * D : 3 * D]
    total[...] = jnp.zeros_like(total)

    def body(s):
        group, column = row_of(index_ref, 0, s.start, s.size), row_of(index_ref, 1, s.start, s.size)
        add_at(total, first_ref[:, s], group, column, groups, n)

    over_blocks(first_ref.shape[1], EDGE_BLOCK, body)
    weight_node = wn1t_ref[1, 0:D]

    def start(j):
        return cot_ref[:, j * n : (j + 1) * n] + dot(weight_node, table[j * D : (j + 1) * D, :])

    target_grads(total, weight, start, grad_ref, groups, n)


def down_rest_kernel(rows_a, rows_b, first_ref, second_ref, hidden_ref, r0, r1, r2, r3, r4, r5, sums_ref, edge_in, node_in,
                     table, summed_ref, node_hidden_ref, node_second_ref, local_ref, *rest):
    packed_ref, slots, one_ref, two_ref, wn1_grad, wn2_grad, edge_sums, node_sums = rest[-8:]
    step = pl.program_id(0)

    @pl.when(step == 0)
    def _():
        clear((one_ref, two_ref, wn1_grad, wn2_grad))
        edge_sums[...] = edge_in[...]
        node_sums[...] = node_in[...]

    s = pl.ds(pl.multiple_of(step * EDGE_BLOCK, EDGE_BLOCK), EDGE_BLOCK)
    first = first_ref[:, s]
    rows = jnp.where(step == 0, rows_a[...], rows_b[...])
    edge_weight_grads(first, second_ref[:, s], rows, hidden_ref[:, s], one_ref, two_ref, edge_sums)

    @pl.when(step == pl.num_programs(0) - 1)
    def _():
        groups, n = groups_of(local_ref.shape[1])
        for j in range(groups):
            t, rows = slice(j * n, (j + 1) * n), slice(j * D, (j + 1) * D)
            inputs = jnp.concatenate([local_ref[:, t], summed_ref[rows, :]], axis=0)
            node_weight_grads(table[rows, :], node_second_ref[:, t], inputs, node_hidden_ref[:, t], wn1_grad, wn2_grad, node_sums)
        slot_table(slots, (r0, r1, r2, r3, r4, r5))
        write_packed(packed_ref, one_ref[...], slot_weight_grads(sums_ref, slots), two_ref[...],
                     wn1_grad[...], wn2_grad[...], pack_columns(edge_sums, node_sums))


def write_packed(packed_ref, one, slot_grads, two, wn1_grad, wn2_grad, columns):
    packed_ref[0] = jnp.concatenate([one[:, 0:D], slot_grads], axis=1)
    packed_ref[1] = jnp.concatenate([one[:, D : 2 * D], two], axis=1)
    packed_ref[2] = wn1_grad
    packed_ref[3] = jnp.concatenate([wn2_grad, columns], axis=1)


def up_backward_kernel(index_ref, rows_ref, h0, h1, h2, h3, h4, h5,
                       send_ref, cot_ref, local_ref, summed_ref, r0, r1, r2, r3, r4, r5, slope_ref, normed_ref, hidden_ref, factor_ref, alive_ref, packed_down_ref,
                       node_hidden_ref, node_slope_ref, node_normed_ref, node_factor_ref, w1t_ref, w2_ref, wn1t_ref, wn2_ref, columns_ref,
                       partner_ref, cross_ref, own_ref, first_ref, grad_ref, keep_ref,
                       slots, table, back, total, sums, start, one_ref, two_ref, edge_sums, node_sums, wn1_grad, wn2_grad, pieces):
    groups, n = groups_of(local_ref.shape[1])
    columns = columns_ref[0]
    clear((back, total, sums, one_ref, two_ref, edge_sums, node_sums, wn1_grad, wn2_grad))
    slot_table(slots, (r0, r1, r2, r3, r4, r5))
    add_back(back, (h0, h1, h2, h3, h4, h5), send_ref, groups, n, False)
    wn2 = wn2_ref[0]
    wn1 = wn1t_ref[0]
    w1 = w1t_ref[0]

    def second_layer(j, unused):
        s = slice(j * n, (j + 1) * n)
        grad = cot_ref[:, s] + back[j * D : (j + 1) * D, :]
        return grad, node_second_grad(grad, node_normed_ref[:, s], node_factor_ref[:, s], columns, node_sums)

    def node_grads(j, held):
        grad, second = held
        s = slice(j * n, (j + 1) * n)
        inputs = jnp.concatenate([local_ref[:, s], summed_ref[:, s]], axis=0)
        first = (dot(wn2, second) * node_slope_ref[:, s]).astype(B16)
        node_weight_grads(first, second, inputs, node_hidden_ref[:, s], wn1_grad, wn2_grad, node_sums)
        table[j * D : (j + 1) * D, :] = first
        start[:, j * n : (j + 1) * n] = grad + dot(wn1[0:D], first)

    pipelined((second_layer, node_grads), range(groups))
    weight_two = w2_ref[0]

    def grad_rows(span, unused):
        a, size = span[2].start, span[2].size
        return pick(table, row_of(index_ref, 0, a, size), row_of(index_ref, 1, a, size), groups, n)

    def second_grad(span, rows):
        return edge_second(rows, span[2], columns, wn1[D : 2 * D], alive_ref, normed_ref, factor_ref, edge_sums)

    def first_grad(span, second):
        s = span[2]
        first = edge_first(second, s, weight_two, slope_ref)
        first_ref[:, s] = first
        edge_weight_grads(first, second, rows_ref[:, s], hidden_ref[:, s], one_ref, two_ref, edge_sums)
        return first

    def sum_rows(span, first):
        s = span[2]
        rows = [row_of(index_ref, i, s.start, s.size) for i in range(4)]
        add_at(total, first, rows[0], rows[1], groups, n)
        add_at(sums, first, rows[2], rows[3], SLOT_GROUPS, SLOT_COLS)

    pipelined((grad_rows, second_grad, first_grad, sum_rows), spans_of((first_ref,), CHUNK))
    slot_gradients((partner_ref, cross_ref, own_ref), sums, w1[D : 2 * D])
    target_grads(total, w1[2 * D : 3 * D], lambda j: start[:, j * n : (j + 1) * n], grad_ref, groups, n)
    slot_grads = slot_weight_grads(sums, slots)
    write_packed(pieces, one_ref[...], slot_grads, two_ref[...], wn1_grad[...], wn2_grad[...],
                 pack_columns(edge_sums, node_sums))
    unused, core = level_and_core()
    for p in range(4):
        pieces[4 + p] = packed_down_ref[p]
    for p in range(4):
        keep_ref[p] = pieces[core * 4 + p]
        partner_ref[4 + p] = pieces[(1 - core) * 4 + p].astype(B16)


def feat_grad_kernel(up_ref, down_ref, w1t_ref, *rest):
    out_up, out_down = rest[-2:]
    out_up[...] = dot(w1t_ref[0, 0:D], up_ref[...])
    out_down[...] = dot(w1t_ref[1, 0:D], down_ref[...])


def lower_grad_kernel(h0, h1, h2, h3, h4, h5, send_ref, start_ref, out_ref, total):
    groups, n = groups_of(start_ref.shape[1])
    clear((total,))
    add_back(total, (h0, h1, h2, h3, h4, h5), send_ref, groups, n, True)
    for j in range(groups):
        s = slice(j * n, (j + 1) * n)
        out_ref[:, s] = start_ref[:, s] + total[j * D : (j + 1) * D, :]


def unpack_kernel(own_ref, other_ref, w1_ref, w2_ref, wn1_ref, wn2_ref, biases_ref, gains_ref, pieces):
    unused, core = level_and_core()
    for p in range(4):
        pieces[core * 4 + p] = own_ref[p].astype(F32)
        pieces[(1 - core) * 4 + p] = other_ref[p].astype(F32)
    for k in range(2):
        w1_ref[k] = jnp.concatenate([pieces[4 * k], pieces[4 * k + 1, :, 0:D]], axis=1)
        w2_ref[k] = pieces[4 * k + 1, :, D : 2 * D]
        wn1_ref[k] = pieces[4 * k + 2]
        wn2_ref[k] = pieces[4 * k + 3, :, 0:D]
        rows = pieces[4 * k + 3].T
        for i in range(6):
            biases_ref[i, k : k + 1] = rows[D + i : D + i + 1]
        gains_ref[k] = rows[D + 6 : D + 8]


def shape(dims, dtype=F32):
    return jax.ShapeDtypeStruct(dims, dtype)


def call(kernel, name, outs, scratch, scalars=0, stored=(), streamed=None, final=(), raw=()):
    steps, stream_in, stream_out = streamed if streamed else (1, (), ())

    def run(*operands, after=()):
        def whole(space):
            return pl.BlockSpec(memory_space=space)

        def cut(x):
            return pl.BlockSpec((x.shape[0], x.shape[1] // steps), lambda i: (0, i))

        in_specs, placed = [], []
        for i, x in enumerate(operands):
            if i < scalars:
                in_specs.append(whole(pltpu.SMEM))
            elif i in stream_in:
                in_specs.append(cut(x))
            elif i in raw:
                in_specs.append(whole(pltpu.HBM))
                x = pltpu.with_memory_space_constraint(x, pltpu.HBM)
            else:
                in_specs.append(whole(pltpu.VMEM))
                x = pltpu.with_memory_space_constraint(x, pltpu.VMEM)
            placed.append(x)
        in_specs += [whole(pl.ANY) for _ in after]
        out_specs, out_shape = [], []
        for i, x in enumerate(outs):
            if i in stream_out:
                out_specs.append(cut(x))
                out_shape.append(x)
            elif i in stored:
                out_specs.append(whole(pl.ANY))
                out_shape.append(x)
            elif i in final:
                out_specs.append(whole(pltpu.VMEM))
                out_shape.append(x)
            else:
                out_specs.append(whole(pltpu.VMEM))
                out_shape.append(pltpu.VMEM(x.shape, x.dtype))
        return pl.pallas_call(
            kernel,
            name=name,
            grid=(steps,) if streamed else (),
            in_specs=in_specs,
            out_specs=out_specs,
            out_shape=out_shape,
            scratch_shapes=scratch,
            compiler_params=pltpu.CompilerParams(vmem_limit_bytes=VMEM_BYTES),
        )(*placed, *after)

    return run


def core_swap(block):
    return lax.ppermute(block, "band", [(i, i ^ 1) for i in range(lax.axis_size("band"))])


def cross_swap(block):
    last = lax.axis_size("band") - 1
    pairs = [(i, i + 1) for i in range(1, last, 2)]
    return lax.ppermute(block, "band", pairs + [(b, a) for a, b in pairs] + [(0, 0), (last, last)])


def along_level(block, step):
    count = lax.axis_size("level")
    return lax.ppermute(block, "level", [(i, (i + step) % count) for i in range(count)])


def along_band(block, step):
    count = lax.axis_size("band")
    return lax.ppermute(block, "band", [(i, (i + step) % count) for i in range(count)])


def across_bands(blocks):
    below, above, own = blocks
    return [along_band(above, 1), along_band(below, -1), own]


def along_levels(blocks, sign):
    return blocks + [along_level(jnp.stack([b[d] for b in blocks]), sign * d) for d in (1, 2, 3)]


def chip_ring(block, step, core_strides):
    count = lax.axis_size("band")
    pairs = []
    for i in range(count):
        stride = core_strides[i % 2]
        at = (i // stride) % 4
        pairs.append((i, i + (((at + step) % 4) - at) * stride))
    return lax.ppermute(block, "band", pairs)


def rounded(values):
    return lax.reduce_precision(values, 8, 7)


def sum_of_four(values, first, second, third):
    return (values + second.astype(F32)) + (first.astype(F32) + third.astype(F32))


def sum_along(values, core_strides):
    own = rounded(values)
    sent = own.astype(B16)
    return sum_of_four(own, *(chip_ring(sent, d, core_strides) for d in (1, 2, 3)))


def shards(
    lower_nodes, latent, up_feat, down_feat, up_send, up_counts, up_senders, up_targets,
    down_send, down_counts, down_senders, down_targets,
    edge_w1, edge_w2, node_w1, node_w2, biases, norm_gains, lower_cot, upper_cot,
):
    lower, upper = lower_nodes.T, latent.T
    feat_up, feat_down = up_feat.T, down_feat.T
    cot_lower, cot_upper = lower_cot.T, upper_cot.T
    w1, wn1 = edge_w1.transpose(0, 2, 1), node_w1.transpose(0, 2, 1)
    w2, wn2 = edge_w2, node_w2
    edges, lower_rows, upper_rows = up_feat.shape[0], lower_nodes.shape[0], latent.shape[0]
    dense = (edges // 128, 128)
    senders_up, targets_up, senders_down, targets_down = (
        x.reshape(dense) for x in (up_senders, up_targets, down_senders, down_targets))
    bias_rows = biases.transpose(1, 0, 2)

    lower_groups, lower_n = groups_of(lower_rows)
    upper_groups, upper_n = groups_of(upper_rows)
    lower_table, upper_table = (lower_groups * D, lower_n), (upper_groups * D, upper_n)
    slots = pltpu.VMEM((SLOT_GROUPS * D, SLOT_COLS), B16)
    block, four = shape((4, D, 128), B16), shape((4, D, 128))
    wide32, wide16, row = shape((D, edges)), shape((D, edges), B16), shape((1, edges))
    steps = edges // EDGE_BLOCK

    early = (up_send, lower, senders_up, targets_up, senders_down, targets_down, upper, w1, bias_rows, norm_gains,
             down_send, w2, wn1, wn2)
    count = len(early)
    (*sent, up_send, lower, senders_up, targets_up, senders_down, targets_down, upper, w1, bias_rows,
     norm_gains, down_send, w2, wn1, wn2) = call(
        functools.partial(send_kernel, count), "send_lower", [block] * 3 + [shape(x.shape, x.dtype) for x in early],
        [pltpu.VMEM(lower_table, B16), pltpu.SemaphoreType.DMA((count,))], 0, raw=range(count),
    )(*early)
    index, lives = shape((4, *dense), jnp.int32), shape((1, *dense))
    turned = [shape((2, D, 8)), shape((2, 3 * D, D), B16), shape((2, D, D), B16), shape((2, 2 * D, D), B16), shape((2, D, D), B16)]
    index_up, alive_up, index_down, alive_down, columns, w1t, w2t, wn1t, wn2t = call(
        functools.partial(tables_kernel, upper_rows, lower_rows), "edge_tables", [index, lives, index, lives] + turned,
        [pltpu.SMEM((1, 12), jnp.int32), pltpu.SMEM((1, 12), jnp.int32), pltpu.SemaphoreType.DMA((2,))], 0, raw=(0, 1),
    )(up_counts, down_counts, senders_up, targets_up, senders_down, targets_down, w1, w2, wn1, wn2, bias_rows, norm_gains)

    def part(k, block, first, size, name, table, index, feat, local, after):
        return call(
            functools.partial(part_kernel, k, block, first), name, [shape((D, size)), shape((2 * D, size), B16)],
            [pltpu.VMEM(table, B16), pltpu.SemaphoreType.DMA], 0, raw=(1,),
        )(index, feat, local, w1, columns, after=after)

    sent = [core_swap(sent[0]), cross_swap(sent[1]), sent[2]]
    half = edges // 2
    part_a, rows_a = part(1, half // 2, 0, half, "part_down_a", lower_table, index_down, feat_down, lower, ())
    sent, part_a = lax.optimization_barrier((sent, part_a))
    part_up, rows_up = part(0, EDGE_BLOCK, 0, edges, "part_up", upper_table, index_up, feat_up, upper, (sent[0], sent[1]))
    up_slots = along_levels(sent, 1)
    up_slots, part_up = lax.optimization_barrier((up_slots, part_up))
    (upper_new, summed_up, s0, s1, s2, slope, normed, hidden, factor, *nodes_up) = call(
        up_forward_kernel, "up_forward",
        [shape((D, upper_rows)), shape((D, upper_rows), B16)] + [block] * 3 + [wide32, wide32, wide16, row,
         shape((D, upper_rows), B16), shape((D, upper_rows)), shape((D, upper_rows)), shape((1, upper_rows))],
        [slots, pltpu.VMEM(upper_table, F32), pltpu.VMEM(upper_table, B16), pltpu.VMEM((D, upper_rows), F32),
         pltpu.SemaphoreType.DMA], 0, (0,),
    )(part_up, alive_up, index_up, *up_slots, upper, down_send, w1, w2t, wn1, wn2t, columns)
    sent = across_bands([s0, s1, s2])
    part_b, rows_b = part(1, half // 2, half, half, "part_down_b", lower_table, index_down, feat_down, lower, (sent[0], sent[1]))
    down_slots = along_levels(sent, 1)
    down_slots, part_b = lax.optimization_barrier((down_slots, part_b))
    sums_shape = shape((SLOT_GROUPS * D, SLOT_COLS))
    node16 = shape((D, lower_rows), B16)
    (lower_new, g0, g1, g2, first_down, second_down, hidden_down, sums_down, edge_sums, node_sums, *nodes) = call(
        down_kernel, "down_sweep",
        [shape((D, lower_rows))] + [block] * 3 + [wide16] * 3 + [sums_shape, four, four, shape(lower_table, B16),
         shape(lower_table, B16), node16, node16],
        [slots, pltpu.VMEM(lower_table, F32), pltpu.VMEM((D, edges), F32),
         pltpu.VMEM((D, edges), F32), pltpu.VMEM((1, edges), F32),
         pltpu.VMEM((D, lower_rows), F32), pltpu.SemaphoreType.DMA], 0, (0,),
    )(part_a, part_b, alive_down, index_down, *down_slots, lower, cot_lower, w1, w1t, w2, w2t, wn1, wn1t, wn2, wn2t, columns)
    back = across_bands([g0, g1, g2])
    (packed_down,) = call(
        down_rest_kernel, "down_rest", [four],
        [slots, pltpu.VMEM((D, 2 * D), F32), pltpu.VMEM((D, D), F32), pltpu.VMEM((D, 2 * D), F32), pltpu.VMEM((D, D), F32),
         pltpu.VMEM((4, D, 128), F32), pltpu.VMEM((4, D, 128), F32)], 0, (), (steps, (), ()),
    )(rows_a, rows_b, first_down, second_down, hidden_down, *down_slots, sums_down, edge_sums, node_sums, *nodes, lower,
      after=(back[0], back[1]))
    down_back = along_levels(back, -1)
    down_back, packed_down = lax.optimization_barrier((down_back, packed_down))
    (partner, cross, own, first_up, grad_latent, keep) = call(
        up_backward_kernel, "up_backward",
        [shape((8, D, 128), B16), block, block, wide16, shape((D, upper_rows)), four],
        [slots, pltpu.VMEM(upper_table, B16), pltpu.VMEM(upper_table, F32), pltpu.VMEM(upper_table, F32),
         pltpu.VMEM((SLOT_GROUPS * D, SLOT_COLS), F32), pltpu.VMEM((D, upper_rows), F32),
         pltpu.VMEM((D, 2 * D), F32), pltpu.VMEM((D, D), F32), pltpu.VMEM((4, D, 128), F32), pltpu.VMEM((4, D, 128), F32),
         pltpu.VMEM((D, 2 * D), F32), pltpu.VMEM((D, D), F32), pltpu.VMEM((8, D, 128), F32)], 0, (), None, (4,),
    )(index_up, rows_up, *down_back, down_send, cot_upper, upper, summed_up, *up_slots,
      slope, normed, hidden, factor, alive_up, packed_down, *nodes_up, w1t, w2, wn1t, wn2, columns)

    partner = core_swap(partner)
    total = rounded(rounded(keep) + partner[4:].astype(F32))
    cross, keep = lax.optimization_barrier((cross, total))
    cross = cross_swap(cross)
    total = sum_along(total, (2, 8))
    total, cross = lax.optimization_barrier((total, cross))
    blocks = (partner, cross, own)
    total = rounded(total)
    levels = [
        along_level(jnp.concatenate([jnp.stack([b[d] for b in blocks]), total.astype(B16)]), -d) for d in (1, 2, 3)
    ]
    (start_lower,) = call(
        down_targets_kernel, "down_targets", [shape((D, lower_rows))], [pltpu.VMEM(lower_table, F32)],
    )(index_down, first_down, cot_lower, nodes[0], w1t, wn1t, after=(total,))
    levels, start_lower = lax.optimization_barrier((levels, start_lower))
    total = sum_of_four(total, *(b[3:] for b in levels))
    (grad_lower,) = call(lower_grad_kernel, "lower_grad", [shape((D, lower_rows))], [pltpu.VMEM(lower_table, F32)], 0, (), None, (0,))(
        *blocks, *levels, up_send, start_lower)
    feat_grad_up, feat_grad_down = call(
        feat_grad_kernel, "feat_grads", [wide32, wide32], [], 0, (), (steps, (0, 1), (0, 1)),
    )(first_up, first_down, w1t, after=(levels[0],))
    total = sum_along(total, (8, 2))
    total, grad_lower, feat_grad_up = lax.optimization_barrier((total, grad_lower, feat_grad_up))
    total = rounded(total).astype(B16)
    w1_grad, w2_grad, wn1_grad, wn2_grad, bias_grad, gain_grad = call(
        unpack_kernel, "unpack",
        [shape((2, D, 3 * D)), shape((2, D, D)), shape((2, D, 2 * D)), shape((2, D, D)), shape((6, 2, D)), shape((2, 2, D))],
        [pltpu.VMEM((8, D, 128), F32)], 0, (), None, range(6))(total, core_swap(total))
    return (
        lower_new.T, upper_new.T, grad_lower.T, grad_latent.T, feat_grad_up.T, feat_grad_down.T,
        w1_grad.transpose(0, 2, 1), w2_grad, wn1_grad.transpose(0, 2, 1), wn2_grad, bias_grad.transpose(1, 0, 2), gain_grad,
    )


def solution(mesh):
    rows, index, whole = P(("band", "level"), None), P(("band", "level")), P()
    placed = (rows,) * 6 + (index, index) + (rows,) * 2 + (index, index) + (whole,) * 6 + (rows,) * 2
    return jax.shard_map(
        shards,
        mesh=mesh,
        in_specs=placed,
        out_specs=(rows,) * 6 + (whole,) * 6,
        check_vma=False,
    )
```
